32 devices in a mesh: dp: 32 (over z, y, x, core).
Axes of the slice: x: 2, y: 2, z: 4, core: 2. Of those that a mesh axis runs over, the one named last changes fastest.
Arguments:
- images: float32 [192, 196, 768], P('dp'), may hold values from -6 to 6
- mask: int32 [192], P('dp'), may hold values 0 or 1
- cotangent: float32 [192, 196, 768], P('dp'), may hold values from -6 to 6
- w_token_in: float32 [75264], P('dp'), may hold values from -0.4375 to 0.4375
- w_token_out: float32 [75264], P('dp'), may hold values from -0.3125 to 0.3125
- bias_token_in: float32 [384], replicated, may hold values from -3 to 3
- bias_token_out: float32 [196], replicated, may hold values from -3 to 3
- gain_one: float32 [768], P('dp'), may hold values from 0.1 to 1.9
- shift_one: float32 [768], P('dp'), may hold values from -3 to 3
- gain_two: float32 [768], P('dp'), may hold values from 0.1 to 1.9
- shift_two: float32 [768], P('dp'), may hold values from -3 to 3
- w_expand: float32 [3072, 768], P('dp'), may hold values from -0.21875 to 0.21875
- bias_expand: float32 [3072], P('dp'), may hold values from -3 to 3
- w_reduce: float32 [3072, 768], P('dp'), may hold values from -0.109375 to 0.109375
- bias_reduce: float32 [768], P('dp'), may hold values from -3 to 3
Outputs:
- block_output: float32 [192, 196, 768], P('dp')
- image_grad: float32 [192, 196, 768], P('dp')
- grad_token_in: float32 [75264], P('dp')
- grad_token_out: float32 [75264], P('dp')
- grad_bias_token_in: float32 [384], replicated
- grad_bias_token_out: float32 [196], replicated
- grad_gain_one: float32 [768], P('dp')
- grad_shift_one: float32 [768], P('dp')
- grad_gain_two: float32 [768], P('dp')
- grad_shift_two: float32 [768], P('dp')
- grad_expand: float32 [3072, 768], P('dp')
- grad_bias_expand: float32 [3072], P('dp')
- grad_reduce: float32 [3072, 768], P('dp')
- grad_bias_reduce: float32 [768], P('dp')
The draws below stay inside these ranges and needn't reach their ends.
All inputs are finite; a program needn't handle non-finite values. No bound on the sum of `mask` on one device may be relied on, other than what follows from the above.
Results may differ from the reference program's by a relative error of at most 0.0095.
Values may be sent and summed in bfloat16 or wider, within the bound.
A program may use at most 192 MiB of HBM per device.

```python
import jax
import jax.numpy as jnp
from jax import lax

D = 768
DC = 3072
DS = 384
P_SIZE = 196
IMAGES = 192


def place_ends(entries, rng, smallest, high):
    extent = entries.shape
    spot = [jax.random.randint(jax.random.fold_in(rng, axis), (), 0, extent[axis]) for axis in range(len(extent))]
    entries = entries.at[tuple(spot)].set(smallest)
    longest = extent.index(max(extent))
    spot[longest] = (spot[longest] + 1) % extent[longest]
    return entries.at[tuple(spot)].set(high)


def strengthened(result, key, source, target, parts, factor):
    def block_of(axis_at):
        return (jnp.arange(result.shape[axis_at]) // (result.shape[axis_at] // parts)).reshape((-1,) + (1,) * (result.ndim - 1 - axis_at))

    first = jax.random.permutation(key, parts)[block_of(target)]
    other_side = (block_of(target) + parts // 2) % parts
    return jnp.where((block_of(source) == first) | (block_of(source) == other_side), factor * result, result)


def level_of(rng, shape, split, smallest, largest):
    gain, own = 1.0, jax.random.fold_in(rng, 6)
    for axis_at, blocks in split:
        steps = jnp.exp(jax.random.uniform(jax.random.fold_in(own, axis_at), (blocks,), jnp.float32, smallest / len(split), largest / len(split)))
        gain = gain * jnp.repeat(steps, shape[axis_at] // blocks).reshape([-1 if axis == axis_at else 1 for axis in range(len(shape))])
    return gain


def normal_values(own_key, extent, width, limit, pieces=(), held_as=jnp.bfloat16):
    gain = level_of(own_key, extent, pieces, -0.22, 0.18) if pieces else 1.0
    result = jax.random.normal(own_key, extent, jnp.float32) * width * gain
    return jnp.minimum(jnp.maximum(result, -limit), limit).astype(held_as)


def heavy_noise(stream_key, shape, scale, bound, split, heavy, dtype=jnp.bfloat16):
    drawn = scale * jax.random.normal(stream_key, shape, jnp.float32)
    if split:
        drawn = drawn * level_of(stream_key, shape, split, -0.22, 0.18)
    return jnp.clip(strengthened(drawn, jax.random.fold_in(stream_key, 3), *heavy), -bound, bound).astype(dtype)


def setup_inputs(seed: int = 0) -> dict:
    splits = jax.random.split(jax.random.key(seed), 16)
    return {
        "images": normal_values(splits[0], (IMAGES, P_SIZE, D), 1.0, 6.0, ((0, 32),), jnp.float32),
        "mask": place_ends((jax.random.randint(splits[1], (IMAGES,), 0, 4) < 3).astype(jnp.int32), jax.random.fold_in(splits[1], 1), 0, 1),
        "cotangent": heavy_noise(splits[2], (IMAGES, P_SIZE, D), 1.0, 6.0, ((0, 32),), (0, 2, 32, 2.75), jnp.float32),
        "w_token_in": normal_values(splits[3], (P_SIZE * DS,), P_SIZE ** -0.5, 0.4375, ((0, 32),), jnp.float32),
        "w_token_out": normal_values(splits[4], (DS * P_SIZE,), DS ** -0.5, 0.3125, ((0, 32),), jnp.float32),
        "bias_token_in": normal_values(splits[5], (DS,), 0.5, 3.0, (), jnp.float32),
        "bias_token_out": normal_values(splits[6], (P_SIZE,), 0.5, 3.0, (), jnp.float32),
        "gain_one": jnp.clip(1.0 + 0.18 * jax.random.normal(splits[7], (D,), jnp.float32), 0.1, 1.9),
        "shift_one": normal_values(splits[8], (D,), 0.5, 3.0, ((0, 32),), jnp.float32),
        "gain_two": jnp.clip(1.0 + 0.18 * jax.random.normal(splits[9], (D,), jnp.float32), 0.1, 1.9),
        "shift_two": normal_values(splits[10], (D,), 0.5, 3.0, ((0, 32),), jnp.float32),
        "w_expand": normal_values(splits[11], (DC, D), D ** -0.5, 0.21875, ((0, 32),), jnp.float32),
        "bias_expand": normal_values(splits[12], (DC,), 0.5, 3.0, ((0, 32),), jnp.float32),
        "w_reduce": normal_values(splits[13], (DC, D), DC ** -0.5, 0.109375, ((0, 32),), jnp.float32),
        "bias_reduce": normal_values(splits[14], (D,), 0.5, 3.0, ((0, 32),), jnp.float32),
    }


@jax.custom_vjp
def low(v):
    return lax.optimization_barrier(v.astype(jnp.bfloat16)).astype(jnp.float32)

@jax.custom_vjp
def low_back(v):
    return v

def low_keep(v):
    return (low(v), None)

def low_pass(kept, grad):
    return (grad,)

def back_keep(v):
    return (v, None)

def back_low(kept, grad):
    return (low(grad),)
low.defvjp(low_keep, low_pass)
low_back.defvjp(back_keep, back_low)
EPS = 1e-06
HIGH = lax.Precision.HIGHEST

def gelu_exact(v):
    return 0.5 * v * (1.0 + lax.erf(v * 0.7071067811865476))

def layer_norm(v):
    centered = v - lax.optimization_barrier(jnp.mean(v, axis=-1, keepdims=True))
    return centered * lax.rsqrt(lax.optimization_barrier(jnp.mean(centered * centered, axis=-1, keepdims=True)) + EPS)

def block_fn(params, images_blk, keep_blk):
    tin, tout, c_one, c_two, g_one, b_one, g_two, b_two, w_in, c_in, w_out, c_four = params
    mixed_in = low(layer_norm(images_blk) * g_one + b_one)
    pre_t = low_back(jnp.einsum('ps,bpd->bsd', tin, mixed_in, precision=HIGH) + c_one[None, :, None])
    act_t = low(gelu_exact(pre_t))
    back = low_back(jnp.einsum('sp,bsd->bpd', tout, act_t, precision=HIGH) + c_two[None, :, None])
    middle = images_blk + back
    zed = low(layer_norm(middle) * g_two + b_two)
    pre_c = low_back(jnp.einsum('bpd,fd->bpf', zed, w_in, precision=HIGH) + c_in)
    act_c = low(gelu_exact(pre_c))
    branch = low_back(jnp.einsum('bpf,fd->bpd', act_c, w_out, precision=HIGH) + c_four)
    return (middle + branch) * keep_blk[:, None, None]

def reference(images, mask, cotangent, w_token_in, w_token_out, bias_token_in, bias_token_out, gain_one, shift_one, gain_two, shift_two, w_expand, bias_expand, w_reduce, bias_reduce):
    keep = mask.astype(jnp.float32)
    blocks = IMAGES // 16
    params = (w_token_in.reshape(P_SIZE, DS), w_token_out.reshape(DS, P_SIZE), bias_token_in, bias_token_out, gain_one, shift_one, gain_two, shift_two, w_expand, bias_expand, w_reduce, bias_reduce)

    def forward(images_all, params_all):
        tin, tout, c_one, c_two, g_one, b_one, g_two, b_two, w_in, c_in, w_out, c_four = params_all
        rounded = (low(tin), low(tout), c_one, c_two, low(g_one), low(b_one), low(g_two), low(b_two), low(w_in), low(c_in), low(w_out), low(c_four))
        step = jax.checkpoint(lambda blk: block_fn(rounded, blk[0], blk[1]))
        return lax.map(step, (images_all.reshape(blocks, 16, P_SIZE, D), keep.reshape(blocks, 16)))
    outputs, pull = jax.vjp(forward, images, params)
    image_grad, grads = pull(cotangent.reshape(blocks, 16, P_SIZE, D))
    g_tin, g_tout, g_c1, g_c2, g_g1, g_b1, g_g2, g_b2, g_win, g_cin, g_wout, g_c4 = grads
    return (outputs.reshape(IMAGES, P_SIZE, D), image_grad, g_tin.reshape(P_SIZE * DS), g_tout.reshape(DS * P_SIZE), g_c1, g_c2, g_g1, g_b1, g_g2, g_b2, g_win, g_cin, g_wout, g_c4)
```

```python
import jax
import jax.numpy as jnp
from jax import lax
from jax.experimental import pallas as pl
from jax.experimental.pallas import tpu as pltpu
from jax.sharding import PartitionSpec as P

EPS = 1e-06


def gelu_exact(v):
    return 0.5 * v * (1.0 + lax.erf(v * 0.7071067811865476))


def gelu_slope(v):
    return 0.5 * (1.0 + lax.erf(v * 0.7071067811865476)) + v * 0.3989422804014327 * jnp.exp(
        -0.5 * v * v
    )


def normalize(v):
    centered = v - jnp.mean(v, axis=-1, keepdims=True)
    scale = lax.rsqrt(jnp.mean(centered * centered, axis=-1, keepdims=True) + EPS)
    return (centered * scale, scale)


def norm_back(grad_in, normed, scale, gain):
    scaled = grad_in * gain
    return scale * (
        scaled
        - jnp.mean(scaled, axis=-1, keepdims=True)
        - normed * jnp.mean(scaled * normed, axis=-1, keepdims=True)
    )


WIDE = jnp.float32
LOW = jnp.bfloat16
MESH = pl.DeviceIdType.MESH
NT = (((1,), (1,)), ((), ()))
TN = (((0,), (0,)), ((), ()))
NN = (((1,), (0,)), ((), ()))
PLANE = 8


def dot(a, b, dims):
    return lax.dot_general(a, b, dims, preferred_element_type=WIDE)


def gelu_parts(v):
    cdf = 0.5 * (1.0 + lax.erf(v * 0.7071067811865476))
    return v * cdf, cdf + v * 0.3989422804014327 * jnp.exp(-0.5 * v * v)


def padded(v, rows):
    return jnp.concatenate([v, jnp.zeros((rows - v.shape[0], v.shape[1]), v.dtype)], axis=0)


def block_kernel(
    mask,
    images,
    cotangent,
    w_in,
    w_out,
    tin,
    tin_t,
    tout,
    tout_t,
    vecs,
    c_one,
    c_two,
    c_in,
    block_out,
    image_grad,
    grad_in,
    grad_out,
    grad_tin,
    grad_tout,
    grad_c_one,
    grad_c_two,
    grad_vecs,
    grad_c_in,
    im,
    cot,
    mixed,
    act_t,
    slope_t,
    mid,
    total,
    grad_zed,
    zed,
    top,
    weights,
    act,
    grad_pre,
    c_in_rel,
    own_sum,
    keep_sum,
    send_one,
    recv_one,
    send_two,
    recv_two,
    send_three,
    recv_three,
    send_four,
    recv_four,
    in_sem,
    out_sem,
    ag_send,
    ag_recv,
    rs_send,
    rs_recv,
):
    count, patches, width = im.shape
    planes = weights.shape[1]
    shard = w_in.shape[0]
    half = 4 * shard
    chunk = 8 * shard
    pad = mixed.shape[1]
    pair = zed.shape[1]
    lot = pair // 2
    blocks = count // 2
    me = lax.axis_index("dp")
    core = me % 2
    col = (me // 2) % 2
    row = (me // 4) % 2
    z = me // PLANE
    by_core = me + 1 - 2 * core
    by_x = me + 2 - 4 * col
    by_y = me + 4 - 8 * row

    def plane_of(k):
        out, bit = z, 1
        while bit < planes:
            out = out + bit * ((k // bit) % 2) * (1 - 2 * ((z // bit) % 2))
            bit *= 2
        return out

    def by_z(k):
        return me + PLANE * (plane_of(k) - z)

    def ag(stage, k, mat):
        near, far = (by_x, by_y) if mat == 0 else (by_y, by_x)
        step = 1 if mat == 0 else 2
        if stage == 0:
            src, dst, size, to = 0, 0, shard, by_z(k)
            source = weights.at[mat, 0, pl.ds(src, size)]
        else:
            src, dst, size, to = {
                1: (0, step * shard, shard, near),
                2: (0, (3 - step) * shard, shard, far),
                3: (step * shard, 3 * shard, shard, far),
                4: (0, half, half, by_core),
            }[stage]
            source = weights.at[mat, k, pl.ds(src, size)]
        return pltpu.make_async_remote_copy(
            src_ref=source,
            dst_ref=weights.at[mat, k, pl.ds(dst, size)],
            send_sem=ag_send.at[stage, k, mat],
            recv_sem=ag_recv.at[stage, k, mat],
            device_id=(to,),
            device_id_type=MESH,
        )

    def rs(stage, k, mat):
        slot = k % 2
        near, far = (by_x, by_y) if mat == 0 else (by_y, by_x)
        src, dst, to = [
            lambda: (send_one.at[mat], recv_one.at[slot, mat], by_core),
            lambda: (send_two.at[mat], recv_two.at[slot, mat], near),
            lambda: (send_three.at[mat], recv_three.at[slot, mat], far),
            lambda: (send_four.at[slot, mat], recv_four.at[k, mat], by_z(k)),
        ][stage]()
        return pltpu.make_async_remote_copy(
            src_ref=src,
            dst_ref=dst,
            send_sem=rs_send.at[stage, k, mat],
            recv_sem=rs_recv.at[stage, k, mat],
            device_id=(to,),
            device_id_type=MESH,
        )

    def load(b):
        return (
            pltpu.make_async_copy(images.at[b], im.at[b], in_sem.at[0, b]),
            pltpu.make_async_copy(cotangent.at[b], cot.at[b], in_sem.at[1, b]),
        )

    for b in range(count):
        for copy in load(b):
            copy.start()
    weights[0, 0, 0:shard] = w_in[...].astype(LOW)
    weights[1, 0, 0:shard] = w_out[...].astype(LOW)

    barrier = pltpu.get_barrier_semaphore()
    peers = [by_core, by_x, by_y] + [by_z(k) for k in range(1, planes)]
    for peer in peers:
        pl.semaphore_signal(barrier, inc=1, device_id=(peer,), device_id_type=MESH)
    pl.semaphore_wait(barrier, len(peers))

    mats = (0, 1)

    def ag_direct(k):
        for mat in mats:
            ag(1, k, mat).start()
        for mat in mats:
            ag(2, k, mat).start()

    def ag_forward(k):
        for mat in mats:
            ag(1, k, mat).wait_recv()
            ag(3, k, mat).start()

    def ag_core(k):
        for mat in mats:
            ag(2, k, mat).wait_recv()
            ag(3, k, mat).wait_recv()
            ag(4, k, mat).start()

    def ag_plane(k):
        for mat in mats:
            ag(0, k, mat).wait_recv()
        ag_direct(k)

    def ag_plane_next(k):
        for mat in mats:
            ag(0, k, mat).start()

    def ag_ready(k):
        for mat in mats:
            ag(4, k, mat).wait_recv()

    ag_direct(0)
    ag_plane_next(1)

    gain_one, shift_one = vecs[0:1, :], vecs[1:2, :]
    gain_two, shift_two, c_four = vecs[2:3, :], vecs[3:4, :], vecs[4:5, :]
    for k in range(planes):
        for place in range(PLANE):
            near = plane_of(k) * PLANE + (
                (row + (place // 2) % 2) % 2 * 4 + (col + place % 2) % 2 * 2 + (core + place // 4) % 2
            )
            c_in_rel[k, :, place * shard : (place + 1) * shard] = c_in[near]

    grad_vecs[...] = jnp.zeros_like(grad_vecs)
    grad_tin[...] = jnp.zeros_like(grad_tin)
    grad_tout[...] = jnp.zeros_like(grad_tout)
    grad_c_one[...] = jnp.zeros_like(grad_c_one)
    grad_c_two[...] = jnp.zeros_like(grad_c_two)

    def token_forward(b, carry):
        for copy in load(b):
            copy.wait()
        x = im[b]
        normed, _ = normalize(x)
        mixed[b] = padded(normed * gain_one + shift_one, pad).astype(LOW)
        pre_t = dot(tin_t[...], mixed[b], NN) + c_one[...]
        value, slope = gelu_parts(pre_t)
        act_t[b] = value.astype(LOW)
        slope_t[b] = slope.astype(LOW)
        mid[b] = x + dot(tout_t[...], act_t[b], NN)[0:patches] + c_two[...]
        return carry

    def channel_inputs(r, carry):
        parts, tops = [], []
        for h in range(2):
            b = 2 * r + h
            keep = mask[b].astype(WIDE)
            normed, _ = normalize(mid[b])
            parts.append(padded(normed * gain_two + shift_two, lot))
            tops.append(padded(cot[b] * keep, lot))
        zed[r] = jnp.concatenate(parts, axis=0).astype(LOW)
        top[r] = jnp.concatenate(tops, axis=0).astype(LOW)
        grad_vecs[4:5, :] += jnp.sum(top[r].astype(WIDE), axis=0, keepdims=True)
        return carry

    lax.fori_loop(0, 2, token_forward, 0)
    ag_forward(0)
    lax.fori_loop(2, 4, token_forward, 0)
    ag_plane(1)
    ag_plane_next(2)
    lax.fori_loop(4, count, token_forward, 0)
    ag_core(0)
    ag_forward(1)
    lax.fori_loop(0, blocks, channel_inputs, 0)
    total[...] = jnp.zeros_like(total)
    grad_zed[...] = jnp.zeros_like(grad_zed)

    def rs_two(k):
        for mat in mats:
            rs(0, k, mat).wait_recv()
            own_sum[mat] += recv_one[k % 2, mat].astype(WIDE)
            if mat == 0:
                first, second = (1, 2), (3, 4)
            else:
                first, second = (2, 3), (3, 4)

            @pl.when(k > 0)
            def _():
                rs(1, k - 1, mat).wait_send()

            send_two[mat, 0:shard] = own_sum[mat, first[0] * shard : first[1] * shard].astype(LOW)
            send_two[mat, shard : 2 * shard] = own_sum[mat, second[0] * shard : second[1] * shard].astype(LOW)
            rs(1, k, mat).start()

    def rs_three(k):
        for mat in mats:
            rs(1, k, mat).wait_recv()
            other = 2 if mat == 0 else 1

            @pl.when(k > 0)
            def _():
                rs(2, k - 1, mat).wait_send()

            keep_sum[mat] = own_sum[mat, 0:shard] + recv_two[k % 2, mat, 0:shard].astype(WIDE)
            send_three[mat] = (
                own_sum[mat, other * shard : (other + 1) * shard]
                + recv_two[k % 2, mat, shard : 2 * shard].astype(WIDE)
            ).astype(LOW)
            rs(2, k, mat).start()

    def rs_four(k):
        for mat in mats:
            rs(2, k, mat).wait_recv()
            summed = keep_sum[mat] + recv_three[k % 2, mat].astype(WIDE)
            result = grad_in if mat == 0 else grad_out

            @pl.when(k == 0)
            def _():
                result[...] = summed

            @pl.when(k > 0)
            def _():
                @pl.when(k > 2)
                def _():
                    rs(3, k - 2, mat).wait_send()

                send_four[k % 2, mat] = summed.astype(LOW)
                rs(3, k, mat).start()

    def rs_last():
        for mat in mats:
            result = grad_in if mat == 0 else grad_out
            for k in range(1, planes):
                rs(3, k, mat).wait_recv()
                result[...] += recv_four[k, mat].astype(WIDE)

    tile = chunk // 3

    def channel_chunk(k, carry):
        ag_ready(k)

        def rows(r, inner):
            for s in range(3):
                part = slice(s * tile, (s + 1) * tile)
                pre = dot(zed[r], weights[0, k, part], NT) + c_in_rel[k, :, part]
                value, slope = gelu_parts(pre)
                act[pl.ds(r * pair, pair), part] = value.astype(LOW)
                back = (dot(top[r], weights[1, k, part], NT) * slope).astype(LOW)
                grad_pre[pl.ds(r * pair, pair), part] = back
            up = dot(act[pl.ds(r * pair, pair), :], weights[1, k], NN)
            down = dot(grad_pre[pl.ds(r * pair, pair), :], weights[0, k], NN)
            for h in range(2):
                total[2 * r + h] += up[h * lot : h * lot + patches]
                grad_zed[2 * r + h] += down[h * lot : h * lot + patches]

            @pl.when((r == 0) & (k + 1 < planes) & (k > 0))
            def _():
                ag_forward(k + 1)

            @pl.when((r == 2) & (k > 0))
            def _():
                rs_three(k - 1)

            return inner

        lax.fori_loop(0, blocks, rows, 0)

        @pl.when(k + 1 < planes)
        def _():
            ag_core(k + 1)

        @pl.when(k + 2 < planes)
        def _():
            ag_plane(k + 2)

        @pl.when(k + 3 < planes)
        def _():
            ag_plane_next(k + 3)

        back_sum = jnp.sum(grad_pre[...].astype(WIDE), axis=0, keepdims=True)
        for place in range(PLANE):
            near = plane_of(k) * PLANE + (
                (row + (place // 2) % 2) % 2 * 4 + (col + place % 2) % 2 * 2 + (core + place // 4) % 2
            )
            grad_c_in[near] = back_sum[:, place * shard : (place + 1) * shard]

        flat_top = top[...].reshape(blocks * pair, width)
        flat_zed = zed[...].reshape(blocks * pair, width)
        for mat, left, right in ((1, act, flat_top), (0, grad_pre, flat_zed)):
            @pl.when(k > 0)
            def _():
                rs(0, k - 1, mat).wait_send()

            send_one[mat] = dot(left[:, half:chunk], right, TN).astype(LOW)
            rs(0, k, mat).start()

        @pl.when(k > 0)
        def _():
            rs_four(k - 1)

        for mat, left, right in ((1, act, flat_top), (0, grad_pre, flat_zed)):
            own_sum[mat] = dot(left[:, 0:half], right, TN)
        rs_two(k)
        return carry

    lax.fori_loop(0, planes, channel_chunk, 0)

    def store(b):
        return (
            pltpu.make_async_copy(total.at[b], block_out.at[b], out_sem.at[0, b]),
            pltpu.make_async_copy(grad_zed.at[b], image_grad.at[b], out_sem.at[1, b]),
        )

    def token_backward(b, carry):
        keep = mask[b].astype(WIDE)
        total[b] = (mid[b] + total[b] + c_four) * keep
        store(b)[0].start()
        normed, scale = normalize(mid[b])
        down = grad_zed[b]
        grad_vecs[2:3, :] += jnp.sum(down * normed, axis=0, keepdims=True)
        grad_vecs[3:4, :] += jnp.sum(down, axis=0, keepdims=True)
        grad_mid = cot[b] * keep + norm_back(down, normed, scale, gain_two)
        back = padded(grad_mid, pad).astype(LOW)
        grad_c_two[...] += jnp.sum(back.astype(WIDE), axis=1, keepdims=True)
        grad_tout[...] += dot(act_t[b], back, NT)
        back_t = (dot(tout[...], back, NN) * slope_t[b].astype(WIDE)).astype(LOW)
        grad_c_one[...] += jnp.sum(back_t.astype(WIDE), axis=1, keepdims=True)
        grad_tin[...] += dot(mixed[b], back_t, NT)
        grad_mixed = dot(tin[...], back_t, NN)[0:patches]
        normed, scale = normalize(im[b])
        grad_vecs[0:1, :] += jnp.sum(grad_mixed * normed, axis=0, keepdims=True)
        grad_vecs[1:2, :] += jnp.sum(grad_mixed, axis=0, keepdims=True)
        grad_zed[b] = grad_mid + norm_back(grad_mixed, normed, scale, gain_one)
        store(b)[1].start()

        @pl.when(b == count // 2)
        def _():
            rs_three(planes - 1)

        return carry

    lax.fori_loop(0, count, token_backward, 0)
    rs_four(planes - 1)
    rs_last()

    for mat in mats:
        for k in range(planes):
            for stage in range(5):
                if stage > 0 or k > 0:
                    ag(stage, k, mat).wait_send()
        for stage in range(3):
            rs(stage, planes - 1, mat).wait_send()
        for k in range(max(1, planes - 2), planes):
            rs(3, k, mat).wait_send()
    for b in range(count):
        for copy in store(b):
            copy.wait()


def fast_shards(
    images,
    mask,
    cotangent,
    w_token_in,
    w_token_out,
    bias_token_in,
    bias_token_out,
    gain_one,
    shift_one,
    gain_two,
    shift_two,
    w_expand,
    bias_expand,
    w_reduce,
    bias_reduce,
):
    devices = lax.axis_size("dp")
    planes = devices // PLANE
    count, patches, width = images.shape
    hidden_tok = bias_token_in.shape[0]
    shard = w_expand.shape[0]
    pad = -(-patches // 16) * 16
    lot = -(-patches // 8) * 8
    pair = 2 * lot
    blocks = count // 2
    chunk = 8 * shard
    half = 4 * shard

    small = [w_token_in, w_token_out, gain_one, shift_one, gain_two, shift_two, bias_reduce, bias_expand]
    sizes = [piece.shape[0] for piece in small]
    packed = jnp.concatenate([piece.astype(LOW) for piece in small])
    gathered = lax.all_gather(packed, "dp", axis=0)
    ends = [sum(sizes[: i + 1]) for i in range(len(sizes))]
    pieces = [gathered[:, end - size : end].reshape(-1) for end, size in zip(ends, sizes)]
    tin = jnp.pad(pieces[0].reshape(patches, hidden_tok), ((0, pad - patches), (0, 0)))
    tout = jnp.pad(pieces[1].reshape(hidden_tok, patches), ((0, 0), (0, pad - patches)))
    vecs = jnp.concatenate([jnp.stack(pieces[2:7]), jnp.zeros((3, width), LOW)]).astype(WIDE)
    c_in = pieces[7].reshape(devices, 1, shard).astype(WIDE)

    vmem = pl.BlockSpec(memory_space=pltpu.VMEM)
    hbm = pl.BlockSpec(memory_space=pl.ANY)
    shape = jax.ShapeDtypeStruct
    outs = pl.pallas_call(
        block_kernel,
        out_shape=(
            shape(images.shape, WIDE),
            shape(images.shape, WIDE),
            shape(w_expand.shape, WIDE),
            shape(w_reduce.shape, WIDE),
            shape((pad, hidden_tok), WIDE),
            shape((hidden_tok, pad), WIDE),
            shape((hidden_tok, 1), WIDE),
            shape((pad, 1), WIDE),
            shape((8, width), WIDE),
            shape((devices, 1, shard), WIDE),
        ),
        in_specs=[pl.BlockSpec(memory_space=pltpu.SMEM), hbm, hbm] + [vmem] * 10,
        out_specs=[hbm, hbm] + [vmem] * 8,
        scratch_shapes=[
            pltpu.VMEM(images.shape, WIDE),
            pltpu.VMEM(images.shape, WIDE),
            pltpu.VMEM((count, pad, width), LOW),
            pltpu.VMEM((count, hidden_tok, width), LOW),
            pltpu.VMEM((count, hidden_tok, width), LOW),
            pltpu.VMEM(images.shape, WIDE),
            pltpu.VMEM(images.shape, WIDE),
            pltpu.VMEM(images.shape, WIDE),
            pltpu.VMEM((blocks, pair, width), LOW),
            pltpu.VMEM((blocks, pair, width), LOW),
            pltpu.VMEM((2, planes, chunk, width), LOW),
            pltpu.VMEM((blocks * pair, chunk), LOW),
            pltpu.VMEM((blocks * pair, chunk), LOW),
            pltpu.VMEM((planes, 1, chunk), WIDE),
            pltpu.VMEM((2, half, width), WIDE),
            pltpu.VMEM((2, shard, width), WIDE),
            pltpu.VMEM((2, half, width), LOW),
            pltpu.VMEM((2, 2, half, width), LOW),
            pltpu.VMEM((2, 2 * shard, width), LOW),
            pltpu.VMEM((2, 2, 2 * shard, width), LOW),
            pltpu.VMEM((2, shard, width), LOW),
            pltpu.VMEM((2, 2, shard, width), LOW),
            pltpu.VMEM((2, 2, shard, width), LOW),
            pltpu.VMEM((planes, 2, shard, width), LOW),
            pltpu.SemaphoreType.DMA((2, count)),
            pltpu.SemaphoreType.DMA((2, count)),
            pltpu.SemaphoreType.DMA((5, planes, 2)),
            pltpu.SemaphoreType.DMA((5, planes, 2)),
            pltpu.SemaphoreType.DMA((4, planes, 2)),
            pltpu.SemaphoreType.DMA((4, planes, 2)),
        ],
        compiler_params=pltpu.CompilerParams(
            collective_id=0, has_side_effects=True, vmem_limit_bytes=63 * 2**20
        ),
    )(
        mask,
        images,
        cotangent,
        w_expand,
        w_reduce,
        tin,
        tin.T,
        tout,
        tout.T,
        vecs,
        bias_token_in[:, None],
        bias_token_out[:, None],
        c_in,
    )
    block_output, image_grad, own_win, own_wout, g_tin, g_tout, g_c1, g_c2, g_vecs, g_cin = outs
    bias_sums = lax.psum((g_c1[:, 0], g_c2[:patches, 0]), "dp")
    flat = [
        g_tin[:patches].reshape(devices, -1),
        g_tout[:, :patches].reshape(devices, -1),
        *[g_vecs[i].reshape(devices, -1) for i in range(5)],
        g_cin.reshape(devices, -1),
    ]
    mine = lax.psum_scatter(jnp.concatenate(flat, axis=1), "dp", scatter_dimension=0, tiled=True)[0]
    own = [mine[end - size : end] for end, size in zip(ends, sizes)]
    return (
        block_output,
        image_grad,
        own[0],
        own[1],
        bias_sums[0],
        bias_sums[1],
        own[2],
        own[3],
        own[4],
        own[5],
        own_win,
        own[7],
        own_wout,
        own[6],
    )


def fits(devices):
    planes = devices // PLANE
    return devices % PLANE == 0 and planes & (planes - 1) == 0 and planes >= 2


def choose(
    images,
    mask,
    cotangent,
    w_token_in,
    w_token_out,
    bias_token_in,
    bias_token_out,
    gain_one,
    shift_one,
    gain_two,
    shift_two,
    w_expand,
    bias_expand,
    w_reduce,
    bias_reduce,
):
    args = (
        images,
        mask,
        cotangent,
        w_token_in,
        w_token_out,
        bias_token_in,
        bias_token_out,
        gain_one,
        shift_one,
        gain_two,
        shift_two,
        w_expand,
        bias_expand,
        w_reduce,
        bias_reduce,
    )
    shard = w_expand.shape[0]
    whole = shard % 16 == 0 and (4 * shard) % 128 == 0 and images.shape[0] % 2 == 0
    if fits(lax.axis_size("dp")) and whole:
        return fast_shards(*args)
    return shards(*args)


def shards(
    images,
    mask,
    cotangent,
    w_token_in,
    w_token_out,
    bias_token_in,
    bias_token_out,
    gain_one,
    shift_one,
    gain_two,
    shift_two,
    w_expand,
    bias_expand,
    w_reduce,
    bias_reduce,
):
    low_type = jnp.bfloat16
    wide = jnp.float32
    count, patches, width = images.shape
    hidden_tok = bias_token_in.shape[0]
    rows = count * patches
    keep = mask.astype(wide)[:, None, None]
    small_local = (
        w_token_in.astype(low_type),
        w_token_out.astype(low_type),
        gain_one.astype(low_type),
        shift_one.astype(low_type),
        gain_two.astype(low_type),
        shift_two.astype(low_type),
        bias_reduce.astype(low_type),
    )
    channel_local = (
        w_expand.astype(low_type),
        w_reduce.astype(low_type),
        bias_expand.astype(low_type),
    )
    small_all = (
        lax.all_gather(small_local[0], "dp", axis=0, tiled=True),
        lax.all_gather(small_local[1], "dp", axis=0, tiled=True),
        lax.all_gather(small_local[2], "dp", axis=0, tiled=True),
        lax.all_gather(small_local[3], "dp", axis=0, tiled=True),
        lax.all_gather(small_local[4], "dp", axis=0, tiled=True),
        lax.all_gather(small_local[5], "dp", axis=0, tiled=True),
        lax.all_gather(small_local[6], "dp", axis=0, tiled=True),
    )
    tin = small_all[0].reshape(patches, hidden_tok)
    tout = small_all[1].reshape(hidden_tok, patches)
    g_one, b_one, g_two, b_two, c_four = [piece.astype(wide) for piece in small_all[2:]]
    normed_one, scale_one = normalize(images)
    mixed_in = (normed_one * g_one + b_one).astype(low_type)
    pre_t = (
        jnp.einsum("ps,bpd->bsd", tin, mixed_in, preferred_element_type=wide)
        + bias_token_in[None, :, None]
    )
    act_t = gelu_exact(pre_t).astype(low_type)
    middle = (
        images
        + jnp.einsum("sp,bsd->bpd", tout, act_t, preferred_element_type=wide)
        + bias_token_out[None, :, None]
    )
    normed_two, scale_two = normalize(middle.reshape(rows, width))
    zed = (normed_two * g_two + b_two).astype(low_type)
    whole_channel = (
        lax.all_gather(channel_local[0], "dp", axis=0, tiled=True),
        lax.all_gather(channel_local[1], "dp", axis=0, tiled=True),
        lax.all_gather(channel_local[2], "dp", axis=0, tiled=True),
    )
    w_in, w_out, c_in = whole_channel
    pre = (
        jnp.einsum("td,fd->tf", zed, w_in, preferred_element_type=wide) + c_in.astype(wide)[None, :]
    )
    act = gelu_exact(pre).astype(low_type)
    reduced = jnp.dot(act, w_out, preferred_element_type=wide)
    block_output = (middle + (reduced + c_four).reshape(count, patches, width)) * keep
    grad_top = cotangent * keep
    grad_branch = grad_top.reshape(rows, width).astype(low_type)
    grad_c_four = jnp.sum(grad_branch.astype(wide), axis=0)
    small_all = (
        lax.all_gather(small_local[0], "dp", axis=0, tiled=True),
        lax.all_gather(small_local[1], "dp", axis=0, tiled=True),
        lax.all_gather(small_local[2], "dp", axis=0, tiled=True),
        lax.all_gather(small_local[3], "dp", axis=0, tiled=True),
        lax.all_gather(small_local[4], "dp", axis=0, tiled=True),
        lax.all_gather(small_local[5], "dp", axis=0, tiled=True),
        lax.all_gather(small_local[6], "dp", axis=0, tiled=True),
    )
    tin = small_all[0].reshape(patches, hidden_tok)
    tout = small_all[1].reshape(hidden_tok, patches)
    g_one, b_one, g_two, b_two, c_four = [piece.astype(wide) for piece in small_all[2:]]
    whole_channel = (
        lax.all_gather(channel_local[0], "dp", axis=0, tiled=True),
        lax.all_gather(channel_local[1], "dp", axis=0, tiled=True),
        lax.all_gather(channel_local[2], "dp", axis=0, tiled=True),
    )
    w_in, w_out, c_in = whole_channel
    pre = (
        jnp.einsum("td,fd->tf", zed, w_in, preferred_element_type=wide) + c_in.astype(wide)[None, :]
    )
    act = gelu_exact(pre).astype(low_type)
    grad_act = jnp.einsum("td,fd->tf", grad_branch, w_out, preferred_element_type=wide)
    grad_pre = (grad_act * gelu_slope(pre)).astype(low_type)
    grad_zed = jnp.dot(grad_pre, w_in, preferred_element_type=wide)
    grad_in = jnp.einsum("tf,td->fd", grad_pre, zed, preferred_element_type=wide)
    grad_out = jnp.einsum("tf,td->fd", act, grad_branch, preferred_element_type=wide)
    grad_cin = jnp.sum(grad_pre.astype(wide), axis=0)
    grad_zed, grad_win, grad_wout, grad_cin = (grad_zed, grad_in, grad_out, grad_cin)
    grad_g_two = jnp.sum(grad_zed * normed_two, axis=0)
    grad_b_two = jnp.sum(grad_zed, axis=0)
    grad_mid = grad_top + norm_back(grad_zed, normed_two, scale_two, g_two).reshape(
        count, patches, width
    )
    grad_back = grad_mid.astype(low_type)
    grad_c_two = jnp.sum(grad_back.astype(wide), axis=(0, 2))
    grad_tout = jnp.einsum("bsd,bpd->sp", act_t, grad_back, preferred_element_type=wide)
    grad_act_t = jnp.einsum("sp,bpd->bsd", tout, grad_back, preferred_element_type=wide)
    grad_pre_t = (grad_act_t * gelu_slope(pre_t)).astype(low_type)
    grad_c_one = jnp.sum(grad_pre_t.astype(wide), axis=(0, 2))
    grad_tin = jnp.einsum("bpd,bsd->ps", mixed_in, grad_pre_t, preferred_element_type=wide)
    grad_mixed = jnp.einsum("ps,bsd->bpd", tin, grad_pre_t, preferred_element_type=wide)
    grad_g_one = jnp.sum(grad_mixed * normed_one, axis=(0, 1))
    grad_b_one = jnp.sum(grad_mixed, axis=(0, 1))
    image_grad = grad_mid + norm_back(grad_mixed, normed_one, scale_one, g_one)
    bias_sums = lax.psum((grad_c_one, grad_c_two), "dp")
    flat_tin = grad_tin.reshape(patches * hidden_tok)
    flat_tout = grad_tout.reshape(hidden_tok * patches)
    owned = (
        lax.psum_scatter(flat_tin, "dp", scatter_dimension=0, tiled=True),
        lax.psum_scatter(flat_tout, "dp", scatter_dimension=0, tiled=True),
        lax.psum_scatter(grad_g_one, "dp", scatter_dimension=0, tiled=True),
        lax.psum_scatter(grad_b_one, "dp", scatter_dimension=0, tiled=True),
        lax.psum_scatter(grad_g_two, "dp", scatter_dimension=0, tiled=True),
        lax.psum_scatter(grad_b_two, "dp", scatter_dimension=0, tiled=True),
        lax.psum_scatter(grad_win, "dp", scatter_dimension=0, tiled=True),
        lax.psum_scatter(grad_cin, "dp", scatter_dimension=0, tiled=True),
        lax.psum_scatter(grad_wout, "dp", scatter_dimension=0, tiled=True),
        lax.psum_scatter(grad_c_four, "dp", scatter_dimension=0, tiled=True),
    )
    (
        own_tin,
        own_tout,
        own_g_one,
        own_b_one,
        own_g_two,
        own_b_two,
        own_win,
        own_cin,
        own_wout,
        own_c_four,
    ) = owned
    return (
        block_output,
        image_grad,
        own_tin,
        own_tout,
        bias_sums[0],
        bias_sums[1],
        own_g_one,
        own_b_one,
        own_g_two,
        own_b_two,
        own_win,
        own_cin,
        own_wout,
        own_c_four,
    )


def solution(mesh):
    placed = (
        P("dp", None, None),
        P("dp"),
        P("dp", None, None),
        P("dp"),
        P("dp"),
        P(),
        P(),
        P("dp"),
        P("dp"),
        P("dp"),
        P("dp"),
        P("dp", None),
        P("dp"),
        P("dp", None),
        P("dp"),
    )
    return jax.shard_map(
        choose,
        mesh=mesh,
        in_specs=placed,
        out_specs=(
            P("dp", None, None),
            P("dp", None, None),
            P("dp"),
            P("dp"),
            P(),
            P(),
            P("dp"),
            P("dp"),
            P("dp"),
            P("dp"),
            P("dp", None),
            P("dp"),
            P("dp", None),
            P("dp"),
        ),
        check_vma=False,
    )
```

```python
import math

import jax
import jax.numpy as jnp
from jax import lax
from jax.experimental import pallas as pl
from jax.experimental.pallas import tpu as pltpu
from jax.sharding import PartitionSpec as P

EPS = 1e-06


def gelu_exact(v):
    return 0.5 * v * (1.0 + lax.erf(v * 0.7071067811865476))


def gelu_slope(v):
    return 0.5 * (1.0 + lax.erf(v * 0.7071067811865476)) + v * 0.3989422804014327 * jnp.exp(
        -0.5 * v * v
    )


def normalize(v):
    centered = v - jnp.mean(v, axis=-1, keepdims=True)
    scale = lax.rsqrt(jnp.mean(centered * centered, axis=-1, keepdims=True) + EPS)
    return (centered * scale, scale)


def norm_back(grad_in, normed, scale, gain):
    scaled = grad_in * gain
    return scale * (
        scaled
        - jnp.mean(scaled, axis=-1, keepdims=True)
        - normed * jnp.mean(scaled * normed, axis=-1, keepdims=True)
    )


WIDE = jnp.float32
LOW = jnp.bfloat16
MESH = pl.DeviceIdType.MESH
NT = (((1,), (1,)), ((), ()))
TN = (((0,), (0,)), ((), ()))
NN = (((1,), (0,)), ((), ()))
PLANE = 8


def dot(a, b, dims):
    return lax.dot_general(a, b, dims, preferred_element_type=WIDE)


def gelu_parts(v):
    cdf = 0.5 * (1.0 + lax.erf(v * 0.7071067811865476))
    return v * cdf, cdf + v * 0.3989422804014327 * jnp.exp(-0.5 * v * v)


def padded(v, rows):
    return jnp.concatenate([v, jnp.zeros((rows - v.shape[0], v.shape[1]), v.dtype)], axis=0)


def block_kernel(
    mask,
    images,
    cotangent,
    w_in,
    w_out,
    tin_own,
    tout_own,
    gain_one_own,
    shift_one_own,
    gain_two_own,
    shift_two_own,
    c_four_own,
    c_in_own,
    c_one,
    c_two,
    block_out,
    image_grad,
    grad_in,
    grad_out,
    small_out,
    biases_out,
    im,
    cot,
    mixed,
    act_t,
    slope_t,
    mid,
    total,
    grad_zed,
    zed,
    top,
    weights,
    act,
    grad_pre,
    c_in_rel,
    own_sum,
    keep_sum,
    send_one,
    recv_one,
    send_two,
    recv_two,
    send_three,
    recv_three,
    send_four,
    recv_four,
    tin,
    tin_t,
    tout,
    tout_t,
    vecs,
    c_in,
    lines,
    small_own,
    small_all,
    grad_tin,
    grad_tout,
    grad_vecs,
    grad_c_in,
    small_sum,
    small_core,
    small_plane,
    small_z,
    biases,
    biases_in,
    in_sem,
    out_sem,
    ag_send,
    ag_recv,
    rs_send,
    rs_recv,
    sg_send,
    sg_recv,
    ss_send,
    ss_recv,
    bs_send,
    bs_recv,
):
    count, patches, width = im.shape
    planes = weights.shape[1]
    shard = w_in.shape[0]
    half = 4 * shard
    chunk = 8 * shard
    pad = mixed.shape[1]
    pair = zed.shape[1]
    lot = pair // 2
    blocks = count // 2
    me = lax.axis_index("dp")
    core = me % 2
    col = (me // 2) % 2
    row = (me // 4) % 2
    z = me // PLANE
    by_core = me + 1 - 2 * core
    by_x = me + 2 - 4 * col
    by_y = me + 4 - 8 * row
    by_both = by_x + by_y - me

    def plane_of(k):
        out, bit = z, 1
        while bit < planes:
            out = out + bit * ((k // bit) % 2) * (1 - 2 * ((z // bit) % 2))
            bit *= 2
        return out

    def by_z(k):
        return me + PLANE * (plane_of(k) - z)

    def ag(stage, k, mat):
        near, far = (by_x, by_y) if mat == 0 else (by_y, by_x)
        step = 1 if mat == 0 else 2
        if stage == 0:
            src, dst, size, to = 0, 0, shard, by_z(k)
            source = weights.at[mat, 0, pl.ds(src, size)]
        else:
            src, dst, size, to = {
                1: (0, step * shard, shard, near),
                2: (0, (3 - step) * shard, shard, far),
                3: (step * shard, 3 * shard, shard, far),
                4: (0, half, half, by_core),
            }[stage]
            source = weights.at[mat, k, pl.ds(src, size)]
        return pltpu.make_async_remote_copy(
            src_ref=source,
            dst_ref=weights.at[mat, k, pl.ds(dst, size)],
            send_sem=ag_send.at[stage, k, mat],
            recv_sem=ag_recv.at[stage, k, mat],
            device_id=(to,),
            device_id_type=MESH,
        )

    def rs(stage, k, mat):
        slot = k % 2
        near, far = (by_x, by_y) if mat == 0 else (by_y, by_x)
        src, dst, to = [
            lambda: (send_one.at[mat], recv_one.at[slot, mat], by_core),
            lambda: (send_two.at[mat], recv_two.at[slot, mat], near),
            lambda: (send_three.at[mat], recv_three.at[slot, mat], far),
            lambda: (send_four.at[slot, mat], recv_four.at[k, mat], by_z(k)),
        ][stage]()
        return pltpu.make_async_remote_copy(
            src_ref=src,
            dst_ref=dst,
            send_sem=rs_send.at[stage, k, mat],
            recv_sem=rs_recv.at[stage, k, mat],
            device_id=(to,),
            device_id_type=MESH,
        )

    def small_gather(stage, k):
        src, dst, to = [
            lambda: (small_all.at[0, 0], small_all.at[0, k], by_z(k)),
            lambda: (small_all.at[0], small_all.at[k], (me, by_x, by_y, by_both)[k]),
            lambda: (small_all.at[pl.ds(0, 4)], small_all.at[pl.ds(4, 4)], by_core),
        ][stage]()
        return pltpu.make_async_remote_copy(
            src_ref=src,
            dst_ref=dst,
            send_sem=sg_send.at[stage, k],
            recv_sem=sg_recv.at[stage, k],
            device_id=(to,),
            device_id_type=MESH,
        )

    def small_reduce(stage, k):
        src, dst, to = [
            lambda: (small_all.at[pl.ds(4, 4)], small_core, by_core),
            lambda: (small_all.at[k], small_plane.at[k], (me, by_x, by_y, by_both)[k]),
            lambda: (small_all.at[0, k], small_z.at[k], by_z(k)),
        ][stage]()
        return pltpu.make_async_remote_copy(
            src_ref=src,
            dst_ref=dst,
            send_sem=ss_send.at[stage, k],
            recv_sem=ss_recv.at[stage, k],
            device_id=(to,),
            device_id_type=MESH,
        )

    def bias_reduce(stage, k):
        to = [lambda: by_core, lambda: (me, by_x, by_y, by_both)[k], lambda: by_z(k)][stage]()
        return pltpu.make_async_remote_copy(
            src_ref=biases.at[stage],
            dst_ref=biases_in.at[stage, k],
            send_sem=bs_send.at[stage, k],
            recv_sem=bs_recv.at[stage, k],
            device_id=(to,),
            device_id_type=MESH,
        )

    unit = tin_own.shape[1]
    lines_in = tin_own.shape[0]
    first_lines = (lines_in + 1) // 2
    lines_out = tout_own.shape[0]
    own_vec = gain_one_own.shape[1]
    hidden_tok = c_one.shape[1]
    turns = hidden_tok // unit
    devices = planes * PLANE

    def place_of(d):
        dz, dy, dx, dc = d // PLANE, (d // 4) % 2, (d // 2) % 2, d % 2
        far = (dc + core) % 2 * 4 + (dy + row) % 2 * 2 + (dx + col) % 2
        k, bit = 0, 1
        while bit < planes:
            k = k + bit * ((dz // bit + z // bit) % 2)
            bit *= 2
        return far, k

    def load(b):
        return (
            pltpu.make_async_copy(images.at[b], im.at[b], in_sem.at[0, b]),
            pltpu.make_async_copy(cotangent.at[b], total.at[b], in_sem.at[1, b]),
        )

    def reload(b):
        return pltpu.make_async_copy(cotangent.at[b], cot.at[b % 2], in_sem.at[2, b])

    for b in range(count):
        for copy in load(b):
            copy.start()
    small_own[...] = jnp.zeros_like(small_own)
    small_own[0:first_lines, 0:unit] = tin_own[0:first_lines, :]
    small_own[0 : lines_in - first_lines, 64 : 64 + unit] = tin_own[first_lines:lines_in, :]
    for i, piece in enumerate((gain_one_own, shift_one_own, gain_two_own, shift_two_own, c_four_own)):
        small_own[24 + i : 25 + i, 64 : 64 + own_vec] = piece[...]
    small_own[31:32, 0:shard] = c_in_own[...]
    small_own[32 : 32 + lines_out, :] = tout_own[:, 0:128]
    small_own[48 : 48 + lines_out, 0 : patches - 128] = tout_own[:, 128:patches]
    small_all[0, 0] = small_own[...].astype(LOW)
    weights[0, 0, 0:shard] = w_in[...].astype(LOW)
    weights[1, 0, 0:shard] = w_out[...].astype(LOW)

    barrier = pltpu.get_barrier_semaphore()
    peers = [by_core, by_x, by_y, by_both] + [by_z(k) for k in range(1, planes)]
    for peer in peers:
        pl.semaphore_signal(barrier, inc=1, device_id=(peer,), device_id_type=MESH)
    pl.semaphore_wait(barrier, len(peers))

    mats = (0, 1)

    def ag_direct(k):
        for mat in mats:
            ag(1, k, mat).start()
        for mat in mats:
            ag(2, k, mat).start()

    def ag_forward(k):
        for mat in mats:
            ag(1, k, mat).wait_recv()
            ag(3, k, mat).start()

    def ag_core(k):
        for mat in mats:
            ag(2, k, mat).wait_recv()
            ag(3, k, mat).wait_recv()
            ag(4, k, mat).start()

    def ag_plane(k):
        for mat in mats:
            ag(0, k, mat).wait_recv()
        ag_direct(k)

    def ag_plane_next(k):
        for mat in mats:
            ag(0, k, mat).start()

    def ag_ready(k):
        for mat in mats:
            ag(4, k, mat).wait_recv()

    for k in range(1, planes):
        small_gather(0, k).start()
    for mat in mats:
        ag(1, 0, mat).start()

    grad_vecs[...] = jnp.zeros_like(grad_vecs)
    grad_tin[...] = jnp.zeros_like(grad_tin)
    grad_tout[...] = jnp.zeros_like(grad_tout)

    def channel_top(r, carry):
        tops = []
        for h in range(2):
            b = 2 * r + h
            load(b)[1].wait()
            tops.append(padded(total[b] * mask[b].astype(WIDE), lot))
        top[r] = jnp.concatenate(tops, axis=0).astype(LOW)
        grad_vecs[4:5, :] += jnp.sum(top[r].astype(WIDE), axis=0, keepdims=True)
        return carry

    def first_norm(b, carry):
        load(b)[0].wait()
        mid[b] = normalize(im[b])[0]
        return carry

    lax.fori_loop(0, blocks, channel_top, 0)
    for k in range(1, planes):
        small_gather(0, k).wait_recv()
    for k in range(1, 4):
        small_gather(1, k).start()
    for mat in mats:
        ag(2, 0, mat).start()
    ag_plane_next(1)
    lax.fori_loop(0, count, first_norm, 0)
    for k in range(1, 4):
        small_gather(1, k).wait_recv()
    small_gather(2, 0).start()
    small_gather(2, 0).wait_recv()

    tin[...] = jnp.zeros_like(tin)
    tout[...] = jnp.zeros_like(tout)
    for d in range(devices):
        far, k = place_of(d)
        message = small_all[far, k].astype(WIDE)
        lines[d * lines_in : d * lines_in + first_lines, :] = message[0:first_lines, :]
        shifted = jnp.concatenate([message[0:24, 64:128], message[0:24, 0:64]], axis=1)
        lines[d * lines_in + first_lines : (d + 1) * lines_in, :] = shifted[0 : lines_in - first_lines, :]
        vecs[:, d * own_vec : (d + 1) * own_vec] = message[24:32, 64 : 64 + own_vec]
        c_in[d] = message[31:32, 0:shard]
        tout[d * lines_out : (d + 1) * lines_out, 0:128] = message[32 : 32 + lines_out, :]
        tout[d * lines_out : (d + 1) * lines_out, 128:patches] = message[48 : 48 + lines_out, 0 : patches - 128]
    for turn in range(turns):
        tin[0:patches, turn * unit : (turn + 1) * unit] = lines[pl.ds(turn, patches, stride=turns), :][:, 0:unit]
    for rest, into, at in ((c_one[...], tin, patches), (c_two[...], tout, hidden_tok)):
        for i in range(3):
            term = rest.astype(LOW).astype(WIDE)
            into[at + i : at + i + 1, 0 : rest.shape[1]] = term
            rest = rest - term
    tin_t[...] = tin[...].T.astype(LOW)
    tout_t[...] = tout[...].T.astype(LOW)
    ones = jnp.ones((3, width), WIDE)

    gain_one, shift_one = vecs[0:1, :], vecs[1:2, :]
    gain_two, shift_two, c_four = vecs[2:3, :], vecs[3:4, :], vecs[4:5, :]
    for k in range(planes):
        for place in range(PLANE):
            near = plane_of(k) * PLANE + (
                (row + (place // 2) % 2) % 2 * 4 + (col + place % 2) % 2 * 2 + (core + place // 4) % 2
            )
            c_in_rel[k, :, place * shard : (place + 1) * shard] = c_in[near]

    def token_forward(b, carry):
        fed = mid[b] * gain_one + shift_one
        mixed[b] = padded(jnp.concatenate([fed, ones], axis=0), pad).astype(LOW)
        value, slope = gelu_parts(dot(tin_t[...], mixed[b], NN))
        act_t[b] = padded(jnp.concatenate([value, ones], axis=0), act_t.shape[1]).astype(LOW)
        slope_t[b] = slope.astype(LOW)
        mid[b] = im[b] + dot(tout_t[...], act_t[b], NN)[0:patches]
        return carry

    def channel_inputs(r, carry):
        parts = []
        for h in range(2):
            normed, _ = normalize(mid[2 * r + h])
            parts.append(padded(normed * gain_two + shift_two, lot))
        zed[r] = jnp.concatenate(parts, axis=0).astype(LOW)
        return carry

    lax.fori_loop(0, 2, token_forward, 0)
    ag_forward(0)
    lax.fori_loop(2, 4, token_forward, 0)
    ag_plane(1)
    ag_plane_next(2)
    lax.fori_loop(4, count, token_forward, 0)
    ag_core(0)
    ag_forward(1)
    lax.fori_loop(0, blocks, channel_inputs, 0)
    total[...] = jnp.zeros_like(total)
    grad_zed[...] = jnp.zeros_like(grad_zed)

    def rs_two(k):
        for mat in mats:
            rs(0, k, mat).wait_recv()
            own_sum[mat] += recv_one[k % 2, mat].astype(WIDE)
            if mat == 0:
                first, second = (1, 2), (3, 4)
            else:
                first, second = (2, 3), (3, 4)

            @pl.when(k > 0)
            def _():
                rs(1, k - 1, mat).wait_send()

            send_two[mat, 0:shard] = own_sum[mat, first[0] * shard : first[1] * shard].astype(LOW)
            send_two[mat, shard : 2 * shard] = own_sum[mat, second[0] * shard : second[1] * shard].astype(LOW)
            rs(1, k, mat).start()

    def rs_three(k):
        for mat in mats:
            rs(1, k, mat).wait_recv()
            other = 2 if mat == 0 else 1

            @pl.when(k > 0)
            def _():
                rs(2, k - 1, mat).wait_send()

            keep_sum[mat] = own_sum[mat, 0:shard] + recv_two[k % 2, mat, 0:shard].astype(WIDE)
            send_three[mat] = (
                own_sum[mat, other * shard : (other + 1) * shard]
                + recv_two[k % 2, mat, shard : 2 * shard].astype(WIDE)
            ).astype(LOW)
            rs(2, k, mat).start()

    def rs_four(k):
        for mat in mats:
            rs(2, k, mat).wait_recv()
            summed = keep_sum[mat] + recv_three[k % 2, mat].astype(WIDE)
            result = grad_in if mat == 0 else grad_out

            @pl.when(k == 0)
            def _():
                result[...] = summed

            @pl.when(k > 0)
            def _():
                @pl.when(k > 2)
                def _():
                    rs(3, k - 2, mat).wait_send()

                send_four[k % 2, mat] = summed.astype(LOW)
                rs(3, k, mat).start()

    def rs_last():
        for mat in mats:
            result = grad_in if mat == 0 else grad_out
            for k in range(1, planes):
                rs(3, k, mat).wait_recv()
                result[...] += recv_four[k, mat].astype(WIDE)

    tile = chunk // 3

    def channel_chunk(k, carry):
        ag_ready(k)

        def rows(r, inner):
            for s in range(3):
                part = slice(s * tile, (s + 1) * tile)
                pre = dot(zed[r], weights[0, k, part], NT) + c_in_rel[k, :, part]
                value, slope = gelu_parts(pre)
                act[pl.ds(r * pair, pair), part] = value.astype(LOW)
                back = (dot(top[r], weights[1, k, part], NT) * slope).astype(LOW)
                grad_pre[pl.ds(r * pair, pair), part] = back
            up = dot(act[pl.ds(r * pair, pair), :], weights[1, k], NN)
            down = dot(grad_pre[pl.ds(r * pair, pair), :], weights[0, k], NN)
            for h in range(2):
                total[2 * r + h] += up[h * lot : h * lot + patches]
                grad_zed[2 * r + h] += down[h * lot : h * lot + patches]

            @pl.when((r == 0) & (k + 1 < planes) & (k > 0))
            def _():
                ag_forward(k + 1)

            @pl.when((r == 2) & (k > 0))
            def _():
                rs_three(k - 1)

            return inner

        lax.fori_loop(0, blocks, rows, 0)

        @pl.when(k + 1 < planes)
        def _():
            ag_core(k + 1)

        @pl.when(k + 2 < planes)
        def _():
            ag_plane(k + 2)

        @pl.when(k + 3 < planes)
        def _():
            ag_plane_next(k + 3)

        back_sum = jnp.sum(grad_pre[...].astype(WIDE), axis=0, keepdims=True)
        for place in range(PLANE):
            near = plane_of(k) * PLANE + (
                (row + (place // 2) % 2) % 2 * 4 + (col + place % 2) % 2 * 2 + (core + place // 4) % 2
            )
            grad_c_in[near] = back_sum[:, place * shard : (place + 1) * shard]

        flat_top = top[...].reshape(blocks * pair, width)
        flat_zed = zed[...].reshape(blocks * pair, width)
        for mat, left, right in ((1, act, flat_top), (0, grad_pre, flat_zed)):
            @pl.when(k > 0)
            def _():
                rs(0, k - 1, mat).wait_send()

            send_one[mat] = dot(left[:, half:chunk], right, TN).astype(LOW)
            rs(0, k, mat).start()

        @pl.when(k > 0)
        def _():
            rs_four(k - 1)

        for mat, left, right in ((1, act, flat_top), (0, grad_pre, flat_zed)):
            own_sum[mat] = dot(left[:, 0:half], right, TN)
        rs_two(k)
        return carry

    for b in range(2):
        reload(b).start()
    lax.fori_loop(0, planes, channel_chunk, 0)

    def store(b):
        return (
            pltpu.make_async_copy(total.at[b], block_out.at[b], out_sem.at[0, b]),
            pltpu.make_async_copy(grad_zed.at[b], image_grad.at[b], out_sem.at[1, b]),
        )

    tin_low = tin[...].astype(LOW)
    tout_low = tout[0:hidden_tok, :].astype(LOW)

    def token_backward(b, carry):
        keep = mask[b].astype(WIDE)
        total[b] = (mid[b] + total[b] + c_four) * keep
        store(b)[0].start()
        normed, scale = normalize(mid[b])
        down = grad_zed[b]
        grad_vecs[2:3, :] += jnp.sum(down * normed, axis=0, keepdims=True)
        grad_vecs[3:4, :] += jnp.sum(down, axis=0, keepdims=True)
        reload(b).wait()
        grad_mid = cot[b % 2] * keep + norm_back(down, normed, scale, gain_two)

        @pl.when(b + 2 < count)
        def _():
            reload(b + 2).start()

        back = padded(grad_mid, pad).astype(LOW)
        grad_tout[...] += dot(act_t[b], back, NT)
        back_t = (dot(tout_low, back, NN) * slope_t[b].astype(WIDE)).astype(LOW)
        grad_tin[:, 0:hidden_tok] += dot(mixed[b], back_t, NT)
        grad_mixed = dot(tin_low, back_t, NN)[0:patches]
        normed, scale = normalize(im[b])
        grad_vecs[0:1, :] += jnp.sum(grad_mixed * normed, axis=0, keepdims=True)
        grad_vecs[1:2, :] += jnp.sum(grad_mixed, axis=0, keepdims=True)
        grad_zed[b] = grad_mid + norm_back(grad_mixed, normed, scale, gain_one)
        store(b)[1].start()

        @pl.when(b == count // 2)
        def _():
            rs_three(planes - 1)

        return carry

    lax.fori_loop(0, count, token_backward, 0)

    biases[0] = jnp.zeros_like(biases[0])
    for i in range(hidden_tok // 128):
        biases[0, i : i + 1, :] = grad_tin[patches : patches + 1, i * 128 : (i + 1) * 128]
    biases[0, 3:4, :] = grad_tout[hidden_tok : hidden_tok + 1, 0:128]
    biases[0, 4:5, 0 : patches - 128] = grad_tout[hidden_tok : hidden_tok + 1, 128:patches]
    bias_reduce(0, 0).start()
    for turn in range(turns):
        lines[pl.ds(turn, patches, stride=turns), :] = grad_tin[0:patches, turn * unit : turn * unit + 128]
    for d in range(devices):
        far, k = place_of(d)
        low = lines[d * lines_in : d * lines_in + first_lines, :]
        high = lines[d * lines_in + first_lines : (d + 1) * lines_in, :]
        small_sum[far, k, 0:first_lines, 0:64] = low[:, 0:64]
        small_sum[far, k, 0 : lines_in - first_lines, 64:128] = high[:, 0:64]
        small_sum[far, k, 24:29, 64 : 64 + own_vec] = grad_vecs[0:5, d * own_vec : (d + 1) * own_vec]
        small_sum[far, k, 31:32, 0:shard] = grad_c_in[d]
        small_sum[far, k, 32 : 32 + lines_out, :] = grad_tout[d * lines_out : (d + 1) * lines_out, 0:128]
        small_sum[far, k, 48 : 48 + lines_out, 0 : patches - 128] = grad_tout[
            d * lines_out : (d + 1) * lines_out, 128:patches
        ]
    for k in range(1, planes):
        small_gather(0, k).wait_send()
    for far in range(1, 4):
        small_gather(1, far).wait_send()
    small_gather(2, 0).wait_send()
    for far in range(4, PLANE):
        small_all[far] = small_sum[far].astype(LOW)
    small_reduce(0, 0).start()
    rs_four(planes - 1)
    bias_reduce(0, 0).wait_recv()
    biases[1] = biases[0] + biases_in[0, 0]
    small_reduce(0, 0).wait_recv()
    for far in range(4):
        small_sum[far] += small_core[far].astype(WIDE)
    for far in range(1, 4):
        small_all[far] = small_sum[far].astype(LOW)
        small_reduce(1, far).start()
        bias_reduce(1, far).start()
    for far in range(1, 4):
        small_reduce(1, far).wait_recv()
        bias_reduce(1, far).wait_recv()
        small_sum[0] += small_plane[far].astype(WIDE)
    biases[2] = (biases[1] + biases_in[1, 1]) + (biases_in[1, 2] + biases_in[1, 3])
    for k in range(1, planes):
        small_all[0, k] = small_sum[0, k].astype(LOW)
        small_reduce(2, k).start()
        bias_reduce(2, k).start()
    rs_last()
    summed = small_sum[0, 0]
    tree = [biases[2]]
    for k in range(1, planes):
        small_reduce(2, k).wait_recv()
        bias_reduce(2, k).wait_recv()
        summed = summed + small_z[k].astype(WIDE)
        tree.append(biases_in[2, k])
    small_out[...] = summed
    while len(tree) > 1:
        tree = [tree[i] + tree[i + 1] for i in range(0, len(tree), 2)]
    biases_out[...] = tree[0]

    for mat in mats:
        for k in range(planes):
            for stage in range(5):
                if stage > 0 or k > 0:
                    ag(stage, k, mat).wait_send()
        for stage in range(3):
            rs(stage, planes - 1, mat).wait_send()
        for k in range(max(1, planes - 2), planes):
            rs(3, k, mat).wait_send()
    small_reduce(0, 0).wait_send()
    bias_reduce(0, 0).wait_send()
    for far in range(1, 4):
        small_reduce(1, far).wait_send()
        bias_reduce(1, far).wait_send()
    for k in range(1, planes):
        small_reduce(2, k).wait_send()
        bias_reduce(2, k).wait_send()
    for b in range(count):
        for copy in store(b):
            copy.wait()


def finish_kernel(
    block_in,
    image_in,
    w_in,
    w_out,
    small,
    biases,
    block_out,
    image_out,
    w_in_out,
    w_out_out,
    tin,
    tout,
    gain_one,
    shift_one,
    gain_two,
    shift_two,
    c_four,
    c_in,
    c_one,
    c_two,
):
    block_out[...] = block_in[...]
    image_out[...] = image_in[...]
    w_in_out[...] = w_in[...]
    w_out_out[...] = w_out[...]
    lines_in, unit = tin.shape
    first_lines = (lines_in + 1) // 2
    lines_out, patches = tout.shape
    tin[0:first_lines, :] = small[0:first_lines, 0:unit]
    tin[first_lines:lines_in, :] = small[0 : lines_in - first_lines, 64 : 64 + unit]
    tout[:, 0:128] = small[32 : 32 + lines_out, :]
    tout[:, 128:patches] = small[48 : 48 + lines_out, 0 : patches - 128]
    for i, piece in enumerate((gain_one, shift_one, gain_two, shift_two, c_four)):
        piece[...] = small[24 + i : 25 + i, 64 : 64 + piece.shape[1]]
    c_in[...] = small[31:32, 0 : c_in.shape[1]]
    for i in range(c_one.shape[1] // 128):
        c_one[:, i * 128 : (i + 1) * 128] = biases[i : i + 1, :]
    c_two[:, 0:128] = biases[3:4, :]
    c_two[:, 128:patches] = biases[4:5, 0 : patches - 128]


def fast_shards(
    images,
    mask,
    cotangent,
    w_token_in,
    w_token_out,
    bias_token_in,
    bias_token_out,
    gain_one,
    shift_one,
    gain_two,
    shift_two,
    w_expand,
    bias_expand,
    w_reduce,
    bias_reduce,
):
    devices = lax.axis_size("dp")
    planes = devices // PLANE
    count, patches, width = images.shape
    hidden_tok = bias_token_in.shape[0]
    shard = w_expand.shape[0]
    pad = -(-patches // 16) * 16
    lot = -(-patches // 8) * 8
    pair = 2 * lot
    blocks = count // 2
    chunk = 8 * shard
    half = 4 * shard

    unit = math.gcd(w_token_in.shape[0], hidden_tok)
    lines_in = w_token_in.shape[0] // unit
    lines_out = w_token_out.shape[0] // patches
    own_vec = gain_one.shape[0]
    hidden_pad = hidden_tok + 16

    vmem = pl.BlockSpec(memory_space=pltpu.VMEM)
    hbm = pl.BlockSpec(memory_space=pl.ANY)
    shape = jax.ShapeDtypeStruct
    outs = pl.pallas_call(
        block_kernel,
        out_shape=(
            shape(images.shape, WIDE),
            shape(images.shape, WIDE),
            shape(w_expand.shape, WIDE),
            shape(w_reduce.shape, WIDE),
            shape((64, 128), WIDE),
            shape((8, 128), WIDE),
        ),
        in_specs=[pl.BlockSpec(memory_space=pltpu.SMEM), hbm, hbm] + [vmem] * 12,
        out_specs=[hbm, hbm] + [vmem] * 4,
        scratch_shapes=[
            pltpu.VMEM(images.shape, WIDE),
            pltpu.VMEM((2,) + images.shape[1:], WIDE),
            pltpu.VMEM((count, pad, width), LOW),
            pltpu.VMEM((count, hidden_pad, width), LOW),
            pltpu.VMEM((count, hidden_tok, width), LOW),
            pltpu.VMEM(images.shape, WIDE),
            pltpu.VMEM(images.shape, WIDE),
            pltpu.VMEM(images.shape, WIDE),
            pltpu.VMEM((blocks, pair, width), LOW),
            pltpu.VMEM((blocks, pair, width), LOW),
            pltpu.VMEM((2, planes, chunk, width), LOW),
            pltpu.VMEM((blocks * pair, chunk), LOW),
            pltpu.VMEM((blocks * pair, chunk), LOW),
            pltpu.VMEM((planes, 1, chunk), WIDE),
            pltpu.VMEM((2, half, width), WIDE),
            pltpu.VMEM((2, shard, width), WIDE),
            pltpu.VMEM((2, half, width), LOW),
            pltpu.VMEM((2, 2, half, width), LOW),
            pltpu.VMEM((2, 2 * shard, width), LOW),
            pltpu.VMEM((2, 2, 2 * shard, width), LOW),
            pltpu.VMEM((2, shard, width), LOW),
            pltpu.VMEM((2, 2, shard, width), LOW),
            pltpu.VMEM((2, 2, shard, width), LOW),
            pltpu.VMEM((planes, 2, shard, width), LOW),
            pltpu.VMEM((pad, hidden_tok), WIDE),
            pltpu.VMEM((hidden_tok, pad), LOW),
            pltpu.VMEM((hidden_pad, pad), WIDE),
            pltpu.VMEM((pad, hidden_pad), LOW),
            pltpu.VMEM((8, width), WIDE),
            pltpu.VMEM((devices, 1, shard), WIDE),
            pltpu.VMEM((devices * lines_in, 128), WIDE),
            pltpu.VMEM((64, 128), WIDE),
            pltpu.VMEM((PLANE, planes, 64, 128), LOW),
            pltpu.VMEM((pad, hidden_tok + 128), WIDE),
            pltpu.VMEM((hidden_pad, pad), WIDE),
            pltpu.VMEM((8, width), WIDE),
            pltpu.VMEM((devices, 1, shard), WIDE),
            pltpu.VMEM((PLANE, planes, 64, 128), WIDE),
            pltpu.VMEM((4, planes, 64, 128), LOW),
            pltpu.VMEM((4, planes, 64, 128), LOW),
            pltpu.VMEM((planes, 64, 128), LOW),
            pltpu.VMEM((3, 8, 128), WIDE),
            pltpu.VMEM((3, max(4, planes), 8, 128), WIDE),
            pltpu.SemaphoreType.DMA((3, count)),
            pltpu.SemaphoreType.DMA((2, count)),
            pltpu.SemaphoreType.DMA((5, planes, 2)),
            pltpu.SemaphoreType.DMA((5, planes, 2)),
            pltpu.SemaphoreType.DMA((4, planes, 2)),
            pltpu.SemaphoreType.DMA((4, planes, 2)),
        ]
        + [pltpu.SemaphoreType.DMA((3, max(4, planes)))] * 6,
        compiler_params=pltpu.CompilerParams(
            collective_id=0, has_side_effects=True, vmem_limit_bytes=63 * 2**20
        ),
    )(
        mask,
        images,
        cotangent,
        w_expand,
        w_reduce,
        w_token_in.reshape(lines_in, unit),
        w_token_out.reshape(lines_out, patches),
        gain_one.reshape(1, -1),
        shift_one.reshape(1, -1),
        gain_two.reshape(1, -1),
        shift_two.reshape(1, -1),
        bias_reduce.reshape(1, -1),
        bias_expand.reshape(1, -1),
        bias_token_in.reshape(1, -1),
        bias_token_out.reshape(1, -1),
    )
    image = pl.BlockSpec((1, patches, width), lambda b: (b, 0, 0))
    flat = pl.pallas_call(
        finish_kernel,
        out_shape=(
            shape(images.shape, WIDE),
            shape(images.shape, WIDE),
            shape(w_expand.shape, WIDE),
            shape(w_reduce.shape, WIDE),
            shape((lines_in, unit), WIDE),
            shape((lines_out, patches), WIDE),
            *[shape((1, own_vec), WIDE)] * 5,
            shape((1, shard), WIDE),
            shape((1, hidden_tok), WIDE),
            shape((1, patches), WIDE),
        ),
        grid=(count,),
        in_specs=[image] * 2 + [vmem] * 4,
        out_specs=[image] * 2 + [vmem] * 12,
    )(*outs)
    block_output, image_grad, own_win, own_wout, *rest = flat
    g_tin, g_tout, g_one, b_one, g_two, b_two, c_four, c_in, c_one, c_two = [part.reshape(-1) for part in rest]
    return (
        block_output,
        image_grad,
        g_tin,
        g_tout,
        c_one,
        c_two,
        g_one,
        b_one,
        g_two,
        b_two,
        own_win,
        c_in,
        own_wout,
        c_four,
    )


def fits(devices, images, w_token_in, w_token_out, bias_token_in, gain_one, w_expand):
    planes = devices // PLANE
    patches = images.shape[1]
    hidden_tok = bias_token_in.shape[0]
    shard = w_expand.shape[0]
    unit = math.gcd(w_token_in.shape[0], hidden_tok)
    return (
        devices % PLANE == 0
        and planes & (planes - 1) == 0
        and planes >= 2
        and images.shape[0] % 2 == 0
        and shard % 16 == 0
        and shard <= 128
        and (4 * shard) % 128 == 0
        and 128 < patches <= 205
        and unit <= 64
        and w_token_in.shape[0] // unit <= 49
        and w_token_out.shape[0] % patches == 0
        and w_token_out.shape[0] // patches <= 16
        and gain_one.shape[0] <= 64
        and hidden_tok == 384
    )


def choose(
    images,
    mask,
    cotangent,
    w_token_in,
    w_token_out,
    bias_token_in,
    bias_token_out,
    gain_one,
    shift_one,
    gain_two,
    shift_two,
    w_expand,
    bias_expand,
    w_reduce,
    bias_reduce,
):
    args = (
        images,
        mask,
        cotangent,
        w_token_in,
        w_token_out,
        bias_token_in,
        bias_token_out,
        gain_one,
        shift_one,
        gain_two,
        shift_two,
        w_expand,
        bias_expand,
        w_reduce,
        bias_reduce,
    )
    if fits(lax.axis_size("dp"), images, w_token_in, w_token_out, bias_token_in, gain_one, w_expand):
        return fast_shards(*args)
    return shards(*args)


def shards(
    images,
    mask,
    cotangent,
    w_token_in,
    w_token_out,
    bias_token_in,
    bias_token_out,
    gain_one,
    shift_one,
    gain_two,
    shift_two,
    w_expand,
    bias_expand,
    w_reduce,
    bias_reduce,
):
    low_type = jnp.bfloat16
    wide = jnp.float32
    count, patches, width = images.shape
    hidden_tok = bias_token_in.shape[0]
    rows = count * patches
    keep = mask.astype(wide)[:, None, None]
    small_local = (
        w_token_in.astype(low_type),
        w_token_out.astype(low_type),
        gain_one.astype(low_type),
        shift_one.astype(low_type),
        gain_two.astype(low_type),
        shift_two.astype(low_type),
        bias_reduce.astype(low_type),
    )
    channel_local = (
        w_expand.astype(low_type),
        w_reduce.astype(low_type),
        bias_expand.astype(low_type),
    )
    small_all = (
        lax.all_gather(small_local[0], "dp", axis=0, tiled=True),
        lax.all_gather(small_local[1], "dp", axis=0, tiled=True),
        lax.all_gather(small_local[2], "dp", axis=0, tiled=True),
        lax.all_gather(small_local[3], "dp", axis=0, tiled=True),
        lax.all_gather(small_local[4], "dp", axis=0, tiled=True),
        lax.all_gather(small_local[5], "dp", axis=0, tiled=True),
        lax.all_gather(small_local[6], "dp", axis=0, tiled=True),
    )
    tin = small_all[0].reshape(patches, hidden_tok)
    tout = small_all[1].reshape(hidden_tok, patches)
    g_one, b_one, g_two, b_two, c_four = [piece.astype(wide) for piece in small_all[2:]]
    normed_one, scale_one = normalize(images)
    mixed_in = (normed_one * g_one + b_one).astype(low_type)
    pre_t = (
        jnp.einsum("ps,bpd->bsd", tin, mixed_in, preferred_element_type=wide)
        + bias_token_in[None, :, None]
    )
    act_t = gelu_exact(pre_t).astype(low_type)
    middle = (
        images
        + jnp.einsum("sp,bsd->bpd", tout, act_t, preferred_element_type=wide)
        + bias_token_out[None, :, None]
    )
    normed_two, scale_two = normalize(middle.reshape(rows, width))
    zed = (normed_two * g_two + b_two).astype(low_type)
    whole_channel = (
        lax.all_gather(channel_local[0], "dp", axis=0, tiled=True),
        lax.all_gather(channel_local[1], "dp", axis=0, tiled=True),
        lax.all_gather(channel_local[2], "dp", axis=0, tiled=True),
    )
    w_in, w_out, c_in = whole_channel
    pre = (
        jnp.einsum("td,fd->tf", zed, w_in, preferred_element_type=wide) + c_in.astype(wide)[None, :]
    )
    act = gelu_exact(pre).astype(low_type)
    reduced = jnp.dot(act, w_out, preferred_element_type=wide)
    block_output = (middle + (reduced + c_four).reshape(count, patches, width)) * keep
    grad_top = cotangent * keep
    grad_branch = grad_top.reshape(rows, width).astype(low_type)
    grad_c_four = jnp.sum(grad_branch.astype(wide), axis=0)
    small_all = (
        lax.all_gather(small_local[0], "dp", axis=0, tiled=True),
        lax.all_gather(small_local[1], "dp", axis=0, tiled=True),
        lax.all_gather(small_local[2], "dp", axis=0, tiled=True),
        lax.all_gather(small_local[3], "dp", axis=0, tiled=True),
        lax.all_gather(small_local[4], "dp", axis=0, tiled=True),
        lax.all_gather(small_local[5], "dp", axis=0, tiled=True),
        lax.all_gather(small_local[6], "dp", axis=0, tiled=True),
    )
    tin = small_all[0].reshape(patches, hidden_tok)
    tout = small_all[1].reshape(hidden_tok, patches)
    g_one, b_one, g_two, b_two, c_four = [piece.astype(wide) for piece in small_all[2:]]
    whole_channel = (
        lax.all_gather(channel_local[0], "dp", axis=0, tiled=True),
        lax.all_gather(channel_local[1], "dp", axis=0, tiled=True),
        lax.all_gather(channel_local[2], "dp", axis=0, tiled=True),
    )
    w_in, w_out, c_in = whole_channel
    pre = (
        jnp.einsum("td,fd->tf", zed, w_in, preferred_element_type=wide) + c_in.astype(wide)[None, :]
    )
    act = gelu_exact(pre).astype(low_type)
    grad_act = jnp.einsum("td,fd->tf", grad_branch, w_out, preferred_element_type=wide)
    grad_pre = (grad_act * gelu_slope(pre)).astype(low_type)
    grad_zed = jnp.dot(grad_pre, w_in, preferred_element_type=wide)
    grad_in = jnp.einsum("tf,td->fd", grad_pre, zed, preferred_element_type=wide)
    grad_out = jnp.einsum("tf,td->fd", act, grad_branch, preferred_element_type=wide)
    grad_cin = jnp.sum(grad_pre.astype(wide), axis=0)
    grad_zed, grad_win, grad_wout, grad_cin = (grad_zed, grad_in, grad_out, grad_cin)
    grad_g_two = jnp.sum(grad_zed * normed_two, axis=0)
    grad_b_two = jnp.sum(grad_zed, axis=0)
    grad_mid = grad_top + norm_back(grad_zed, normed_two, scale_two, g_two).reshape(
        count, patches, width
    )
    grad_back = grad_mid.astype(low_type)
    grad_c_two = jnp.sum(grad_back.astype(wide), axis=(0, 2))
    grad_tout = jnp.einsum("bsd,bpd->sp", act_t, grad_back, preferred_element_type=wide)
    grad_act_t = jnp.einsum("sp,bpd->bsd", tout, grad_back, preferred_element_type=wide)
    grad_pre_t = (grad_act_t * gelu_slope(pre_t)).astype(low_type)
    grad_c_one = jnp.sum(grad_pre_t.astype(wide), axis=(0, 2))
    grad_tin = jnp.einsum("bpd,bsd->ps", mixed_in, grad_pre_t, preferred_element_type=wide)
    grad_mixed = jnp.einsum("ps,bsd->bpd", tin, grad_pre_t, preferred_element_type=wide)
    grad_g_one = jnp.sum(grad_mixed * normed_one, axis=(0, 1))
    grad_b_one = jnp.sum(grad_mixed, axis=(0, 1))
    image_grad = grad_mid + norm_back(grad_mixed, normed_one, scale_one, g_one)
    bias_sums = lax.psum((grad_c_one, grad_c_two), "dp")
    flat_tin = grad_tin.reshape(patches * hidden_tok)
    flat_tout = grad_tout.reshape(hidden_tok * patches)
    owned = (
        lax.psum_scatter(flat_tin, "dp", scatter_dimension=0, tiled=True),
        lax.psum_scatter(flat_tout, "dp", scatter_dimension=0, tiled=True),
        lax.psum_scatter(grad_g_one, "dp", scatter_dimension=0, tiled=True),
        lax.psum_scatter(grad_b_one, "dp", scatter_dimension=0, tiled=True),
        lax.psum_scatter(grad_g_two, "dp", scatter_dimension=0, tiled=True),
        lax.psum_scatter(grad_b_two, "dp", scatter_dimension=0, tiled=True),
        lax.psum_scatter(grad_win, "dp", scatter_dimension=0, tiled=True),
        lax.psum_scatter(grad_cin, "dp", scatter_dimension=0, tiled=True),
        lax.psum_scatter(grad_wout, "dp", scatter_dimension=0, tiled=True),
        lax.psum_scatter(grad_c_four, "dp", scatter_dimension=0, tiled=True),
    )
    (
        own_tin,
        own_tout,
        own_g_one,
        own_b_one,
        own_g_two,
        own_b_two,
        own_win,
        own_cin,
        own_wout,
        own_c_four,
    ) = owned
    return (
        block_output,
        image_grad,
        own_tin,
        own_tout,
        bias_sums[0],
        bias_sums[1],
        own_g_one,
        own_b_one,
        own_g_two,
        own_b_two,
        own_win,
        own_cin,
        own_wout,
        own_c_four,
    )


def solution(mesh):
    placed = (
        P("dp", None, None),
        P("dp"),
        P("dp", None, None),
        P("dp"),
        P("dp"),
        P(),
        P(),
        P("dp"),
        P("dp"),
        P("dp"),
        P("dp"),
        P("dp", None),
        P("dp"),
        P("dp", None),
        P("dp"),
    )
    return jax.shard_map(
        choose,
        mesh=mesh,
        in_specs=placed,
        out_specs=(
            P("dp", None, None),
            P("dp", None, None),
            P("dp"),
            P("dp"),
            P(),
            P(),
            P("dp"),
            P("dp"),
            P("dp"),
            P("dp"),
            P("dp", None),
            P("dp"),
            P("dp", None),
            P("dp"),
        ),
        check_vma=False,
    )
```

```python
import math

import jax
import jax.numpy as jnp
from jax import lax
from jax.experimental import pallas as pl
from jax.experimental.pallas import tpu as pltpu
from jax.sharding import PartitionSpec as P

EPS = 1e-06


def gelu_exact(v):
    return 0.5 * v * (1.0 + lax.erf(v * 0.7071067811865476))


def gelu_slope(v):
    return 0.5 * (1.0 + lax.erf(v * 0.7071067811865476)) + v * 0.3989422804014327 * jnp.exp(
        -0.5 * v * v
    )


def normalize(v):
    centered = v - jnp.mean(v, axis=-1, keepdims=True)
    scale = lax.rsqrt(jnp.mean(centered * centered, axis=-1, keepdims=True) + EPS)
    return (centered * scale, scale)


def norm_back(grad_in, normed, scale, gain):
    scaled = grad_in * gain
    return scale * (
        scaled
        - jnp.mean(scaled, axis=-1, keepdims=True)
        - normed * jnp.mean(scaled * normed, axis=-1, keepdims=True)
    )


WIDE = jnp.float32
LOW = jnp.bfloat16
MESH = pl.DeviceIdType.MESH
NT = (((1,), (1,)), ((), ()))
TN = (((0,), (0,)), ((), ()))
NN = (((1,), (0,)), ((), ()))
PLANE = 8


def dot(a, b, dims):
    return lax.dot_general(a, b, dims, preferred_element_type=WIDE)


def gelu_parts(v):
    cdf = 0.5 * (1.0 + lax.erf(v * 0.7071067811865476))
    return v * cdf, cdf + v * 0.3989422804014327 * jnp.exp(-0.5 * v * v)


def padded(v, rows):
    return jnp.concatenate([v, jnp.zeros((rows - v.shape[0], v.shape[1]), v.dtype)], axis=0)


def block_kernel(
    mask,
    images,
    cotangent,
    w_in,
    w_out,
    tin_own,
    tout_own,
    gain_one_own,
    shift_one_own,
    gain_two_own,
    shift_two_own,
    c_four_own,
    c_in_own,
    c_one,
    c_two,
    total,
    grad_zed,
    grad_in,
    grad_out,
    small_out,
    biases_out,
    cot,
    mixed,
    act_t,
    slope_t,
    mid,
    zed,
    top,
    weights,
    act,
    grad_pre,
    c_in_rel,
    own_sum,
    keep_sum,
    send_one,
    recv_one,
    send_two,
    recv_two,
    send_three,
    recv_three,
    send_four,
    recv_four,
    tin,
    tin_t,
    tout,
    tout_t,
    vecs,
    c_in,
    lines,
    small_own,
    small_all,
    grad_tin,
    grad_tout,
    grad_vecs,
    grad_c_in,
    small_sum,
    small_core,
    small_plane,
    small_z,
    biases,
    biases_in,
    late,
    late_in,
    in_sem,
    ag_send,
    ag_recv,
    rs_send,
    rs_recv,
    sg_send,
    sg_recv,
    ss_send,
    ss_recv,
    bs_send,
    bs_recv,
    ls_send,
    ls_recv,
):
    count, patches, width = images.shape
    planes = weights.shape[1]
    shard = w_in.shape[0]
    half = 4 * shard
    chunk = 8 * shard
    pad = mixed.shape[1]
    pair = zed.shape[1]
    lot = pair // 2
    blocks = count // 2
    me = lax.axis_index("dp")
    core = me % 2
    col = (me // 2) % 2
    row = (me // 4) % 2
    z = me // PLANE
    by_core = me + 1 - 2 * core
    by_x = me + 2 - 4 * col
    by_y = me + 4 - 8 * row
    by_both = by_x + by_y - me

    def plane_of(k):
        out, bit = z, 1
        while bit < planes:
            out = out + bit * ((k // bit) % 2) * (1 - 2 * ((z // bit) % 2))
            bit *= 2
        return out

    def by_z(k):
        return me + PLANE * (plane_of(k) - z)

    def ag(stage, k, mat):
        near, far = (by_x, by_y) if mat == 0 else (by_y, by_x)
        step = 1 if mat == 0 else 2
        if stage == 0:
            src, dst, size, to = 0, 0, shard, by_z(k)
            source = weights.at[mat, 0, pl.ds(src, size)]
        else:
            src, dst, size, to = {
                1: (0, step * shard, shard, near),
                2: (0, (3 - step) * shard, shard, far),
                3: (step * shard, 3 * shard, shard, far),
                4: (0, half, half, by_core),
            }[stage]
            source = weights.at[mat, k, pl.ds(src, size)]
        return pltpu.make_async_remote_copy(
            src_ref=source,
            dst_ref=weights.at[mat, k, pl.ds(dst, size)],
            send_sem=ag_send.at[stage, k, mat],
            recv_sem=ag_recv.at[stage, k, mat],
            device_id=(to,),
            device_id_type=MESH,
        )

    def plane_at(i):
        return (i + 1) % planes

    def rs(stage, i, mat):
        slot, k = i % 2, plane_at(i)
        near, far = (by_x, by_y) if mat == 0 else (by_y, by_x)
        src, dst, to = [
            lambda: (send_one.at[mat], recv_one.at[slot, mat], by_core),
            lambda: (send_two.at[mat], recv_two.at[slot, mat], near),
            lambda: (send_three.at[mat], recv_three.at[slot, mat], far),
            lambda: (send_four.at[slot, mat], recv_four.at[i, mat], by_z(k)),
        ][stage]()
        return pltpu.make_async_remote_copy(
            src_ref=src,
            dst_ref=dst,
            send_sem=rs_send.at[stage, i, mat],
            recv_sem=rs_recv.at[stage, i, mat],
            device_id=(to,),
            device_id_type=MESH,
        )

    def small_gather(stage, k):
        src, dst, to = [
            lambda: (small_all.at[0, 0], small_all.at[0, k], by_z(k)),
            lambda: (small_all.at[0], small_all.at[k], (me, by_x, by_y, by_both)[k]),
            lambda: (small_all.at[pl.ds(0, 4)], small_all.at[pl.ds(4, 4)], by_core),
        ][stage]()
        return pltpu.make_async_remote_copy(
            src_ref=src,
            dst_ref=dst,
            send_sem=sg_send.at[stage, k],
            recv_sem=sg_recv.at[stage, k],
            device_id=(to,),
            device_id_type=MESH,
        )

    def small_reduce(stage, k):
        src, dst, to = [
            lambda: (small_all.at[pl.ds(4, 4)], small_core, by_core),
            lambda: (small_all.at[k], small_plane.at[k], (me, by_x, by_y, by_both)[k]),
            lambda: (small_all.at[0, k], small_z.at[k], by_z(k)),
        ][stage]()
        return pltpu.make_async_remote_copy(
            src_ref=src,
            dst_ref=dst,
            send_sem=ss_send.at[stage, k],
            recv_sem=ss_recv.at[stage, k],
            device_id=(to,),
            device_id_type=MESH,
        )

    def bias_reduce(stage, k):
        to = [lambda: by_core, lambda: (me, by_x, by_y, by_both)[k], lambda: by_z(k)][stage]()
        return pltpu.make_async_remote_copy(
            src_ref=biases.at[stage],
            dst_ref=biases_in.at[stage, k],
            send_sem=bs_send.at[stage, k],
            recv_sem=bs_recv.at[stage, k],
            device_id=(to,),
            device_id_type=MESH,
        )

    def late_reduce(stage, k):
        to = [lambda: by_core, lambda: (me, by_x, by_y, by_both)[k], lambda: by_z(k)][stage]()
        return pltpu.make_async_remote_copy(
            src_ref=late.at[stage],
            dst_ref=late_in.at[stage, k],
            send_sem=ls_send.at[stage, k],
            recv_sem=ls_recv.at[stage, k],
            device_id=(to,),
            device_id_type=MESH,
        )

    hidden_tok = c_one.shape[0]
    unit = math.gcd(tin_own.shape[0], hidden_tok)
    lines_in = tin_own.shape[0] // unit
    first_lines = (lines_in + 1) // 2
    lines_out = tout_own.shape[0] // patches
    own_vec = gain_one_own.shape[0]
    turns = hidden_tok // unit
    devices = planes * PLANE

    def place_of(d):
        dz, dy, dx, dc = d // PLANE, (d // 4) % 2, (d // 2) % 2, d % 2
        far = (dc + core) % 2 * 4 + (dy + row) % 2 * 2 + (dx + col) % 2
        k, bit = 0, 1
        while bit < planes:
            k = k + bit * ((dz // bit + z // bit) % 2)
            bit *= 2
        return far, k

    def load(b):
        return pltpu.make_async_copy(images.at[b], grad_zed.at[b], in_sem.at[0, b])

    def load_top(b):
        return pltpu.make_async_copy(cotangent.at[b], total.at[b], in_sem.at[1, b])

    def reload_image(b):
        return pltpu.make_async_copy(images.at[b], mid.at[b], in_sem.at[3, b])

    def reload(b):
        return pltpu.make_async_copy(cotangent.at[b], cot.at[b % 2], in_sem.at[2, b])

    for b in range(count):
        load_top(b).start()
    for b in range(count):
        load(b).start()
    small_own[...] = jnp.zeros_like(small_own)
    for i in range(lines_in):
        at, lane = (i, 0) if i < first_lines else (i - first_lines, 64)
        small_own[at : at + 1, lane : lane + unit] = tin_own[i * unit : (i + 1) * unit].reshape(1, unit)
    for i, piece in enumerate((gain_one_own, shift_one_own, gain_two_own, shift_two_own, c_four_own)):
        small_own[24 + i : 25 + i, 64 : 64 + own_vec] = piece[...].reshape(1, own_vec)
    small_own[31:32, 0:shard] = c_in_own[...].reshape(1, shard)
    for i in range(lines_out):
        line = tout_own[i * patches : (i + 1) * patches].reshape(1, patches)
        small_own[32 + i : 33 + i, :] = line[:, 0:128]
        small_own[48 + i : 49 + i, 0 : patches - 128] = line[:, 128:patches]
    small_all[0, 0] = small_own[...].astype(LOW)
    weights[0, 0, 0:shard] = w_in[...].astype(LOW)
    weights[1, 0, 0:shard] = w_out[...].astype(LOW)

    barrier = pltpu.get_barrier_semaphore()
    peers = [by_core, by_x, by_y, by_both] + [by_z(k) for k in range(1, planes)]
    for peer in peers:
        pl.semaphore_signal(barrier, inc=1, device_id=(peer,), device_id_type=MESH)
    pl.semaphore_wait(barrier, len(peers))

    mats = (0, 1)

    def ag_planes(distance):
        for k in range(1, planes):
            away = plane_of(k) - z

            @pl.when((away == distance) | (away == -distance))
            def _():
                for mat in mats:
                    ag(0, k, mat).start()

    def ag_direct(k):
        for mat in mats:
            ag(0, k, mat).wait_recv()
        for mat in mats:
            ag(1, k, mat).start()
        for mat in mats:
            ag(2, k, mat).start()

    def ag_forward(k):
        for mat in mats:
            ag(1, k, mat).wait_recv()
            ag(3, k, mat).start()

    def ag_core(k):
        for mat in mats:
            ag(2, k, mat).wait_recv()
            ag(3, k, mat).wait_recv()
            ag(4, k, mat).start()

    def ag_ready(k):
        for mat in mats:
            ag(4, k, mat).wait_recv()

    for k in range(1, planes):
        small_gather(0, k).start()
    for mat in mats:
        ag(1, 0, mat).start()
    ag_planes(1)

    grad_vecs[...] = jnp.zeros_like(grad_vecs)
    grad_tin[...] = jnp.zeros_like(grad_tin)
    grad_tout[...] = jnp.zeros_like(grad_tout)

    def channel_top(r, carry):
        tops = []
        for h in range(2):
            b = 2 * r + h
            load_top(b).wait()
            tops.append(padded(total[b] * mask[b].astype(WIDE), lot))
        top[r] = jnp.concatenate(tops, axis=0).astype(LOW)
        grad_vecs[2:3, :] += jnp.sum(top[r].astype(WIDE), axis=0, keepdims=True)
        return carry

    def first_norm(b, carry):
        load(b).wait()
        mid[b] = normalize(grad_zed[b])[0]
        return carry

    lax.fori_loop(0, blocks, channel_top, 0)
    for k in range(1, planes):
        small_gather(0, k).wait_recv()
    for k in range(1, 4):
        small_gather(1, k).start()
    for mat in mats:
        ag(2, 0, mat).start()
    ag_planes(2)
    lax.fori_loop(0, count, first_norm, 0)
    ag_forward(0)
    for distance in range(3, planes):
        ag_planes(distance)
    for k in range(1, 4):
        small_gather(1, k).wait_recv()
    small_gather(2, 0).start()
    ag_direct(plane_at(0))
    small_gather(2, 0).wait_recv()

    tin[...] = jnp.zeros_like(tin)
    tout[...] = jnp.zeros_like(tout)
    for d in range(devices):
        far, k = place_of(d)
        message = small_all[far, k].astype(WIDE)
        lines[d * lines_in : d * lines_in + first_lines, :] = message[0:first_lines, :]
        shifted = jnp.concatenate([message[0:24, 64:128], message[0:24, 0:64]], axis=1)
        lines[d * lines_in + first_lines : (d + 1) * lines_in, :] = shifted[0 : lines_in - first_lines, :]
        vecs[:, d * own_vec : (d + 1) * own_vec] = message[24:32, 64 : 64 + own_vec]
        c_in[d] = message[31:32, 0:shard]
        tout[d * lines_out : (d + 1) * lines_out, 0:128] = message[32 : 32 + lines_out, :]
        tout[d * lines_out : (d + 1) * lines_out, 128:patches] = message[48 : 48 + lines_out, 0 : patches - 128]
    for turn in range(turns):
        tin[0:patches, turn * unit : (turn + 1) * unit] = lines[pl.ds(turn, patches, stride=turns), :][:, 0:unit]
    for rest, into, at in ((c_one, tin, patches), (c_two, tout, hidden_tok)):
        rest = rest[...].reshape(1, rest.shape[0])
        for i in range(3):
            term = rest.astype(LOW).astype(WIDE)
            into[at + i : at + i + 1, 0 : rest.shape[1]] = term
            rest = rest - term
    tin_t[...] = tin[...].T.astype(LOW)
    tout_t[...] = tout[...].T.astype(LOW)
    ones = jnp.ones((3, width), WIDE)

    gain_one, shift_one = vecs[0:1, :], vecs[1:2, :]
    gain_two, shift_two, c_four = vecs[2:3, :], vecs[3:4, :], vecs[4:5, :]
    for k in range(planes):
        for place in range(PLANE):
            near = plane_of(k) * PLANE + (
                (row + (place // 2) % 2) % 2 * 4 + (col + place % 2) % 2 * 2 + (core + place // 4) % 2
            )
            c_in_rel[k, :, place * shard : (place + 1) * shard] = c_in[near]

    def token_forward(b, carry):
        fed = mid[b] * gain_one + shift_one
        mixed[b] = padded(jnp.concatenate([fed, ones], axis=0), pad).astype(LOW)
        value, slope = gelu_parts(dot(tin_t[...], mixed[b], NN))
        act_t[b] = padded(jnp.concatenate([value, ones], axis=0), act_t.shape[1]).astype(LOW)
        slope_t[b] = slope.astype(LOW)
        mid[b] = grad_zed[b] + dot(tout_t[...], act_t[b], NN)[0:patches]
        return carry

    def channel_inputs(r, carry):
        parts = []
        for h in range(2):
            normed, _ = normalize(mid[2 * r + h])
            parts.append(padded(normed * gain_two + shift_two, lot))
        zed[r] = jnp.concatenate(parts, axis=0).astype(LOW)
        return carry

    first, second = count // 3, 2 * count // 3
    lax.fori_loop(0, first, token_forward, 0)
    ag_core(0)
    lax.fori_loop(first, second, token_forward, 0)
    ag_forward(plane_at(0))
    lax.fori_loop(second, count, token_forward, 0)
    if planes > 2:
        ag_direct(plane_at(1))
    lax.fori_loop(0, blocks, channel_inputs, 0)
    ag_core(plane_at(0))
    total[...] = jnp.zeros_like(total)
    grad_zed[...] = jnp.zeros_like(grad_zed)

    def rs_two(i):
        for mat in mats:
            rs(0, i, mat).wait_recv()
            own_sum[mat] += recv_one[i % 2, mat].astype(WIDE)
            first, second = (1, 3) if mat == 0 else (2, 3)

            @pl.when(i > 0)
            def _():
                rs(1, i - 1, mat).wait_send()

            send_two[mat, 0:shard] = own_sum[mat, first * shard : (first + 1) * shard].astype(LOW)
            send_two[mat, shard : 2 * shard] = own_sum[mat, second * shard : (second + 1) * shard].astype(LOW)
            rs(1, i, mat).start()

    def rs_three(i):
        for mat in mats:
            rs(1, i, mat).wait_recv()
            other = 2 if mat == 0 else 1

            @pl.when(i > 0)
            def _():
                rs(2, i - 1, mat).wait_send()

            keep_sum[mat] = own_sum[mat, 0:shard] + recv_two[i % 2, mat, 0:shard].astype(WIDE)
            send_three[mat] = (
                own_sum[mat, other * shard : (other + 1) * shard]
                + recv_two[i % 2, mat, shard : 2 * shard].astype(WIDE)
            ).astype(LOW)
            rs(2, i, mat).start()

    def rs_four(i):
        for mat in mats:
            rs(2, i, mat).wait_recv()

            @pl.when(i > 1)
            def _():
                rs(3, i - 2, mat).wait_send()

            send_four[i % 2, mat] = (keep_sum[mat] + recv_three[i % 2, mat].astype(WIDE)).astype(LOW)
            rs(3, i, mat).start()

    def rs_last():
        last = planes - 1
        for mat in mats:
            result = grad_in if mat == 0 else grad_out
            rs(2, last, mat).wait_recv()
            summed = keep_sum[mat] + recv_three[last % 2, mat].astype(WIDE)
            for i in range(last):
                rs(3, i, mat).wait_recv()
                summed = summed + recv_four[i, mat].astype(WIDE)
            result[...] = summed

    tile = chunk // 3

    def channel_chunk(i, carry):
        k = plane_at(i)
        ag_ready(k)

        def rows(r, inner):
            for s in range(3):
                part = slice(s * tile, (s + 1) * tile)
                pre = dot(zed[r], weights[0, k, part], NT) + c_in_rel[k, :, part]
                value, slope = gelu_parts(pre)
                act[pl.ds(r * pair, pair), part] = value.astype(LOW)
                back = (dot(top[r], weights[1, k, part], NT) * slope).astype(LOW)
                grad_pre[pl.ds(r * pair, pair), part] = back
            up = dot(act[pl.ds(r * pair, pair), :], weights[1, k], NN)
            down = dot(grad_pre[pl.ds(r * pair, pair), :], weights[0, k], NN)
            for h in range(2):
                total[2 * r + h] += up[h * lot : h * lot + patches]
                grad_zed[2 * r + h] += down[h * lot : h * lot + patches]

            @pl.when((r == 0) & (i + 2 < planes))
            def _():
                ag_forward(i + 2)

            @pl.when((r == 1) & (i + 3 < planes))
            def _():
                ag_direct(i + 3)

            @pl.when((r == 1) & (i > 1))
            def _():
                rs_four(i - 2)

            return inner

        lax.fori_loop(0, blocks, rows, 0)

        @pl.when(i + 2 < planes)
        def _():
            ag_core(i + 2)

        back_sum = jnp.sum(grad_pre[...].astype(WIDE), axis=0, keepdims=True)
        for place in range(PLANE):
            near = plane_of(k) * PLANE + (
                (row + (place // 2) % 2) % 2 * 4 + (col + place % 2) % 2 * 2 + (core + place // 4) % 2
            )
            grad_c_in[near] = back_sum[:, place * shard : (place + 1) * shard]

        flat_top = top[...].reshape(blocks * pair, width)
        flat_zed = zed[...].reshape(blocks * pair, width)
        for mat, left, right in ((1, act, flat_top), (0, grad_pre, flat_zed)):
            @pl.when(i > 0)
            def _():
                rs(0, i - 1, mat).wait_send()

            send_one[mat] = dot(left[:, half:chunk], right, TN).astype(LOW)
            rs(0, i, mat).start()

        @pl.when(i > 0)
        def _():
            rs_three(i - 1)

        for mat, left, right in ((1, act, flat_top), (0, grad_pre, flat_zed)):
            own_sum[mat] = dot(left[:, 0:half], right, TN)
        rs_two(i)
        return carry

    for b in range(2):
        reload(b).start()
    lax.fori_loop(0, planes, channel_chunk, 0)

    tin_low = tin[...].astype(LOW)
    tout_low = tout[0:hidden_tok, :].astype(LOW)

    def token_backward(b, carry):
        keep = mask[b].astype(WIDE)
        total[b] = (mid[b] + total[b] + c_four) * keep
        normed, scale = normalize(mid[b])
        down = grad_zed[b]
        grad_vecs[0:1, :] += jnp.sum(down * normed, axis=0, keepdims=True)
        grad_vecs[1:2, :] += jnp.sum(down, axis=0, keepdims=True)
        reload(b).wait()
        grad_mid = cot[b % 2] * keep + norm_back(down, normed, scale, gain_two)

        @pl.when(b + 2 < count)
        def _():
            reload(b + 2).start()

        back = padded(grad_mid, pad).astype(LOW)
        grad_tout[...] += dot(act_t[b], back, NT)
        grad_zed[b] = grad_mid
        slope_t[b] = (dot(tout_low, back, NN) * slope_t[b].astype(WIDE)).astype(LOW)
        grad_tin[:, 0:hidden_tok] += dot(mixed[b], slope_t[b], NT)

        reload_image(b).start()

        @pl.when((b == 0) & (planes > 1))
        def _():
            rs_four(planes - 2)

        return carry

    def image_backward(b, carry):
        grad_mixed = dot(tin_low, slope_t[b], NN)[0:patches]
        reload_image(b).wait()
        normed, scale = normalize(mid[b])
        late[0, 0:1, :] += jnp.sum(grad_mixed * normed, axis=0, keepdims=True)
        late[0, 1:2, :] += jnp.sum(grad_mixed, axis=0, keepdims=True)
        grad_zed[b] += norm_back(grad_mixed, normed, scale, gain_one)

        @pl.when(b == 1)
        def _():
            small_second()

        @pl.when(b == count - 2)
        def _():
            small_third()

        return carry

    late[0] = jnp.zeros_like(late[0])
    lax.fori_loop(0, count, token_backward, 0)

    biases[0] = jnp.zeros_like(biases[0])
    for i in range(hidden_tok // 128):
        biases[0, i : i + 1, :] = grad_tin[patches : patches + 1, i * 128 : (i + 1) * 128]
    biases[0, 3:4, :] = grad_tout[hidden_tok : hidden_tok + 1, 0:128]
    biases[0, 4:5, 0 : patches - 128] = grad_tout[hidden_tok : hidden_tok + 1, 128:patches]
    bias_reduce(0, 0).start()
    for turn in range(turns):
        lines[pl.ds(turn, patches, stride=turns), :] = grad_tin[0:patches, turn * unit : turn * unit + 128]
    for d in range(devices):
        far, k = place_of(d)
        low = lines[d * lines_in : d * lines_in + first_lines, :]
        high = lines[d * lines_in + first_lines : (d + 1) * lines_in, :]
        small_sum[far, k, 0:first_lines, 0:64] = low[:, 0:64]
        small_sum[far, k, 0 : lines_in - first_lines, 64:128] = high[:, 0:64]
        small_sum[far, k, 24:27, 64 : 64 + own_vec] = grad_vecs[0:3, d * own_vec : (d + 1) * own_vec]
        small_sum[far, k, 31:32, 0:shard] = grad_c_in[d]
        small_sum[far, k, 32 : 32 + lines_out, :] = grad_tout[d * lines_out : (d + 1) * lines_out, 0:128]
        small_sum[far, k, 48 : 48 + lines_out, 0 : patches - 128] = grad_tout[
            d * lines_out : (d + 1) * lines_out, 128:patches
        ]
    for k in range(1, planes):
        small_gather(0, k).wait_send()
    for far in range(1, 4):
        small_gather(1, far).wait_send()
    small_gather(2, 0).wait_send()
    for far in range(4, PLANE):
        small_all[far] = small_sum[far].astype(LOW)
    small_reduce(0, 0).start()
    rs_three(planes - 1)

    def small_second():
        bias_reduce(0, 0).wait_recv()
        biases[1] = biases[0] + biases_in[0, 0]
        small_reduce(0, 0).wait_recv()
        for far in range(4):
            small_sum[far] += small_core[far].astype(WIDE)
        for far in range(1, 4):
            small_all[far] = small_sum[far].astype(LOW)
            small_reduce(1, far).start()
            bias_reduce(1, far).start()

    def small_third():
        for far in range(1, 4):
            small_reduce(1, far).wait_recv()
            bias_reduce(1, far).wait_recv()
            small_sum[0] += small_plane[far].astype(WIDE)
        biases[2] = (biases[1] + biases_in[1, 1]) + (biases_in[1, 2] + biases_in[1, 3])
        for k in range(1, planes):
            small_all[0, k] = small_sum[0, k].astype(LOW)
            small_reduce(2, k).start()
            bias_reduce(2, k).start()

    lax.fori_loop(0, count, image_backward, 0)
    late_reduce(0, 0).start()
    rs_last()
    late_reduce(0, 0).wait_recv()
    late[1] = late[0] + late_in[0, 0]
    for far in range(1, 4):
        late_reduce(1, far).start()
    summed = small_sum[0, 0]
    tree = [biases[2]]
    for k in range(1, planes):
        small_reduce(2, k).wait_recv()
        bias_reduce(2, k).wait_recv()
        summed = summed + small_z[k].astype(WIDE)
        tree.append(biases_in[2, k])
    small_out[...] = summed
    late_sum = late[1]
    for far in range(1, 4):
        late_reduce(1, far).wait_recv()
        late_sum = late_sum + late_in[1, far]
    late[2] = late_sum
    for k in range(1, planes):
        late_reduce(2, k).start()
    for k in range(1, planes):
        late_reduce(2, k).wait_recv()
        late_sum = late_sum + late_in[2, k]
    late_sum = pltpu.roll(padded(late_sum, 8), width - own_vec * me, 1)
    small_out[27:29, 64 : 64 + own_vec] = late_sum[0:2, 0:own_vec]
    while len(tree) > 1:
        tree = [tree[i] + tree[i + 1] for i in range(0, len(tree), 2)]
    biases_out[...] = tree[0]

    for mat in mats:
        for k in range(planes):
            for stage in range(5):
                if stage > 0 or k > 0:
                    ag(stage, k, mat).wait_send()
        for stage in range(3):
            rs(stage, planes - 1, mat).wait_send()
        for i in range(max(0, planes - 3), planes - 1):
            rs(3, i, mat).wait_send()
    late_reduce(0, 0).wait_send()
    for far in range(1, 4):
        late_reduce(1, far).wait_send()
    for k in range(1, planes):
        late_reduce(2, k).wait_send()
    small_reduce(0, 0).wait_send()
    bias_reduce(0, 0).wait_send()
    for far in range(1, 4):
        small_reduce(1, far).wait_send()
        bias_reduce(1, far).wait_send()
    for k in range(1, planes):
        small_reduce(2, k).wait_send()
        bias_reduce(2, k).wait_send()


def finish_kernel(
    block_in,
    image_in,
    w_in,
    w_out,
    small,
    biases,
    block_out,
    image_out,
    w_in_out,
    w_out_out,
    tin,
    tout,
    gain_one,
    shift_one,
    gain_two,
    shift_two,
    c_four,
    c_in,
    c_one,
    c_two,
    sem,
):
    copies = [
        pltpu.make_async_copy(block_in, block_out, sem.at[0]),
        pltpu.make_async_copy(image_in, image_out, sem.at[1]),
        pltpu.make_async_copy(w_in, w_in_out, sem.at[2]),
        pltpu.make_async_copy(w_out, w_out_out, sem.at[3]),
    ]
    for copy in copies:
        copy.start()
    hidden_tok, patches = c_one.shape[0], c_two.shape[0]
    unit = math.gcd(tin.shape[0], hidden_tok)
    lines_in = tin.shape[0] // unit
    first_lines = (lines_in + 1) // 2
    for i in range(lines_in):
        at, lane = (i, 0) if i < first_lines else (i - first_lines, 64)
        tin[i * unit : (i + 1) * unit] = small[at : at + 1, lane : lane + unit].reshape(unit)
    for i in range(tout.shape[0] // patches):
        tout[i * patches : i * patches + 128] = small[32 + i : 33 + i, :].reshape(128)
        tout[i * patches + 128 : (i + 1) * patches] = small[48 + i : 49 + i, 0 : patches - 128].reshape(
            patches - 128
        )
    for i, piece in enumerate((gain_two, shift_two, c_four, gain_one, shift_one)):
        own_vec = piece.shape[0]
        piece[...] = small[24 + i : 25 + i, 64 : 64 + own_vec].reshape(own_vec)
    shard = c_in.shape[0]
    c_in[...] = small[31:32, 0:shard].reshape(shard)
    for i in range(hidden_tok // 128):
        c_one[i * 128 : (i + 1) * 128] = biases[i : i + 1, :].reshape(128)
    c_two[0:128] = biases[3:4, :].reshape(128)
    c_two[128:patches] = biases[4:5, 0 : patches - 128].reshape(patches - 128)
    for copy in copies:
        copy.wait()


def fast_shards(
    images,
    mask,
    cotangent,
    w_token_in,
    w_token_out,
    bias_token_in,
    bias_token_out,
    gain_one,
    shift_one,
    gain_two,
    shift_two,
    w_expand,
    bias_expand,
    w_reduce,
    bias_reduce,
):
    devices = lax.axis_size("dp")
    planes = devices // PLANE
    count, patches, width = images.shape
    hidden_tok = bias_token_in.shape[0]
    shard = w_expand.shape[0]
    pad = -(-patches // 16) * 16
    lot = -(-patches // 8) * 8
    pair = 2 * lot
    blocks = count // 2
    chunk = 8 * shard
    half = 4 * shard

    unit = math.gcd(w_token_in.shape[0], hidden_tok)
    lines_in = w_token_in.shape[0] // unit
    hidden_pad = hidden_tok + 16

    vmem = pl.BlockSpec(memory_space=pltpu.VMEM)
    hbm = pl.BlockSpec(memory_space=pl.ANY)
    shape = jax.ShapeDtypeStruct
    outs = pl.pallas_call(
        block_kernel,
        out_shape=(
            pltpu.VMEM(images.shape, WIDE),
            pltpu.VMEM(images.shape, WIDE),
            pltpu.VMEM(w_expand.shape, WIDE),
            pltpu.VMEM(w_reduce.shape, WIDE),
            pltpu.VMEM((64, 128), WIDE),
            pltpu.VMEM((8, 128), WIDE),
        ),
        in_specs=[pl.BlockSpec(memory_space=pltpu.SMEM), hbm, hbm] + [vmem] * 12,
        out_specs=[vmem] * 6,
        scratch_shapes=[
            pltpu.VMEM((2,) + images.shape[1:], WIDE),
            pltpu.VMEM((count, pad, width), LOW),
            pltpu.VMEM((count, hidden_pad, width), LOW),
            pltpu.VMEM((count, hidden_tok, width), LOW),
            pltpu.VMEM(images.shape, WIDE),
            pltpu.VMEM((blocks, pair, width), LOW),
            pltpu.VMEM((blocks, pair, width), LOW),
            pltpu.VMEM((2, planes, chunk, width), LOW),
            pltpu.VMEM((blocks * pair, chunk), LOW),
            pltpu.VMEM((blocks * pair, chunk), LOW),
            pltpu.VMEM((planes, 1, chunk), WIDE),
            pltpu.VMEM((2, half, width), WIDE),
            pltpu.VMEM((2, shard, width), WIDE),
            pltpu.VMEM((2, half, width), LOW),
            pltpu.VMEM((2, 2, half, width), LOW),
            pltpu.VMEM((2, 2 * shard, width), LOW),
            pltpu.VMEM((2, 2, 2 * shard, width), LOW),
            pltpu.VMEM((2, shard, width), LOW),
            pltpu.VMEM((2, 2, shard, width), LOW),
            pltpu.VMEM((2, 2, shard, width), LOW),
            pltpu.VMEM((planes - 1, 2, shard, width), LOW),
            pltpu.VMEM((pad, hidden_tok), WIDE),
            pltpu.VMEM((hidden_tok, pad), LOW),
            pltpu.VMEM((hidden_pad, pad), WIDE),
            pltpu.VMEM((pad, hidden_pad), LOW),
            pltpu.VMEM((8, width), WIDE),
            pltpu.VMEM((devices, 1, shard), WIDE),
            pltpu.VMEM((devices * lines_in, 128), WIDE),
            pltpu.VMEM((64, 128), WIDE),
            pltpu.VMEM((PLANE, planes, 64, 128), LOW),
            pltpu.VMEM((pad, hidden_tok + 128), WIDE),
            pltpu.VMEM((hidden_pad, pad), WIDE),
            pltpu.VMEM((8, width), WIDE),
            pltpu.VMEM((devices, 1, shard), WIDE),
            pltpu.VMEM((PLANE, planes, 64, 128), WIDE),
            pltpu.VMEM((4, planes, 64, 128), LOW),
            pltpu.VMEM((4, planes, 64, 128), LOW),
            pltpu.VMEM((planes, 64, 128), LOW),
            pltpu.VMEM((3, 8, 128), WIDE),
            pltpu.VMEM((3, max(4, planes), 8, 128), WIDE),
            pltpu.VMEM((3, 2, width), WIDE),
            pltpu.VMEM((3, max(4, planes), 2, width), WIDE),
            pltpu.SemaphoreType.DMA((4, count)),
            pltpu.SemaphoreType.DMA((5, planes, 2)),
            pltpu.SemaphoreType.DMA((5, planes, 2)),
            pltpu.SemaphoreType.DMA((4, planes, 2)),
            pltpu.SemaphoreType.DMA((4, planes, 2)),
        ]
        + [pltpu.SemaphoreType.DMA((3, max(4, planes)))] * 8,
        compiler_params=pltpu.CompilerParams(
            collective_id=0, has_side_effects=True, vmem_limit_bytes=55 * 2**20
        ),
    )(
        mask,
        images,
        cotangent,
        w_expand,
        w_reduce,
        w_token_in,
        w_token_out,
        gain_one,
        shift_one,
        gain_two,
        shift_two,
        bias_reduce,
        bias_expand,
        bias_token_in,
        bias_token_out,
    )
    flat = pl.pallas_call(
        finish_kernel,
        out_shape=(
            shape(images.shape, WIDE),
            shape(images.shape, WIDE),
            shape(w_expand.shape, WIDE),
            shape(w_reduce.shape, WIDE),
            shape(w_token_in.shape, WIDE),
            shape(w_token_out.shape, WIDE),
            *[shape(gain_one.shape, WIDE)] * 5,
            shape(bias_expand.shape, WIDE),
            shape(bias_token_in.shape, WIDE),
            shape(bias_token_out.shape, WIDE),
        ),
        in_specs=[vmem] * 6,
        out_specs=[hbm] * 4 + [vmem] * 10,
        scratch_shapes=[pltpu.SemaphoreType.DMA((4,))],
        compiler_params=pltpu.CompilerParams(vmem_limit_bytes=16 * 2**20),
    )(*outs)
    block_output, image_grad, own_win, own_wout, *rest = flat
    g_tin, g_tout, g_one, b_one, g_two, b_two, c_four, c_in, c_one, c_two = rest
    return (
        block_output,
        image_grad,
        g_tin,
        g_tout,
        c_one,
        c_two,
        g_one,
        b_one,
        g_two,
        b_two,
        own_win,
        c_in,
        own_wout,
        c_four,
    )


def fits(devices, images, w_token_in, w_token_out, bias_token_in, gain_one, w_expand):
    planes = devices // PLANE
    patches = images.shape[1]
    hidden_tok = bias_token_in.shape[0]
    shard = w_expand.shape[0]
    unit = math.gcd(w_token_in.shape[0], hidden_tok)
    return (
        devices % PLANE == 0
        and planes & (planes - 1) == 0
        and planes >= 2
        and images.shape[0] % 2 == 0
        and shard % 16 == 0
        and shard <= 128
        and (4 * shard) % 128 == 0
        and 128 < patches <= 205
        and unit <= 64
        and w_token_in.shape[0] // unit <= 49
        and w_token_out.shape[0] % patches == 0
        and w_token_out.shape[0] // patches <= 16
        and gain_one.shape[0] <= 64
        and hidden_tok == 384
    )


def choose(
    images,
    mask,
    cotangent,
    w_token_in,
    w_token_out,
    bias_token_in,
    bias_token_out,
    gain_one,
    shift_one,
    gain_two,
    shift_two,
    w_expand,
    bias_expand,
    w_reduce,
    bias_reduce,
):
    args = (
        images,
        mask,
        cotangent,
        w_token_in,
        w_token_out,
        bias_token_in,
        bias_token_out,
        gain_one,
        shift_one,
        gain_two,
        shift_two,
        w_expand,
        bias_expand,
        w_reduce,
        bias_reduce,
    )
    if fits(lax.axis_size("dp"), images, w_token_in, w_token_out, bias_token_in, gain_one, w_expand):
        return fast_shards(*args)
    return shards(*args)


def shards(
    images,
    mask,
    cotangent,
    w_token_in,
    w_token_out,
    bias_token_in,
    bias_token_out,
    gain_one,
    shift_one,
    gain_two,
    shift_two,
    w_expand,
    bias_expand,
    w_reduce,
    bias_reduce,
):
    low_type = jnp.bfloat16
    wide = jnp.float32
    count, patches, width = images.shape
    hidden_tok = bias_token_in.shape[0]
    rows = count * patches
    keep = mask.astype(wide)[:, None, None]
    small_local = (
        w_token_in.astype(low_type),
        w_token_out.astype(low_type),
        gain_one.astype(low_type),
        shift_one.astype(low_type),
        gain_two.astype(low_type),
        shift_two.astype(low_type),
        bias_reduce.astype(low_type),
    )
    channel_local = (
        w_expand.astype(low_type),
        w_reduce.astype(low_type),
        bias_expand.astype(low_type),
    )
    small_all = (
        lax.all_gather(small_local[0], "dp", axis=0, tiled=True),
        lax.all_gather(small_local[1], "dp", axis=0, tiled=True),
        lax.all_gather(small_local[2], "dp", axis=0, tiled=True),
        lax.all_gather(small_local[3], "dp", axis=0, tiled=True),
        lax.all_gather(small_local[4], "dp", axis=0, tiled=True),
        lax.all_gather(small_local[5], "dp", axis=0, tiled=True),
        lax.all_gather(small_local[6], "dp", axis=0, tiled=True),
    )
    tin = small_all[0].reshape(patches, hidden_tok)
    tout = small_all[1].reshape(hidden_tok, patches)
    g_one, b_one, g_two, b_two, c_four = [piece.astype(wide) for piece in small_all[2:]]
    normed_one, scale_one = normalize(images)
    mixed_in = (normed_one * g_one + b_one).astype(low_type)
    pre_t = (
        jnp.einsum("ps,bpd->bsd", tin, mixed_in, preferred_element_type=wide)
        + bias_token_in[None, :, None]
    )
    act_t = gelu_exact(pre_t).astype(low_type)
    middle = (
        images
        + jnp.einsum("sp,bsd->bpd", tout, act_t, preferred_element_type=wide)
        + bias_token_out[None, :, None]
    )
    normed_two, scale_two = normalize(middle.reshape(rows, width))
    zed = (normed_two * g_two + b_two).astype(low_type)
    whole_channel = (
        lax.all_gather(channel_local[0], "dp", axis=0, tiled=True),
        lax.all_gather(channel_local[1], "dp", axis=0, tiled=True),
        lax.all_gather(channel_local[2], "dp", axis=0, tiled=True),
    )
    w_in, w_out, c_in = whole_channel
    pre = (
        jnp.einsum("td,fd->tf", zed, w_in, preferred_element_type=wide) + c_in.astype(wide)[None, :]
    )
    act = gelu_exact(pre).astype(low_type)
    reduced = jnp.dot(act, w_out, preferred_element_type=wide)
    block_output = (middle + (reduced + c_four).reshape(count, patches, width)) * keep
    grad_top = cotangent * keep
    grad_branch = grad_top.reshape(rows, width).astype(low_type)
    grad_c_four = jnp.sum(grad_branch.astype(wide), axis=0)
    small_all = (
        lax.all_gather(small_local[0], "dp", axis=0, tiled=True),
        lax.all_gather(small_local[1], "dp", axis=0, tiled=True),
        lax.all_gather(small_local[2], "dp", axis=0, tiled=True),
        lax.all_gather(small_local[3], "dp", axis=0, tiled=True),
        lax.all_gather(small_local[4], "dp", axis=0, tiled=True),
        lax.all_gather(small_local[5], "dp", axis=0, tiled=True),
        lax.all_gather(small_local[6], "dp", axis=0, tiled=True),
    )
    tin = small_all[0].reshape(patches, hidden_tok)
    tout = small_all[1].reshape(hidden_tok, patches)
    g_one, b_one, g_two, b_two, c_four = [piece.astype(wide) for piece in small_all[2:]]
    whole_channel = (
        lax.all_gather(channel_local[0], "dp", axis=0, tiled=True),
        lax.all_gather(channel_local[1], "dp", axis=0, tiled=True),
        lax.all_gather(channel_local[2], "dp", axis=0, tiled=True),
    )
    w_in, w_out, c_in = whole_channel
    pre = (
        jnp.einsum("td,fd->tf", zed, w_in, preferred_element_type=wide) + c_in.astype(wide)[None, :]
    )
    act = gelu_exact(pre).astype(low_type)
    grad_act = jnp.einsum("td,fd->tf", grad_branch, w_out, preferred_element_type=wide)
    grad_pre = (grad_act * gelu_slope(pre)).astype(low_type)
    grad_zed = jnp.dot(grad_pre, w_in, preferred_element_type=wide)
    grad_in = jnp.einsum("tf,td->fd", grad_pre, zed, preferred_element_type=wide)
    grad_out = jnp.einsum("tf,td->fd", act, grad_branch, preferred_element_type=wide)
    grad_cin = jnp.sum(grad_pre.astype(wide), axis=0)
    grad_zed, grad_win, grad_wout, grad_cin = (grad_zed, grad_in, grad_out, grad_cin)
    grad_g_two = jnp.sum(grad_zed * normed_two, axis=0)
    grad_b_two = jnp.sum(grad_zed, axis=0)
    grad_mid = grad_top + norm_back(grad_zed, normed_two, scale_two, g_two).reshape(
        count, patches, width
    )
    grad_back = grad_mid.astype(low_type)
    grad_c_two = jnp.sum(grad_back.astype(wide), axis=(0, 2))
    grad_tout = jnp.einsum("bsd,bpd->sp", act_t, grad_back, preferred_element_type=wide)
    grad_act_t = jnp.einsum("sp,bpd->bsd", tout, grad_back, preferred_element_type=wide)
    grad_pre_t = (grad_act_t * gelu_slope(pre_t)).astype(low_type)
    grad_c_one = jnp.sum(grad_pre_t.astype(wide), axis=(0, 2))
    grad_tin = jnp.einsum("bpd,bsd->ps", mixed_in, grad_pre_t, preferred_element_type=wide)
    grad_mixed = jnp.einsum("ps,bsd->bpd", tin, grad_pre_t, preferred_element_type=wide)
    grad_g_one = jnp.sum(grad_mixed * normed_one, axis=(0, 1))
    grad_b_one = jnp.sum(grad_mixed, axis=(0, 1))
    image_grad = grad_mid + norm_back(grad_mixed, normed_one, scale_one, g_one)
    bias_sums = lax.psum((grad_c_one, grad_c_two), "dp")
    flat_tin = grad_tin.reshape(patches * hidden_tok)
    flat_tout = grad_tout.reshape(hidden_tok * patches)
    owned = (
        lax.psum_scatter(flat_tin, "dp", scatter_dimension=0, tiled=True),
        lax.psum_scatter(flat_tout, "dp", scatter_dimension=0, tiled=True),
        lax.psum_scatter(grad_g_one, "dp", scatter_dimension=0, tiled=True),
        lax.psum_scatter(grad_b_one, "dp", scatter_dimension=0, tiled=True),
        lax.psum_scatter(grad_g_two, "dp", scatter_dimension=0, tiled=True),
        lax.psum_scatter(grad_b_two, "dp", scatter_dimension=0, tiled=True),
        lax.psum_scatter(grad_win, "dp", scatter_dimension=0, tiled=True),
        lax.psum_scatter(grad_cin, "dp", scatter_dimension=0, tiled=True),
        lax.psum_scatter(grad_wout, "dp", scatter_dimension=0, tiled=True),
        lax.psum_scatter(grad_c_four, "dp", scatter_dimension=0, tiled=True),
    )
    (
        own_tin,
        own_tout,
        own_g_one,
        own_b_one,
        own_g_two,
        own_b_two,
        own_win,
        own_cin,
        own_wout,
        own_c_four,
    ) = owned
    return (
        block_output,
        image_grad,
        own_tin,
        own_tout,
        bias_sums[0],
        bias_sums[1],
        own_g_one,
        own_b_one,
        own_g_two,
        own_b_two,
        own_win,
        own_cin,
        own_wout,
        own_c_four,
    )


def solution(mesh):
    placed = (
        P("dp", None, None),
        P("dp"),
        P("dp", None, None),
        P("dp"),
        P("dp"),
        P(),
        P(),
        P("dp"),
        P("dp"),
        P("dp"),
        P("dp"),
        P("dp", None),
        P("dp"),
        P("dp", None),
        P("dp"),
    )
    return jax.shard_map(
        choose,
        mesh=mesh,
        in_specs=placed,
        out_specs=(
            P("dp", None, None),
            P("dp", None, None),
            P("dp"),
            P("dp"),
            P(),
            P(),
            P("dp"),
            P("dp"),
            P("dp"),
            P("dp"),
            P("dp", None),
            P("dp"),
            P("dp", None),
            P("dp"),
        ),
        check_vma=False,
    )
```

```python
import math

import jax
import jax.numpy as jnp
from jax import lax
from jax.experimental import pallas as pl
from jax.experimental.pallas import tpu as pltpu
from jax.sharding import PartitionSpec as P

EPS = 1e-06


def gelu_exact(v):
    return 0.5 * v * (1.0 + lax.erf(v * 0.7071067811865476))


def gelu_slope(v):
    return 0.5 * (1.0 + lax.erf(v * 0.7071067811865476)) + v * 0.3989422804014327 * jnp.exp(
        -0.5 * v * v
    )


def normalize(v):
    centered = v - jnp.mean(v, axis=-1, keepdims=True)
    scale = lax.rsqrt(jnp.mean(centered * centered, axis=-1, keepdims=True) + EPS)
    return (centered * scale, scale)


def norm_back(grad_in, normed, scale, gain):
    scaled = grad_in * gain
    return scale * (
        scaled
        - jnp.mean(scaled, axis=-1, keepdims=True)
        - normed * jnp.mean(scaled * normed, axis=-1, keepdims=True)
    )


WIDE = jnp.float32
LOW = jnp.bfloat16
MESH = pl.DeviceIdType.MESH
NT = (((1,), (1,)), ((), ()))
TN = (((0,), (0,)), ((), ()))
NN = (((1,), (0,)), ((), ()))
PLANE = 8


def dot(a, b, dims):
    return lax.dot_general(a, b, dims, preferred_element_type=WIDE)


def gelu_parts(v):
    cdf = 0.5 * (1.0 + lax.erf(v * 0.7071067811865476))
    return v * cdf, cdf + v * 0.3989422804014327 * jnp.exp(-0.5 * v * v)


def padded(v, rows):
    return jnp.concatenate([v, jnp.zeros((rows - v.shape[0], v.shape[1]), v.dtype)], axis=0)


def block_kernel(
    mask,
    images,
    cotangent,
    w_in,
    w_out,
    tin_own,
    tout_own,
    gain_one_own,
    shift_one_own,
    gain_two_own,
    shift_two_own,
    c_four_own,
    c_in_own,
    c_one,
    c_two,
    total,
    grad_zed,
    grad_in,
    grad_out,
    small_out,
    biases_out,
    cot,
    mixed,
    act_t,
    slope_t,
    mid,
    zed,
    top,
    weights,
    act,
    grad_pre,
    c_in_rel,
    own_sum,
    keep_sum,
    send_one,
    recv_one,
    send_two,
    recv_two,
    send_three,
    recv_three,
    send_four,
    recv_four,
    tin,
    tin_t,
    tout,
    tout_t,
    vecs,
    c_in,
    lines,
    small_own,
    small_all,
    grad_tin,
    grad_tout,
    grad_vecs,
    grad_c_in,
    small_sum,
    small_core,
    small_plane,
    small_z,
    biases,
    biases_in,
    late,
    late_in,
    scales,
    in_sem,
    ag_send,
    ag_recv,
    rs_send,
    rs_recv,
    sg_send,
    sg_recv,
    ss_send,
    ss_recv,
    bs_send,
    bs_recv,
    ls_send,
    ls_recv,
):
    count, patches, width = images.shape
    planes = weights.shape[1]
    shard = w_in.shape[0]
    half = 4 * shard
    chunk = 8 * shard
    pad = mixed.shape[1]
    pair = zed.shape[1]
    lot = pair // 2
    blocks = count // 2
    me = lax.axis_index("dp")
    core = me % 2
    col = (me // 2) % 2
    row = (me // 4) % 2
    z = me // PLANE
    by_core = me + 1 - 2 * core
    by_x = me + 2 - 4 * col
    by_y = me + 4 - 8 * row
    by_both = by_x + by_y - me

    def plane_of(k):
        out, bit = z, 1
        while bit < planes:
            out = out + bit * ((k // bit) % 2) * (1 - 2 * ((z // bit) % 2))
            bit *= 2
        return out

    def by_z(k):
        return me + PLANE * (plane_of(k) - z)

    def ag(stage, k, mat):
        near, far = (by_x, by_y) if mat == 0 else (by_y, by_x)
        step = 1 if mat == 0 else 2
        if stage == 0:
            src, dst, size, to = 0, 0, shard, by_z(k)
            source = weights.at[mat, 0, pl.ds(src, size)]
        else:
            src, dst, size, to = {
                1: (0, step * shard, shard, near),
                2: (0, (3 - step) * shard, shard, far),
                3: (step * shard, 3 * shard, shard, far),
                4: (0, half, 3 * shard, by_core),
                5: (3 * shard, half + 3 * shard, shard, by_core),
            }[stage]
            source = weights.at[mat, k, pl.ds(src, size)]
        return pltpu.make_async_remote_copy(
            src_ref=source,
            dst_ref=weights.at[mat, k, pl.ds(dst, size)],
            send_sem=ag_send.at[stage, k, mat],
            recv_sem=ag_recv.at[stage, k, mat],
            device_id=(to,),
            device_id_type=MESH,
        )

    def plane_at(i):
        return (i + 1) % planes

    def rs(stage, i, mat):
        slot, k = i % 2, plane_at(i)
        near, far = (by_x, by_y) if mat == 0 else (by_y, by_x)
        src, dst, to = [
            lambda: (send_one.at[mat], recv_one.at[slot, mat], by_core),
            lambda: (send_two.at[mat], recv_two.at[slot, mat], near),
            lambda: (send_three.at[mat], recv_three.at[slot, mat], far),
            lambda: (send_four.at[slot, mat], recv_four.at[i, mat], by_z(k)),
        ][stage]()
        return pltpu.make_async_remote_copy(
            src_ref=src,
            dst_ref=dst,
            send_sem=rs_send.at[stage, i, mat],
            recv_sem=rs_recv.at[stage, i, mat],
            device_id=(to,),
            device_id_type=MESH,
        )

    def small_gather(stage, k, group):
        src, dst, to = [
            lambda: (small_all.at[group, 0, 0], small_all.at[group, 0, k], by_z(k)),
            lambda: (small_all.at[group, 0], small_all.at[group, k], (me, by_x, by_y, by_both)[k]),
            lambda: (small_all.at[group, pl.ds(0, 4)], small_all.at[group, pl.ds(4, 4)], by_core),
        ][stage]()
        return pltpu.make_async_remote_copy(
            src_ref=src,
            dst_ref=dst,
            send_sem=sg_send.at[stage, k, group],
            recv_sem=sg_recv.at[stage, k, group],
            device_id=(to,),
            device_id_type=MESH,
        )

    def small_reduce(stage, k):
        src, dst, to = [
            lambda: (small_all.at[:, pl.ds(4, 4)], small_core, by_core),
            lambda: (small_all.at[:, k], small_plane.at[:, k], (me, by_x, by_y, by_both)[k]),
            lambda: (small_all.at[:, 0, k], small_z.at[k], by_z(k)),
        ][stage]()
        return pltpu.make_async_remote_copy(
            src_ref=src,
            dst_ref=dst,
            send_sem=ss_send.at[stage, k],
            recv_sem=ss_recv.at[stage, k],
            device_id=(to,),
            device_id_type=MESH,
        )

    def bias_reduce(stage, k):
        to = [lambda: by_core, lambda: (me, by_x, by_y, by_both)[k], lambda: by_z(k)][stage]()
        return pltpu.make_async_remote_copy(
            src_ref=biases.at[stage],
            dst_ref=biases_in.at[stage, k],
            send_sem=bs_send.at[stage, k],
            recv_sem=bs_recv.at[stage, k],
            device_id=(to,),
            device_id_type=MESH,
        )

    def late_reduce(stage, k):
        to = [lambda: by_core, lambda: (me, by_x, by_y, by_both)[k], lambda: by_z(k)][stage]()
        return pltpu.make_async_remote_copy(
            src_ref=late.at[stage],
            dst_ref=late_in.at[stage, k],
            send_sem=ls_send.at[stage, k],
            recv_sem=ls_recv.at[stage, k],
            device_id=(to,),
            device_id_type=MESH,
        )

    hidden_tok = c_one.shape[0]
    unit = math.gcd(tin_own.shape[0], hidden_tok)
    lines_in = tin_own.shape[0] // unit
    first_lines = (lines_in + 1) // 2
    lines_out = tout_own.shape[0] // patches
    own_vec = gain_one_own.shape[0]
    turns = hidden_tok // unit
    devices = planes * PLANE

    def place_of(d):
        dz, dy, dx, dc = d // PLANE, (d // 4) % 2, (d // 2) % 2, d % 2
        far = (dc + core) % 2 * 4 + (dy + row) % 2 * 2 + (dx + col) % 2
        k, bit = 0, 1
        while bit < planes:
            k = k + bit * ((dz // bit + z // bit) % 2)
            bit *= 2
        return far, k

    def load(b):
        return pltpu.make_async_copy(images.at[b], grad_zed.at[b], in_sem.at[0, b])

    def load_top(b):
        return pltpu.make_async_copy(cotangent.at[b], total.at[b], in_sem.at[1, b])

    def reload_image(b):
        return pltpu.make_async_copy(images.at[b], mid.at[b], in_sem.at[3, b])

    def reload(b):
        return pltpu.make_async_copy(cotangent.at[b], cot.at[b % 2], in_sem.at[2, b])

    for b in range(count):
        load_top(b).start()
    for b in range(count):
        load(b).start()
    small_own[...] = jnp.zeros_like(small_own)
    for i in range(lines_in):
        at, lane = (i, 0) if i < first_lines else (i - first_lines, 64)
        small_own[at : at + 1, lane : lane + unit] = tin_own[i * unit : (i + 1) * unit].reshape(1, unit)
    for i, piece in enumerate((gain_one_own, shift_one_own, gain_two_own, shift_two_own, c_four_own)):
        small_own[24 + i : 25 + i, 64 : 64 + own_vec] = piece[...].reshape(1, own_vec)
    small_own[31:32, 0:shard] = c_in_own[...].reshape(1, shard)
    for i in range(lines_out):
        line = tout_own[i * patches : (i + 1) * patches].reshape(1, patches)
        small_own[32 + i : 33 + i, :] = line[:, 0:128]
        small_own[48 + i : 49 + i, 0 : patches - 128] = line[:, 128:patches]
    for group in range(2):
        small_all[group, 0, 0] = small_own[32 * group : 32 * (group + 1)].astype(LOW)
    weights[0, 0, 0:shard] = w_in[...].astype(LOW)
    weights[1, 0, 0:shard] = w_out[...].astype(LOW)

    barrier = pltpu.get_barrier_semaphore()
    peers = [by_core, by_x, by_y, by_both] + [by_z(k) for k in range(1, planes)]
    for peer in peers:
        pl.semaphore_signal(barrier, inc=1, device_id=(peer,), device_id_type=MESH)
    pl.semaphore_wait(barrier, len(peers))

    mats = (0, 1)
    row_of_four = planes == 4
    inner = (z == 1) | (z == 2)

    def ag_pass(which, mat):
        src, dst, to = ((1, 2, by_z(3)), (3, 2, by_z(1)), (2, 3, by_z(1)))[which]
        return pltpu.make_async_remote_copy(
            src_ref=weights.at[mat, src, pl.ds(0, shard)],
            dst_ref=weights.at[mat, dst, pl.ds(0, shard)],
            send_sem=ag_send.at[6, which, mat],
            recv_sem=ag_recv.at[0, dst, mat],
            device_id=(to,),
            device_id_type=MESH,
        )

    def ag_planes():
        for mat in mats:
            ag(0, 1, mat).start()
        if row_of_four:

            @pl.when(inner)
            def _():
                for mat in mats:
                    ag(0, 3, mat).start()

    def ag_planes_pass():
        if row_of_four:

            @pl.when(inner)
            def _():
                for which, came in ((0, 1), (1, 3)):
                    for mat in mats:
                        ag(0, came, mat).wait_recv()
                        ag_pass(which, mat).start()

    def ag_planes_last():
        if row_of_four:

            @pl.when(inner)
            def _():
                for mat in mats:
                    ag(0, 2, mat).wait_recv()
                    ag_pass(2, mat).start()

    def ag_direct(k):
        if row_of_four:

            @pl.when(jnp.logical_not(inner))
            def _():
                for mat in mats:
                    ag(0, k, mat).wait_recv()

        else:
            for mat in mats:
                ag(0, k, mat).wait_recv()
        for mat in mats:
            ag(1, k, mat).start()
        for mat in mats:
            ag(2, k, mat).start()

    def ag_forward(k):
        for mat in mats:
            ag(1, k, mat).wait_recv()
            ag(3, k, mat).start()

    def ag_core(k):
        for mat in mats:
            ag(2, k, mat).wait_recv()
            ag(4, k, mat).start()

    def ag_core_last(k):
        for mat in mats:
            ag(3, k, mat).wait_recv()
            ag(5, k, mat).start()

    def ag_ready(k):
        for mat in mats:
            ag(4, k, mat).wait_recv()
            ag(5, k, mat).wait_recv()

    for group in range(2):
        for k in range(1, planes):
            small_gather(0, k, group).start()
    for mat in mats:
        ag(1, 0, mat).start()
    ag_planes()

    grad_vecs[...] = jnp.zeros_like(grad_vecs)
    grad_tin[...] = jnp.zeros_like(grad_tin)
    grad_tout[...] = jnp.zeros_like(grad_tout)

    def channel_top(r, carry):
        tops = []
        for h in range(2):
            b = 2 * r + h
            load_top(b).wait()
            tops.append(padded(total[b] * mask[b].astype(WIDE), lot))
        top[r] = jnp.concatenate(tops, axis=0).astype(LOW)
        grad_vecs[2:3, :] += jnp.sum(top[r].astype(WIDE), axis=0, keepdims=True)
        return carry

    def first_norm(b, carry):
        load(b).wait()
        mid[b] = normalize(grad_zed[b])[0]
        return carry

    lax.fori_loop(0, blocks, channel_top, 0)
    for group in range(2):
        for k in range(1, planes):
            small_gather(0, k, group).wait_recv()
        for k in range(1, 4):
            small_gather(1, k, group).start()
    for mat in mats:
        ag(2, 0, mat).start()
    lax.fori_loop(0, count, first_norm, 0)
    for k in range(1, 4):
        small_gather(1, k, 0).wait_recv()
    small_gather(2, 0, 0).start()
    ag_planes_pass()
    ag_direct(plane_at(0))

    tin[...] = jnp.zeros_like(tin)
    tout[...] = jnp.zeros_like(tout)

    def unpack(d, group):
        far, k = place_of(d)
        message = small_all[group, far, k].astype(WIDE)
        if group == 0:
            lines[d * lines_in : d * lines_in + first_lines, :] = message[0:first_lines, :]
            shifted = jnp.concatenate([message[0:24, 64:128], message[0:24, 0:64]], axis=1)
            lines[d * lines_in + first_lines : (d + 1) * lines_in, :] = shifted[0 : lines_in - first_lines, :]
            vecs[:, d * own_vec : (d + 1) * own_vec] = message[24:32, 64 : 64 + own_vec]
            c_in[d] = message[31:32, 0:shard]
        else:
            tout[d * lines_out : (d + 1) * lines_out, 0:128] = message[0:lines_out, :]
            tout[d * lines_out : (d + 1) * lines_out, 128:patches] = message[16 : 16 + lines_out, 0 : patches - 128]

    def unpack_half(own, group):
        for parity in range(2):

            @pl.when((core == parity) == own)
            def _():
                for d in range(parity, devices, 2):
                    unpack(d, group)

    unpack_half(True, 0)
    for k in range(1, 4):
        small_gather(1, k, 1).wait_recv()
    small_gather(2, 0, 1).start()
    unpack_half(True, 1)
    for group in range(2):
        small_gather(2, 0, group).wait_recv()
        unpack_half(False, group)
    for turn in range(turns):
        tin[0:patches, turn * unit : (turn + 1) * unit] = lines[pl.ds(turn, patches, stride=turns), :][:, 0:unit]
    for rest, into, at in ((c_one, tin, patches), (c_two, tout, hidden_tok)):
        rest = rest[...].reshape(1, rest.shape[0])
        for i in range(3):
            term = rest.astype(LOW).astype(WIDE)
            into[at + i : at + i + 1, 0 : rest.shape[1]] = term
            rest = rest - term
    tin_t[...] = tin[...].T.astype(LOW)
    tout_t[...] = tout[...].T.astype(LOW)
    ones = jnp.ones((3, width), WIDE)

    gain_one, shift_one = vecs[0:1, :], vecs[1:2, :]
    gain_two, shift_two, c_four = vecs[2:3, :], vecs[3:4, :], vecs[4:5, :]
    for k in range(planes):
        for place in range(PLANE):
            near = plane_of(k) * PLANE + (
                (row + (place // 2) % 2) % 2 * 4 + (col + place % 2) % 2 * 2 + (core + place // 4) % 2
            )
            c_in_rel[k, :, place * shard : (place + 1) * shard] = c_in[near]

    def token_forward(b, carry):
        fed = mid[b] * gain_one + shift_one
        mixed[b] = padded(jnp.concatenate([fed, ones], axis=0), pad).astype(LOW)
        value, slope = gelu_parts(dot(tin_t[...], mixed[b], NN))
        act_t[b] = padded(jnp.concatenate([value, ones], axis=0), act_t.shape[1]).astype(LOW)
        slope_t[b] = slope.astype(LOW)
        mid[b] = grad_zed[b] + dot(tout_t[...], act_t[b], NN)[0:patches]
        return carry

    def channel_inputs(r, carry):
        parts = []
        for h in range(2):
            normed, _ = normalize(mid[2 * r + h])
            total[2 * r + h] = mid[2 * r + h] + c_four
            grad_zed[2 * r + h] = jnp.zeros((patches, width), WIDE)
            parts.append(padded(normed * gain_two + shift_two, lot))
        zed[r] = jnp.concatenate(parts, axis=0).astype(LOW)
        return carry

    lax.fori_loop(0, count // 2, token_forward, 0)
    ag_forward(plane_at(0))
    if planes > 1:
        ag_forward(0)
    lax.fori_loop(count // 2, count - 1, token_forward, 0)
    ag_planes_last()
    ag_core(plane_at(0))
    lax.fori_loop(count - 1, count, token_forward, 0)
    if planes > 2:
        ag_direct(plane_at(1))
    lax.fori_loop(0, blocks, channel_inputs, 0)
    ag_core_last(plane_at(0))

    def rs_two(i, mat):
        rs(0, i, mat).wait_recv()
        own_sum[mat] += recv_one[i % 2, mat].astype(WIDE)
        first, second = (1, 3) if mat == 0 else (2, 3)

        @pl.when(i > 0)
        def _():
            rs(1, i - 1, mat).wait_send()

        send_two[mat, 0:shard] = own_sum[mat, first * shard : (first + 1) * shard].astype(LOW)
        send_two[mat, shard : 2 * shard] = own_sum[mat, second * shard : (second + 1) * shard].astype(LOW)
        rs(1, i, mat).start()

    def rs_three(i):
        for mat in mats:
            rs(1, i, mat).wait_recv()
            other = 2 if mat == 0 else 1

            @pl.when(i > 0)
            def _():
                rs(2, i - 1, mat).wait_send()

            keep_sum[mat] = own_sum[mat, 0:shard] + recv_two[i % 2, mat, 0:shard].astype(WIDE)
            send_three[mat] = (
                own_sum[mat, other * shard : (other + 1) * shard]
                + recv_two[i % 2, mat, shard : 2 * shard].astype(WIDE)
            ).astype(LOW)
            rs(2, i, mat).start()

    def rs_four(i):
        for mat in mats:
            rs(2, i, mat).wait_recv()

            @pl.when(i > 1)
            def _():
                rs(3, i - 2, mat).wait_send()

            send_four[i % 2, mat] = (keep_sum[mat] + recv_three[i % 2, mat].astype(WIDE)).astype(LOW)
            rs(3, i, mat).start()

    def rs_last():
        last = planes - 1
        for mat in mats:
            result = grad_in if mat == 0 else grad_out
            rs(2, last, mat).wait_recv()
            summed = keep_sum[mat] + recv_three[last % 2, mat].astype(WIDE)
            for i in range(last):
                rs(3, i, mat).wait_recv()
                summed = summed + recv_four[i, mat].astype(WIDE)
            result[...] = summed

    tile = chunk // 3

    def channel_chunk(i, carry):
        k = plane_at(i)
        ag_ready(k)

        def rows(r, inner):
            for s in range(3):
                part = slice(s * tile, (s + 1) * tile)
                pre = dot(zed[r], weights[0, k, part], NT) + c_in_rel[k, :, part]
                value, slope = gelu_parts(pre)
                act[pl.ds(r * pair, pair), part] = value.astype(LOW)
                back = (dot(top[r], weights[1, k, part], NT) * slope).astype(LOW)
                grad_pre[pl.ds(r * pair, pair), part] = back
            up = dot(act[pl.ds(r * pair, pair), :], weights[1, k], NN)
            down = dot(grad_pre[pl.ds(r * pair, pair), :], weights[0, k], NN)
            for h in range(2):
                total[2 * r + h] += up[h * lot : h * lot + patches]
                grad_zed[2 * r + h] += down[h * lot : h * lot + patches]

            @pl.when((r == 0) & (i == 0) & (planes > 2))
            def _():
                ag_forward(2)

            @pl.when((r == 0) & (i + 3 < planes))
            def _():
                ag_direct(i + 3)

            @pl.when((r == 1) & (i + 2 < planes))
            def _():
                ag_core(i + 2)

            @pl.when((r == 1) & (i == 0))
            def _():
                ag_core(0)
                ag_core_last(0)

            @pl.when((r == 1) & (i > 1))
            def _():
                rs_four(i - 2)

            return inner

        lax.fori_loop(0, blocks, rows, 0)

        @pl.when(i + 2 < planes)
        def _():
            ag_core_last(i + 2)


        back_sum = jnp.sum(grad_pre[...].astype(WIDE), axis=0, keepdims=True)
        for place in range(PLANE):
            near = plane_of(k) * PLANE + (
                (row + (place // 2) % 2) % 2 * 4 + (col + place % 2) % 2 * 2 + (core + place // 4) % 2
            )
            grad_c_in[near] = back_sum[:, place * shard : (place + 1) * shard]

        flat_top = top[...].reshape(blocks * pair, width)
        flat_zed = zed[...].reshape(blocks * pair, width)
        @pl.when(i > 0)
        def _():
            for mat in mats:
                rs(0, i - 1, mat).wait_send()

        send_one[1] = dot(act[:, half:chunk], flat_top, TN).astype(LOW)
        send_one[0] = dot(grad_pre[:, half:chunk], flat_zed, TN).astype(LOW)
        for mat in mats:
            rs(0, i, mat).start()

        @pl.when(i > 0)
        def _():
            rs_three(i - 1)

        @pl.when(i + 3 < planes)
        def _():
            ag_forward(i + 3)

        own_sum[1] = dot(act[:, 0:half], flat_top, TN)
        own_sum[0] = dot(grad_pre[:, 0:half], flat_zed, TN)
        for mat in mats:
            rs_two(i, mat)
        return carry

    for b in range(2):
        reload(b).start()
    lax.fori_loop(0, planes, channel_chunk, 0)

    tin_low = tin[...].astype(LOW)
    tout_low = tout[0:hidden_tok, :].astype(LOW)

    def token_backward(b, carry):
        keep = mask[b].astype(WIDE)
        normed, scale = normalize(mid[b])
        down = grad_zed[b]
        grad_vecs[0:1, :] += jnp.sum(down * normed, axis=0, keepdims=True)
        grad_vecs[1:2, :] += jnp.sum(down, axis=0, keepdims=True)
        reload(b).wait()
        grad_mid = cot[b % 2] * keep + norm_back(down, normed, scale, gain_two)

        @pl.when(b + 2 < count)
        def _():
            reload(b + 2).start()

        back = padded(grad_mid, pad).astype(LOW)
        grad_tout[...] += dot(act_t[b], back, NT)
        grad_zed[b] = grad_mid
        slope_t[b] = (dot(tout_low, back, NN) * slope_t[b].astype(WIDE)).astype(LOW)
        grad_tin[:, 0:hidden_tok] += dot(mixed[b], slope_t[b], NT)

        reload_image(b).start()

        @pl.when((b == 0) & (planes > 1))
        def _():
            rs_four(planes - 2)

        return carry

    def image_norm(b, carry):
        reload_image(b).wait()
        normed, scale = normalize(mid[b])
        mid[b] = normed
        scales[b] = scale
        grad_mixed = dot(tin_low, slope_t[b], NN)[0:patches]
        weights[b // planes, b % planes, 0:pad] = padded(grad_mixed, pad).astype(LOW)
        late[0, 0:1, :] += jnp.sum(grad_mixed * normed, axis=0, keepdims=True)
        late[0, 1:2, :] += jnp.sum(grad_mixed, axis=0, keepdims=True)

        @pl.when(b == 1)
        def _():
            small_second()

        return carry

    def image_backward(b, carry):
        total[b] *= mask[b].astype(WIDE)
        grad_zed[b] += norm_back(weights[b // planes, b % planes, 0:pad][0:patches].astype(WIDE), mid[b], scales[b], gain_one)
        return carry

    late[0] = jnp.zeros_like(late[0])
    lax.fori_loop(0, count, token_backward, 0)

    biases[0] = jnp.zeros_like(biases[0])
    for i in range(hidden_tok // 128):
        biases[0, i : i + 1, :] = grad_tin[patches : patches + 1, i * 128 : (i + 1) * 128]
    biases[0, 3:4, :] = grad_tout[hidden_tok : hidden_tok + 1, 0:128]
    biases[0, 4:5, 0 : patches - 128] = grad_tout[hidden_tok : hidden_tok + 1, 128:patches]
    bias_reduce(0, 0).start()
    for turn in range(turns):
        lines[pl.ds(turn, patches, stride=turns), :] = grad_tin[0:patches, turn * unit : turn * unit + 128]
    for d in range(devices):
        far, k = place_of(d)
        first, second = small_sum.at[0, far, k], small_sum.at[1, far, k]
        low = lines[d * lines_in : d * lines_in + first_lines, :]
        high = lines[d * lines_in + first_lines : (d + 1) * lines_in, :]
        first[0:first_lines, 0:64] = low[:, 0:64]
        first[0 : lines_in - first_lines, 64:128] = high[:, 0:64]
        first[24:27, 64 : 64 + own_vec] = grad_vecs[0:3, d * own_vec : (d + 1) * own_vec]
        first[31:32, 0:shard] = grad_c_in[d]
        second[0:lines_out, :] = grad_tout[d * lines_out : (d + 1) * lines_out, 0:128]
        second[16 : 16 + lines_out, 0 : patches - 128] = grad_tout[d * lines_out : (d + 1) * lines_out, 128:patches]
    for group in range(2):
        for k in range(1, planes):
            small_gather(0, k, group).wait_send()
        for far in range(1, 4):
            small_gather(1, far, group).wait_send()
        small_gather(2, 0, group).wait_send()
        for far in range(4, PLANE):
            small_all[group, far] = small_sum[group, far].astype(LOW)
    small_reduce(0, 0).start()

    def small_second():
        bias_reduce(0, 0).wait_recv()
        biases[1] = biases[0] + biases_in[0, 0]
        small_reduce(0, 0).wait_recv()
        for far in range(4):
            for group in range(2):
                small_sum[group, far] += small_core[group, far].astype(WIDE)
        for far in range(1, 4):
            for group in range(2):
                small_all[group, far] = small_sum[group, far].astype(LOW)
            small_reduce(1, far).start()
            bias_reduce(1, far).start()

    def small_third():
        for far in range(1, 4):
            small_reduce(1, far).wait_recv()
            bias_reduce(1, far).wait_recv()
            for group in range(2):
                small_sum[group, 0] += small_plane[group, far].astype(WIDE)
        biases[2] = (biases[1] + biases_in[1, 1]) + (biases_in[1, 2] + biases_in[1, 3])
        for k in range(1, planes):
            for group in range(2):
                small_all[group, 0, k] = small_sum[group, 0, k].astype(LOW)
            small_reduce(2, k).start()
            bias_reduce(2, k).start()

    for mat in mats:
        for k in range(planes):
            for stage in range(1, 6):
                ag(stage, k, mat).wait_send()
        ag(0, 1, mat).wait_send()
        if row_of_four:

            @pl.when(inner)
            def _():
                ag(0, 3, mat).wait_send()
                for which in range(3):
                    ag_pass(which, mat).wait_send()

    lax.fori_loop(0, count, image_norm, 0)
    late_reduce(0, 0).start()
    lax.fori_loop(0, 1, image_backward, 0)
    late_reduce(0, 0).wait_recv()
    late[1] = late[0] + late_in[0, 0]
    for far in range(1, 4):
        late_reduce(1, far).start()
    rs_three(planes - 1)
    small_third()
    lax.fori_loop(1, count // 2, image_backward, 0)
    late_sum = late[1]
    for far in range(1, 4):
        late_reduce(1, far).wait_recv()
        late_sum = late_sum + late_in[1, far]
    late[2] = late_sum
    for k in range(1, planes):
        late_reduce(2, k).start()
    lax.fori_loop(count // 2, count, image_backward, 0)
    rs_last()
    summed = [small_sum[group, 0, 0] for group in range(2)]
    tree = [biases[2]]
    for k in range(1, planes):
        small_reduce(2, k).wait_recv()
        bias_reduce(2, k).wait_recv()
        summed = [summed[group] + small_z[k, group].astype(WIDE) for group in range(2)]
        tree.append(biases_in[2, k])
    for group in range(2):
        small_out[32 * group : 32 * (group + 1)] = summed[group]
    for k in range(1, planes):
        late_reduce(2, k).wait_recv()
        late_sum = late_sum + late_in[2, k]
    late_sum = pltpu.roll(padded(late_sum, 8), width - own_vec * me, 1)
    small_out[27:29, 64 : 64 + own_vec] = late_sum[0:2, 0:own_vec]
    while len(tree) > 1:
        tree = [tree[i] + tree[i + 1] for i in range(0, len(tree), 2)]
    biases_out[...] = tree[0]

    for mat in mats:
        for stage in range(3):
            rs(stage, planes - 1, mat).wait_send()
        for i in range(max(0, planes - 3), planes - 1):
            rs(3, i, mat).wait_send()
    late_reduce(0, 0).wait_send()
    for far in range(1, 4):
        late_reduce(1, far).wait_send()
    for k in range(1, planes):
        late_reduce(2, k).wait_send()
    small_reduce(0, 0).wait_send()
    bias_reduce(0, 0).wait_send()
    for far in range(1, 4):
        small_reduce(1, far).wait_send()
        bias_reduce(1, far).wait_send()
    for k in range(1, planes):
        small_reduce(2, k).wait_send()
        bias_reduce(2, k).wait_send()


def finish_kernel(
    block_in,
    image_in,
    w_in,
    w_out,
    small,
    biases,
    block_out,
    image_out,
    w_in_out,
    w_out_out,
    tin,
    tout,
    gain_one,
    shift_one,
    gain_two,
    shift_two,
    c_four,
    c_in,
    c_one,
    c_two,
    sem,
):
    copies = [
        pltpu.make_async_copy(block_in, block_out, sem.at[0]),
        pltpu.make_async_copy(image_in, image_out, sem.at[1]),
        pltpu.make_async_copy(w_in, w_in_out, sem.at[2]),
        pltpu.make_async_copy(w_out, w_out_out, sem.at[3]),
    ]
    for copy in copies:
        copy.start()
    hidden_tok, patches = c_one.shape[0], c_two.shape[0]
    unit = math.gcd(tin.shape[0], hidden_tok)
    lines_in = tin.shape[0] // unit
    first_lines = (lines_in + 1) // 2
    for i in range(lines_in):
        at, lane = (i, 0) if i < first_lines else (i - first_lines, 64)
        tin[i * unit : (i + 1) * unit] = small[at : at + 1, lane : lane + unit].reshape(unit)
    for i in range(tout.shape[0] // patches):
        tout[i * patches : i * patches + 128] = small[32 + i : 33 + i, :].reshape(128)
        tout[i * patches + 128 : (i + 1) * patches] = small[48 + i : 49 + i, 0 : patches - 128].reshape(
            patches - 128
        )
    for i, piece in enumerate((gain_two, shift_two, c_four, gain_one, shift_one)):
        own_vec = piece.shape[0]
        piece[...] = small[24 + i : 25 + i, 64 : 64 + own_vec].reshape(own_vec)
    shard = c_in.shape[0]
    c_in[...] = small[31:32, 0:shard].reshape(shard)
    for i in range(hidden_tok // 128):
        c_one[i * 128 : (i + 1) * 128] = biases[i : i + 1, :].reshape(128)
    c_two[0:128] = biases[3:4, :].reshape(128)
    c_two[128:patches] = biases[4:5, 0 : patches - 128].reshape(patches - 128)
    for copy in copies:
        copy.wait()


def fast_shards(
    images,
    mask,
    cotangent,
    w_token_in,
    w_token_out,
    bias_token_in,
    bias_token_out,
    gain_one,
    shift_one,
    gain_two,
    shift_two,
    w_expand,
    bias_expand,
    w_reduce,
    bias_reduce,
):
    devices = lax.axis_size("dp")
    planes = devices // PLANE
    count, patches, width = images.shape
    hidden_tok = bias_token_in.shape[0]
    shard = w_expand.shape[0]
    pad = -(-patches // 16) * 16
    lot = -(-patches // 8) * 8
    pair = 2 * lot
    blocks = count // 2
    chunk = 8 * shard
    half = 4 * shard

    unit = math.gcd(w_token_in.shape[0], hidden_tok)
    lines_in = w_token_in.shape[0] // unit
    hidden_pad = hidden_tok + 16

    vmem = pl.BlockSpec(memory_space=pltpu.VMEM)
    hbm = pl.BlockSpec(memory_space=pl.ANY)
    shape = jax.ShapeDtypeStruct
    outs = pl.pallas_call(
        block_kernel,
        out_shape=(
            pltpu.VMEM(images.shape, WIDE),
            pltpu.VMEM(images.shape, WIDE),
            pltpu.VMEM(w_expand.shape, WIDE),
            pltpu.VMEM(w_reduce.shape, WIDE),
            pltpu.VMEM((64, 128), WIDE),
            pltpu.VMEM((8, 128), WIDE),
        ),
        in_specs=[pl.BlockSpec(memory_space=pltpu.SMEM), hbm, hbm] + [vmem] * 12,
        out_specs=[vmem] * 6,
        scratch_shapes=[
            pltpu.VMEM((2,) + images.shape[1:], WIDE),
            pltpu.VMEM((count, pad, width), LOW),
            pltpu.VMEM((count, hidden_pad, width), LOW),
            pltpu.VMEM((count, hidden_tok, width), LOW),
            pltpu.VMEM(images.shape, WIDE),
            pltpu.VMEM((blocks, pair, width), LOW),
            pltpu.VMEM((blocks, pair, width), LOW),
            pltpu.VMEM((2, planes, chunk, width), LOW),
            pltpu.VMEM((blocks * pair, chunk), LOW),
            pltpu.VMEM((blocks * pair, chunk), LOW),
            pltpu.VMEM((planes, 1, chunk), WIDE),
            pltpu.VMEM((2, half, width), WIDE),
            pltpu.VMEM((2, shard, width), WIDE),
            pltpu.VMEM((2, half, width), LOW),
            pltpu.VMEM((2, 2, half, width), LOW),
            pltpu.VMEM((2, 2 * shard, width), LOW),
            pltpu.VMEM((2, 2, 2 * shard, width), LOW),
            pltpu.VMEM((2, shard, width), LOW),
            pltpu.VMEM((2, 2, shard, width), LOW),
            pltpu.VMEM((2, 2, shard, width), LOW),
            pltpu.VMEM((planes - 1, 2, shard, width), LOW),
            pltpu.VMEM((pad, hidden_tok), WIDE),
            pltpu.VMEM((hidden_tok, pad), LOW),
            pltpu.VMEM((hidden_pad, pad), WIDE),
            pltpu.VMEM((pad, hidden_pad), LOW),
            pltpu.VMEM((8, width), WIDE),
            pltpu.VMEM((devices, 1, shard), WIDE),
            pltpu.VMEM((devices * lines_in, 128), WIDE),
            pltpu.VMEM((64, 128), WIDE),
            pltpu.VMEM((2, PLANE, planes, 32, 128), LOW),
            pltpu.VMEM((pad, hidden_tok + 128), WIDE),
            pltpu.VMEM((hidden_pad, pad), WIDE),
            pltpu.VMEM((8, width), WIDE),
            pltpu.VMEM((devices, 1, shard), WIDE),
            pltpu.VMEM((2, PLANE, planes, 32, 128), WIDE),
            pltpu.VMEM((2, 4, planes, 32, 128), LOW),
            pltpu.VMEM((2, 4, planes, 32, 128), LOW),
            pltpu.VMEM((planes, 2, 32, 128), LOW),
            pltpu.VMEM((3, 8, 128), WIDE),
            pltpu.VMEM((3, max(4, planes), 8, 128), WIDE),
            pltpu.VMEM((3, 2, width), WIDE),
            pltpu.VMEM((3, max(4, planes), 2, width), WIDE),
            pltpu.VMEM((count, patches, 1), WIDE),
            pltpu.SemaphoreType.DMA((4, count)),
            pltpu.SemaphoreType.DMA((7, planes, 2)),
            pltpu.SemaphoreType.DMA((7, planes, 2)),
            pltpu.SemaphoreType.DMA((4, planes, 2)),
            pltpu.SemaphoreType.DMA((4, planes, 2)),
        ]
        + [pltpu.SemaphoreType.DMA((3, max(4, planes), 2))] * 2
        + [pltpu.SemaphoreType.DMA((3, max(4, planes)))] * 6,
        compiler_params=pltpu.CompilerParams(
            collective_id=0, has_side_effects=True, vmem_limit_bytes=55 * 2**20
        ),
    )(
        mask,
        images,
        cotangent,
        w_expand,
        w_reduce,
        w_token_in,
        w_token_out,
        gain_one,
        shift_one,
        gain_two,
        shift_two,
        bias_reduce,
        bias_expand,
        bias_token_in,
        bias_token_out,
    )
    flat = pl.pallas_call(
        finish_kernel,
        out_shape=(
            shape(images.shape, WIDE),
            shape(images.shape, WIDE),
            shape(w_expand.shape, WIDE),
            shape(w_reduce.shape, WIDE),
            shape(w_token_in.shape, WIDE),
            shape(w_token_out.shape, WIDE),
            *[shape(gain_one.shape, WIDE)] * 5,
            shape(bias_expand.shape, WIDE),
            shape(bias_token_in.shape, WIDE),
            shape(bias_token_out.shape, WIDE),
        ),
        in_specs=[vmem] * 6,
        out_specs=[hbm] * 4 + [vmem] * 10,
        scratch_shapes=[pltpu.SemaphoreType.DMA((4,))],
        compiler_params=pltpu.CompilerParams(vmem_limit_bytes=16 * 2**20),
    )(*outs)
    block_output, image_grad, own_win, own_wout, *rest = flat
    g_tin, g_tout, g_one, b_one, g_two, b_two, c_four, c_in, c_one, c_two = rest
    return (
        block_output,
        image_grad,
        g_tin,
        g_tout,
        c_one,
        c_two,
        g_one,
        b_one,
        g_two,
        b_two,
        own_win,
        c_in,
        own_wout,
        c_four,
    )


def fits(devices, images, w_token_in, w_token_out, bias_token_in, gain_one, w_expand):
    planes = devices // PLANE
    patches = images.shape[1]
    hidden_tok = bias_token_in.shape[0]
    shard = w_expand.shape[0]
    unit = math.gcd(w_token_in.shape[0], hidden_tok)
    return (
        devices % PLANE == 0
        and planes in (2, 4)
        and images.shape[0] % 2 == 0
        and images.shape[0] <= 2 * planes
        and shard % 16 == 0
        and shard <= 128
        and (4 * shard) % 128 == 0
        and 128 < patches <= 205
        and unit <= 64
        and w_token_in.shape[0] // unit <= 49
        and w_token_out.shape[0] % patches == 0
        and w_token_out.shape[0] // patches <= 16
        and gain_one.shape[0] <= 64
        and hidden_tok == 384
    )


def choose(
    images,
    mask,
    cotangent,
    w_token_in,
    w_token_out,
    bias_token_in,
    bias_token_out,
    gain_one,
    shift_one,
    gain_two,
    shift_two,
    w_expand,
    bias_expand,
    w_reduce,
    bias_reduce,
):
    args = (
        images,
        mask,
        cotangent,
        w_token_in,
        w_token_out,
        bias_token_in,
        bias_token_out,
        gain_one,
        shift_one,
        gain_two,
        shift_two,
        w_expand,
        bias_expand,
        w_reduce,
        bias_reduce,
    )
    if fits(lax.axis_size("dp"), images, w_token_in, w_token_out, bias_token_in, gain_one, w_expand):
        return fast_shards(*args)
    return shards(*args)


def shards(
    images,
    mask,
    cotangent,
    w_token_in,
    w_token_out,
    bias_token_in,
    bias_token_out,
    gain_one,
    shift_one,
    gain_two,
    shift_two,
    w_expand,
    bias_expand,
    w_reduce,
    bias_reduce,
):
    low_type = jnp.bfloat16
    wide = jnp.float32
    count, patches, width = images.shape
    hidden_tok = bias_token_in.shape[0]
    rows = count * patches
    keep = mask.astype(wide)[:, None, None]
    small_local = (
        w_token_in.astype(low_type),
        w_token_out.astype(low_type),
        gain_one.astype(low_type),
        shift_one.astype(low_type),
        gain_two.astype(low_type),
        shift_two.astype(low_type),
        bias_reduce.astype(low_type),
    )
    channel_local = (
        w_expand.astype(low_type),
        w_reduce.astype(low_type),
        bias_expand.astype(low_type),
    )
    small_all = (
        lax.all_gather(small_local[0], "dp", axis=0, tiled=True),
        lax.all_gather(small_local[1], "dp", axis=0, tiled=True),
        lax.all_gather(small_local[2], "dp", axis=0, tiled=True),
        lax.all_gather(small_local[3], "dp", axis=0, tiled=True),
        lax.all_gather(small_local[4], "dp", axis=0, tiled=True),
        lax.all_gather(small_local[5], "dp", axis=0, tiled=True),
        lax.all_gather(small_local[6], "dp", axis=0, tiled=True),
    )
    tin = small_all[0].reshape(patches, hidden_tok)
    tout = small_all[1].reshape(hidden_tok, patches)
    g_one, b_one, g_two, b_two, c_four = [piece.astype(wide) for piece in small_all[2:]]
    normed_one, scale_one = normalize(images)
    mixed_in = (normed_one * g_one + b_one).astype(low_type)
    pre_t = (
        jnp.einsum("ps,bpd->bsd", tin, mixed_in, preferred_element_type=wide)
        + bias_token_in[None, :, None]
    )
    act_t = gelu_exact(pre_t).astype(low_type)
    middle = (
        images
        + jnp.einsum("sp,bsd->bpd", tout, act_t, preferred_element_type=wide)
        + bias_token_out[None, :, None]
    )
    normed_two, scale_two = normalize(middle.reshape(rows, width))
    zed = (normed_two * g_two + b_two).astype(low_type)
    whole_channel = (
        lax.all_gather(channel_local[0], "dp", axis=0, tiled=True),
        lax.all_gather(channel_local[1], "dp", axis=0, tiled=True),
        lax.all_gather(channel_local[2], "dp", axis=0, tiled=True),
    )
    w_in, w_out, c_in = whole_channel
    pre = (
        jnp.einsum("td,fd->tf", zed, w_in, preferred_element_type=wide) + c_in.astype(wide)[None, :]
    )
    act = gelu_exact(pre).astype(low_type)
    reduced = jnp.dot(act, w_out, preferred_element_type=wide)
    block_output = (middle + (reduced + c_four).reshape(count, patches, width)) * keep
    grad_top = cotangent * keep
    grad_branch = grad_top.reshape(rows, width).astype(low_type)
    grad_c_four = jnp.sum(grad_branch.astype(wide), axis=0)
    small_all = (
        lax.all_gather(small_local[0], "dp", axis=0, tiled=True),
        lax.all_gather(small_local[1], "dp", axis=0, tiled=True),
        lax.all_gather(small_local[2], "dp", axis=0, tiled=True),
        lax.all_gather(small_local[3], "dp", axis=0, tiled=True),
        lax.all_gather(small_local[4], "dp", axis=0, tiled=True),
        lax.all_gather(small_local[5], "dp", axis=0, tiled=True),
        lax.all_gather(small_local[6], "dp", axis=0, tiled=True),
    )
    tin = small_all[0].reshape(patches, hidden_tok)
    tout = small_all[1].reshape(hidden_tok, patches)
    g_one, b_one, g_two, b_two, c_four = [piece.astype(wide) for piece in small_all[2:]]
    whole_channel = (
        lax.all_gather(channel_local[0], "dp", axis=0, tiled=True),
        lax.all_gather(channel_local[1], "dp", axis=0, tiled=True),
        lax.all_gather(channel_local[2], "dp", axis=0, tiled=True),
    )
    w_in, w_out, c_in = whole_channel
    pre = (
        jnp.einsum("td,fd->tf", zed, w_in, preferred_element_type=wide) + c_in.astype(wide)[None, :]
    )
    act = gelu_exact(pre).astype(low_type)
    grad_act = jnp.einsum("td,fd->tf", grad_branch, w_out, preferred_element_type=wide)
    grad_pre = (grad_act * gelu_slope(pre)).astype(low_type)
    grad_zed = jnp.dot(grad_pre, w_in, preferred_element_type=wide)
    grad_in = jnp.einsum("tf,td->fd", grad_pre, zed, preferred_element_type=wide)
    grad_out = jnp.einsum("tf,td->fd", act, grad_branch, preferred_element_type=wide)
    grad_cin = jnp.sum(grad_pre.astype(wide), axis=0)
    grad_zed, grad_win, grad_wout, grad_cin = (grad_zed, grad_in, grad_out, grad_cin)
    grad_g_two = jnp.sum(grad_zed * normed_two, axis=0)
    grad_b_two = jnp.sum(grad_zed, axis=0)
    grad_mid = grad_top + norm_back(grad_zed, normed_two, scale_two, g_two).reshape(
        count, patches, width
    )
    grad_back = grad_mid.astype(low_type)
    grad_c_two = jnp.sum(grad_back.astype(wide), axis=(0, 2))
    grad_tout = jnp.einsum("bsd,bpd->sp", act_t, grad_back, preferred_element_type=wide)
    grad_act_t = jnp.einsum("sp,bpd->bsd", tout, grad_back, preferred_element_type=wide)
    grad_pre_t = (grad_act_t * gelu_slope(pre_t)).astype(low_type)
    grad_c_one = jnp.sum(grad_pre_t.astype(wide), axis=(0, 2))
    grad_tin = jnp.einsum("bpd,bsd->ps", mixed_in, grad_pre_t, preferred_element_type=wide)
    grad_mixed = jnp.einsum("ps,bsd->bpd", tin, grad_pre_t, preferred_element_type=wide)
    grad_g_one = jnp.sum(grad_mixed * normed_one, axis=(0, 1))
    grad_b_one = jnp.sum(grad_mixed, axis=(0, 1))
    image_grad = grad_mid + norm_back(grad_mixed, normed_one, scale_one, g_one)
    bias_sums = lax.psum((grad_c_one, grad_c_two), "dp")
    flat_tin = grad_tin.reshape(patches * hidden_tok)
    flat_tout = grad_tout.reshape(hidden_tok * patches)
    owned = (
        lax.psum_scatter(flat_tin, "dp", scatter_dimension=0, tiled=True),
        lax.psum_scatter(flat_tout, "dp", scatter_dimension=0, tiled=True),
        lax.psum_scatter(grad_g_one, "dp", scatter_dimension=0, tiled=True),
        lax.psum_scatter(grad_b_one, "dp", scatter_dimension=0, tiled=True),
        lax.psum_scatter(grad_g_two, "dp", scatter_dimension=0, tiled=True),
        lax.psum_scatter(grad_b_two, "dp", scatter_dimension=0, tiled=True),
        lax.psum_scatter(grad_win, "dp", scatter_dimension=0, tiled=True),
        lax.psum_scatter(grad_cin, "dp", scatter_dimension=0, tiled=True),
        lax.psum_scatter(grad_wout, "dp", scatter_dimension=0, tiled=True),
        lax.psum_scatter(grad_c_four, "dp", scatter_dimension=0, tiled=True),
    )
    (
        own_tin,
        own_tout,
        own_g_one,
        own_b_one,
        own_g_two,
        own_b_two,
        own_win,
        own_cin,
        own_wout,
        own_c_four,
    ) = owned
    return (
        block_output,
        image_grad,
        own_tin,
        own_tout,
        bias_sums[0],
        bias_sums[1],
        own_g_one,
        own_b_one,
        own_g_two,
        own_b_two,
        own_win,
        own_cin,
        own_wout,
        own_c_four,
    )


def solution(mesh):
    placed = (
        P("dp", None, None),
        P("dp"),
        P("dp", None, None),
        P("dp"),
        P("dp"),
        P(),
        P(),
        P("dp"),
        P("dp"),
        P("dp"),
        P("dp"),
        P("dp", None),
        P("dp"),
        P("dp", None),
        P("dp"),
    )
    return jax.shard_map(
        choose,
        mesh=mesh,
        in_specs=placed,
        out_specs=(
            P("dp", None, None),
            P("dp", None, None),
            P("dp"),
            P("dp"),
            P(),
            P(),
            P("dp"),
            P("dp"),
            P("dp"),
            P("dp"),
            P("dp", None),
            P("dp"),
            P("dp", None),
            P("dp"),
        ),
        check_vma=False,
    )
```

```python
import math

import jax
import jax.numpy as jnp
from jax import lax
from jax.experimental import pallas as pl
from jax.experimental.pallas import tpu as pltpu
from jax.sharding import PartitionSpec as P

EPS = 1e-06


def gelu_exact(v):
    return 0.5 * v * (1.0 + lax.erf(v * 0.7071067811865476))


def gelu_slope(v):
    return 0.5 * (1.0 + lax.erf(v * 0.7071067811865476)) + v * 0.3989422804014327 * jnp.exp(
        -0.5 * v * v
    )


def normalize(v):
    centered = v - jnp.mean(v, axis=-1, keepdims=True)
    scale = lax.rsqrt(jnp.mean(centered * centered, axis=-1, keepdims=True) + EPS)
    return (centered * scale, scale)


def norm_back(grad_in, normed, scale, gain):
    scaled = grad_in * gain
    return scale * (
        scaled
        - jnp.mean(scaled, axis=-1, keepdims=True)
        - normed * jnp.mean(scaled * normed, axis=-1, keepdims=True)
    )


WIDE = jnp.float32
LOW = jnp.bfloat16
MESH = pl.DeviceIdType.MESH
NT = (((1,), (1,)), ((), ()))
TN = (((0,), (0,)), ((), ()))
NN = (((1,), (0,)), ((), ()))
PLANE = 8


def dot(a, b, dims):
    return lax.dot_general(a, b, dims, preferred_element_type=WIDE)


def gelu_parts(v):
    cdf = 0.5 * (1.0 + lax.erf(v * 0.7071067811865476))
    return v * cdf, cdf + v * 0.3989422804014327 * jnp.exp(-0.5 * v * v)


def padded(v, rows):
    return jnp.concatenate([v, jnp.zeros((rows - v.shape[0], v.shape[1]), v.dtype)], axis=0)


def block_kernel(
    mask,
    images,
    cotangent,
    w_in,
    w_out,
    tin_own,
    tout_own,
    gain_one_own,
    shift_one_own,
    gain_two_own,
    shift_two_own,
    c_four_own,
    c_in_own,
    c_one,
    c_two,
    total,
    grad_zed,
    grad_in,
    grad_out,
    small_out,
    biases_out,
    cot,
    mixed,
    act_t,
    slope_t,
    mid,
    zed,
    top,
    weights,
    act,
    grad_pre,
    c_in_rel,
    own_sum,
    keep_sum,
    send_one,
    recv_one,
    send_two,
    recv_two,
    send_three,
    recv_three,
    send_four,
    recv_four,
    send_far,
    recv_far,
    tin,
    tin_t,
    tout,
    tout_t,
    vecs,
    c_in,
    lines,
    small_own,
    small_all,
    grad_tin,
    grad_tout,
    grad_vecs,
    grad_c_in,
    small_sum,
    small_core,
    small_plane,
    small_z,
    biases,
    biases_in,
    late,
    late_in,
    scales,
    in_sem,
    ag_send,
    ag_recv,
    rs_send,
    rs_recv,
    sg_send,
    sg_recv,
    ss_send,
    ss_recv,
    bs_send,
    bs_recv,
    ls_send,
    ls_recv,
):
    count, patches, width = images.shape
    planes = weights.shape[1]
    shard = w_in.shape[0]
    half = 4 * shard
    chunk = 8 * shard
    pad = mixed.shape[1]
    pair = zed.shape[1]
    lot = pair // 2
    blocks = count // 2
    me = lax.axis_index("dp")
    core = me % 2
    col = (me // 2) % 2
    row = (me // 4) % 2
    z = me // PLANE
    by_core = me + 1 - 2 * core
    by_x = me + 2 - 4 * col
    by_y = me + 4 - 8 * row
    by_both = by_x + by_y - me

    def plane_of(k):
        out, bit = z, 1
        while bit < planes:
            out = out + bit * ((k // bit) % 2) * (1 - 2 * ((z // bit) % 2))
            bit *= 2
        return out

    def by_z(k):
        return me + PLANE * (plane_of(k) - z)

    def ag(stage, k, mat):
        near, far = (by_x, by_y) if mat == 0 else (by_y, by_x)
        step = 1 if mat == 0 else 2
        if stage == 0:
            src, dst, size, to = 0, 0, shard, by_z(k)
            source = weights.at[mat, 0, pl.ds(src, size)]
        else:
            src, dst, size, to = {
                1: (0, step * shard, shard, near),
                2: (0, (3 - step) * shard, shard, far),
                3: (step * shard, 3 * shard, shard, far),
                4: (0, half, 3 * shard, by_core),
                5: (3 * shard, half + 3 * shard, shard, by_core),
            }[stage]
            source = weights.at[mat, k, pl.ds(src, size)]
        return pltpu.make_async_remote_copy(
            src_ref=source,
            dst_ref=weights.at[mat, k, pl.ds(dst, size)],
            send_sem=ag_send.at[stage, k, mat],
            recv_sem=ag_recv.at[stage, k, mat],
            device_id=(to,),
            device_id_type=MESH,
        )

    def plane_at(i):
        return (i + 1) % planes

    def rs(stage, i, mat):
        slot, k = i % 2, plane_at(i)
        near, far = (by_x, by_y) if mat == 0 else (by_y, by_x)
        src, dst, to = [
            lambda: (send_one.at[mat], recv_one.at[slot, mat], by_core),
            lambda: (send_two.at[mat], recv_two.at[slot, mat], near),
            lambda: (send_three.at[mat], recv_three.at[slot, mat], far),
            lambda: (send_four.at[slot, mat], recv_four.at[i - 1, mat], by_z(k)),
            lambda: (send_far.at[mat], recv_far.at[mat], by_z(k)),
        ][stage]()
        return pltpu.make_async_remote_copy(
            src_ref=src,
            dst_ref=dst,
            send_sem=rs_send.at[stage, i, mat],
            recv_sem=rs_recv.at[stage, i, mat],
            device_id=(to,),
            device_id_type=MESH,
        )

    def small_gather(stage, k, group):
        src, dst, to = [
            lambda: (small_all.at[group, 0, 0], small_all.at[group, 0, k], by_z(k)),
            lambda: (small_all.at[group, 0], small_all.at[group, k], (me, by_x, by_y, by_both)[k]),
            lambda: (small_all.at[group, pl.ds(0, 4)], small_all.at[group, pl.ds(4, 4)], by_core),
        ][stage]()
        return pltpu.make_async_remote_copy(
            src_ref=src,
            dst_ref=dst,
            send_sem=sg_send.at[stage, k, group],
            recv_sem=sg_recv.at[stage, k, group],
            device_id=(to,),
            device_id_type=MESH,
        )

    def small_reduce(stage, k):
        src, dst, to = [
            lambda: (small_all.at[:, pl.ds(4, 4)], small_core, by_core),
            lambda: (small_all.at[:, k], small_plane.at[:, k], (me, by_x, by_y, by_both)[k]),
            lambda: (small_all.at[:, 0, k], small_z.at[k], by_z(k)),
        ][stage]()
        return pltpu.make_async_remote_copy(
            src_ref=src,
            dst_ref=dst,
            send_sem=ss_send.at[stage, k],
            recv_sem=ss_recv.at[stage, k],
            device_id=(to,),
            device_id_type=MESH,
        )

    def bias_reduce(stage, k):
        to = [lambda: by_core, lambda: (me, by_x, by_y, by_both)[k], lambda: by_z(k)][stage]()
        return pltpu.make_async_remote_copy(
            src_ref=biases.at[stage],
            dst_ref=biases_in.at[stage, k],
            send_sem=bs_send.at[stage, k],
            recv_sem=bs_recv.at[stage, k],
            device_id=(to,),
            device_id_type=MESH,
        )

    def late_reduce(stage, k):
        to = [lambda: by_core, lambda: (me, by_x, by_y, by_both)[k], lambda: by_z(k)][stage]()
        return pltpu.make_async_remote_copy(
            src_ref=late.at[stage],
            dst_ref=late_in.at[stage, k],
            send_sem=ls_send.at[stage, k],
            recv_sem=ls_recv.at[stage, k],
            device_id=(to,),
            device_id_type=MESH,
        )

    hidden_tok = c_one.shape[0]
    unit = math.gcd(tin_own.shape[0], hidden_tok)
    lines_in = tin_own.shape[0] // unit
    first_lines = (lines_in + 1) // 2
    lines_out = tout_own.shape[0] // patches
    own_vec = gain_one_own.shape[0]
    turns = hidden_tok // unit
    devices = planes * PLANE

    def place_of(d):
        dz, dy, dx, dc = d // PLANE, (d // 4) % 2, (d // 2) % 2, d % 2
        far = (dc + core) % 2 * 4 + (dy + row) % 2 * 2 + (dx + col) % 2
        k, bit = 0, 1
        while bit < planes:
            k = k + bit * ((dz // bit + z // bit) % 2)
            bit *= 2
        return far, k

    def load(b):
        return pltpu.make_async_copy(images.at[b], grad_zed.at[b], in_sem.at[0, b])

    def load_top(b):
        return pltpu.make_async_copy(cotangent.at[b], total.at[b], in_sem.at[1, b])

    def reload_image(b):
        return pltpu.make_async_copy(images.at[b], mid.at[b], in_sem.at[3, b])

    def reload(b):
        return pltpu.make_async_copy(cotangent.at[b], cot.at[b % 2], in_sem.at[2, b])

    for b in range(count):
        load_top(b).start()
    for b in range(count):
        load(b).start()
    small_own[...] = jnp.zeros_like(small_own)
    for i in range(lines_in):
        at, lane = (i, 0) if i < first_lines else (i - first_lines, 64)
        small_own[at : at + 1, lane : lane + unit] = tin_own[i * unit : (i + 1) * unit].reshape(1, unit)
    for i, piece in enumerate((gain_one_own, shift_one_own, gain_two_own, shift_two_own, c_four_own)):
        small_own[24 + i : 25 + i, 64 : 64 + own_vec] = piece[...].reshape(1, own_vec)
    small_own[31:32, 0:shard] = c_in_own[...].reshape(1, shard)
    for i in range(lines_out):
        line = tout_own[i * patches : (i + 1) * patches].reshape(1, patches)
        small_own[32 + i : 33 + i, :] = line[:, 0:128]
        small_own[48 + i : 49 + i, 0 : patches - 128] = line[:, 128:patches]
    for group in range(2):
        small_all[group, 0, 0] = small_own[32 * group : 32 * (group + 1)].astype(LOW)
    weights[0, 0, 0:shard] = w_in[...].astype(LOW)
    weights[1, 0, 0:shard] = w_out[...].astype(LOW)

    barrier = pltpu.get_barrier_semaphore()
    peers = [by_core, by_x, by_y, by_both] + [by_z(k) for k in range(1, planes)]
    for peer in peers:
        pl.semaphore_signal(barrier, inc=1, device_id=(peer,), device_id_type=MESH)
    pl.semaphore_wait(barrier, len(peers))

    mats = (0, 1)
    inner = (z == 1) | (z == 2)

    def ag_pass(which, mat):
        src, dst, to = ((1, 2, by_z(3)), (3, 2, by_z(1)), (2, 3, by_z(1)))[which]
        return pltpu.make_async_remote_copy(
            src_ref=weights.at[mat, src, pl.ds(0, shard)],
            dst_ref=weights.at[mat, dst, pl.ds(0, shard)],
            send_sem=ag_send.at[6, which, mat],
            recv_sem=ag_recv.at[0, dst, mat],
            device_id=(to,),
            device_id_type=MESH,
        )

    def ag_planes():
        for mat in mats:
            ag(0, 1, mat).start()

        @pl.when(inner)
        def _():
            for mat in mats:
                ag(0, 3, mat).start()

    def ag_planes_pass():
        @pl.when(inner)
        def _():
            for which, came in ((0, 1), (1, 3)):
                for mat in mats:
                    ag(0, came, mat).wait_recv()
                    ag_pass(which, mat).start()

    def ag_planes_last():
        @pl.when(inner)
        def _():
            for mat in mats:
                ag(0, 2, mat).wait_recv()
                ag_pass(2, mat).start()

    def ag_direct(k):
        @pl.when(jnp.logical_not(inner))
        def _():
            for mat in mats:
                ag(0, k, mat).wait_recv()

        for stage in (1, 2):
            for mat in mats:
                ag(stage, k, mat).start()

    def ag_forward(k):
        for mat in mats:
            ag(1, k, mat).wait_recv()
            ag(3, k, mat).start()

    def ag_core(k):
        for mat in mats:
            ag(2, k, mat).wait_recv()
            ag(4, k, mat).start()

    def ag_core_last(k):
        for mat in mats:
            ag(3, k, mat).wait_recv()
            ag(5, k, mat).start()

    def ag_ready(k):
        for mat in mats:
            ag(4, k, mat).wait_recv()
            ag(5, k, mat).wait_recv()

    for group in range(2):
        for k in range(1, planes):
            small_gather(0, k, group).start()
    for mat in mats:
        ag(1, 0, mat).start()
    ag_planes()

    grad_vecs[...] = jnp.zeros_like(grad_vecs)
    grad_tin[...] = jnp.zeros_like(grad_tin)
    grad_tout[...] = jnp.zeros_like(grad_tout)

    def channel_top(r, carry):
        tops = []
        for h in range(2):
            b = 2 * r + h
            load_top(b).wait()
            tops.append(padded(total[b] * mask[b].astype(WIDE), lot))
        top[r] = jnp.concatenate(tops, axis=0).astype(LOW)
        grad_vecs[2:3, :] += jnp.sum(top[r].astype(WIDE), axis=0, keepdims=True)
        return carry

    def first_norm(b, carry):
        load(b).wait()
        mid[b] = normalize(grad_zed[b])[0]
        return carry

    lax.fori_loop(0, blocks, channel_top, 0)
    for group in range(2):
        for k in range(1, planes):
            small_gather(0, k, group).wait_recv()
        for k in range(1, 4):
            small_gather(1, k, group).start()
    lax.fori_loop(0, count, first_norm, 0)
    for k in range(1, 4):
        small_gather(1, k, 0).wait_recv()
    small_gather(2, 0, 0).start()

    tin[...] = jnp.zeros_like(tin)
    tout[...] = jnp.zeros_like(tout)

    def unpack(d, group):
        far, k = place_of(d)
        message = small_all[group, far, k].astype(WIDE)
        if group == 0:
            lines[d * lines_in : d * lines_in + first_lines, :] = message[0:first_lines, :]
            shifted = jnp.concatenate([message[0:24, 64:128], message[0:24, 0:64]], axis=1)
            lines[d * lines_in + first_lines : (d + 1) * lines_in, :] = shifted[0 : lines_in - first_lines, :]
            vecs[:, d * own_vec : (d + 1) * own_vec] = message[24:32, 64 : 64 + own_vec]
            c_in[d] = message[31:32, 0:shard]
        else:
            tout[d * lines_out : (d + 1) * lines_out, 0:128] = message[0:lines_out, :]
            tout[d * lines_out : (d + 1) * lines_out, 128:patches] = message[16 : 16 + lines_out, 0 : patches - 128]

    def unpack_half(own, group):
        for parity in range(2):

            @pl.when((core == parity) == own)
            def _():
                for d in range(parity, devices, 2):
                    unpack(d, group)

    unpack_half(True, 0)
    for k in range(1, 4):
        small_gather(1, k, 1).wait_recv()
    small_gather(2, 0, 1).start()
    unpack_half(True, 1)
    ag_planes_pass()
    ag_direct(plane_at(0))
    for group in range(2):
        small_gather(2, 0, group).wait_recv()
        unpack_half(False, group)
    for turn in range(turns):
        tin[0:patches, turn * unit : (turn + 1) * unit] = lines[pl.ds(turn, patches, stride=turns), :][:, 0:unit]
    for rest, into, at in ((c_one, tin, patches), (c_two, tout, hidden_tok)):
        rest = rest[...].reshape(1, rest.shape[0])
        for i in range(3):
            term = rest.astype(LOW).astype(WIDE)
            into[at + i : at + i + 1, 0 : rest.shape[1]] = term
            rest = rest - term
    tin_t[...] = tin[...].T.astype(LOW)
    tout_t[...] = tout[...].T.astype(LOW)
    ones = jnp.ones((3, width), WIDE)

    gain_one, shift_one = vecs[0:1, :], vecs[1:2, :]
    gain_two, shift_two, c_four = vecs[2:3, :], vecs[3:4, :], vecs[4:5, :]
    def token_forward(b, carry):
        fed = mid[b] * gain_one + shift_one
        mixed[b] = padded(jnp.concatenate([fed, ones], axis=0), pad).astype(LOW)
        value, slope = gelu_parts(dot(tin_t[...], mixed[b], NN))
        act_t[b] = padded(jnp.concatenate([value, ones], axis=0), act_t.shape[1]).astype(LOW)
        slope_t[b] = slope.astype(LOW)
        mid[b] = grad_zed[b] + dot(tout_t[...], act_t[b], NN)[0:patches]
        return carry

    def channel_inputs(r, carry):
        parts = []
        for h in range(2):
            normed, _ = normalize(mid[2 * r + h])
            total[2 * r + h] = mid[2 * r + h] + c_four
            grad_zed[2 * r + h] = jnp.zeros((patches, width), WIDE)
            parts.append(padded(normed * gain_two + shift_two, lot))
        zed[r] = jnp.concatenate(parts, axis=0).astype(LOW)
        return carry

    first = 2 * count // 3
    lax.fori_loop(0, first, token_forward, 0)
    ag_forward(plane_at(0))
    lax.fori_loop(first, count, token_forward, 0)
    ag_core(plane_at(0))
    ag_planes_last()
    lax.fori_loop(0, blocks, channel_inputs, 0)
    ag_direct(plane_at(1))
    for k in range(planes):
        for place in range(PLANE):
            near = plane_of(k) * PLANE + (
                (row + (place // 2) % 2) % 2 * 4 + (col + place % 2) % 2 * 2 + (core + place // 4) % 2
            )
            c_in_rel[k, :, place * shard : (place + 1) * shard] = c_in[near]

    ag_core_last(plane_at(0))

    def rs_two(i, mat):
        rs(0, i, mat).wait_recv()
        own_sum[mat] += recv_one[i % 2, mat].astype(WIDE)

        @pl.when(i == 0)
        def _():
            send_far[mat] = own_sum[mat].astype(LOW)
            rs(4, 0, mat).start()

        @pl.when(i == planes - 1)
        def _():
            rs(4, 0, mat).wait_recv()
            own_sum[mat] += recv_far[mat].astype(WIDE)

        @pl.when(i > 1)
        def _():
            rs(1, i - 1, mat).wait_send()

        @pl.when(i > 0)
        def _():
            first, second = (1, 3) if mat == 0 else (2, 3)
            send_two[mat, 0:shard] = own_sum[mat, first * shard : (first + 1) * shard].astype(LOW)
            send_two[mat, shard : 2 * shard] = own_sum[mat, second * shard : (second + 1) * shard].astype(LOW)
            rs(1, i, mat).start()

    def rs_three(i):
        for mat in mats:
            rs(1, i, mat).wait_recv()
            other = 2 if mat == 0 else 1

            @pl.when(i > 1)
            def _():
                rs(2, i - 1, mat).wait_send()

            keep_sum[mat] = own_sum[mat, 0:shard] + recv_two[i % 2, mat, 0:shard].astype(WIDE)
            send_three[mat] = (
                own_sum[mat, other * shard : (other + 1) * shard]
                + recv_two[i % 2, mat, shard : 2 * shard].astype(WIDE)
            ).astype(LOW)
            rs(2, i, mat).start()

    def rs_four(i):
        for mat in mats:
            rs(2, i, mat).wait_recv()

            send_four[i % 2, mat] = (keep_sum[mat] + recv_three[i % 2, mat].astype(WIDE)).astype(LOW)
            rs(3, i, mat).start()

    def rs_last():
        last = planes - 1
        for mat in mats:
            result = grad_in if mat == 0 else grad_out
            rs(2, last, mat).wait_recv()
            summed = keep_sum[mat] + recv_three[last % 2, mat].astype(WIDE)
            for i in range(1, last):
                rs(3, i, mat).wait_recv()
                summed = summed + recv_four[i - 1, mat].astype(WIDE)
            result[...] = summed

    tile = chunk // 3

    def channel_chunk(i, carry):
        k = plane_at(i)
        ag_ready(k)

        def rows(r, inner):
            for s in range(3):
                part = slice(s * tile, (s + 1) * tile)
                pre = dot(zed[r], weights[0, k, part], NT) + c_in_rel[k, :, part]
                value, slope = gelu_parts(pre)
                act[pl.ds(r * pair, pair), part] = value.astype(LOW)
                back = (dot(top[r], weights[1, k, part], NT) * slope).astype(LOW)
                grad_pre[pl.ds(r * pair, pair), part] = back
            up = dot(act[pl.ds(r * pair, pair), :], weights[1, k], NN)
            down = dot(grad_pre[pl.ds(r * pair, pair), :], weights[0, k], NN)
            for h in range(2):
                total[2 * r + h] += up[h * lot : h * lot + patches]
                grad_zed[2 * r + h] += down[h * lot : h * lot + patches]

            @pl.when((r == 0) & (i == 1))
            def _():
                ag_forward(plane_at(2))

            @pl.when((r == 0) & (i == 3))
            def _():
                rs_four(1)

            @pl.when((r == 1) & (i == 0))
            def _():
                ag_forward(plane_at(1))
                ag_direct(plane_at(2))

            @pl.when((r == 1) & (i == 1))
            def _():
                ag_core(plane_at(2))
                for mat in mats:
                    ag(2, 0, mat).start()
                ag_forward(0)

            @pl.when((r == 1) & (i == 2))
            def _():
                ag_core(0)
                ag_core_last(0)

            @pl.when((r == 2) & (i == 0))
            def _():
                ag_core(plane_at(1))

            return inner

        lax.fori_loop(0, blocks, rows, 0)


        back_sum = jnp.sum(grad_pre[...].astype(WIDE), axis=0, keepdims=True)
        for place in range(PLANE):
            near = plane_of(k) * PLANE + (
                (row + (place // 2) % 2) % 2 * 4 + (col + place % 2) % 2 * 2 + (core + place // 4) % 2
            )
            grad_c_in[near] = back_sum[:, place * shard : (place + 1) * shard]

        flat_top = top[...].reshape(blocks * pair, width)
        flat_zed = zed[...].reshape(blocks * pair, width)
        @pl.when(i > 0)
        def _():
            for mat in mats:
                rs(0, i - 1, mat).wait_send()

        send_one[1] = dot(act[:, half:chunk], flat_top, TN).astype(LOW)
        send_one[0] = dot(grad_pre[:, half:chunk], flat_zed, TN).astype(LOW)
        for mat in mats:
            rs(0, i, mat).start()

        @pl.when(i < 2)
        def _():
            ag_core_last(plane_at(i + 1))

        @pl.when(i > 1)
        def _():
            rs_three(i - 1)

        own_sum[1] = dot(act[:, 0:half], flat_top, TN)
        own_sum[0] = dot(grad_pre[:, 0:half], flat_zed, TN)
        for mat in mats:
            rs_two(i, mat)
        return carry

    for b in range(2):
        reload(b).start()
    lax.fori_loop(0, planes, channel_chunk, 0)

    tin_low = tin[...].astype(LOW)
    tout_low = tout[0:hidden_tok, :].astype(LOW)

    def token_backward(b, carry):
        keep = mask[b].astype(WIDE)
        normed, scale = normalize(mid[b])
        down = grad_zed[b]
        grad_vecs[0:1, :] += jnp.sum(down * normed, axis=0, keepdims=True)
        grad_vecs[1:2, :] += jnp.sum(down, axis=0, keepdims=True)
        reload(b).wait()
        grad_mid = cot[b % 2] * keep + norm_back(down, normed, scale, gain_two)

        @pl.when(b + 2 < count)
        def _():
            reload(b + 2).start()

        back = padded(grad_mid, pad).astype(LOW)
        grad_tout[...] += dot(act_t[b], back, NT)
        grad_zed[b] = grad_mid
        slope_t[b] = (dot(tout_low, back, NN) * slope_t[b].astype(WIDE)).astype(LOW)
        grad_tin[:, 0:hidden_tok] += dot(mixed[b], slope_t[b], NT)

        reload_image(b).start()

        @pl.when(b == 2)
        def _():
            rs_four(planes - 2)

        return carry

    def image_norm(b, carry):
        reload_image(b).wait()
        normed, scale = normalize(mid[b])
        mid[b] = normed
        scales[b] = scale
        grad_mixed = dot(tin_low, slope_t[b], NN)[0:patches]
        weights[b // planes, b % planes, 0:pad] = padded(grad_mixed, pad).astype(LOW)
        late[0, 0:1, :] += jnp.sum(grad_mixed * normed, axis=0, keepdims=True)
        late[0, 1:2, :] += jnp.sum(grad_mixed, axis=0, keepdims=True)

        @pl.when(b == 1)
        def _():
            small_second()

        return carry

    def image_backward(b, carry):
        total[b] *= mask[b].astype(WIDE)
        grad_zed[b] += norm_back(weights[b // planes, b % planes, 0:pad][0:patches].astype(WIDE), mid[b], scales[b], gain_one)
        return carry

    late[0] = jnp.zeros_like(late[0])
    lax.fori_loop(0, count, token_backward, 0)

    biases[0] = jnp.zeros_like(biases[0])
    for i in range(hidden_tok // 128):
        biases[0, i : i + 1, :] = grad_tin[patches : patches + 1, i * 128 : (i + 1) * 128]
    biases[0, 3:4, :] = grad_tout[hidden_tok : hidden_tok + 1, 0:128]
    biases[0, 4:5, 0 : patches - 128] = grad_tout[hidden_tok : hidden_tok + 1, 128:patches]
    bias_reduce(0, 0).start()
    for turn in range(turns):
        lines[pl.ds(turn, patches, stride=turns), :] = grad_tin[0:patches, turn * unit : turn * unit + 128]
    for d in range(devices):
        far, k = place_of(d)
        first, second = small_sum.at[0, far, k], small_sum.at[1, far, k]
        low = lines[d * lines_in : d * lines_in + first_lines, :]
        high = lines[d * lines_in + first_lines : (d + 1) * lines_in, :]
        first[0:first_lines, 0:64] = low[:, 0:64]
        first[0 : lines_in - first_lines, 64:128] = high[:, 0:64]
        first[24:27, 64 : 64 + own_vec] = grad_vecs[0:3, d * own_vec : (d + 1) * own_vec]
        first[31:32, 0:shard] = grad_c_in[d]
        second[0:lines_out, :] = grad_tout[d * lines_out : (d + 1) * lines_out, 0:128]
        second[16 : 16 + lines_out, 0 : patches - 128] = grad_tout[d * lines_out : (d + 1) * lines_out, 128:patches]
    for group in range(2):
        for k in range(1, planes):
            small_gather(0, k, group).wait_send()
        for far in range(1, 4):
            small_gather(1, far, group).wait_send()
        small_gather(2, 0, group).wait_send()
        for far in range(4, PLANE):
            small_all[group, far] = small_sum[group, far].astype(LOW)
    small_reduce(0, 0).start()

    def small_second():
        bias_reduce(0, 0).wait_recv()
        biases[1] = biases[0] + biases_in[0, 0]
        small_reduce(0, 0).wait_recv()
        for far in range(4):
            for group in range(2):
                small_sum[group, far] += small_core[group, far].astype(WIDE)
        for far in range(1, 4):
            for group in range(2):
                small_all[group, far] = small_sum[group, far].astype(LOW)
            small_reduce(1, far).start()
            bias_reduce(1, far).start()

    def small_third():
        for far in range(1, 4):
            small_reduce(1, far).wait_recv()
            bias_reduce(1, far).wait_recv()
            for group in range(2):
                small_sum[group, 0] += small_plane[group, far].astype(WIDE)
        biases[2] = (biases[1] + biases_in[1, 1]) + (biases_in[1, 2] + biases_in[1, 3])
        for k in range(1, planes):
            for group in range(2):
                small_all[group, 0, k] = small_sum[group, 0, k].astype(LOW)
            small_reduce(2, k).start()
            bias_reduce(2, k).start()

    for mat in mats:
        for k in range(planes):
            for stage in range(1, 6):
                ag(stage, k, mat).wait_send()
        ag(0, 1, mat).wait_send()

        @pl.when(inner)
        def _():
            ag(0, 3, mat).wait_send()
            for which in range(3):
                ag_pass(which, mat).wait_send()

    lax.fori_loop(0, count, image_norm, 0)
    late_reduce(0, 0).start()
    lax.fori_loop(0, 1, image_backward, 0)
    late_reduce(0, 0).wait_recv()
    late[1] = late[0] + late_in[0, 0]
    for far in range(1, 4):
        late_reduce(1, far).start()
    rs_three(planes - 1)
    small_third()
    lax.fori_loop(1, count // 2, image_backward, 0)
    late_sum = late[1]
    for far in range(1, 4):
        late_reduce(1, far).wait_recv()
        late_sum = late_sum + late_in[1, far]
    late[2] = late_sum
    for k in range(1, planes):
        late_reduce(2, k).start()
    lax.fori_loop(count // 2, count, image_backward, 0)
    rs_last()
    summed = [small_sum[group, 0, 0] for group in range(2)]
    tree = [biases[2]]
    for k in range(1, planes):
        small_reduce(2, k).wait_recv()
        bias_reduce(2, k).wait_recv()
        summed = [summed[group] + small_z[k, group].astype(WIDE) for group in range(2)]
        tree.append(biases_in[2, k])
    for group in range(2):
        small_out[32 * group : 32 * (group + 1)] = summed[group]
    for k in range(1, planes):
        late_reduce(2, k).wait_recv()
        late_sum = late_sum + late_in[2, k]
    late_sum = pltpu.roll(padded(late_sum, 8), width - own_vec * me, 1)
    small_out[27:29, 64 : 64 + own_vec] = late_sum[0:2, 0:own_vec]
    while len(tree) > 1:
        tree = [tree[i] + tree[i + 1] for i in range(0, len(tree), 2)]
    biases_out[...] = tree[0]

    for mat in mats:
        for stage in range(3):
            rs(stage, planes - 1, mat).wait_send()
        rs(4, 0, mat).wait_send()
        for i in range(1, planes - 1):
            rs(3, i, mat).wait_send()
    late_reduce(0, 0).wait_send()
    for far in range(1, 4):
        late_reduce(1, far).wait_send()
    for k in range(1, planes):
        late_reduce(2, k).wait_send()
    small_reduce(0, 0).wait_send()
    bias_reduce(0, 0).wait_send()
    for far in range(1, 4):
        small_reduce(1, far).wait_send()
        bias_reduce(1, far).wait_send()
    for k in range(1, planes):
        small_reduce(2, k).wait_send()
        bias_reduce(2, k).wait_send()


def finish_kernel(
    block_in,
    image_in,
    w_in,
    w_out,
    small,
    biases,
    block_out,
    image_out,
    w_in_out,
    w_out_out,
    tin,
    tout,
    gain_one,
    shift_one,
    gain_two,
    shift_two,
    c_four,
    c_in,
    c_one,
    c_two,
    sem,
):
    copies = [
        pltpu.make_async_copy(block_in, block_out, sem.at[0]),
        pltpu.make_async_copy(image_in, image_out, sem.at[1]),
        pltpu.make_async_copy(w_in, w_in_out, sem.at[2]),
        pltpu.make_async_copy(w_out, w_out_out, sem.at[3]),
    ]
    for copy in copies:
        copy.start()
    hidden_tok, patches = c_one.shape[0], c_two.shape[0]
    unit = math.gcd(tin.shape[0], hidden_tok)
    lines_in = tin.shape[0] // unit
    first_lines = (lines_in + 1) // 2
    for i in range(lines_in):
        at, lane = (i, 0) if i < first_lines else (i - first_lines, 64)
        tin[i * unit : (i + 1) * unit] = small[at : at + 1, lane : lane + unit].reshape(unit)
    for i in range(tout.shape[0] // patches):
        tout[i * patches : i * patches + 128] = small[32 + i : 33 + i, :].reshape(128)
        tout[i * patches + 128 : (i + 1) * patches] = small[48 + i : 49 + i, 0 : patches - 128].reshape(
            patches - 128
        )
    for i, piece in enumerate((gain_two, shift_two, c_four, gain_one, shift_one)):
        own_vec = piece.shape[0]
        piece[...] = small[24 + i : 25 + i, 64 : 64 + own_vec].reshape(own_vec)
    shard = c_in.shape[0]
    c_in[...] = small[31:32, 0:shard].reshape(shard)
    for i in range(hidden_tok // 128):
        c_one[i * 128 : (i + 1) * 128] = biases[i : i + 1, :].reshape(128)
    c_two[0:128] = biases[3:4, :].reshape(128)
    c_two[128:patches] = biases[4:5, 0 : patches - 128].reshape(patches - 128)
    for copy in copies:
        copy.wait()


def fast_shards(
    images,
    mask,
    cotangent,
    w_token_in,
    w_token_out,
    bias_token_in,
    bias_token_out,
    gain_one,
    shift_one,
    gain_two,
    shift_two,
    w_expand,
    bias_expand,
    w_reduce,
    bias_reduce,
):
    devices = lax.axis_size("dp")
    planes = devices // PLANE
    count, patches, width = images.shape
    hidden_tok = bias_token_in.shape[0]
    shard = w_expand.shape[0]
    pad = -(-patches // 16) * 16
    lot = -(-patches // 8) * 8
    pair = 2 * lot
    blocks = count // 2
    chunk = 8 * shard
    half = 4 * shard

    unit = math.gcd(w_token_in.shape[0], hidden_tok)
    lines_in = w_token_in.shape[0] // unit
    hidden_pad = hidden_tok + 16

    vmem = pl.BlockSpec(memory_space=pltpu.VMEM)
    hbm = pl.BlockSpec(memory_space=pl.ANY)
    shape = jax.ShapeDtypeStruct
    outs = pl.pallas_call(
        block_kernel,
        out_shape=(
            pltpu.VMEM(images.shape, WIDE),
            pltpu.VMEM(images.shape, WIDE),
            pltpu.VMEM(w_expand.shape, WIDE),
            pltpu.VMEM(w_reduce.shape, WIDE),
            pltpu.VMEM((64, 128), WIDE),
            pltpu.VMEM((8, 128), WIDE),
        ),
        in_specs=[pl.BlockSpec(memory_space=pltpu.SMEM), hbm, hbm] + [vmem] * 12,
        out_specs=[vmem] * 6,
        scratch_shapes=[
            pltpu.VMEM((2,) + images.shape[1:], WIDE),
            pltpu.VMEM((count, pad, width), LOW),
            pltpu.VMEM((count, hidden_pad, width), LOW),
            pltpu.VMEM((count, hidden_tok, width), LOW),
            pltpu.VMEM(images.shape, WIDE),
            pltpu.VMEM((blocks, pair, width), LOW),
            pltpu.VMEM((blocks, pair, width), LOW),
            pltpu.VMEM((2, planes, chunk, width), LOW),
            pltpu.VMEM((blocks * pair, chunk), LOW),
            pltpu.VMEM((blocks * pair, chunk), LOW),
            pltpu.VMEM((planes, 1, chunk), WIDE),
            pltpu.VMEM((2, half, width), WIDE),
            pltpu.VMEM((2, shard, width), WIDE),
            pltpu.VMEM((2, half, width), LOW),
            pltpu.VMEM((2, 2, half, width), LOW),
            pltpu.VMEM((2, 2 * shard, width), LOW),
            pltpu.VMEM((2, 2, 2 * shard, width), LOW),
            pltpu.VMEM((2, shard, width), LOW),
            pltpu.VMEM((2, 2, shard, width), LOW),
            pltpu.VMEM((2, 2, shard, width), LOW),
            pltpu.VMEM((planes - 2, 2, shard, width), LOW),
            pltpu.VMEM((2, half, width), LOW),
            pltpu.VMEM((2, half, width), LOW),
            pltpu.VMEM((pad, hidden_tok), WIDE),
            pltpu.VMEM((hidden_tok, pad), LOW),
            pltpu.VMEM((hidden_pad, pad), WIDE),
            pltpu.VMEM((pad, hidden_pad), LOW),
            pltpu.VMEM((8, width), WIDE),
            pltpu.VMEM((devices, 1, shard), WIDE),
            pltpu.VMEM((devices * lines_in, 128), WIDE),
            pltpu.VMEM((64, 128), WIDE),
            pltpu.VMEM((2, PLANE, planes, 32, 128), LOW),
            pltpu.VMEM((pad, hidden_tok + 128), WIDE),
            pltpu.VMEM((hidden_pad, pad), WIDE),
            pltpu.VMEM((8, width), WIDE),
            pltpu.VMEM((devices, 1, shard), WIDE),
            pltpu.VMEM((2, PLANE, planes, 32, 128), WIDE),
            pltpu.VMEM((2, 4, planes, 32, 128), LOW),
            pltpu.VMEM((2, 4, planes, 32, 128), LOW),
            pltpu.VMEM((planes, 2, 32, 128), LOW),
            pltpu.VMEM((3, 8, 128), WIDE),
            pltpu.VMEM((3, max(4, planes), 8, 128), WIDE),
            pltpu.VMEM((3, 2, width), WIDE),
            pltpu.VMEM((3, max(4, planes), 2, width), WIDE),
            pltpu.VMEM((count, patches, 1), WIDE),
            pltpu.SemaphoreType.DMA((4, count)),
            pltpu.SemaphoreType.DMA((7, planes, 2)),
            pltpu.SemaphoreType.DMA((7, planes, 2)),
            pltpu.SemaphoreType.DMA((5, planes, 2)),
            pltpu.SemaphoreType.DMA((5, planes, 2)),
        ]
        + [pltpu.SemaphoreType.DMA((3, max(4, planes), 2))] * 2
        + [pltpu.SemaphoreType.DMA((3, max(4, planes)))] * 6,
        compiler_params=pltpu.CompilerParams(
            collective_id=0, has_side_effects=True, vmem_limit_bytes=55 * 2**20
        ),
    )(
        mask,
        images,
        cotangent,
        w_expand,
        w_reduce,
        w_token_in,
        w_token_out,
        gain_one,
        shift_one,
        gain_two,
        shift_two,
        bias_reduce,
        bias_expand,
        bias_token_in,
        bias_token_out,
    )
    flat = pl.pallas_call(
        finish_kernel,
        out_shape=(
            shape(images.shape, WIDE),
            shape(images.shape, WIDE),
            shape(w_expand.shape, WIDE),
            shape(w_reduce.shape, WIDE),
            shape(w_token_in.shape, WIDE),
            shape(w_token_out.shape, WIDE),
            *[shape(gain_one.shape, WIDE)] * 5,
            shape(bias_expand.shape, WIDE),
            shape(bias_token_in.shape, WIDE),
            shape(bias_token_out.shape, WIDE),
        ),
        in_specs=[vmem] * 6,
        out_specs=[hbm] * 4 + [vmem] * 10,
        scratch_shapes=[pltpu.SemaphoreType.DMA((4,))],
        compiler_params=pltpu.CompilerParams(vmem_limit_bytes=16 * 2**20),
    )(*outs)
    block_output, image_grad, own_win, own_wout, *rest = flat
    g_tin, g_tout, g_one, b_one, g_two, b_two, c_four, c_in, c_one, c_two = rest
    return (
        block_output,
        image_grad,
        g_tin,
        g_tout,
        c_one,
        c_two,
        g_one,
        b_one,
        g_two,
        b_two,
        own_win,
        c_in,
        own_wout,
        c_four,
    )


def fits(devices, images, w_token_in, w_token_out, bias_token_in, gain_one, w_expand):
    planes = devices // PLANE
    patches = images.shape[1]
    hidden_tok = bias_token_in.shape[0]
    shard = w_expand.shape[0]
    unit = math.gcd(w_token_in.shape[0], hidden_tok)
    return (
        devices % PLANE == 0
        and planes == 4
        and images.shape[0] % 2 == 0
        and images.shape[0] <= 2 * planes
        and shard % 16 == 0
        and shard <= 128
        and (4 * shard) % 128 == 0
        and 128 < patches <= 205
        and unit <= 64
        and w_token_in.shape[0] // unit <= 49
        and w_token_out.shape[0] % patches == 0
        and w_token_out.shape[0] // patches <= 16
        and gain_one.shape[0] <= 64
        and hidden_tok == 384
    )


def choose(
    images,
    mask,
    cotangent,
    w_token_in,
    w_token_out,
    bias_token_in,
    bias_token_out,
    gain_one,
    shift_one,
    gain_two,
    shift_two,
    w_expand,
    bias_expand,
    w_reduce,
    bias_reduce,
):
    args = (
        images,
        mask,
        cotangent,
        w_token_in,
        w_token_out,
        bias_token_in,
        bias_token_out,
        gain_one,
        shift_one,
        gain_two,
        shift_two,
        w_expand,
        bias_expand,
        w_reduce,
        bias_reduce,
    )
    if fits(lax.axis_size("dp"), images, w_token_in, w_token_out, bias_token_in, gain_one, w_expand):
        return fast_shards(*args)
    return shards(*args)


def shards(
    images,
    mask,
    cotangent,
    w_token_in,
    w_token_out,
    bias_token_in,
    bias_token_out,
    gain_one,
    shift_one,
    gain_two,
    shift_two,
    w_expand,
    bias_expand,
    w_reduce,
    bias_reduce,
):
    low_type = jnp.bfloat16
    wide = jnp.float32
    count, patches, width = images.shape
    hidden_tok = bias_token_in.shape[0]
    rows = count * patches
    keep = mask.astype(wide)[:, None, None]
    small_local = (
        w_token_in.astype(low_type),
        w_token_out.astype(low_type),
        gain_one.astype(low_type),
        shift_one.astype(low_type),
        gain_two.astype(low_type),
        shift_two.astype(low_type),
        bias_reduce.astype(low_type),
    )
    channel_local = (
        w_expand.astype(low_type),
        w_reduce.astype(low_type),
        bias_expand.astype(low_type),
    )
    small_all = (
        lax.all_gather(small_local[0], "dp", axis=0, tiled=True),
        lax.all_gather(small_local[1], "dp", axis=0, tiled=True),
        lax.all_gather(small_local[2], "dp", axis=0, tiled=True),
        lax.all_gather(small_local[3], "dp", axis=0, tiled=True),
        lax.all_gather(small_local[4], "dp", axis=0, tiled=True),
        lax.all_gather(small_local[5], "dp", axis=0, tiled=True),
        lax.all_gather(small_local[6], "dp", axis=0, tiled=True),
    )
    tin = small_all[0].reshape(patches, hidden_tok)
    tout = small_all[1].reshape(hidden_tok, patches)
    g_one, b_one, g_two, b_two, c_four = [piece.astype(wide) for piece in small_all[2:]]
    normed_one, scale_one = normalize(images)
    mixed_in = (normed_one * g_one + b_one).astype(low_type)
    pre_t = (
        jnp.einsum("ps,bpd->bsd", tin, mixed_in, preferred_element_type=wide)
        + bias_token_in[None, :, None]
    )
    act_t = gelu_exact(pre_t).astype(low_type)
    middle = (
        images
        + jnp.einsum("sp,bsd->bpd", tout, act_t, preferred_element_type=wide)
        + bias_token_out[None, :, None]
    )
    normed_two, scale_two = normalize(middle.reshape(rows, width))
    zed = (normed_two * g_two + b_two).astype(low_type)
    whole_channel = (
        lax.all_gather(channel_local[0], "dp", axis=0, tiled=True),
        lax.all_gather(channel_local[1], "dp", axis=0, tiled=True),
        lax.all_gather(channel_local[2], "dp", axis=0, tiled=True),
    )
    w_in, w_out, c_in = whole_channel
    pre = (
        jnp.einsum("td,fd->tf", zed, w_in, preferred_element_type=wide) + c_in.astype(wide)[None, :]
    )
    act = gelu_exact(pre).astype(low_type)
    reduced = jnp.dot(act, w_out, preferred_element_type=wide)
    block_output = (middle + (reduced + c_four).reshape(count, patches, width)) * keep
    grad_top = cotangent * keep
    grad_branch = grad_top.reshape(rows, width).astype(low_type)
    grad_c_four = jnp.sum(grad_branch.astype(wide), axis=0)
    small_all = (
        lax.all_gather(small_local[0], "dp", axis=0, tiled=True),
        lax.all_gather(small_local[1], "dp", axis=0, tiled=True),
        lax.all_gather(small_local[2], "dp", axis=0, tiled=True),
        lax.all_gather(small_local[3], "dp", axis=0, tiled=True),
        lax.all_gather(small_local[4], "dp", axis=0, tiled=True),
        lax.all_gather(small_local[5], "dp", axis=0, tiled=True),
        lax.all_gather(small_local[6], "dp", axis=0, tiled=True),
    )
    tin = small_all[0].reshape(patches, hidden_tok)
    tout = small_all[1].reshape(hidden_tok, patches)
    g_one, b_one, g_two, b_two, c_four = [piece.astype(wide) for piece in small_all[2:]]
    whole_channel = (
        lax.all_gather(channel_local[0], "dp", axis=0, tiled=True),
        lax.all_gather(channel_local[1], "dp", axis=0, tiled=True),
        lax.all_gather(channel_local[2], "dp", axis=0, tiled=True),
    )
    w_in, w_out, c_in = whole_channel
    pre = (
        jnp.einsum("td,fd->tf", zed, w_in, preferred_element_type=wide) + c_in.astype(wide)[None, :]
    )
    act = gelu_exact(pre).astype(low_type)
    grad_act = jnp.einsum("td,fd->tf", grad_branch, w_out, preferred_element_type=wide)
    grad_pre = (grad_act * gelu_slope(pre)).astype(low_type)
    grad_zed = jnp.dot(grad_pre, w_in, preferred_element_type=wide)
    grad_in = jnp.einsum("tf,td->fd", grad_pre, zed, preferred_element_type=wide)
    grad_out = jnp.einsum("tf,td->fd", act, grad_branch, preferred_element_type=wide)
    grad_cin = jnp.sum(grad_pre.astype(wide), axis=0)
    grad_zed, grad_win, grad_wout, grad_cin = (grad_zed, grad_in, grad_out, grad_cin)
    grad_g_two = jnp.sum(grad_zed * normed_two, axis=0)
    grad_b_two = jnp.sum(grad_zed, axis=0)
    grad_mid = grad_top + norm_back(grad_zed, normed_two, scale_two, g_two).reshape(
        count, patches, width
    )
    grad_back = grad_mid.astype(low_type)
    grad_c_two = jnp.sum(grad_back.astype(wide), axis=(0, 2))
    grad_tout = jnp.einsum("bsd,bpd->sp", act_t, grad_back, preferred_element_type=wide)
    grad_act_t = jnp.einsum("sp,bpd->bsd", tout, grad_back, preferred_element_type=wide)
    grad_pre_t = (grad_act_t * gelu_slope(pre_t)).astype(low_type)
    grad_c_one = jnp.sum(grad_pre_t.astype(wide), axis=(0, 2))
    grad_tin = jnp.einsum("bpd,bsd->ps", mixed_in, grad_pre_t, preferred_element_type=wide)
    grad_mixed = jnp.einsum("ps,bsd->bpd", tin, grad_pre_t, preferred_element_type=wide)
    grad_g_one = jnp.sum(grad_mixed * normed_one, axis=(0, 1))
    grad_b_one = jnp.sum(grad_mixed, axis=(0, 1))
    image_grad = grad_mid + norm_back(grad_mixed, normed_one, scale_one, g_one)
    bias_sums = lax.psum((grad_c_one, grad_c_two), "dp")
    flat_tin = grad_tin.reshape(patches * hidden_tok)
    flat_tout = grad_tout.reshape(hidden_tok * patches)
    owned = (
        lax.psum_scatter(flat_tin, "dp", scatter_dimension=0, tiled=True),
        lax.psum_scatter(flat_tout, "dp", scatter_dimension=0, tiled=True),
        lax.psum_scatter(grad_g_one, "dp", scatter_dimension=0, tiled=True),
        lax.psum_scatter(grad_b_one, "dp", scatter_dimension=0, tiled=True),
        lax.psum_scatter(grad_g_two, "dp", scatter_dimension=0, tiled=True),
        lax.psum_scatter(grad_b_two, "dp", scatter_dimension=0, tiled=True),
        lax.psum_scatter(grad_win, "dp", scatter_dimension=0, tiled=True),
        lax.psum_scatter(grad_cin, "dp", scatter_dimension=0, tiled=True),
        lax.psum_scatter(grad_wout, "dp", scatter_dimension=0, tiled=True),
        lax.psum_scatter(grad_c_four, "dp", scatter_dimension=0, tiled=True),
    )
    (
        own_tin,
        own_tout,
        own_g_one,
        own_b_one,
        own_g_two,
        own_b_two,
        own_win,
        own_cin,
        own_wout,
        own_c_four,
    ) = owned
    return (
        block_output,
        image_grad,
        own_tin,
        own_tout,
        bias_sums[0],
        bias_sums[1],
        own_g_one,
        own_b_one,
        own_g_two,
        own_b_two,
        own_win,
        own_cin,
        own_wout,
        own_c_four,
    )


def solution(mesh):
    placed = (
        P("dp", None, None),
        P("dp"),
        P("dp", None, None),
        P("dp"),
        P("dp"),
        P(),
        P(),
        P("dp"),
        P("dp"),
        P("dp"),
        P("dp"),
        P("dp", None),
        P("dp"),
        P("dp", None),
        P("dp"),
    )
    return jax.shard_map(
        choose,
        mesh=mesh,
        in_specs=placed,
        out_specs=(
            P("dp", None, None),
            P("dp", None, None),
            P("dp"),
            P("dp"),
            P(),
            P(),
            P("dp"),
            P("dp"),
            P("dp"),
            P("dp"),
            P("dp", None),
            P("dp"),
            P("dp", None),
            P("dp"),
        ),
        check_vma=False,
    )
```

```python
import math

import jax
import jax.numpy as jnp
from jax import lax
from jax.experimental import pallas as pl
from jax.experimental.pallas import tpu as pltpu
from jax.sharding import PartitionSpec as P

EPS = 1e-06


def gelu_exact(v):
    return 0.5 * v * (1.0 + lax.erf(v * 0.7071067811865476))


def gelu_slope(v):
    return 0.5 * (1.0 + lax.erf(v * 0.7071067811865476)) + v * 0.3989422804014327 * jnp.exp(
        -0.5 * v * v
    )


def norm_parts(v):
    middle = jnp.mean(v, axis=-1, keepdims=True)
    centered = v - middle
    scale = lax.rsqrt(jnp.mean(centered * centered, axis=-1, keepdims=True) + EPS)
    return (centered * scale, middle, scale)


def normalize(v):
    centered = v - jnp.mean(v, axis=-1, keepdims=True)
    scale = lax.rsqrt(jnp.mean(centered * centered, axis=-1, keepdims=True) + EPS)
    return (centered * scale, scale)


def norm_back(grad_in, normed, scale, gain):
    scaled = grad_in * gain
    return scale * (
        scaled
        - jnp.mean(scaled, axis=-1, keepdims=True)
        - normed * jnp.mean(scaled * normed, axis=-1, keepdims=True)
    )


WIDE = jnp.float32
LOW = jnp.bfloat16
MESH = pl.DeviceIdType.MESH
NT = (((1,), (1,)), ((), ()))
TN = (((0,), (0,)), ((), ()))
NN = (((1,), (0,)), ((), ()))
PLANE = 8


def dot(a, b, dims):
    return lax.dot_general(a, b, dims, preferred_element_type=WIDE)


def gelu_parts(v):
    cdf = 0.5 * (1.0 + lax.erf(v * 0.7071067811865476))
    return v * cdf, cdf + v * 0.3989422804014327 * jnp.exp(-0.5 * v * v)


def padded(v, rows):
    return jnp.concatenate([v, jnp.zeros((rows - v.shape[0], v.shape[1]), v.dtype)], axis=0)


def block_kernel(
    mask,
    images,
    cotangent,
    w_in,
    w_out,
    tin_own,
    tout_own,
    gain_one_own,
    shift_one_own,
    gain_two_own,
    shift_two_own,
    c_four_own,
    c_in_own,
    c_one,
    c_two,
    total,
    grad_zed,
    grad_in,
    grad_out,
    small_out,
    biases_out,
    cot,
    mixed,
    act_t,
    slope_t,
    mid,
    zed,
    top,
    weights,
    act,
    grad_pre,
    c_in_rel,
    own_sum,
    keep_sum,
    send_one,
    recv_one,
    send_two,
    recv_two,
    send_three,
    recv_three,
    send_four,
    recv_four,
    recv_far,
    tin,
    tin_t,
    tout,
    tout_t,
    vecs,
    c_in,
    lines,
    small_own,
    small_all,
    grad_tin,
    grad_tout,
    grad_vecs,
    grad_c_in,
    small_sum,
    small_core,
    small_plane,
    small_z,
    biases,
    biases_in,
    late,
    late_in,
    figures,
    in_sem,
    ag_send,
    ag_recv,
    rs_send,
    rs_recv,
    sg_send,
    sg_recv,
    ss_send,
    ss_recv,
    bs_send,
    bs_recv,
    ls_send,
    ls_recv,
):
    count, patches, width = images.shape
    planes = weights.shape[1]
    shard = w_in.shape[0]
    half = 4 * shard
    chunk = 8 * shard
    pad = mixed.shape[1]
    blocks = count // 2
    pair = zed.shape[0] // blocks
    lot = pair // 2
    me = lax.axis_index("dp")
    core = me % 2
    col = (me // 2) % 2
    row = (me // 4) % 2
    z = me // PLANE
    by_core = me + 1 - 2 * core
    by_x = me + 2 - 4 * col
    by_y = me + 4 - 8 * row
    by_both = by_x + by_y - me

    def plane_of(k):
        out, bit = z, 1
        while bit < planes:
            out = out + bit * ((k // bit) % 2) * (1 - 2 * ((z // bit) % 2))
            bit *= 2
        return out

    def by_z(k):
        return me + PLANE * (plane_of(k) - z)

    def ag(stage, k, mat):
        near, far = (by_x, by_y) if mat == 0 else (by_y, by_x)
        step = 1 if mat == 0 else 2
        if stage == 0:
            src, dst, size, to = 0, 0, shard, by_z(k)
            source = weights.at[mat, 0, pl.ds(src, size)]
        else:
            src, dst, size, to = {
                1: (0, step * shard, shard, near),
                2: (0, (3 - step) * shard, shard, far),
                3: (step * shard, 3 * shard, shard, far),
                4: (0, half, 3 * shard, by_core),
                5: (3 * shard, half + 3 * shard, shard, by_core),
            }[stage]
            source = weights.at[mat, k, pl.ds(src, size)]
        return pltpu.make_async_remote_copy(
            src_ref=source,
            dst_ref=weights.at[mat, k, pl.ds(dst, size)],
            send_sem=ag_send.at[stage, k, mat],
            recv_sem=ag_recv.at[stage, k, mat],
            device_id=(to,),
            device_id_type=MESH,
        )

    middle = ((z + 1) // 2) % 2

    def plane_at(i):
        return (1 - middle) * ((i + 1) % planes) + middle * (planes - 1 - i)

    def rs(stage, i, mat):
        slot, k = i % 2, plane_at(i)
        near, far = (by_x, by_y) if mat == 0 else (by_y, by_x)
        src, dst, to = [
            lambda: (send_one.at[mat], recv_one.at[slot, mat], by_core),
            lambda: (send_two.at[mat], recv_two.at[slot, mat], near),
            lambda: (send_three.at[mat], recv_three.at[slot, mat], far),
            lambda: (send_four.at[slot, mat], recv_four.at[k - 1, mat], by_z(k)),
            lambda: (weights.at[mat, k, pl.ds(0, half)], recv_far.at[(k - 1) // 2, mat], by_z(k)),
        ][stage]()
        at = i if stage < 3 else k
        return pltpu.make_async_remote_copy(
            src_ref=src,
            dst_ref=dst,
            send_sem=rs_send.at[stage, at, mat],
            recv_sem=rs_recv.at[stage, at, mat],
            device_id=(to,),
            device_id_type=MESH,
        )

    def came_from(stage, k, mat):
        place = recv_four.at[k - 1, mat] if stage == 3 else recv_far.at[(k - 1) // 2, mat]
        pltpu.make_async_remote_copy(
            src_ref=place,
            dst_ref=place,
            send_sem=rs_send.at[stage, k, mat],
            recv_sem=rs_recv.at[stage, k, mat],
            device_id=(by_z(k),),
            device_id_type=MESH,
        ).wait_recv()
        return place[...].astype(WIDE)

    def small_gather(stage, k, group):
        src, dst, to = [
            lambda: (small_all.at[group, 0, 0], small_all.at[group, 0, k], by_z(k)),
            lambda: (small_all.at[group, 0], small_all.at[group, k], (me, by_x, by_y, by_both)[k]),
            lambda: (small_all.at[group, pl.ds(0, 4)], small_all.at[group, pl.ds(4, 4)], by_core),
        ][stage]()
        return pltpu.make_async_remote_copy(
            src_ref=src,
            dst_ref=dst,
            send_sem=sg_send.at[stage, k, group],
            recv_sem=sg_recv.at[stage, k, group],
            device_id=(to,),
            device_id_type=MESH,
        )

    def small_reduce(stage, k, group):
        src, dst, to = [
            lambda: (small_all.at[group, pl.ds(4, 4)], small_core.at[group], by_core),
            lambda: (small_all.at[group, k], small_plane.at[group, k], (me, by_x, by_y, by_both)[k]),
            lambda: (small_all.at[group, 0, k], small_z.at[k, group], by_z(k)),
        ][stage]()
        return pltpu.make_async_remote_copy(
            src_ref=src,
            dst_ref=dst,
            send_sem=ss_send.at[stage, k, group],
            recv_sem=ss_recv.at[stage, k, group],
            device_id=(to,),
            device_id_type=MESH,
        )

    def bias_reduce(stage, k):
        to = [lambda: by_core, lambda: (me, by_x, by_y, by_both)[k], lambda: by_z(k)][stage]()
        return pltpu.make_async_remote_copy(
            src_ref=biases.at[stage],
            dst_ref=biases_in.at[stage, k],
            send_sem=bs_send.at[stage, k],
            recv_sem=bs_recv.at[stage, k],
            device_id=(to,),
            device_id_type=MESH,
        )

    def late_reduce(stage, k):
        to = [lambda: by_core, lambda: (me, by_x, by_y, by_both)[k], lambda: by_z(k)][stage]()
        return pltpu.make_async_remote_copy(
            src_ref=late.at[stage],
            dst_ref=late_in.at[stage, k],
            send_sem=ls_send.at[stage, k],
            recv_sem=ls_recv.at[stage, k],
            device_id=(to,),
            device_id_type=MESH,
        )

    hidden_tok = c_one.shape[0]
    unit = math.gcd(tin_own.shape[0], hidden_tok)
    lines_in = tin_own.shape[0] // unit
    first_lines = (lines_in + 1) // 2
    lines_out = tout_own.shape[0] // patches
    own_vec = gain_one_own.shape[0]
    turns = hidden_tok // unit
    devices = planes * PLANE

    def place_of(d):
        dz, dy, dx, dc = d // PLANE, (d // 4) % 2, (d // 2) % 2, d % 2
        far = (dc + core) % 2 * 4 + (dy + row) % 2 * 2 + (dx + col) % 2
        k, bit = 0, 1
        while bit < planes:
            k = k + bit * ((dz // bit + z // bit) % 2)
            bit *= 2
        return far, k

    def load(b):
        return pltpu.make_async_copy(images.at[b], grad_zed.at[b], in_sem.at[0, b])

    def load_top(b):
        return pltpu.make_async_copy(cotangent.at[b], total.at[b], in_sem.at[1, b])

    def reload_image(b):
        return pltpu.make_async_copy(images.at[b], mid.at[b], in_sem.at[3, b])

    def reload(b):
        return pltpu.make_async_copy(cotangent.at[b], cot.at[b % 2], in_sem.at[2, b])

    for b in range(count):
        load_top(b).start()
    for b in range(count):
        load(b).start()
    small_own[...] = jnp.zeros_like(small_own)
    for i in range(lines_in):
        at, lane = (i, 0) if i < first_lines else (i - first_lines, 64)
        small_own[at : at + 1, lane : lane + unit] = tin_own[i * unit : (i + 1) * unit].reshape(1, unit)
    for i, piece in enumerate((gain_one_own, shift_one_own, gain_two_own, shift_two_own, c_four_own)):
        small_own[24 + i : 25 + i, 64 : 64 + own_vec] = piece[...].reshape(1, own_vec)
    small_own[31:32, 0:shard] = c_in_own[...].reshape(1, shard)
    for i in range(lines_out):
        line = tout_own[i * patches : (i + 1) * patches].reshape(1, patches)
        small_own[32 + i : 33 + i, :] = line[:, 0:128]
        small_own[48 + i : 49 + i, 0 : patches - 128] = line[:, 128:patches]
    for group in range(2):
        small_all[group, 0, 0] = small_own[32 * group : 32 * (group + 1)].astype(LOW)
    weights[0, 0, 0:shard] = w_in[...].astype(LOW)
    weights[1, 0, 0:shard] = w_out[...].astype(LOW)

    barrier = pltpu.get_barrier_semaphore()
    peers = [by_core, by_x, by_y, by_both] + [by_z(k) for k in range(1, planes)]
    for peer in peers:
        pl.semaphore_signal(barrier, inc=1, device_id=(peer,), device_id_type=MESH)
    pl.semaphore_wait(barrier, len(peers))

    mats = (0, 1)
    inner = middle == 1

    def ag_pass(which, mat):
        src, dst, to = ((1, 2, by_z(3)), (3, 2, by_z(1)), (2, 3, by_z(1)))[which]
        return pltpu.make_async_remote_copy(
            src_ref=weights.at[mat, src, pl.ds(0, shard)],
            dst_ref=weights.at[mat, dst, pl.ds(0, shard)],
            send_sem=ag_send.at[6, which, mat],
            recv_sem=ag_recv.at[0, dst, mat],
            device_id=(to,),
            device_id_type=MESH,
        )

    def ag_planes():
        for mat in mats:
            ag(0, 1, mat).start()

        @pl.when(inner)
        def _():
            for mat in mats:
                ag(0, 3, mat).start()

    def ag_planes_pass():
        @pl.when(inner)
        def _():
            for which, came in ((0, 1), (1, 3)):
                for mat in mats:
                    ag(0, came, mat).wait_recv()
                    ag_pass(which, mat).start()

    def ag_planes_last():
        @pl.when(inner)
        def _():
            for mat in mats:
                ag(0, 2, mat).wait_recv()
                ag_pass(2, mat).start()

    def ag_direct(k):
        @pl.when(jnp.logical_not(inner))
        def _():
            for mat in mats:
                ag(0, k, mat).wait_recv()

        for stage in (1, 2):
            for mat in mats:
                ag(stage, k, mat).start()

    def ag_forward(k):
        for mat in mats:
            ag(1, k, mat).wait_recv()
            ag(3, k, mat).start()

    def ag_core(k):
        for mat in mats:
            ag(2, k, mat).wait_recv()
            ag(4, k, mat).start()

    def ag_core_last(k):
        for mat in mats:
            ag(3, k, mat).wait_recv()
            ag(5, k, mat).start()

    def ag_ready(k):
        for mat in mats:
            ag(4, k, mat).wait_recv()
            ag(5, k, mat).wait_recv()

    for group in range(2):
        for k in range(1, planes):
            small_gather(0, k, group).start()
    for mat in mats:
        ag(1, 0, mat).start()
    ag_planes()

    grad_vecs[...] = jnp.zeros_like(grad_vecs)
    grad_tin[...] = jnp.zeros_like(grad_tin)
    grad_tout[...] = jnp.zeros_like(grad_tout)

    def channel_top(r, carry):
        tops = []
        for h in range(2):
            b = 2 * r + h
            load_top(b).wait()
            tops.append(padded(total[b] * mask[b].astype(WIDE), lot))
        rounded = jnp.concatenate(tops, axis=0).astype(LOW)
        top[pl.ds(r * pair, pair), :] = rounded
        grad_vecs[2:3, :] += jnp.sum(rounded.astype(WIDE), axis=0, keepdims=True)
        return carry

    def first_norm(b, carry):
        load(b).wait()
        mid[b], figures[b, :, 0:1], figures[b, :, 1:2] = norm_parts(grad_zed[b])
        return carry

    lax.fori_loop(0, blocks, channel_top, 0)
    for group in range(2):
        for k in range(1, planes):
            small_gather(0, k, group).wait_recv()
        for k in range(1, 4):
            small_gather(1, k, group).start()
    lax.fori_loop(0, count, first_norm, 0)
    for k in range(1, 4):
        small_gather(1, k, 0).wait_recv()
    small_gather(2, 0, 0).start()

    tin[...] = jnp.zeros_like(tin)
    tout[...] = jnp.zeros_like(tout)

    def unpack(d, group):
        far, k = place_of(d)
        message = small_all[group, far, k].astype(WIDE)
        if group == 0:
            lines[d * lines_in : d * lines_in + first_lines, :] = message[0:first_lines, :]
            shifted = jnp.concatenate([message[0:24, 64:128], message[0:24, 0:64]], axis=1)
            lines[d * lines_in + first_lines : (d + 1) * lines_in, :] = shifted[0 : lines_in - first_lines, :]
            vecs[:, d * own_vec : (d + 1) * own_vec] = message[24:32, 64 : 64 + own_vec]
            c_in[d] = message[31:32, 0:shard]
        else:
            tout[d * lines_out : (d + 1) * lines_out, 0:128] = message[0:lines_out, :]
            tout[d * lines_out : (d + 1) * lines_out, 128:patches] = message[16 : 16 + lines_out, 0 : patches - 128]

    def unpack_half(own, group):
        for parity in range(2):

            @pl.when((core == parity) == own)
            def _():
                for d in range(parity, devices, 2):
                    unpack(d, group)

    unpack_half(True, 0)
    for k in range(1, 4):
        small_gather(1, k, 1).wait_recv()
    small_gather(2, 0, 1).start()
    unpack_half(True, 1)
    ag_planes_pass()
    ag_direct(plane_at(0))
    for group in range(2):
        small_gather(2, 0, group).wait_recv()
        unpack_half(False, group)
    for turn in range(turns):
        tin[0:patches, turn * unit : (turn + 1) * unit] = lines[pl.ds(turn, patches, stride=turns), :][:, 0:unit]
    for rest, into, at in ((c_one, tin, patches), (c_two, tout, hidden_tok)):
        rest = rest[...].reshape(1, rest.shape[0])
        for i in range(3):
            term = rest.astype(LOW).astype(WIDE)
            into[at + i : at + i + 1, 0 : rest.shape[1]] = term
            rest = rest - term
    tin_t[...] = tin[...].T.astype(LOW)
    tout_t[...] = tout[...].T.astype(LOW)
    ones = jnp.ones((3, width), WIDE)

    gain_one, shift_one = vecs[0:1, :], vecs[1:2, :]
    gain_two, shift_two, c_four = vecs[2:3, :], vecs[3:4, :], vecs[4:5, :]
    def singles(work, start, stop):
        def one(b, carry):
            work(b)
            return carry

        lax.fori_loop(start, stop, one, 0)

    def pairs(work, start, stop):
        def two(r, carry):
            for h in range(2):
                work(2 * r + h)
            return carry

        lax.fori_loop(start // 2, stop // 2, two, 0)

    def token_forward(b):
        fed = mid[b] * gain_one + shift_one
        mixed[b] = padded(jnp.concatenate([fed, ones], axis=0), pad).astype(LOW)
        value, slope = gelu_parts(dot(tin_t[...], mixed[b], NN))
        act_t[b] = padded(jnp.concatenate([value, ones], axis=0), act_t.shape[1]).astype(LOW)
        slope_t[b] = slope.astype(LOW)
        mid[b] = grad_zed[b] + dot(tout_t[...], act_t[b], NN)[0:patches]

    def channel_inputs(r, carry):
        parts = []
        for h in range(2):
            total[2 * r + h] = mid[2 * r + h] + c_four
            normed, _, figures[2 * r + h, :, 2:3] = norm_parts(mid[2 * r + h])
            mid[2 * r + h] = normed
            grad_zed[2 * r + h] = jnp.zeros((patches, width), WIDE)
            parts.append(padded(normed * gain_two + shift_two, lot))
        zed[pl.ds(r * pair, pair), :] = jnp.concatenate(parts, axis=0).astype(LOW)
        return carry

    first = 4
    singles(token_forward, 0, first)
    ag_forward(plane_at(0))
    singles(token_forward, first, count)
    ag_core(plane_at(0))
    ag_planes_last()
    lax.fori_loop(0, blocks, channel_inputs, 0)
    ag_direct(plane_at(1))
    for k in range(planes):
        for place in range(PLANE):
            near = plane_of(k) * PLANE + (
                (row + (place // 2) % 2) % 2 * 4 + (col + place % 2) % 2 * 2 + (core + place // 4) % 2
            )
            c_in_rel[k, :, place * shard : (place + 1) * shard] = c_in[near]

    ag_core_last(plane_at(0))

    def rs_two(i, mat):
        rs(0, i, mat).wait_recv()
        slot = i % 2
        first, second = (1, 3) if mat == 0 else (2, 3)

        def part(n):
            return slice(n * shard, (n + 1) * shard)

        @pl.when(i == 0)
        def _():
            weights[mat, plane_at(i), 0:half] = (own_sum[mat] + recv_one[slot, mat].astype(WIDE)).astype(LOW)
            rs(4, 0, mat).start()

        @pl.when((i == planes - 1) & inner)
        def _():
            own_sum[mat] += came_from(4, 1, mat) + came_from(4, 3, mat)

        @pl.when(i > 1)
        def _():
            rs(1, i - 1, mat).wait_send()

        @pl.when(i > 0)
        def _():
            for n, to in ((first, part(0)), (second, part(1))):
                send_two[mat, to] = (own_sum[mat, part(n)] + recv_one[slot, mat, part(n)].astype(WIDE)).astype(LOW)
            rs(1, i, mat).start()
            for n in (0, 3 - first):
                own_sum[mat, part(n)] += recv_one[slot, mat, part(n)].astype(WIDE)

    def rs_three(i):
        for mat in mats:
            rs(1, i, mat).wait_recv()
            other = 2 if mat == 0 else 1

            @pl.when(i > 1)
            def _():
                rs(2, i - 1, mat).wait_send()

            keep_sum[mat] = own_sum[mat, 0:shard] + recv_two[i % 2, mat, 0:shard].astype(WIDE)
            send_three[mat] = (
                own_sum[mat, other * shard : (other + 1) * shard]
                + recv_two[i % 2, mat, shard : 2 * shard].astype(WIDE)
            ).astype(LOW)
            rs(2, i, mat).start()

    def rs_four(i):
        for mat in mats:
            rs(2, i, mat).wait_recv()

            send_four[i % 2, mat] = (keep_sum[mat] + recv_three[i % 2, mat].astype(WIDE)).astype(LOW)
            rs(3, i, mat).start()

    def rs_last():
        last = planes - 1
        for mat in mats:
            result = grad_in if mat == 0 else grad_out
            rs(2, last, mat).wait_recv()
            summed = keep_sum[mat] + recv_three[last % 2, mat].astype(WIDE)
            result[...] = summed + came_from(3, 2, mat)

            @pl.when(jnp.logical_not(inner))
            def _():
                result[...] += came_from(3, 1, mat) + came_from(3, 3, mat)


    tile = chunk // 3

    def channel_chunk(i, carry):
        k = plane_at(i)
        ag_ready(k)

        def rows(r):
            for s in range(3):
                part = slice(s * tile, (s + 1) * tile)
                pre = dot(zed[r * pair : (r + 1) * pair, :], weights[0, k, part], NT) + c_in_rel[k, :, part]
                value, slope = gelu_parts(pre)
                act[r * pair : (r + 1) * pair, part] = value.astype(LOW)
                back = (dot(top[r * pair : (r + 1) * pair, :], weights[1, k, part], NT) * slope).astype(LOW)
                grad_pre[r * pair : (r + 1) * pair, part] = back
            up = dot(act[r * pair : (r + 1) * pair, :], weights[1, k], NN)
            down = dot(grad_pre[r * pair : (r + 1) * pair, :], weights[0, k], NN)
            for h in range(2):
                total[2 * r + h] += up[h * lot : h * lot + patches]
                grad_zed[2 * r + h] += down[h * lot : h * lot + patches]

        rows(0)

        @pl.when(i == 0)
        def _():
            ag_forward(plane_at(1))

        @pl.when(i == 1)
        def _():
            ag_forward(plane_at(2))
            ag_forward(0)

        @pl.when(i == 3)
        def _():
            rs_four(1)

        for r in range(1, blocks):
            rows(r)

        @pl.when(i == 0)
        def _():
            ag_core(plane_at(1))
            ag_direct(plane_at(2))
            for mat in mats:
                ag(2, 0, mat).start()

        @pl.when(i == 1)
        def _():
            ag_core(plane_at(2))

        @pl.when(i == 2)
        def _():
            ag_core(0)
            ag_core_last(0)

        back_sum = jnp.sum(grad_pre[...].astype(WIDE), axis=0, keepdims=True)
        for place in range(PLANE):
            near = plane_of(k) * PLANE + (
                (row + (place // 2) % 2) % 2 * 4 + (col + place % 2) % 2 * 2 + (core + place // 4) % 2
            )
            grad_c_in[near] = back_sum[:, place * shard : (place + 1) * shard]

        @pl.when(i > 0)
        def _():
            for mat in mats:
                rs(0, i - 1, mat).wait_send()

        send_one[1] = dot(act[:, half:chunk], top[...], TN).astype(LOW)
        send_one[0] = dot(grad_pre[:, half:chunk], zed[...], TN).astype(LOW)
        for mat in mats:
            rs(0, i, mat).start()

        @pl.when(i > 1)
        def _():
            rs_three(i - 1)

        @pl.when(i == 0)
        def _():
            for mat in mats:
                for stage in range(1, 6):
                    ag(stage, k, mat).wait_send()

                @pl.when(inner)
                def _():
                    ag_pass(1, mat).wait_send()

        own_sum[1] = dot(act[:, 0:half], top[...], TN)
        own_sum[0] = dot(grad_pre[:, 0:half], zed[...], TN)
        @pl.when(i < 2)
        def _():
            ag_core_last(plane_at(i + 1))

        for mat in mats:
            rs_two(i, mat)
        return carry

    for b in range(2):
        reload(b).start()
    lax.fori_loop(0, planes, channel_chunk, 0)

    tin_low = tin[...].astype(LOW)
    tout_low = tout[0:hidden_tok, :].astype(LOW)

    def kept(b):
        return weights.at[b // planes, b % planes, 0:pad]

    def middle_backward(b, carry):
        keep = mask[b].astype(WIDE)
        reload(b).wait()
        normed = mid[b]
        down = grad_zed[b]
        grad_vecs[0:1, :] += jnp.sum(down * normed, axis=0, keepdims=True)
        grad_vecs[1:2, :] += jnp.sum(down, axis=0, keepdims=True)
        grad_mid = cot[b % 2] * keep + norm_back(down, normed, figures[b, :, 2:3], gain_two)
        grad_zed[b] = grad_mid
        back = padded(grad_mid, pad).astype(LOW)
        grad_tout[...] += dot(act_t[b], back, NT)
        slope_t[b] = (dot(tout_low, back, NN) * slope_t[b].astype(WIDE)).astype(LOW)
        grad_tin[:, 0:hidden_tok] += dot(mixed[b], slope_t[b], NT)
        reload_image(b).start()

        @pl.when(b + 2 < count)
        def _():
            reload(b + 2).start()

        return carry

    def token_backward(b):
        slope_t[b] = (dot(tout_low, kept(b)[...], NN) * slope_t[b].astype(WIDE)).astype(LOW)
        grad_tin[:, 0:hidden_tok] += dot(mixed[b], slope_t[b], NT)

    def image_norm(b):
        normed = (mid[b] - figures[b, :, 0:1]) * figures[b, :, 1:2]
        mid[b] = normed
        grad_mixed = dot(tin_low, slope_t[b], NN)
        kept(b)[...] = grad_mixed.astype(LOW)
        late[0, 0:1, :] += jnp.sum(grad_mixed[0:patches] * normed, axis=0, keepdims=True)
        late[0, 1:2, :] += jnp.sum(grad_mixed[0:patches], axis=0, keepdims=True)

    def image_backward(b):
        total[b] *= mask[b].astype(WIDE)
        grad_zed[b] += norm_back(kept(b)[...][0:patches].astype(WIDE), mid[b], figures[b, :, 1:2], gain_one)

    def small_first(group):
        for k in range(1, planes):
            small_gather(0, k, group).wait_send()
        for far in range(1, 4):
            small_gather(1, far, group).wait_send()
        small_gather(2, 0, group).wait_send()
        if group == 0:
            for turn in range(turns):
                lines[pl.ds(turn, patches, stride=turns), :] = grad_tin[0:patches, turn * unit : turn * unit + 128]
        for d in range(devices):
            far, k = place_of(d)
            message = small_sum.at[group, far, k]
            if group == 0:
                low = lines[d * lines_in : d * lines_in + first_lines, :]
                high = lines[d * lines_in + first_lines : (d + 1) * lines_in, :]
                message[0:first_lines, 0:64] = low[:, 0:64]
                message[0 : lines_in - first_lines, 64:128] = high[:, 0:64]
                message[24:27, 64 : 64 + own_vec] = grad_vecs[0:3, d * own_vec : (d + 1) * own_vec]
                message[31:32, 0:shard] = grad_c_in[d]
            else:
                message[0:lines_out, :] = grad_tout[d * lines_out : (d + 1) * lines_out, 0:128]
                message[16 : 16 + lines_out, 0 : patches - 128] = grad_tout[
                    d * lines_out : (d + 1) * lines_out, 128:patches
                ]
        for far in range(4, PLANE):
            small_all[group, far] = small_sum[group, far].astype(LOW)
        small_reduce(0, 0, group).start()
        if group == 0:
            biases[0] = jnp.zeros_like(biases[0])
            for i in range(hidden_tok // 128):
                biases[0, i : i + 1, :] = grad_tin[patches : patches + 1, i * 128 : (i + 1) * 128]
            biases[0, 3:4, :] = grad_tout[hidden_tok : hidden_tok + 1, 0:128]
            biases[0, 4:5, 0 : patches - 128] = grad_tout[hidden_tok : hidden_tok + 1, 128:patches]
            bias_reduce(0, 0).start()

    def small_second(group):
        small_reduce(0, 0, group).wait_recv()
        for far in range(4):
            small_sum[group, far] += small_core[group, far].astype(WIDE)
        for far in range(1, 4):
            small_all[group, far] = small_sum[group, far].astype(LOW)
            small_reduce(1, far, group).start()
        if group == 0:
            bias_reduce(0, 0).wait_recv()
            biases[1] = biases[0] + biases_in[0, 0]
            for far in range(1, 4):
                bias_reduce(1, far).start()

    def small_third(group):
        for far in range(1, 4):
            small_reduce(1, far, group).wait_recv()
            small_sum[group, 0] += small_plane[group, far].astype(WIDE)
        for k in range(1, planes):
            small_all[group, 0, k] = small_sum[group, 0, k].astype(LOW)
            small_reduce(2, k, group).start()
        if group == 0:
            for far in range(1, 4):
                bias_reduce(1, far).wait_recv()
            biases[2] = (biases[1] + biases_in[1, 1]) + (biases_in[1, 2] + biases_in[1, 3])
            for k in range(1, planes):
                bias_reduce(2, k).start()

    for mat in mats:
        for i in range(1, planes):
            for stage in range(1, 6):
                ag(stage, plane_at(i), mat).wait_send()
        ag(0, 1, mat).wait_send()
        rs(4, 0, mat).wait_send()

        @pl.when(inner)
        def _():
            ag(0, 3, mat).wait_send()
            for which in (0, 2):
                ag_pass(which, mat).wait_send()

    late[0] = jnp.zeros_like(late[0])
    lax.fori_loop(0, 2, middle_backward, 0)
    rs_four(planes - 2)
    lax.fori_loop(2, count, middle_backward, 0)
    small_first(1)
    small_first(0)
    for b in range(count):
        reload_image(b).wait()
    pairs(image_norm, 0, 2)
    small_second(1)
    pairs(image_norm, 2, count)
    small_second(0)
    late_reduce(0, 0).start()
    pairs(image_backward, 0, 2)
    late_reduce(0, 0).wait_recv()
    late[1] = late[0] + late_in[0, 0]
    for far in range(1, 4):
        late_reduce(1, far).start()
    rs_three(planes - 1)
    small_third(1)
    pairs(image_backward, 2, count)
    small_third(0)
    late_sum = late[1]
    for far in range(1, 4):
        late_reduce(1, far).wait_recv()
        late_sum = late_sum + late_in[1, far]
    late[2] = late_sum
    for k in range(1, planes):
        late_reduce(2, k).start()
    rs_last()
    summed = [small_sum[group, 0, 0] for group in range(2)]
    tree = [biases[2]]
    for k in range(1, planes):
        for group in range(2):
            small_reduce(2, k, group).wait_recv()
        bias_reduce(2, k).wait_recv()
        summed = [summed[group] + small_z[k, group].astype(WIDE) for group in range(2)]
        tree.append(biases_in[2, k])
    for group in range(2):
        small_out[32 * group : 32 * (group + 1)] = summed[group]
    for k in range(1, planes):
        late_reduce(2, k).wait_recv()
        late_sum = late_sum + late_in[2, k]
    late_sum = pltpu.roll(padded(late_sum, 8), width - own_vec * me, 1)
    small_out[27:29, 64 : 64 + own_vec] = late_sum[0:2, 0:own_vec]
    while len(tree) > 1:
        tree = [tree[i] + tree[i + 1] for i in range(0, len(tree), 2)]
    biases_out[...] = tree[0]

    for mat in mats:
        for stage in range(3):
            rs(stage, planes - 1, mat).wait_send()
        for i in range(1, planes - 1):
            rs(3, i, mat).wait_send()
    late_reduce(0, 0).wait_send()
    for far in range(1, 4):
        late_reduce(1, far).wait_send()
    for k in range(1, planes):
        late_reduce(2, k).wait_send()
    bias_reduce(0, 0).wait_send()
    for far in range(1, 4):
        bias_reduce(1, far).wait_send()
    for k in range(1, planes):
        bias_reduce(2, k).wait_send()
    for group in range(2):
        small_reduce(0, 0, group).wait_send()
        for far in range(1, 4):
            small_reduce(1, far, group).wait_send()
        for k in range(1, planes):
            small_reduce(2, k, group).wait_send()


def finish_kernel(
    block_in,
    image_in,
    w_in,
    w_out,
    small,
    biases,
    block_out,
    image_out,
    w_in_out,
    w_out_out,
    tin,
    tout,
    gain_one,
    shift_one,
    gain_two,
    shift_two,
    c_four,
    c_in,
    c_one,
    c_two,
    sem,
):
    copies = [
        pltpu.make_async_copy(block_in, block_out, sem.at[0]),
        pltpu.make_async_copy(image_in, image_out, sem.at[1]),
        pltpu.make_async_copy(w_in, w_in_out, sem.at[2]),
        pltpu.make_async_copy(w_out, w_out_out, sem.at[3]),
    ]
    for copy in copies:
        copy.start()
    hidden_tok, patches = c_one.shape[0], c_two.shape[0]
    unit = math.gcd(tin.shape[0], hidden_tok)
    lines_in = tin.shape[0] // unit
    first_lines = (lines_in + 1) // 2
    for i in range(lines_in):
        at, lane = (i, 0) if i < first_lines else (i - first_lines, 64)
        tin[i * unit : (i + 1) * unit] = small[at : at + 1, lane : lane + unit].reshape(unit)
    for i in range(tout.shape[0] // patches):
        tout[i * patches : i * patches + 128] = small[32 + i : 33 + i, :].reshape(128)
        tout[i * patches + 128 : (i + 1) * patches] = small[48 + i : 49 + i, 0 : patches - 128].reshape(
            patches - 128
        )
    for i, piece in enumerate((gain_two, shift_two, c_four, gain_one, shift_one)):
        own_vec = piece.shape[0]
        piece[...] = small[24 + i : 25 + i, 64 : 64 + own_vec].reshape(own_vec)
    shard = c_in.shape[0]
    c_in[...] = small[31:32, 0:shard].reshape(shard)
    for i in range(hidden_tok // 128):
        c_one[i * 128 : (i + 1) * 128] = biases[i : i + 1, :].reshape(128)
    c_two[0:128] = biases[3:4, :].reshape(128)
    c_two[128:patches] = biases[4:5, 0 : patches - 128].reshape(patches - 128)
    for copy in copies:
        copy.wait()


def fast_shards(
    images,
    mask,
    cotangent,
    w_token_in,
    w_token_out,
    bias_token_in,
    bias_token_out,
    gain_one,
    shift_one,
    gain_two,
    shift_two,
    w_expand,
    bias_expand,
    w_reduce,
    bias_reduce,
):
    devices = lax.axis_size("dp")
    planes = devices // PLANE
    count, patches, width = images.shape
    hidden_tok = bias_token_in.shape[0]
    shard = w_expand.shape[0]
    pad = -(-patches // 16) * 16
    lot = -(-patches // 8) * 8
    pair = 2 * lot
    blocks = count // 2
    chunk = 8 * shard
    half = 4 * shard

    unit = math.gcd(w_token_in.shape[0], hidden_tok)
    lines_in = w_token_in.shape[0] // unit
    hidden_pad = hidden_tok + 16

    owned = (
        w_expand,
        w_reduce,
        w_token_in,
        w_token_out,
        gain_one,
        shift_one,
        gain_two,
        shift_two,
        bias_reduce,
        bias_expand,
        bias_token_in,
        bias_token_out,
    )
    vmem = pl.BlockSpec(memory_space=pltpu.VMEM)
    hbm = pl.BlockSpec(memory_space=pl.ANY)
    shape = jax.ShapeDtypeStruct
    outs = pl.pallas_call(
        block_kernel,
        out_shape=(
            pltpu.VMEM(images.shape, WIDE),
            pltpu.VMEM(images.shape, WIDE),
            pltpu.VMEM(w_expand.shape, WIDE),
            pltpu.VMEM(w_reduce.shape, WIDE),
            pltpu.VMEM((64, 128), WIDE),
            pltpu.VMEM((8, 128), WIDE),
        ),
        in_specs=[pl.BlockSpec(memory_space=pltpu.SMEM), hbm, hbm] + [vmem] * 12,
        out_specs=[vmem] * 6,
        scratch_shapes=[
            pltpu.VMEM((2,) + images.shape[1:], WIDE),
            pltpu.VMEM((count, pad, width), LOW),
            pltpu.VMEM((count, hidden_pad, width), LOW),
            pltpu.VMEM((count, hidden_tok, width), LOW),
            pltpu.VMEM(images.shape, WIDE),
            pltpu.VMEM((blocks * pair, width), LOW),
            pltpu.VMEM((blocks * pair, width), LOW),
            pltpu.VMEM((2, planes, chunk, width), LOW),
            pltpu.VMEM((blocks * pair, chunk), LOW),
            pltpu.VMEM((blocks * pair, chunk), LOW),
            pltpu.VMEM((planes, 1, chunk), WIDE),
            pltpu.VMEM((2, half, width), WIDE),
            pltpu.VMEM((2, shard, width), WIDE),
            pltpu.VMEM((2, half, width), LOW),
            pltpu.VMEM((2, 2, half, width), LOW),
            pltpu.VMEM((2, 2 * shard, width), LOW),
            pltpu.VMEM((2, 2, 2 * shard, width), LOW),
            pltpu.VMEM((2, shard, width), LOW),
            pltpu.VMEM((2, 2, shard, width), LOW),
            pltpu.VMEM((2, 2, shard, width), LOW),
            pltpu.VMEM((planes - 1, 2, shard, width), LOW),
            pltpu.VMEM((2, 2, half, width), LOW),
            pltpu.VMEM((pad, hidden_tok), WIDE),
            pltpu.VMEM((hidden_tok, pad), LOW),
            pltpu.VMEM((hidden_pad, pad), WIDE),
            pltpu.VMEM((pad, hidden_pad), LOW),
            pltpu.VMEM((8, width), WIDE),
            pltpu.VMEM((devices, 1, shard), WIDE),
            pltpu.VMEM((devices * lines_in, 128), WIDE),
            pltpu.VMEM((64, 128), WIDE),
            pltpu.VMEM((2, PLANE, planes, 32, 128), LOW),
            pltpu.VMEM((pad, hidden_tok + 128), WIDE),
            pltpu.VMEM((hidden_pad, pad), WIDE),
            pltpu.VMEM((8, width), WIDE),
            pltpu.VMEM((devices, 1, shard), WIDE),
            pltpu.VMEM((2, PLANE, planes, 32, 128), WIDE),
            pltpu.VMEM((2, 4, planes, 32, 128), LOW),
            pltpu.VMEM((2, 4, planes, 32, 128), LOW),
            pltpu.VMEM((planes, 2, 32, 128), LOW),
            pltpu.VMEM((3, 8, 128), WIDE),
            pltpu.VMEM((3, max(4, planes), 8, 128), WIDE),
            pltpu.VMEM((3, 2, width), WIDE),
            pltpu.VMEM((3, max(4, planes), 2, width), WIDE),
            pltpu.VMEM((count, patches, 4), WIDE),
            pltpu.SemaphoreType.DMA((4, count)),
            pltpu.SemaphoreType.DMA((7, planes, 2)),
            pltpu.SemaphoreType.DMA((7, planes, 2)),
            pltpu.SemaphoreType.DMA((5, planes, 2)),
            pltpu.SemaphoreType.DMA((5, planes, 2)),
        ]
        + [pltpu.SemaphoreType.DMA((3, max(4, planes), 2))] * 4
        + [pltpu.SemaphoreType.DMA((3, max(4, planes)))] * 4,
        compiler_params=pltpu.CompilerParams(
            collective_id=0, has_side_effects=True, vmem_limit_bytes=56 * 2**20
        ),
    )(
        mask,
        images,
        cotangent,
        *owned,
    )
    flat = pl.pallas_call(
        finish_kernel,
        out_shape=(
            shape(images.shape, WIDE),
            shape(images.shape, WIDE),
            shape(w_expand.shape, WIDE),
            shape(w_reduce.shape, WIDE),
            shape(w_token_in.shape, WIDE),
            shape(w_token_out.shape, WIDE),
            *[shape(gain_one.shape, WIDE)] * 5,
            shape(bias_expand.shape, WIDE),
            shape(bias_token_in.shape, WIDE),
            shape(bias_token_out.shape, WIDE),
        ),
        in_specs=[vmem] * 6,
        out_specs=[hbm] * 4 + [vmem] * 10,
        scratch_shapes=[pltpu.SemaphoreType.DMA((4,))],
        compiler_params=pltpu.CompilerParams(vmem_limit_bytes=16 * 2**20),
    )(*outs)
    block_output, image_grad, own_win, own_wout, *rest = flat
    g_tin, g_tout, g_one, b_one, g_two, b_two, c_four, c_in, c_one, c_two = rest
    return (
        block_output,
        image_grad,
        g_tin,
        g_tout,
        c_one,
        c_two,
        g_one,
        b_one,
        g_two,
        b_two,
        own_win,
        c_in,
        own_wout,
        c_four,
    )


def fits(devices, images, w_token_in, w_token_out, bias_token_in, gain_one, w_expand):
    planes = devices // PLANE
    patches = images.shape[1]
    hidden_tok = bias_token_in.shape[0]
    shard = w_expand.shape[0]
    unit = math.gcd(w_token_in.shape[0], hidden_tok)
    return (
        devices % PLANE == 0
        and planes == 4
        and images.shape[0] % 2 == 0
        and 6 <= images.shape[0] <= 2 * planes
        and shard % 16 == 0
        and shard <= 128
        and (4 * shard) % 128 == 0
        and 128 < patches <= 205
        and unit <= 64
        and w_token_in.shape[0] // unit <= 49
        and w_token_out.shape[0] % patches == 0
        and w_token_out.shape[0] // patches <= 16
        and gain_one.shape[0] <= 64
        and hidden_tok == 384
    )


def choose(
    images,
    mask,
    cotangent,
    w_token_in,
    w_token_out,
    bias_token_in,
    bias_token_out,
    gain_one,
    shift_one,
    gain_two,
    shift_two,
    w_expand,
    bias_expand,
    w_reduce,
    bias_reduce,
):
    args = (
        images,
        mask,
        cotangent,
        w_token_in,
        w_token_out,
        bias_token_in,
        bias_token_out,
        gain_one,
        shift_one,
        gain_two,
        shift_two,
        w_expand,
        bias_expand,
        w_reduce,
        bias_reduce,
    )
    if fits(lax.axis_size("dp"), images, w_token_in, w_token_out, bias_token_in, gain_one, w_expand):
        return fast_shards(*args)
    return shards(*args)


def shards(
    images,
    mask,
    cotangent,
    w_token_in,
    w_token_out,
    bias_token_in,
    bias_token_out,
    gain_one,
    shift_one,
    gain_two,
    shift_two,
    w_expand,
    bias_expand,
    w_reduce,
    bias_reduce,
):
    low_type = jnp.bfloat16
    wide = jnp.float32
    count, patches, width = images.shape
    hidden_tok = bias_token_in.shape[0]
    rows = count * patches
    keep = mask.astype(wide)[:, None, None]
    small_local = (
        w_token_in.astype(low_type),
        w_token_out.astype(low_type),
        gain_one.astype(low_type),
        shift_one.astype(low_type),
        gain_two.astype(low_type),
        shift_two.astype(low_type),
        bias_reduce.astype(low_type),
    )
    channel_local = (
        w_expand.astype(low_type),
        w_reduce.astype(low_type),
        bias_expand.astype(low_type),
    )
    small_all = (
        lax.all_gather(small_local[0], "dp", axis=0, tiled=True),
        lax.all_gather(small_local[1], "dp", axis=0, tiled=True),
        lax.all_gather(small_local[2], "dp", axis=0, tiled=True),
        lax.all_gather(small_local[3], "dp", axis=0, tiled=True),
        lax.all_gather(small_local[4], "dp", axis=0, tiled=True),
        lax.all_gather(small_local[5], "dp", axis=0, tiled=True),
        lax.all_gather(small_local[6], "dp", axis=0, tiled=True),
    )
    tin = small_all[0].reshape(patches, hidden_tok)
    tout = small_all[1].reshape(hidden_tok, patches)
    g_one, b_one, g_two, b_two, c_four = [piece.astype(wide) for piece in small_all[2:]]
    normed_one, scale_one = normalize(images)
    mixed_in = (normed_one * g_one + b_one).astype(low_type)
    pre_t = (
        jnp.einsum("ps,bpd->bsd", tin, mixed_in, preferred_element_type=wide)
        + bias_token_in[None, :, None]
    )
    act_t = gelu_exact(pre_t).astype(low_type)
    middle = (
        images
        + jnp.einsum("sp,bsd->bpd", tout, act_t, preferred_element_type=wide)
        + bias_token_out[None, :, None]
    )
    normed_two, scale_two = normalize(middle.reshape(rows, width))
    zed = (normed_two * g_two + b_two).astype(low_type)
    whole_channel = (
        lax.all_gather(channel_local[0], "dp", axis=0, tiled=True),
        lax.all_gather(channel_local[1], "dp", axis=0, tiled=True),
        lax.all_gather(channel_local[2], "dp", axis=0, tiled=True),
    )
    w_in, w_out, c_in = whole_channel
    pre = (
        jnp.einsum("td,fd->tf", zed, w_in, preferred_element_type=wide) + c_in.astype(wide)[None, :]
    )
    act = gelu_exact(pre).astype(low_type)
    reduced = jnp.dot(act, w_out, preferred_element_type=wide)
    block_output = (middle + (reduced + c_four).reshape(count, patches, width)) * keep
    grad_top = cotangent * keep
    grad_branch = grad_top.reshape(rows, width).astype(low_type)
    grad_c_four = jnp.sum(grad_branch.astype(wide), axis=0)
    small_all = (
        lax.all_gather(small_local[0], "dp", axis=0, tiled=True),
        lax.all_gather(small_local[1], "dp", axis=0, tiled=True),
        lax.all_gather(small_local[2], "dp", axis=0, tiled=True),
        lax.all_gather(small_local[3], "dp", axis=0, tiled=True),
        lax.all_gather(small_local[4], "dp", axis=0, tiled=True),
        lax.all_gather(small_local[5], "dp", axis=0, tiled=True),
        lax.all_gather(small_local[6], "dp", axis=0, tiled=True),
    )
    tin = small_all[0].reshape(patches, hidden_tok)
    tout = small_all[1].reshape(hidden_tok, patches)
    g_one, b_one, g_two, b_two, c_four = [piece.astype(wide) for piece in small_all[2:]]
    whole_channel = (
        lax.all_gather(channel_local[0], "dp", axis=0, tiled=True),
        lax.all_gather(channel_local[1], "dp", axis=0, tiled=True),
        lax.all_gather(channel_local[2], "dp", axis=0, tiled=True),
    )
    w_in, w_out, c_in = whole_channel
    pre = (
        jnp.einsum("td,fd->tf", zed, w_in, preferred_element_type=wide) + c_in.astype(wide)[None, :]
    )
    act = gelu_exact(pre).astype(low_type)
    grad_act = jnp.einsum("td,fd->tf", grad_branch, w_out, preferred_element_type=wide)
    grad_pre = (grad_act * gelu_slope(pre)).astype(low_type)
    grad_zed = jnp.dot(grad_pre, w_in, preferred_element_type=wide)
    grad_in = jnp.einsum("tf,td->fd", grad_pre, zed, preferred_element_type=wide)
    grad_out = jnp.einsum("tf,td->fd", act, grad_branch, preferred_element_type=wide)
    grad_cin = jnp.sum(grad_pre.astype(wide), axis=0)
    grad_zed, grad_win, grad_wout, grad_cin = (grad_zed, grad_in, grad_out, grad_cin)
    grad_g_two = jnp.sum(grad_zed * normed_two, axis=0)
    grad_b_two = jnp.sum(grad_zed, axis=0)
    grad_mid = grad_top + norm_back(grad_zed, normed_two, scale_two, g_two).reshape(
        count, patches, width
    )
    grad_back = grad_mid.astype(low_type)
    grad_c_two = jnp.sum(grad_back.astype(wide), axis=(0, 2))
    grad_tout = jnp.einsum("bsd,bpd->sp", act_t, grad_back, preferred_element_type=wide)
    grad_act_t = jnp.einsum("sp,bpd->bsd", tout, grad_back, preferred_element_type=wide)
    grad_pre_t = (grad_act_t * gelu_slope(pre_t)).astype(low_type)
    grad_c_one = jnp.sum(grad_pre_t.astype(wide), axis=(0, 2))
    grad_tin = jnp.einsum("bpd,bsd->ps", mixed_in, grad_pre_t, preferred_element_type=wide)
    grad_mixed = jnp.einsum("ps,bsd->bpd", tin, grad_pre_t, preferred_element_type=wide)
    grad_g_one = jnp.sum(grad_mixed * normed_one, axis=(0, 1))
    grad_b_one = jnp.sum(grad_mixed, axis=(0, 1))
    image_grad = grad_mid + norm_back(grad_mixed, normed_one, scale_one, g_one)
    bias_sums = lax.psum((grad_c_one, grad_c_two), "dp")
    flat_tin = grad_tin.reshape(patches * hidden_tok)
    flat_tout = grad_tout.reshape(hidden_tok * patches)
    owned = (
        lax.psum_scatter(flat_tin, "dp", scatter_dimension=0, tiled=True),
        lax.psum_scatter(flat_tout, "dp", scatter_dimension=0, tiled=True),
        lax.psum_scatter(grad_g_one, "dp", scatter_dimension=0, tiled=True),
        lax.psum_scatter(grad_b_one, "dp", scatter_dimension=0, tiled=True),
        lax.psum_scatter(grad_g_two, "dp", scatter_dimension=0, tiled=True),
        lax.psum_scatter(grad_b_two, "dp", scatter_dimension=0, tiled=True),
        lax.psum_scatter(grad_win, "dp", scatter_dimension=0, tiled=True),
        lax.psum_scatter(grad_cin, "dp", scatter_dimension=0, tiled=True),
        lax.psum_scatter(grad_wout, "dp", scatter_dimension=0, tiled=True),
        lax.psum_scatter(grad_c_four, "dp", scatter_dimension=0, tiled=True),
    )
    (
        own_tin,
        own_tout,
        own_g_one,
        own_b_one,
        own_g_two,
        own_b_two,
        own_win,
        own_cin,
        own_wout,
        own_c_four,
    ) = owned
    return (
        block_output,
        image_grad,
        own_tin,
        own_tout,
        bias_sums[0],
        bias_sums[1],
        own_g_one,
        own_b_one,
        own_g_two,
        own_b_two,
        own_win,
        own_cin,
        own_wout,
        own_c_four,
    )


def solution(mesh):
    placed = (
        P("dp", None, None),
        P("dp"),
        P("dp", None, None),
        P("dp"),
        P("dp"),
        P(),
        P(),
        P("dp"),
        P("dp"),
        P("dp"),
        P("dp"),
        P("dp", None),
        P("dp"),
        P("dp", None),
        P("dp"),
    )
    return jax.shard_map(
        choose,
        mesh=mesh,
        in_specs=placed,
        out_specs=(
            P("dp", None, None),
            P("dp", None, None),
            P("dp"),
            P("dp"),
            P(),
            P(),
            P("dp"),
            P("dp"),
            P("dp"),
            P("dp"),
            P("dp", None),
            P("dp"),
            P("dp", None),
            P("dp"),
        ),
        check_vma=False,
    )
```

```python
import math

import jax
import jax.numpy as jnp
from jax import lax
from jax.experimental import pallas as pl
from jax.experimental.pallas import tpu as pltpu
from jax.sharding import PartitionSpec as P

EPS = 1e-06


def gelu_exact(v):
    return 0.5 * v * (1.0 + lax.erf(v * 0.7071067811865476))


def gelu_slope(v):
    return 0.5 * (1.0 + lax.erf(v * 0.7071067811865476)) + v * 0.3989422804014327 * jnp.exp(
        -0.5 * v * v
    )


def norm_parts(v):
    middle = jnp.mean(v, axis=-1, keepdims=True)
    centered = v - middle
    scale = lax.rsqrt(jnp.mean(centered * centered, axis=-1, keepdims=True) + EPS)
    return (centered * scale, middle, scale)


def normalize(v):
    centered = v - jnp.mean(v, axis=-1, keepdims=True)
    scale = lax.rsqrt(jnp.mean(centered * centered, axis=-1, keepdims=True) + EPS)
    return (centered * scale, scale)


def norm_back(grad_in, normed, scale, gain):
    scaled = grad_in * gain
    return scale * (
        scaled
        - jnp.mean(scaled, axis=-1, keepdims=True)
        - normed * jnp.mean(scaled * normed, axis=-1, keepdims=True)
    )


WIDE = jnp.float32
LOW = jnp.bfloat16
MESH = pl.DeviceIdType.MESH
NT = (((1,), (1,)), ((), ()))
TN = (((0,), (0,)), ((), ()))
NN = (((1,), (0,)), ((), ()))
PLANE = 8


def dot(a, b, dims):
    return lax.dot_general(a, b, dims, preferred_element_type=WIDE)


def gelu_parts(v):
    cdf = 0.5 * (1.0 + lax.erf(v * 0.7071067811865476))
    return v * cdf, cdf + v * 0.3989422804014327 * jnp.exp(-0.5 * v * v)


def padded(v, rows):
    return jnp.concatenate([v, jnp.zeros((rows - v.shape[0], v.shape[1]), v.dtype)], axis=0)


def block_kernel(
    mask,
    images,
    cotangent,
    w_in,
    w_out,
    tin_own,
    tout_own,
    gain_one_own,
    shift_one_own,
    gain_two_own,
    shift_two_own,
    c_four_own,
    c_in_own,
    c_one,
    c_two,
    total,
    grad_zed,
    grad_in,
    grad_out,
    small_out,
    biases_out,
    mixed,
    act_t,
    slope_t,
    mid,
    zed,
    top,
    weights,
    act,
    grad_pre,
    c_in_rel,
    own_sum,
    keep_sum,
    send_one,
    recv_one,
    send_two,
    recv_two,
    send_three,
    recv_three,
    send_four,
    recv_four,
    recv_far,
    tin,
    tin_t,
    tout,
    tout_t,
    vecs,
    c_in,
    lines,
    small_own,
    small_all,
    grad_tin,
    grad_tout,
    grad_vecs,
    grad_c_in,
    small_sum,
    small_core,
    small_plane,
    small_z,
    biases,
    biases_in,
    late,
    late_in,
    figures,
    in_sem,
    ag_send,
    ag_recv,
    rs_send,
    rs_recv,
    sg_send,
    sg_recv,
    ss_send,
    ss_recv,
    bs_send,
    bs_recv,
    ls_send,
    ls_recv,
):
    count, patches, width = images.shape
    planes = weights.shape[1]
    shard = w_in.shape[0]
    half = 4 * shard
    chunk = 8 * shard
    pad = mixed.shape[1]
    blocks = count // 2
    pair = zed.shape[0] // blocks
    lot = pair // 2
    me = lax.axis_index("dp")
    core = me % 2
    col = (me // 2) % 2
    row = (me // 4) % 2
    z = me // PLANE
    by_core = me + 1 - 2 * core
    by_x = me + 2 - 4 * col
    by_y = me + 4 - 8 * row
    by_both = by_x + by_y - me

    def plane_of(k):
        out, bit = z, 1
        while bit < planes:
            out = out + bit * ((k // bit) % 2) * (1 - 2 * ((z // bit) % 2))
            bit *= 2
        return out

    def by_z(k):
        return me + PLANE * (plane_of(k) - z)

    def ag(stage, k, mat):
        near, far = (by_x, by_y) if mat == 0 else (by_y, by_x)
        step = 1 if mat == 0 else 2
        if stage == 0:
            src, dst, size, to = 0, 0, shard, by_z(k)
            source = weights.at[mat, 0, pl.ds(src, size)]
        else:
            src, dst, size, to = {
                1: (0, step * shard, shard, near),
                2: (0, (3 - step) * shard, shard, far),
                3: (step * shard, 3 * shard, shard, far),
                4: (0, half, 3 * shard, by_core),
                5: (3 * shard, half + 3 * shard, shard, by_core),
            }[stage]
            source = weights.at[mat, k, pl.ds(src, size)]
        return pltpu.make_async_remote_copy(
            src_ref=source,
            dst_ref=weights.at[mat, k, pl.ds(dst, size)],
            send_sem=ag_send.at[stage, k, mat],
            recv_sem=ag_recv.at[stage, k, mat],
            device_id=(to,),
            device_id_type=MESH,
        )

    middle = ((z + 1) // 2) % 2

    def plane_at(i):
        return (1 - middle) * ((i + 1) % planes) + middle * (planes - 1 - i)

    def rs(stage, i, mat):
        slot, k = i % 2, plane_at(i)
        near, far = (by_x, by_y) if mat == 0 else (by_y, by_x)
        src, dst, to = [
            lambda: (send_one.at[mat], recv_one.at[slot, mat], by_core),
            lambda: (
                send_two.at[mat, pl.ds(shard, shard)],
                recv_two.at[slot, mat, pl.ds(shard, shard)],
                near,
            ),
            lambda: (send_three.at[mat], recv_three.at[slot, mat], far),
            lambda: (send_four.at[slot, mat], recv_four.at[k - 1, mat], by_z(k)),
            lambda: (weights.at[mat, k, pl.ds(0, half)], recv_far.at[(k - 1) // 2, mat], by_z(k)),
            lambda: (send_two.at[mat, pl.ds(0, shard)], recv_two.at[slot, mat, pl.ds(0, shard)], near),
        ][stage]()
        at = k if stage in (3, 4) else i
        return pltpu.make_async_remote_copy(
            src_ref=src,
            dst_ref=dst,
            send_sem=rs_send.at[stage, at, mat],
            recv_sem=rs_recv.at[stage, at, mat],
            device_id=(to,),
            device_id_type=MESH,
        )

    def came_from(stage, k, mat):
        place = recv_four.at[k - 1, mat] if stage == 3 else recv_far.at[(k - 1) // 2, mat]
        pltpu.make_async_remote_copy(
            src_ref=place,
            dst_ref=place,
            send_sem=rs_send.at[stage, k, mat],
            recv_sem=rs_recv.at[stage, k, mat],
            device_id=(by_z(k),),
            device_id_type=MESH,
        ).wait_recv()
        return place[...].astype(WIDE)

    def small_gather(stage, k, group):
        src, dst, to = [
            lambda: (small_all.at[group, 0, 0], small_all.at[group, 0, k], by_z(k)),
            lambda: (small_all.at[group, 0], small_all.at[group, k], (me, by_x, by_y, by_both)[k]),
            lambda: (small_all.at[group, pl.ds(0, 4)], small_all.at[group, pl.ds(4, 4)], by_core),
        ][stage]()
        return pltpu.make_async_remote_copy(
            src_ref=src,
            dst_ref=dst,
            send_sem=sg_send.at[stage, k, group],
            recv_sem=sg_recv.at[stage, k, group],
            device_id=(to,),
            device_id_type=MESH,
        )

    def small_reduce(stage, k, group):
        src, dst, to = [
            lambda: (small_all.at[group, pl.ds(4, 4)], small_core.at[group], by_core),
            lambda: (small_all.at[group, k], small_plane.at[group, k], (me, by_x, by_y, by_both)[k]),
            lambda: (small_all.at[group, 0, k], small_z.at[k, group], by_z(k)),
        ][stage]()
        return pltpu.make_async_remote_copy(
            src_ref=src,
            dst_ref=dst,
            send_sem=ss_send.at[stage, k, group],
            recv_sem=ss_recv.at[stage, k, group],
            device_id=(to,),
            device_id_type=MESH,
        )

    def bias_reduce(stage, k):
        to = [lambda: by_core, lambda: (me, by_x, by_y, by_both)[k], lambda: by_z(k)][stage]()
        return pltpu.make_async_remote_copy(
            src_ref=biases.at[stage],
            dst_ref=biases_in.at[stage, k],
            send_sem=bs_send.at[stage, k],
            recv_sem=bs_recv.at[stage, k],
            device_id=(to,),
            device_id_type=MESH,
        )

    def late_reduce(stage, k):
        to = [lambda: by_core, lambda: (me, by_x, by_y, by_both)[k], lambda: by_z(k)][stage]()
        return pltpu.make_async_remote_copy(
            src_ref=late.at[stage],
            dst_ref=late_in.at[stage, k],
            send_sem=ls_send.at[stage, k],
            recv_sem=ls_recv.at[stage, k],
            device_id=(to,),
            device_id_type=MESH,
        )

    hidden_tok = c_one.shape[0]
    unit = math.gcd(tin_own.shape[0], hidden_tok)
    lines_in = tin_own.shape[0] // unit
    first_lines = (lines_in + 1) // 2
    lines_out = tout_own.shape[0] // patches
    own_vec = gain_one_own.shape[0]
    turns = hidden_tok // unit
    devices = planes * PLANE

    def place_of(d):
        dz, dy, dx, dc = d // PLANE, (d // 4) % 2, (d // 2) % 2, d % 2
        far = (dc + core) % 2 * 4 + (dy + row) % 2 * 2 + (dx + col) % 2
        k, bit = 0, 1
        while bit < planes:
            k = k + bit * ((dz // bit + z // bit) % 2)
            bit *= 2
        return far, k

    def load(b):
        return pltpu.make_async_copy(images.at[b], grad_zed.at[b], in_sem.at[0, b])

    def load_top(b):
        return pltpu.make_async_copy(cotangent.at[b], total.at[b], in_sem.at[1, b])

    def reload_image(b):
        return pltpu.make_async_copy(images.at[b], mid.at[b], in_sem.at[3, b])

    for b in range(count):
        load_top(b).start()
    for b in range(count):
        load(b).start()
    small_own[...] = jnp.zeros_like(small_own)
    for i in range(lines_in):
        at, lane = (i, 0) if i < first_lines else (i - first_lines, 64)
        small_own[at : at + 1, lane : lane + unit] = tin_own[i * unit : (i + 1) * unit].reshape(1, unit)
    for i, piece in enumerate((gain_one_own, shift_one_own, gain_two_own, shift_two_own, c_four_own)):
        small_own[24 + i : 25 + i, 64 : 64 + own_vec] = piece[...].reshape(1, own_vec)
    small_own[31:32, 0:shard] = c_in_own[...].reshape(1, shard)
    for i in range(lines_out):
        line = tout_own[i * patches : (i + 1) * patches].reshape(1, patches)
        small_own[32 + i : 33 + i, :] = line[:, 0:128]
        small_own[48 + i : 49 + i, 0 : patches - 128] = line[:, 128:patches]
    for group in range(2):
        small_all[group, 0, 0] = small_own[32 * group : 32 * (group + 1)].astype(LOW)
    weights[0, 0, 0:shard] = w_in[...].astype(LOW)
    weights[1, 0, 0:shard] = w_out[...].astype(LOW)

    barrier = pltpu.get_barrier_semaphore()
    peers = [by_core, by_x, by_y, by_both] + [by_z(k) for k in range(1, planes)]
    for peer in peers:
        pl.semaphore_signal(barrier, inc=1, device_id=(peer,), device_id_type=MESH)
    pl.semaphore_wait(barrier, len(peers))

    mats = (0, 1)
    inner = middle == 1

    def ag_pass(which, mat):
        src, dst, to = ((1, 2, by_z(3)), (3, 2, by_z(1)), (2, 3, by_z(1)))[which]
        return pltpu.make_async_remote_copy(
            src_ref=weights.at[mat, src, pl.ds(0, shard)],
            dst_ref=weights.at[mat, dst, pl.ds(0, shard)],
            send_sem=ag_send.at[6, which, mat],
            recv_sem=ag_recv.at[0, dst, mat],
            device_id=(to,),
            device_id_type=MESH,
        )

    def ag_planes():
        for mat in mats:
            ag(0, 1, mat).start()

        @pl.when(inner)
        def _():
            for mat in mats:
                ag(0, 3, mat).start()

    def ag_planes_pass():
        @pl.when(inner)
        def _():
            for which, came in ((0, 1), (1, 3)):
                for mat in mats:
                    ag(0, came, mat).wait_recv()
                    ag_pass(which, mat).start()

    def ag_planes_last():
        @pl.when(inner)
        def _():
            for mat in mats:
                ag(0, 2, mat).wait_recv()
                ag_pass(2, mat).start()

    def ag_direct(k):
        @pl.when(jnp.logical_not(inner))
        def _():
            for mat in mats:
                ag(0, k, mat).wait_recv()

        for stage in (1, 2):
            for mat in mats:
                ag(stage, k, mat).start()

    def ag_forward(k):
        for mat in mats:
            ag(1, k, mat).wait_recv()
            ag(3, k, mat).start()

    def ag_core(k):
        for mat in mats:
            ag(2, k, mat).wait_recv()
            ag(4, k, mat).start()

    def ag_core_last(k):
        for mat in mats:
            ag(3, k, mat).wait_recv()
            ag(5, k, mat).start()

    def ag_ready(k):
        for mat in mats:
            ag(4, k, mat).wait_recv()
            ag(5, k, mat).wait_recv()

    for group in range(2):
        for k in range(1, planes):
            small_gather(0, k, group).start()
    for mat in mats:
        ag(1, 0, mat).start()
    ag_planes()

    grad_vecs[...] = jnp.zeros_like(grad_vecs)
    grad_tin[...] = jnp.zeros_like(grad_tin)
    grad_tout[...] = jnp.zeros_like(grad_tout)

    def channel_top(r, carry):
        tops = []
        for h in range(2):
            b = 2 * r + h
            load_top(b).wait()
            tops.append(padded(total[b] * mask[b].astype(WIDE), lot))
        rounded = jnp.concatenate(tops, axis=0).astype(LOW)
        top[pl.ds(r * pair, pair), :] = rounded
        grad_vecs[2:3, :] += jnp.sum(rounded.astype(WIDE), axis=0, keepdims=True)
        return carry

    def first_norm(b, carry):
        load(b).wait()
        mid[b], figures[b, :, 0:1], figures[b, :, 1:2] = norm_parts(grad_zed[b])
        return carry

    lax.fori_loop(0, blocks, channel_top, 0)
    for group in range(2):
        for k in range(1, planes):
            small_gather(0, k, group).wait_recv()
        for k in range(1, 4):
            small_gather(1, k, group).start()
    lax.fori_loop(0, count, first_norm, 0)
    for k in range(1, 4):
        small_gather(1, k, 0).wait_recv()
    small_gather(2, 0, 0).start()

    tin[...] = jnp.zeros_like(tin)
    tout[...] = jnp.zeros_like(tout)

    def unpack(d, group):
        far, k = place_of(d)
        message = small_all[group, far, k].astype(WIDE)
        if group == 0:
            lines[d * lines_in : d * lines_in + first_lines, :] = message[0:first_lines, :]
            shifted = jnp.concatenate([message[0:24, 64:128], message[0:24, 0:64]], axis=1)
            lines[d * lines_in + first_lines : (d + 1) * lines_in, :] = shifted[0 : lines_in - first_lines, :]
            vecs[:, d * own_vec : (d + 1) * own_vec] = message[24:32, 64 : 64 + own_vec]
            c_in[d] = message[31:32, 0:shard]
        else:
            tout[d * lines_out : (d + 1) * lines_out, 0:128] = message[0:lines_out, :]
            tout[d * lines_out : (d + 1) * lines_out, 128:patches] = message[16 : 16 + lines_out, 0 : patches - 128]

    def unpack_half(own, group):
        for parity in range(2):

            @pl.when((core == parity) == own)
            def _():
                for d in range(parity, devices, 2):
                    unpack(d, group)

    unpack_half(True, 0)
    for k in range(1, 4):
        small_gather(1, k, 1).wait_recv()
    small_gather(2, 0, 1).start()
    unpack_half(True, 1)
    ag_planes_pass()
    ag_direct(plane_at(0))
    for group in range(2):
        small_gather(2, 0, group).wait_recv()
        unpack_half(False, group)
    for turn in range(turns):
        tin[0:patches, turn * unit : (turn + 1) * unit] = lines[pl.ds(turn, patches, stride=turns), :][:, 0:unit]
    for rest, into, at in ((c_one, tin, patches), (c_two, tout, hidden_tok)):
        rest = rest[...].reshape(1, rest.shape[0])
        for i in range(3):
            term = rest.astype(LOW).astype(WIDE)
            into[at + i : at + i + 1, 0 : rest.shape[1]] = term
            rest = rest - term
    tin_t[...] = tin[...].T.astype(LOW)
    tout_t[...] = tout[...].T.astype(LOW)
    ones = jnp.ones((3, width), WIDE)

    gain_one, shift_one = vecs[0:1, :], vecs[1:2, :]
    gain_two, shift_two, c_four = vecs[2:3, :], vecs[3:4, :], vecs[4:5, :]
    def singles(work, start, stop):
        def one(b, carry):
            work(b)
            return carry

        lax.fori_loop(start, stop, one, 0)

    def pairs(work, start, stop):
        def two(r, carry):
            for h in range(2):
                work(2 * r + h)
            return carry

        lax.fori_loop(start // 2, stop // 2, two, 0)

    def token_forward(b):
        fed = mid[b] * gain_one + shift_one
        mixed[b] = padded(jnp.concatenate([fed, ones], axis=0), pad).astype(LOW)
        value, slope = gelu_parts(dot(tin_t[...], mixed[b], NN))
        act_t[b] = padded(jnp.concatenate([value, ones], axis=0), act_t.shape[1]).astype(LOW)
        slope_t[b] = slope.astype(LOW)
        mid[b] = grad_zed[b] + dot(tout_t[...], act_t[b], NN)[0:patches]

    def channel_inputs(r, carry):
        parts = []
        for h in range(2):
            total[2 * r + h] = mid[2 * r + h] + c_four
            normed, _, figures[2 * r + h, :, 2:3] = norm_parts(mid[2 * r + h])
            mid[2 * r + h] = normed
            grad_zed[2 * r + h] = jnp.zeros((patches, width), WIDE)
            parts.append(padded(normed * gain_two + shift_two, lot))
        zed[pl.ds(r * pair, pair), :] = jnp.concatenate(parts, axis=0).astype(LOW)
        return carry

    first = 4
    singles(token_forward, 0, first)
    ag_forward(plane_at(0))
    singles(token_forward, first, count)
    ag_core(plane_at(0))
    ag_planes_last()
    lax.fori_loop(0, blocks, channel_inputs, 0)
    ag_direct(plane_at(1))
    for k in range(planes):
        for place in range(PLANE):
            near = plane_of(k) * PLANE + (
                (row + (place // 2) % 2) % 2 * 4 + (col + place % 2) % 2 * 2 + (core + place // 4) % 2
            )
            c_in_rel[k, :, place * shard : (place + 1) * shard] = c_in[near]

    ag_core_last(plane_at(0))

    def rs_two(i, mat):
        rs(0, i, mat).wait_recv()
        slot = i % 2
        first, second = (1, 3) if mat == 0 else (2, 3)

        def part(n):
            return slice(n * shard, (n + 1) * shard)

        @pl.when(i == 0)
        def _():
            weights[mat, plane_at(i), 0:half] = (own_sum[mat] + recv_one[slot, mat].astype(WIDE)).astype(LOW)
            rs(4, 0, mat).start()

        @pl.when((i == planes - 1) & inner)
        def _():
            own_sum[mat] += came_from(4, 1, mat) + came_from(4, 3, mat)

        @pl.when(i > 1)
        def _():
            for stage in (1, 5):
                rs(stage, i - 1, mat).wait_send()

        @pl.when(i > 0)
        def _():
            for n, to, stage in ((second, part(1), 1), (first, part(0), 5)):
                send_two[mat, to] = (own_sum[mat, part(n)] + recv_one[slot, mat, part(n)].astype(WIDE)).astype(LOW)
                rs(stage, i, mat).start()
            for n in (0, 3 - first):
                own_sum[mat, part(n)] += recv_one[slot, mat, part(n)].astype(WIDE)

    def rs_three(i):
        for mat in mats:
            rs(1, i, mat).wait_recv()
            other = 2 if mat == 0 else 1

            @pl.when(i > 1)
            def _():
                rs(2, i - 1, mat).wait_send()

            send_three[mat] = (
                own_sum[mat, other * shard : (other + 1) * shard]
                + recv_two[i % 2, mat, shard : 2 * shard].astype(WIDE)
            ).astype(LOW)
            rs(2, i, mat).start()

    def rs_keep(i):
        for mat in mats:
            rs(5, i, mat).wait_recv()
            keep_sum[mat] = own_sum[mat, 0:shard] + recv_two[i % 2, mat, 0:shard].astype(WIDE)

    def rs_four(i):
        for mat in mats:
            rs(2, i, mat).wait_recv()

            send_four[i % 2, mat] = (keep_sum[mat] + recv_three[i % 2, mat].astype(WIDE)).astype(LOW)
            rs(3, i, mat).start()

    def rs_last():
        last = planes - 1
        for mat in mats:
            result = grad_in if mat == 0 else grad_out
            rs(2, last, mat).wait_recv()
            summed = keep_sum[mat] + recv_three[last % 2, mat].astype(WIDE)
            result[...] = summed + came_from(3, 2, mat)

            @pl.when(jnp.logical_not(inner))
            def _():
                result[...] += came_from(3, 1, mat) + came_from(3, 3, mat)


    tile = chunk // 3

    def channel_chunk(i, carry):
        k = plane_at(i)

        @pl.when(i == planes - 1)
        def _():
            rs_four(1)

        ag_ready(k)

        def rows(r):
            for s in range(3):
                part = slice(s * tile, (s + 1) * tile)
                pre = dot(zed[r * pair : (r + 1) * pair, :], weights[0, k, part], NT) + c_in_rel[k, :, part]
                value, slope = gelu_parts(pre)
                act[r * pair : (r + 1) * pair, part] = value.astype(LOW)
                back = (dot(top[r * pair : (r + 1) * pair, :], weights[1, k, part], NT) * slope).astype(LOW)
                grad_pre[r * pair : (r + 1) * pair, part] = back
            up = dot(act[r * pair : (r + 1) * pair, :], weights[1, k], NN)
            down = dot(grad_pre[r * pair : (r + 1) * pair, :], weights[0, k], NN)
            for h in range(2):
                total[2 * r + h] += up[h * lot : h * lot + patches]
                grad_zed[2 * r + h] += down[h * lot : h * lot + patches]

        rows(0)

        @pl.when(i == 0)
        def _():
            ag_forward(plane_at(1))

        @pl.when(i == 1)
        def _():
            ag_forward(plane_at(2))
            ag_forward(0)

        for r in range(1, blocks):
            rows(r)

        @pl.when(i == 0)
        def _():
            ag_core(plane_at(1))
            ag_direct(plane_at(2))
            for mat in mats:
                ag(2, 0, mat).start()

        @pl.when(i == 1)
        def _():
            ag_core(plane_at(2))

        @pl.when(i == 2)
        def _():
            ag_core(0)
            ag_core_last(0)

        @pl.when(i > 1)
        def _():
            rs_three(i - 1)

        back_sum = jnp.sum(grad_pre[...].astype(WIDE), axis=0, keepdims=True)
        for place in range(PLANE):
            near = plane_of(k) * PLANE + (
                (row + (place // 2) % 2) % 2 * 4 + (col + place % 2) % 2 * 2 + (core + place // 4) % 2
            )
            grad_c_in[near] = back_sum[:, place * shard : (place + 1) * shard]

        @pl.when(i > 0)
        def _():
            for mat in mats:
                rs(0, i - 1, mat).wait_send()

        send_one[1] = dot(act[:, half:chunk], top[...], TN).astype(LOW)
        send_one[0] = dot(grad_pre[:, half:chunk], zed[...], TN).astype(LOW)
        for mat in mats:
            rs(0, i, mat).start()

        @pl.when(i > 1)
        def _():
            rs_keep(i - 1)

        @pl.when(i == 0)
        def _():
            for mat in mats:
                for stage in range(1, 6):
                    ag(stage, k, mat).wait_send()

                @pl.when(inner)
                def _():
                    ag_pass(1, mat).wait_send()

        own_sum[1] = dot(act[:, 0:half], top[...], TN)
        own_sum[0] = dot(grad_pre[:, 0:half], zed[...], TN)
        @pl.when(i < 2)
        def _():
            ag_core_last(plane_at(i + 1))

        for mat in mats:
            rs_two(i, mat)
        return carry

    lax.fori_loop(0, planes, channel_chunk, 0)

    tin_low = tin[...].astype(LOW)
    tout_low = tout[0:hidden_tok, :].astype(LOW)

    def kept(b):
        return weights.at[b // planes, b % planes, 0:pad]

    def middle_backward(b, above):
        normed = mid[b]
        down = grad_zed[b]
        grad_vecs[0:1, :] += jnp.sum(down * normed, axis=0, keepdims=True)
        grad_vecs[1:2, :] += jnp.sum(down, axis=0, keepdims=True)
        grad_mid = above + norm_back(down, normed, figures[b, :, 2:3], gain_two)
        grad_zed[b] = grad_mid
        back = padded(grad_mid, pad).astype(LOW)
        grad_tout[...] += dot(act_t[b], back, NT)
        slope_t[b] = (dot(tout_low, back, NN) * slope_t[b].astype(WIDE)).astype(LOW)
        grad_tin[:, 0:hidden_tok] += dot(mixed[b], slope_t[b], NT)

    def middle_pair(r, carry):
        above = top[pl.ds(r * pair, pair), :].astype(WIDE)
        for h in range(2):
            middle_backward(2 * r + h, above[h * lot : h * lot + patches])
        for h in range(2):
            reload_image(2 * r + h).start()
        return carry

    def image_norm(b):
        normed = (mid[b] - figures[b, :, 0:1]) * figures[b, :, 1:2]
        mid[b] = normed
        grad_mixed = dot(tin_low, slope_t[b], NN)
        kept(b)[...] = grad_mixed.astype(LOW)
        late[0, 0:1, :] += jnp.sum(grad_mixed[0:patches] * normed, axis=0, keepdims=True)
        late[0, 1:2, :] += jnp.sum(grad_mixed[0:patches], axis=0, keepdims=True)

    def image_backward(b):
        total[b] *= mask[b].astype(WIDE)
        grad_zed[b] += norm_back(kept(b)[...][0:patches].astype(WIDE), mid[b], figures[b, :, 1:2], gain_one)

    def small_first(group):
        for k in range(1, planes):
            small_gather(0, k, group).wait_send()
        for far in range(1, 4):
            small_gather(1, far, group).wait_send()
        small_gather(2, 0, group).wait_send()
        if group == 0:
            for turn in range(turns):
                lines[pl.ds(turn, patches, stride=turns), :] = grad_tin[0:patches, turn * unit : turn * unit + 128]
        for d in range(devices):
            far, k = place_of(d)
            message = small_sum.at[group, far, k]
            if group == 0:
                low = lines[d * lines_in : d * lines_in + first_lines, :]
                high = lines[d * lines_in + first_lines : (d + 1) * lines_in, :]
                message[0:first_lines, 0:64] = low[:, 0:64]
                message[0 : lines_in - first_lines, 64:128] = high[:, 0:64]
                message[24:27, 64 : 64 + own_vec] = grad_vecs[0:3, d * own_vec : (d + 1) * own_vec]
                message[31:32, 0:shard] = grad_c_in[d]
            else:
                message[0:lines_out, :] = grad_tout[d * lines_out : (d + 1) * lines_out, 0:128]
                message[16 : 16 + lines_out, 0 : patches - 128] = grad_tout[
                    d * lines_out : (d + 1) * lines_out, 128:patches
                ]
        for far in range(4, PLANE):
            small_all[group, far] = small_sum[group, far].astype(LOW)
        small_reduce(0, 0, group).start()
        if group == 0:
            biases[0] = jnp.zeros_like(biases[0])
            for i in range(hidden_tok // 128):
                biases[0, i : i + 1, :] = grad_tin[patches : patches + 1, i * 128 : (i + 1) * 128]
            biases[0, 3:4, :] = grad_tout[hidden_tok : hidden_tok + 1, 0:128]
            biases[0, 4:5, 0 : patches - 128] = grad_tout[hidden_tok : hidden_tok + 1, 128:patches]
            bias_reduce(0, 0).start()

    def small_second(group):
        small_reduce(0, 0, group).wait_recv()
        for far in range(4):
            small_sum[group, far] += small_core[group, far].astype(WIDE)
        for far in range(1, 4):
            small_all[group, far] = small_sum[group, far].astype(LOW)
            small_reduce(1, far, group).start()
        if group == 0:
            bias_reduce(0, 0).wait_recv()
            biases[1] = biases[0] + biases_in[0, 0]
            for far in range(1, 4):
                bias_reduce(1, far).start()

    def small_third(group):
        for far in range(1, 4):
            small_reduce(1, far, group).wait_recv()
            small_sum[group, 0] += small_plane[group, far].astype(WIDE)
        for k in range(1, planes):
            small_all[group, 0, k] = small_sum[group, 0, k].astype(LOW)
            small_reduce(2, k, group).start()
        if group == 0:
            for far in range(1, 4):
                bias_reduce(1, far).wait_recv()
            biases[2] = (biases[1] + biases_in[1, 1]) + (biases_in[1, 2] + biases_in[1, 3])
            for k in range(1, planes):
                bias_reduce(2, k).start()

    for mat in mats:
        for i in range(1, planes):
            for stage in range(1, 6):
                ag(stage, plane_at(i), mat).wait_send()
        ag(0, 1, mat).wait_send()
        rs(4, 0, mat).wait_send()

        @pl.when(inner)
        def _():
            ag(0, 3, mat).wait_send()
            for which in (0, 2):
                ag_pass(which, mat).wait_send()

    late[0] = jnp.zeros_like(late[0])
    rs_four(planes - 2)
    lax.fori_loop(0, blocks, middle_pair, 0)
    small_first(1)
    small_first(0)
    for b in range(count):
        reload_image(b).wait()
    pairs(image_norm, 0, 2)
    small_second(1)
    pairs(image_norm, 2, count)
    small_second(0)
    late_reduce(0, 0).start()
    pairs(image_backward, 0, 2)
    late_reduce(0, 0).wait_recv()
    late[1] = late[0] + late_in[0, 0]
    for far in range(1, 4):
        late_reduce(1, far).start()
    rs_three(planes - 1)
    rs_keep(planes - 1)
    small_third(1)
    pairs(image_backward, 2, count)
    small_third(0)
    late_sum = late[1]
    for far in range(1, 4):
        late_reduce(1, far).wait_recv()
        late_sum = late_sum + late_in[1, far]
    late[2] = late_sum
    for k in range(1, planes):
        late_reduce(2, k).start()
    rs_last()
    summed = [small_sum[group, 0, 0] for group in range(2)]
    tree = [biases[2]]
    for k in range(1, planes):
        for group in range(2):
            small_reduce(2, k, group).wait_recv()
        bias_reduce(2, k).wait_recv()
        summed = [summed[group] + small_z[k, group].astype(WIDE) for group in range(2)]
        tree.append(biases_in[2, k])
    for group in range(2):
        small_out[32 * group : 32 * (group + 1)] = summed[group]
    for k in range(1, planes):
        late_reduce(2, k).wait_recv()
        late_sum = late_sum + late_in[2, k]
    late_sum = pltpu.roll(padded(late_sum, 8), width - own_vec * me, 1)
    small_out[27:29, 64 : 64 + own_vec] = late_sum[0:2, 0:own_vec]
    while len(tree) > 1:
        tree = [tree[i] + tree[i + 1] for i in range(0, len(tree), 2)]
    biases_out[...] = tree[0]

    for mat in mats:
        for stage in (0, 1, 2, 5):
            rs(stage, planes - 1, mat).wait_send()
        for i in range(1, planes - 1):
            rs(3, i, mat).wait_send()
    late_reduce(0, 0).wait_send()
    for far in range(1, 4):
        late_reduce(1, far).wait_send()
    for k in range(1, planes):
        late_reduce(2, k).wait_send()
    bias_reduce(0, 0).wait_send()
    for far in range(1, 4):
        bias_reduce(1, far).wait_send()
    for k in range(1, planes):
        bias_reduce(2, k).wait_send()
    for group in range(2):
        small_reduce(0, 0, group).wait_send()
        for far in range(1, 4):
            small_reduce(1, far, group).wait_send()
        for k in range(1, planes):
            small_reduce(2, k, group).wait_send()


def finish_kernel(
    block_in,
    image_in,
    w_in,
    w_out,
    small,
    biases,
    block_out,
    image_out,
    w_in_out,
    w_out_out,
    tin,
    tout,
    gain_one,
    shift_one,
    gain_two,
    shift_two,
    c_four,
    c_in,
    c_one,
    c_two,
    sem,
):
    pieces = [(block_in.at[b], block_out.at[b]) for b in range(block_in.shape[0])]
    pieces += [(image_in.at[b], image_out.at[b]) for b in range(image_in.shape[0])]
    pieces += [(w_in, w_in_out), (w_out, w_out_out)]
    copies = [pltpu.make_async_copy(a, b, sem.at[i]) for i, (a, b) in enumerate(pieces)]
    for copy in copies:
        copy.start()
    hidden_tok, patches = c_one.shape[0], c_two.shape[0]
    unit = math.gcd(tin.shape[0], hidden_tok)
    lines_in = tin.shape[0] // unit
    first_lines = (lines_in + 1) // 2
    for i in range(lines_in):
        at, lane = (i, 0) if i < first_lines else (i - first_lines, 64)
        tin[i * unit : (i + 1) * unit] = small[at : at + 1, lane : lane + unit].reshape(unit)
    for i in range(tout.shape[0] // patches):
        tout[i * patches : i * patches + 128] = small[32 + i : 33 + i, :].reshape(128)
        tout[i * patches + 128 : (i + 1) * patches] = small[48 + i : 49 + i, 0 : patches - 128].reshape(
            patches - 128
        )
    for i, piece in enumerate((gain_two, shift_two, c_four, gain_one, shift_one)):
        own_vec = piece.shape[0]
        piece[...] = small[24 + i : 25 + i, 64 : 64 + own_vec].reshape(own_vec)
    shard = c_in.shape[0]
    c_in[...] = small[31:32, 0:shard].reshape(shard)
    for i in range(hidden_tok // 128):
        c_one[i * 128 : (i + 1) * 128] = biases[i : i + 1, :].reshape(128)
    c_two[0:128] = biases[3:4, :].reshape(128)
    c_two[128:patches] = biases[4:5, 0 : patches - 128].reshape(patches - 128)
    for copy in copies:
        copy.wait()


def fast_shards(
    images,
    mask,
    cotangent,
    w_token_in,
    w_token_out,
    bias_token_in,
    bias_token_out,
    gain_one,
    shift_one,
    gain_two,
    shift_two,
    w_expand,
    bias_expand,
    w_reduce,
    bias_reduce,
):
    devices = lax.axis_size("dp")
    planes = devices // PLANE
    count, patches, width = images.shape
    hidden_tok = bias_token_in.shape[0]
    shard = w_expand.shape[0]
    pad = -(-patches // 16) * 16
    lot = -(-patches // 8) * 8
    pair = 2 * lot
    blocks = count // 2
    chunk = 8 * shard
    half = 4 * shard

    unit = math.gcd(w_token_in.shape[0], hidden_tok)
    lines_in = w_token_in.shape[0] // unit
    hidden_pad = hidden_tok + 16

    owned = (
        w_expand,
        w_reduce,
        w_token_in,
        w_token_out,
        gain_one,
        shift_one,
        gain_two,
        shift_two,
        bias_reduce,
        bias_expand,
        bias_token_in,
        bias_token_out,
    )
    vmem = pl.BlockSpec(memory_space=pltpu.VMEM)
    hbm = pl.BlockSpec(memory_space=pl.ANY)
    shape = jax.ShapeDtypeStruct
    outs = pl.pallas_call(
        block_kernel,
        out_shape=(
            pltpu.VMEM(images.shape, WIDE),
            pltpu.VMEM(images.shape, WIDE),
            pltpu.VMEM(w_expand.shape, WIDE),
            pltpu.VMEM(w_reduce.shape, WIDE),
            pltpu.VMEM((64, 128), WIDE),
            pltpu.VMEM((8, 128), WIDE),
        ),
        in_specs=[pl.BlockSpec(memory_space=pltpu.SMEM), hbm, hbm] + [vmem] * 12,
        out_specs=[vmem] * 6,
        scratch_shapes=[
            pltpu.VMEM((count, pad, width), LOW),
            pltpu.VMEM((count, hidden_pad, width), LOW),
            pltpu.VMEM((count, hidden_tok, width), LOW),
            pltpu.VMEM(images.shape, WIDE),
            pltpu.VMEM((blocks * pair, width), LOW),
            pltpu.VMEM((blocks * pair, width), LOW),
            pltpu.VMEM((2, planes, chunk, width), LOW),
            pltpu.VMEM((blocks * pair, chunk), LOW),
            pltpu.VMEM((blocks * pair, chunk), LOW),
            pltpu.VMEM((planes, 1, chunk), WIDE),
            pltpu.VMEM((2, half, width), WIDE),
            pltpu.VMEM((2, shard, width), WIDE),
            pltpu.VMEM((2, half, width), LOW),
            pltpu.VMEM((2, 2, half, width), LOW),
            pltpu.VMEM((2, 2 * shard, width), LOW),
            pltpu.VMEM((2, 2, 2 * shard, width), LOW),
            pltpu.VMEM((2, shard, width), LOW),
            pltpu.VMEM((2, 2, shard, width), LOW),
            pltpu.VMEM((2, 2, shard, width), LOW),
            pltpu.VMEM((planes - 1, 2, shard, width), LOW),
            pltpu.VMEM((2, 2, half, width), LOW),
            pltpu.VMEM((pad, hidden_tok), WIDE),
            pltpu.VMEM((hidden_tok, pad), LOW),
            pltpu.VMEM((hidden_pad, pad), WIDE),
            pltpu.VMEM((pad, hidden_pad), LOW),
            pltpu.VMEM((8, width), WIDE),
            pltpu.VMEM((devices, 1, shard), WIDE),
            pltpu.VMEM((devices * lines_in, 128), WIDE),
            pltpu.VMEM((64, 128), WIDE),
            pltpu.VMEM((2, PLANE, planes, 32, 128), LOW),
            pltpu.VMEM((pad, hidden_tok + 128), WIDE),
            pltpu.VMEM((hidden_pad, pad), WIDE),
            pltpu.VMEM((8, width), WIDE),
            pltpu.VMEM((devices, 1, shard), WIDE),
            pltpu.VMEM((2, PLANE, planes, 32, 128), WIDE),
            pltpu.VMEM((2, 4, planes, 32, 128), LOW),
            pltpu.VMEM((2, 4, planes, 32, 128), LOW),
            pltpu.VMEM((planes, 2, 32, 128), LOW),
            pltpu.VMEM((3, 8, 128), WIDE),
            pltpu.VMEM((3, max(4, planes), 8, 128), WIDE),
            pltpu.VMEM((3, 2, width), WIDE),
            pltpu.VMEM((3, max(4, planes), 2, width), WIDE),
            pltpu.VMEM((count, patches, 4), WIDE),
            pltpu.SemaphoreType.DMA((4, count)),
            pltpu.SemaphoreType.DMA((7, planes, 2)),
            pltpu.SemaphoreType.DMA((7, planes, 2)),
            pltpu.SemaphoreType.DMA((6, planes, 2)),
            pltpu.SemaphoreType.DMA((6, planes, 2)),
        ]
        + [pltpu.SemaphoreType.DMA((3, max(4, planes), 2))] * 4
        + [pltpu.SemaphoreType.DMA((3, max(4, planes)))] * 4,
        compiler_params=pltpu.CompilerParams(
            collective_id=0, has_side_effects=True, vmem_limit_bytes=56 * 2**20
        ),
    )(
        mask,
        images,
        cotangent,
        *owned,
    )
    flat = pl.pallas_call(
        finish_kernel,
        out_shape=(
            shape(images.shape, WIDE),
            shape(images.shape, WIDE),
            shape(w_expand.shape, WIDE),
            shape(w_reduce.shape, WIDE),
            shape(w_token_in.shape, WIDE),
            shape(w_token_out.shape, WIDE),
            *[shape(gain_one.shape, WIDE)] * 5,
            shape(bias_expand.shape, WIDE),
            shape(bias_token_in.shape, WIDE),
            shape(bias_token_out.shape, WIDE),
        ),
        in_specs=[vmem] * 6,
        out_specs=[hbm] * 4 + [vmem] * 10,
        scratch_shapes=[pltpu.SemaphoreType.DMA((2 * count + 2,))],
        compiler_params=pltpu.CompilerParams(vmem_limit_bytes=16 * 2**20),
    )(*outs)
    block_output, image_grad, own_win, own_wout, *rest = flat
    g_tin, g_tout, g_one, b_one, g_two, b_two, c_four, c_in, c_one, c_two = rest
    return (
        block_output,
        image_grad,
        g_tin,
        g_tout,
        c_one,
        c_two,
        g_one,
        b_one,
        g_two,
        b_two,
        own_win,
        c_in,
        own_wout,
        c_four,
    )


def fits(devices, images, w_token_in, w_token_out, bias_token_in, gain_one, w_expand):
    planes = devices // PLANE
    patches = images.shape[1]
    hidden_tok = bias_token_in.shape[0]
    shard = w_expand.shape[0]
    unit = math.gcd(w_token_in.shape[0], hidden_tok)
    return (
        devices % PLANE == 0
        and planes == 4
        and images.shape[0] % 2 == 0
        and 6 <= images.shape[0] <= 2 * planes
        and shard % 16 == 0
        and shard <= 128
        and (4 * shard) % 128 == 0
        and 128 < patches <= 205
        and unit <= 64
        and w_token_in.shape[0] // unit <= 49
        and w_token_out.shape[0] % patches == 0
        and w_token_out.shape[0] // patches <= 16
        and gain_one.shape[0] <= 64
        and hidden_tok == 384
    )


def choose(
    images,
    mask,
    cotangent,
    w_token_in,
    w_token_out,
    bias_token_in,
    bias_token_out,
    gain_one,
    shift_one,
    gain_two,
    shift_two,
    w_expand,
    bias_expand,
    w_reduce,
    bias_reduce,
):
    args = (
        images,
        mask,
        cotangent,
        w_token_in,
        w_token_out,
        bias_token_in,
        bias_token_out,
        gain_one,
        shift_one,
        gain_two,
        shift_two,
        w_expand,
        bias_expand,
        w_reduce,
        bias_reduce,
    )
    if fits(lax.axis_size("dp"), images, w_token_in, w_token_out, bias_token_in, gain_one, w_expand):
        return fast_shards(*args)
    return shards(*args)


def shards(
    images,
    mask,
    cotangent,
    w_token_in,
    w_token_out,
    bias_token_in,
    bias_token_out,
    gain_one,
    shift_one,
    gain_two,
    shift_two,
    w_expand,
    bias_expand,
    w_reduce,
    bias_reduce,
):
    low_type = jnp.bfloat16
    wide = jnp.float32
    count, patches, width = images.shape
    hidden_tok = bias_token_in.shape[0]
    rows = count * patches
    keep = mask.astype(wide)[:, None, None]
    small_local = (
        w_token_in.astype(low_type),
        w_token_out.astype(low_type),
        gain_one.astype(low_type),
        shift_one.astype(low_type),
        gain_two.astype(low_type),
        shift_two.astype(low_type),
        bias_reduce.astype(low_type),
    )
    channel_local = (
        w_expand.astype(low_type),
        w_reduce.astype(low_type),
        bias_expand.astype(low_type),
    )
    small_all = (
        lax.all_gather(small_local[0], "dp", axis=0, tiled=True),
        lax.all_gather(small_local[1], "dp", axis=0, tiled=True),
        lax.all_gather(small_local[2], "dp", axis=0, tiled=True),
        lax.all_gather(small_local[3], "dp", axis=0, tiled=True),
        lax.all_gather(small_local[4], "dp", axis=0, tiled=True),
        lax.all_gather(small_local[5], "dp", axis=0, tiled=True),
        lax.all_gather(small_local[6], "dp", axis=0, tiled=True),
    )
    tin = small_all[0].reshape(patches, hidden_tok)
    tout = small_all[1].reshape(hidden_tok, patches)
    g_one, b_one, g_two, b_two, c_four = [piece.astype(wide) for piece in small_all[2:]]
    normed_one, scale_one = normalize(images)
    mixed_in = (normed_one * g_one + b_one).astype(low_type)
    pre_t = (
        jnp.einsum("ps,bpd->bsd", tin, mixed_in, preferred_element_type=wide)
        + bias_token_in[None, :, None]
    )
    act_t = gelu_exact(pre_t).astype(low_type)
    middle = (
        images
        + jnp.einsum("sp,bsd->bpd", tout, act_t, preferred_element_type=wide)
        + bias_token_out[None, :, None]
    )
    normed_two, scale_two = normalize(middle.reshape(rows, width))
    zed = (normed_two * g_two + b_two).astype(low_type)
    whole_channel = (
        lax.all_gather(channel_local[0], "dp", axis=0, tiled=True),
        lax.all_gather(channel_local[1], "dp", axis=0, tiled=True),
        lax.all_gather(channel_local[2], "dp", axis=0, tiled=True),
    )
    w_in, w_out, c_in = whole_channel
    pre = (
        jnp.einsum("td,fd->tf", zed, w_in, preferred_element_type=wide) + c_in.astype(wide)[None, :]
    )
    act = gelu_exact(pre).astype(low_type)
    reduced = jnp.dot(act, w_out, preferred_element_type=wide)
    block_output = (middle + (reduced + c_four).reshape(count, patches, width)) * keep
    grad_top = cotangent * keep
    grad_branch = grad_top.reshape(rows, width).astype(low_type)
    grad_c_four = jnp.sum(grad_branch.astype(wide), axis=0)
    small_all = (
        lax.all_gather(small_local[0], "dp", axis=0, tiled=True),
        lax.all_gather(small_local[1], "dp", axis=0, tiled=True),
        lax.all_gather(small_local[2], "dp", axis=0, tiled=True),
        lax.all_gather(small_local[3], "dp", axis=0, tiled=True),
        lax.all_gather(small_local[4], "dp", axis=0, tiled=True),
        lax.all_gather(small_local[5], "dp", axis=0, tiled=True),
        lax.all_gather(small_local[6], "dp", axis=0, tiled=True),
    )
    tin = small_all[0].reshape(patches, hidden_tok)
    tout = small_all[1].reshape(hidden_tok, patches)
    g_one, b_one, g_two, b_two, c_four = [piece.astype(wide) for piece in small_all[2:]]
    whole_channel = (
        lax.all_gather(channel_local[0], "dp", axis=0, tiled=True),
        lax.all_gather(channel_local[1], "dp", axis=0, tiled=True),
        lax.all_gather(channel_local[2], "dp", axis=0, tiled=True),
    )
    w_in, w_out, c_in = whole_channel
    pre = (
        jnp.einsum("td,fd->tf", zed, w_in, preferred_element_type=wide) + c_in.astype(wide)[None, :]
    )
    act = gelu_exact(pre).astype(low_type)
    grad_act = jnp.einsum("td,fd->tf", grad_branch, w_out, preferred_element_type=wide)
    grad_pre = (grad_act * gelu_slope(pre)).astype(low_type)
    grad_zed = jnp.dot(grad_pre, w_in, preferred_element_type=wide)
    grad_in = jnp.einsum("tf,td->fd", grad_pre, zed, preferred_element_type=wide)
    grad_out = jnp.einsum("tf,td->fd", act, grad_branch, preferred_element_type=wide)
    grad_cin = jnp.sum(grad_pre.astype(wide), axis=0)
    grad_zed, grad_win, grad_wout, grad_cin = (grad_zed, grad_in, grad_out, grad_cin)
    grad_g_two = jnp.sum(grad_zed * normed_two, axis=0)
    grad_b_two = jnp.sum(grad_zed, axis=0)
    grad_mid = grad_top + norm_back(grad_zed, normed_two, scale_two, g_two).reshape(
        count, patches, width
    )
    grad_back = grad_mid.astype(low_type)
    grad_c_two = jnp.sum(grad_back.astype(wide), axis=(0, 2))
    grad_tout = jnp.einsum("bsd,bpd->sp", act_t, grad_back, preferred_element_type=wide)
    grad_act_t = jnp.einsum("sp,bpd->bsd", tout, grad_back, preferred_element_type=wide)
    grad_pre_t = (grad_act_t * gelu_slope(pre_t)).astype(low_type)
    grad_c_one = jnp.sum(grad_pre_t.astype(wide), axis=(0, 2))
    grad_tin = jnp.einsum("bpd,bsd->ps", mixed_in, grad_pre_t, preferred_element_type=wide)
    grad_mixed = jnp.einsum("ps,bsd->bpd", tin, grad_pre_t, preferred_element_type=wide)
    grad_g_one = jnp.sum(grad_mixed * normed_one, axis=(0, 1))
    grad_b_one = jnp.sum(grad_mixed, axis=(0, 1))
    image_grad = grad_mid + norm_back(grad_mixed, normed_one, scale_one, g_one)
    bias_sums = lax.psum((grad_c_one, grad_c_two), "dp")
    flat_tin = grad_tin.reshape(patches * hidden_tok)
    flat_tout = grad_tout.reshape(hidden_tok * patches)
    owned = (
        lax.psum_scatter(flat_tin, "dp", scatter_dimension=0, tiled=True),
        lax.psum_scatter(flat_tout, "dp", scatter_dimension=0, tiled=True),
        lax.psum_scatter(grad_g_one, "dp", scatter_dimension=0, tiled=True),
        lax.psum_scatter(grad_b_one, "dp", scatter_dimension=0, tiled=True),
        lax.psum_scatter(grad_g_two, "dp", scatter_dimension=0, tiled=True),
        lax.psum_scatter(grad_b_two, "dp", scatter_dimension=0, tiled=True),
        lax.psum_scatter(grad_win, "dp", scatter_dimension=0, tiled=True),
        lax.psum_scatter(grad_cin, "dp", scatter_dimension=0, tiled=True),
        lax.psum_scatter(grad_wout, "dp", scatter_dimension=0, tiled=True),
        lax.psum_scatter(grad_c_four, "dp", scatter_dimension=0, tiled=True),
    )
    (
        own_tin,
        own_tout,
        own_g_one,
        own_b_one,
        own_g_two,
        own_b_two,
        own_win,
        own_cin,
        own_wout,
        own_c_four,
    ) = owned
    return (
        block_output,
        image_grad,
        own_tin,
        own_tout,
        bias_sums[0],
        bias_sums[1],
        own_g_one,
        own_b_one,
        own_g_two,
        own_b_two,
        own_win,
        own_cin,
        own_wout,
        own_c_four,
    )


def solution(mesh):
    placed = (
        P("dp", None, None),
        P("dp"),
        P("dp", None, None),
        P("dp"),
        P("dp"),
        P(),
        P(),
        P("dp"),
        P("dp"),
        P("dp"),
        P("dp"),
        P("dp", None),
        P("dp"),
        P("dp", None),
        P("dp"),
    )
    return jax.shard_map(
        choose,
        mesh=mesh,
        in_specs=placed,
        out_specs=(
            P("dp", None, None),
            P("dp", None, None),
            P("dp"),
            P("dp"),
            P(),
            P(),
            P("dp"),
            P("dp"),
            P("dp"),
            P("dp"),
            P("dp", None),
            P("dp"),
            P("dp", None),
            P("dp"),
        ),
        check_vma=False,
    )
```

```python
import math

import jax
import jax.numpy as jnp
from jax import lax
from jax.experimental import pallas as pl
from jax.experimental.pallas import tpu as pltpu
from jax.sharding import PartitionSpec as P

EPS = 1e-06


def gelu_exact(v):
    return 0.5 * v * (1.0 + lax.erf(v * 0.7071067811865476))


def gelu_slope(v):
    return 0.5 * (1.0 + lax.erf(v * 0.7071067811865476)) + v * 0.3989422804014327 * jnp.exp(
        -0.5 * v * v
    )


def norm_parts(v):
    middle = jnp.mean(v, axis=-1, keepdims=True)
    centered = v - middle
    scale = lax.rsqrt(jnp.mean(centered * centered, axis=-1, keepdims=True) + EPS)
    return (centered * scale, middle, scale)


def normalize(v):
    centered = v - jnp.mean(v, axis=-1, keepdims=True)
    scale = lax.rsqrt(jnp.mean(centered * centered, axis=-1, keepdims=True) + EPS)
    return (centered * scale, scale)


def norm_back(grad_in, normed, scale, gain):
    scaled = grad_in * gain
    return scale * (
        scaled
        - jnp.mean(scaled, axis=-1, keepdims=True)
        - normed * jnp.mean(scaled * normed, axis=-1, keepdims=True)
    )


WIDE = jnp.float32
LOW = jnp.bfloat16
MESH = pl.DeviceIdType.MESH
NT = (((1,), (1,)), ((), ()))
TN = (((0,), (0,)), ((), ()))
NN = (((1,), (0,)), ((), ()))
PLANE = 8


def dot(a, b, dims):
    return lax.dot_general(a, b, dims, preferred_element_type=WIDE)


def gelu_parts(v):
    cdf = 0.5 * (1.0 + lax.erf(v * 0.7071067811865476))
    return v * cdf, cdf + v * 0.3989422804014327 * jnp.exp(-0.5 * v * v)


def padded(v, rows):
    return jnp.concatenate([v, jnp.zeros((rows - v.shape[0], v.shape[1]), v.dtype)], axis=0)


def block_kernel(
    mask,
    images,
    cotangent,
    w_in,
    w_out,
    tin_own,
    tout_own,
    gain_one_own,
    shift_one_own,
    gain_two_own,
    shift_two_own,
    c_four_own,
    c_in_own,
    c_one,
    c_two,
    total,
    grad_zed,
    grad_in,
    grad_out,
    small_out,
    biases_out,
    mixed,
    act_t,
    slope_t,
    mid,
    zed,
    top,
    weights,
    act,
    grad_pre,
    c_in_rel,
    own_sum,
    keep_sum,
    send_one,
    recv_one,
    send_two,
    recv_two,
    send_three,
    recv_three,
    send_four,
    recv_four,
    recv_far,
    tin,
    tin_t,
    tout,
    tout_t,
    vecs,
    c_in,
    lines,
    small_own,
    small_all,
    grad_tin,
    grad_tout,
    grad_vecs,
    grad_c_in,
    small_sum,
    small_core,
    small_plane,
    small_z,
    biases,
    biases_in,
    late,
    late_in,
    figures,
    in_sem,
    ag_send,
    ag_recv,
    rs_send,
    rs_recv,
    sg_send,
    sg_recv,
    ss_send,
    ss_recv,
    bs_send,
    bs_recv,
    ls_send,
    ls_recv,
):
    count, patches, width = images.shape
    planes = weights.shape[1]
    shard = w_in.shape[0]
    half = 4 * shard
    chunk = 8 * shard
    pad = mixed.shape[1]
    blocks = count // 2
    pair = zed.shape[0] // blocks
    lot = pair // 2
    me = lax.axis_index("dp")
    core = me % 2
    col = (me // 2) % 2
    row = (me // 4) % 2
    z = me // PLANE
    by_core = me + 1 - 2 * core
    by_x = me + 2 - 4 * col
    by_y = me + 4 - 8 * row
    by_both = by_x + by_y - me

    def plane_of(k):
        out, bit = z, 1
        while bit < planes:
            out = out + bit * ((k // bit) % 2) * (1 - 2 * ((z // bit) % 2))
            bit *= 2
        return out

    def by_z(k):
        return me + PLANE * (plane_of(k) - z)

    def ag(stage, k, mat):
        near, far = (by_x, by_y) if mat == 0 else (by_y, by_x)
        step = 1 if mat == 0 else 2
        if stage == 0:
            src, dst, size, to = 0, 0, shard, by_z(k)
            source = weights.at[mat, 0, pl.ds(src, size)]
        else:
            src, dst, size, to = {
                1: (0, step * shard, shard, near),
                2: (0, (3 - step) * shard, shard, far),
                3: (step * shard, 3 * shard, shard, far),
                4: (0, half, 3 * shard, by_core),
                5: (3 * shard, half + 3 * shard, shard, by_core),
            }[stage]
            source = weights.at[mat, k, pl.ds(src, size)]
        return pltpu.make_async_remote_copy(
            src_ref=source,
            dst_ref=weights.at[mat, k, pl.ds(dst, size)],
            send_sem=ag_send.at[stage, k, mat],
            recv_sem=ag_recv.at[stage, k, mat],
            device_id=(to,),
            device_id_type=MESH,
        )

    middle = ((z + 1) // 2) % 2

    def plane_at(i):
        last = planes - 1
        return (1 - middle) * ((i + 1) % planes) + middle * (i % last + last * ((last - i) // last))

    def rs(stage, i, mat):
        slot, k = i % 2, plane_at(i)
        near, far = (by_x, by_y) if mat == 0 else (by_y, by_x)
        src, dst, to = [
            lambda: (send_one.at[mat], recv_one.at[slot, mat], by_core),
            lambda: (
                send_two.at[mat, pl.ds(shard, shard)],
                recv_two.at[slot, mat, pl.ds(shard, shard)],
                near,
            ),
            lambda: (send_three.at[mat], recv_three.at[slot, mat], far),
            lambda: (send_four.at[slot, mat], recv_four.at[k - 1, mat], by_z(k)),
            lambda: (weights.at[mat, k, pl.ds(0, half)], recv_far.at[(k - 1) // 2, mat], by_z(k)),
            lambda: (send_two.at[mat, pl.ds(0, shard)], recv_two.at[slot, mat, pl.ds(0, shard)], near),
        ][stage]()
        at = k if stage in (3, 4) else i
        return pltpu.make_async_remote_copy(
            src_ref=src,
            dst_ref=dst,
            send_sem=rs_send.at[stage, at, mat],
            recv_sem=rs_recv.at[stage, at, mat],
            device_id=(to,),
            device_id_type=MESH,
        )

    def came_from(stage, k, mat):
        place = recv_four.at[k - 1, mat] if stage == 3 else recv_far.at[(k - 1) // 2, mat]
        pltpu.make_async_remote_copy(
            src_ref=place,
            dst_ref=place,
            send_sem=rs_send.at[stage, k, mat],
            recv_sem=rs_recv.at[stage, k, mat],
            device_id=(by_z(k),),
            device_id_type=MESH,
        ).wait_recv()
        return place[...].astype(WIDE)

    def small_gather(stage, k, group):
        src, dst, to = [
            lambda: (small_all.at[group, 0, 0], small_all.at[group, 0, k], by_z(k)),
            lambda: (small_all.at[group, 0], small_all.at[group, k], (me, by_x, by_y, by_both)[k]),
            lambda: (small_all.at[group, pl.ds(0, 4)], small_all.at[group, pl.ds(4, 4)], by_core),
        ][stage]()
        return pltpu.make_async_remote_copy(
            src_ref=src,
            dst_ref=dst,
            send_sem=sg_send.at[stage, k, group],
            recv_sem=sg_recv.at[stage, k, group],
            device_id=(to,),
            device_id_type=MESH,
        )

    def small_reduce(stage, k, group):
        src, dst, to = [
            lambda: (small_all.at[group, pl.ds(4, 4)], small_core.at[group], by_core),
            lambda: (small_all.at[group, k], small_plane.at[group, k], (me, by_x, by_y, by_both)[k]),
            lambda: (small_all.at[group, 0, k], small_z.at[k, group], by_z(k)),
        ][stage]()
        return pltpu.make_async_remote_copy(
            src_ref=src,
            dst_ref=dst,
            send_sem=ss_send.at[stage, k, group],
            recv_sem=ss_recv.at[stage, k, group],
            device_id=(to,),
            device_id_type=MESH,
        )

    def bias_reduce(stage, k):
        to = [lambda: by_core, lambda: (me, by_x, by_y, by_both)[k], lambda: by_z(k)][stage]()
        return pltpu.make_async_remote_copy(
            src_ref=biases.at[stage],
            dst_ref=biases_in.at[stage, k],
            send_sem=bs_send.at[stage, k],
            recv_sem=bs_recv.at[stage, k],
            device_id=(to,),
            device_id_type=MESH,
        )

    def late_reduce(stage, k):
        to = [lambda: by_core, lambda: (me, by_x, by_y, by_both)[k], lambda: by_z(k)][stage]()
        return pltpu.make_async_remote_copy(
            src_ref=late.at[stage],
            dst_ref=late_in.at[stage, k],
            send_sem=ls_send.at[stage, k],
            recv_sem=ls_recv.at[stage, k],
            device_id=(to,),
            device_id_type=MESH,
        )

    hidden_tok = c_one.shape[0]
    unit = math.gcd(tin_own.shape[0], hidden_tok)
    lines_in = tin_own.shape[0] // unit
    first_lines = (lines_in + 1) // 2
    lines_out = tout_own.shape[0] // patches
    own_vec = gain_one_own.shape[0]
    turns = hidden_tok // unit
    devices = planes * PLANE

    def place_of(d):
        dz, dy, dx, dc = d // PLANE, (d // 4) % 2, (d // 2) % 2, d % 2
        far = (dc + core) % 2 * 4 + (dy + row) % 2 * 2 + (dx + col) % 2
        k, bit = 0, 1
        while bit < planes:
            k = k + bit * ((dz // bit + z // bit) % 2)
            bit *= 2
        return far, k

    def load(b):
        return pltpu.make_async_copy(images.at[b], grad_zed.at[b], in_sem.at[0, b])

    def load_top(b):
        return pltpu.make_async_copy(cotangent.at[b], total.at[b], in_sem.at[1, b])

    def reload_image(b):
        return pltpu.make_async_copy(images.at[b], mid.at[b], in_sem.at[3, b])

    for b in range(count):
        load_top(b).start()
    for b in range(count):
        load(b).start()
    small_own[...] = jnp.zeros_like(small_own)
    for i in range(lines_in):
        at, lane = (i, 0) if i < first_lines else (i - first_lines, 64)
        small_own[at : at + 1, lane : lane + unit] = tin_own[i * unit : (i + 1) * unit].reshape(1, unit)
    for i, piece in enumerate((gain_one_own, shift_one_own, gain_two_own, shift_two_own, c_four_own)):
        small_own[24 + i : 25 + i, 64 : 64 + own_vec] = piece[...].reshape(1, own_vec)
    small_own[31:32, 0:shard] = c_in_own[...].reshape(1, shard)
    for i in range(lines_out):
        line = tout_own[i * patches : (i + 1) * patches].reshape(1, patches)
        small_own[32 + i : 33 + i, :] = line[:, 0:128]
        small_own[48 + i : 49 + i, 0 : patches - 128] = line[:, 128:patches]
    for group in range(2):
        small_all[group, 0, 0] = small_own[32 * group : 32 * (group + 1)].astype(LOW)
    weights[0, 0, 0:shard] = w_in[...].astype(LOW)
    weights[1, 0, 0:shard] = w_out[...].astype(LOW)

    barrier = pltpu.get_barrier_semaphore()
    peers = [by_core, by_x, by_y, by_both] + [by_z(k) for k in range(1, planes)]
    for peer in peers:
        pl.semaphore_signal(barrier, inc=1, device_id=(peer,), device_id_type=MESH)
    pl.semaphore_wait(barrier, len(peers))

    mats = (0, 1)
    inner = middle == 1

    def ag_pass(which, mat):
        src, dst, to = ((1, 2, by_z(3)), (3, 2, by_z(1)), (2, 3, by_z(1)))[which]
        return pltpu.make_async_remote_copy(
            src_ref=weights.at[mat, src, pl.ds(0, shard)],
            dst_ref=weights.at[mat, dst, pl.ds(0, shard)],
            send_sem=ag_send.at[6, which, mat],
            recv_sem=ag_recv.at[0, dst, mat],
            device_id=(to,),
            device_id_type=MESH,
        )

    def ag_planes():
        for mat in mats:
            ag(0, 1, mat).start()

        @pl.when(inner)
        def _():
            for mat in mats:
                ag(0, 3, mat).start()

    def ag_planes_pass():
        @pl.when(inner)
        def _():
            for which, came in ((0, 1), (1, 3)):
                for mat in mats:
                    ag(0, came, mat).wait_recv()
                    ag_pass(which, mat).start()

    def ag_planes_last():
        @pl.when(inner)
        def _():
            for mat in mats:
                ag(0, 2, mat).wait_recv()
                ag_pass(2, mat).start()

    def ag_direct(k):
        @pl.when(jnp.logical_not(inner))
        def _():
            for mat in mats:
                ag(0, k, mat).wait_recv()

        for stage in (1, 2):
            for mat in mats:
                ag(stage, k, mat).start()

    def ag_forward(k):
        for mat in mats:
            ag(1, k, mat).wait_recv()
            ag(3, k, mat).start()

    def ag_core(k):
        for mat in mats:
            ag(2, k, mat).wait_recv()
            ag(4, k, mat).start()

    def ag_core_last(k):
        for mat in mats:
            ag(3, k, mat).wait_recv()
            ag(5, k, mat).start()

    def ag_ready(k):
        for mat in mats:
            ag(4, k, mat).wait_recv()
            ag(5, k, mat).wait_recv()

    for group in range(2):
        for k in range(1, planes):
            small_gather(0, k, group).start()
    for mat in mats:
        ag(1, 0, mat).start()
    ag_planes()

    grad_vecs[...] = jnp.zeros_like(grad_vecs)
    grad_tin[...] = jnp.zeros_like(grad_tin)
    grad_tout[...] = jnp.zeros_like(grad_tout)

    def channel_top(r, carry):
        tops = []
        for h in range(2):
            b = 2 * r + h
            load_top(b).wait()
            tops.append(padded(total[b] * mask[b].astype(WIDE), lot))
        rounded = jnp.concatenate(tops, axis=0).astype(LOW)
        top[pl.ds(r * pair, pair), :] = rounded
        grad_vecs[2:3, :] += jnp.sum(rounded.astype(WIDE), axis=0, keepdims=True)
        return carry

    def first_norm(b, carry):
        load(b).wait()
        mid[b], figures[b, :, 0:1], figures[b, :, 1:2] = norm_parts(grad_zed[b])
        return carry

    lax.fori_loop(0, blocks, channel_top, 0)
    for group in range(2):
        for k in range(1, planes):
            small_gather(0, k, group).wait_recv()
        for k in range(1, 4):
            small_gather(1, k, group).start()
    lax.fori_loop(0, count, first_norm, 0)
    for k in range(1, 4):
        small_gather(1, k, 0).wait_recv()
    small_gather(2, 0, 0).start()

    tin[...] = jnp.zeros_like(tin)
    tout[...] = jnp.zeros_like(tout)

    def unpack(d, group):
        far, k = place_of(d)
        message = small_all[group, far, k].astype(WIDE)
        if group == 0:
            lines[d * lines_in : d * lines_in + first_lines, :] = message[0:first_lines, :]
            shifted = jnp.concatenate([message[0:24, 64:128], message[0:24, 0:64]], axis=1)
            lines[d * lines_in + first_lines : (d + 1) * lines_in, :] = shifted[0 : lines_in - first_lines, :]
            vecs[:, d * own_vec : (d + 1) * own_vec] = message[24:32, 64 : 64 + own_vec]
            c_in[d] = message[31:32, 0:shard]
        else:
            tout[d * lines_out : (d + 1) * lines_out, 0:128] = message[0:lines_out, :]
            tout[d * lines_out : (d + 1) * lines_out, 128:patches] = message[16 : 16 + lines_out, 0 : patches - 128]

    def unpack_half(own, group):
        for parity in range(2):

            @pl.when((core == parity) == own)
            def _():
                for d in range(parity, devices, 2):
                    unpack(d, group)

    unpack_half(True, 0)
    for k in range(1, 4):
        small_gather(1, k, 1).wait_recv()
    small_gather(2, 0, 1).start()
    unpack_half(True, 1)
    ag_planes_pass()
    ag_direct(plane_at(0))
    for group in range(2):
        small_gather(2, 0, group).wait_recv()
        unpack_half(False, group)
    for turn in range(turns):
        tin[0:patches, turn * unit : (turn + 1) * unit] = lines[pl.ds(turn, patches, stride=turns), :][:, 0:unit]
    for rest, into, at in ((c_one, tin, patches), (c_two, tout, hidden_tok)):
        rest = rest[...].reshape(1, rest.shape[0])
        for i in range(3):
            term = rest.astype(LOW).astype(WIDE)
            into[at + i : at + i + 1, 0 : rest.shape[1]] = term
            rest = rest - term
    tin_t[...] = tin[...].T.astype(LOW)
    tout_t[...] = tout[...].T.astype(LOW)
    ones = jnp.ones((3, width), WIDE)

    gain_one, shift_one = vecs[0:1, :], vecs[1:2, :]
    gain_two, shift_two, c_four = vecs[2:3, :], vecs[3:4, :], vecs[4:5, :]
    def singles(work, start, stop):
        def one(b, carry):
            work(b)
            return carry

        lax.fori_loop(start, stop, one, 0)

    def pairs(work, start, stop):
        def two(r, carry):
            for h in range(2):
                work(2 * r + h)
            return carry

        lax.fori_loop(start // 2, stop // 2, two, 0)

    def token_forward(b):
        fed = mid[b] * gain_one + shift_one
        mixed[b] = padded(jnp.concatenate([fed, ones], axis=0), pad).astype(LOW)
        value, slope = gelu_parts(dot(tin_t[...], mixed[b], NN))
        act_t[b] = padded(jnp.concatenate([value, ones], axis=0), act_t.shape[1]).astype(LOW)
        slope_t[b] = slope.astype(LOW)
        mid[b] = grad_zed[b] + dot(tout_t[...], act_t[b], NN)[0:patches]

    def channel_inputs(r, carry):
        parts = []
        for h in range(2):
            total[2 * r + h] = mid[2 * r + h] + c_four
            normed, _, figures[2 * r + h, :, 2:3] = norm_parts(mid[2 * r + h])
            mid[2 * r + h] = normed
            grad_zed[2 * r + h] = jnp.zeros((patches, width), WIDE)
            parts.append(padded(normed * gain_two + shift_two, lot))
        zed[pl.ds(r * pair, pair), :] = jnp.concatenate(parts, axis=0).astype(LOW)
        return carry

    first = 4
    singles(token_forward, 0, first)
    ag_forward(plane_at(0))
    singles(token_forward, first, count)
    ag_core(plane_at(0))
    ag_planes_last()
    lax.fori_loop(0, blocks, channel_inputs, 0)
    ag_direct(plane_at(1))
    for k in range(planes):
        for place in range(PLANE):
            near = plane_of(k) * PLANE + (
                (row + (place // 2) % 2) % 2 * 4 + (col + place % 2) % 2 * 2 + (core + place // 4) % 2
            )
            c_in_rel[k, :, place * shard : (place + 1) * shard] = c_in[near]

    ag_core_last(plane_at(0))

    def rs_two(i, mat):
        rs(0, i, mat).wait_recv()
        slot = i % 2
        first, second = (1, 3) if mat == 0 else (2, 3)

        def part(n):
            return slice(n * shard, (n + 1) * shard)

        @pl.when(i == 0)
        def _():
            weights[mat, plane_at(i), 0:half] = (own_sum[mat] + recv_one[slot, mat].astype(WIDE)).astype(LOW)
            rs(4, 0, mat).start()

        @pl.when((i == planes - 1) & inner)
        def _():
            own_sum[mat] += came_from(4, 1, mat) + came_from(4, 3, mat)

        @pl.when(i > 1)
        def _():
            for stage in (1, 5):
                rs(stage, i - 1, mat).wait_send()

        @pl.when(i > 0)
        def _():
            for n, to, stage in ((second, part(1), 1), (first, part(0), 5)):
                send_two[mat, to] = (own_sum[mat, part(n)] + recv_one[slot, mat, part(n)].astype(WIDE)).astype(LOW)
                rs(stage, i, mat).start()
            for n in (0, 3 - first):
                own_sum[mat, part(n)] += recv_one[slot, mat, part(n)].astype(WIDE)

    def rs_three(i):
        for mat in mats:
            rs(1, i, mat).wait_recv()
            other = 2 if mat == 0 else 1

            @pl.when(i > 1)
            def _():
                rs(2, i - 1, mat).wait_send()

            send_three[mat] = (
                own_sum[mat, other * shard : (other + 1) * shard]
                + recv_two[i % 2, mat, shard : 2 * shard].astype(WIDE)
            ).astype(LOW)
            rs(2, i, mat).start()

    def rs_keep(i):
        for mat in mats:
            rs(5, i, mat).wait_recv()
            keep_sum[mat] = own_sum[mat, 0:shard] + recv_two[i % 2, mat, 0:shard].astype(WIDE)

    def rs_four(i):
        for mat in mats:
            rs(2, i, mat).wait_recv()

            send_four[i % 2, mat] = (keep_sum[mat] + recv_three[i % 2, mat].astype(WIDE)).astype(LOW)
            rs(3, i, mat).start()

    def rs_last():
        last = planes - 1
        for mat in mats:
            result = grad_in if mat == 0 else grad_out
            rs(2, last, mat).wait_recv()
            summed = keep_sum[mat] + recv_three[last % 2, mat].astype(WIDE)
            result[...] = summed + came_from(3, 2, mat)

            @pl.when(jnp.logical_not(inner))
            def _():
                result[...] += came_from(3, 1, mat) + came_from(3, 3, mat)


    tile = chunk // 3

    def channel_chunk(i, carry):
        k = plane_at(i)

        @pl.when(i == planes - 1)
        def _():
            rs_four(1)

        ag_ready(k)

        def rows(r):
            for s in range(3):
                part = slice(s * tile, (s + 1) * tile)
                pre = dot(zed[r * pair : (r + 1) * pair, :], weights[0, k, part], NT) + c_in_rel[k, :, part]
                value, slope = gelu_parts(pre)
                act[r * pair : (r + 1) * pair, part] = value.astype(LOW)
                back = (dot(top[r * pair : (r + 1) * pair, :], weights[1, k, part], NT) * slope).astype(LOW)
                grad_pre[r * pair : (r + 1) * pair, part] = back
            up = dot(act[r * pair : (r + 1) * pair, :], weights[1, k], NN)
            down = dot(grad_pre[r * pair : (r + 1) * pair, :], weights[0, k], NN)
            for h in range(2):
                total[2 * r + h] += up[h * lot : h * lot + patches]
                grad_zed[2 * r + h] += down[h * lot : h * lot + patches]

        rows(0)

        @pl.when(i == 0)
        def _():
            ag_forward(plane_at(1))

        @pl.when(i == 1)
        def _():
            ag_forward(plane_at(2))
            ag_forward(0)

        for r in range(1, blocks):
            rows(r)

        @pl.when(i == 0)
        def _():
            ag_core(plane_at(1))
            ag_direct(plane_at(2))
            for mat in mats:
                ag(2, 0, mat).start()

        @pl.when(i == 1)
        def _():
            ag_core(plane_at(2))

        @pl.when(i == 2)
        def _():
            ag_core(0)
            ag_core_last(0)

        @pl.when(i > 1)
        def _():
            rs_three(i - 1)

        back_sum = jnp.sum(grad_pre[...].astype(WIDE), axis=0, keepdims=True)
        for place in range(PLANE):
            near = plane_of(k) * PLANE + (
                (row + (place // 2) % 2) % 2 * 4 + (col + place % 2) % 2 * 2 + (core + place // 4) % 2
            )
            grad_c_in[near] = back_sum[:, place * shard : (place + 1) * shard]

        @pl.when(i > 0)
        def _():
            for mat in mats:
                rs(0, i - 1, mat).wait_send()

        send_one[1] = dot(act[:, half:chunk], top[...], TN).astype(LOW)
        send_one[0] = dot(grad_pre[:, half:chunk], zed[...], TN).astype(LOW)
        for mat in mats:
            rs(0, i, mat).start()

        @pl.when(i > 1)
        def _():
            rs_keep(i - 1)

        @pl.when(i == 0)
        def _():
            for mat in mats:
                for stage in range(1, 6):
                    ag(stage, k, mat).wait_send()

                @pl.when(inner)
                def _():
                    ag_pass(1, mat).wait_send()

        own_sum[1] = dot(act[:, 0:half], top[...], TN)
        own_sum[0] = dot(grad_pre[:, 0:half], zed[...], TN)
        @pl.when(i < 2)
        def _():
            ag_core_last(plane_at(i + 1))

        for mat in mats:
            rs_two(i, mat)
        return carry

    lax.fori_loop(0, planes, channel_chunk, 0)

    tin_low = tin[...].astype(LOW)
    tout_low = tout[0:hidden_tok, :].astype(LOW)

    def kept(b):
        return weights.at[b // planes, b % planes, 0:pad]

    def middle_backward(b, above):
        normed = mid[b]
        down = grad_zed[b]
        grad_vecs[0:1, :] += jnp.sum(down * normed, axis=0, keepdims=True)
        grad_vecs[1:2, :] += jnp.sum(down, axis=0, keepdims=True)
        grad_mid = above + norm_back(down, normed, figures[b, :, 2:3], gain_two)
        grad_zed[b] = grad_mid
        back = padded(grad_mid, pad).astype(LOW)
        grad_tout[...] += dot(act_t[b], back, NT)
        slope_t[b] = (dot(tout_low, back, NN) * slope_t[b].astype(WIDE)).astype(LOW)
        grad_tin[:, 0:hidden_tok] += dot(mixed[b], slope_t[b], NT)

    def middle_pair(r, carry):
        above = top[pl.ds(r * pair, pair), :].astype(WIDE)
        for h in range(2):
            middle_backward(2 * r + h, above[h * lot : h * lot + patches])
        for h in range(2):
            reload_image(2 * r + h).start()
        return carry

    def image_norm(b):
        normed = (mid[b] - figures[b, :, 0:1]) * figures[b, :, 1:2]
        mid[b] = normed
        grad_mixed = dot(tin_low, slope_t[b], NN)
        kept(b)[...] = grad_mixed.astype(LOW)
        late[0, 0:1, :] += jnp.sum(grad_mixed[0:patches] * normed, axis=0, keepdims=True)
        late[0, 1:2, :] += jnp.sum(grad_mixed[0:patches], axis=0, keepdims=True)

    def image_backward(b):
        total[b] *= mask[b].astype(WIDE)
        grad_zed[b] += norm_back(kept(b)[...][0:patches].astype(WIDE), mid[b], figures[b, :, 1:2], gain_one)

    def small_first(group):
        for k in range(1, planes):
            small_gather(0, k, group).wait_send()
        for far in range(1, 4):
            small_gather(1, far, group).wait_send()
        small_gather(2, 0, group).wait_send()
        if group == 0:
            for turn in range(turns):
                lines[pl.ds(turn, patches, stride=turns), :] = grad_tin[0:patches, turn * unit : turn * unit + 128]
        for d in range(devices):
            far, k = place_of(d)
            message = small_sum.at[group, far, k]
            if group == 0:
                low = lines[d * lines_in : d * lines_in + first_lines, :]
                high = lines[d * lines_in + first_lines : (d + 1) * lines_in, :]
                message[0:first_lines, 0:64] = low[:, 0:64]
                message[0 : lines_in - first_lines, 64:128] = high[:, 0:64]
                message[24:27, 64 : 64 + own_vec] = grad_vecs[0:3, d * own_vec : (d + 1) * own_vec]
                message[31:32, 0:shard] = grad_c_in[d]
            else:
                message[0:lines_out, :] = grad_tout[d * lines_out : (d + 1) * lines_out, 0:128]
                message[16 : 16 + lines_out, 0 : patches - 128] = grad_tout[
                    d * lines_out : (d + 1) * lines_out, 128:patches
                ]
        for far in range(4, PLANE):
            small_all[group, far] = small_sum[group, far].astype(LOW)
        small_reduce(0, 0, group).start()
        if group == 0:
            biases[0] = jnp.zeros_like(biases[0])
            for i in range(hidden_tok // 128):
                biases[0, i : i + 1, :] = grad_tin[patches : patches + 1, i * 128 : (i + 1) * 128]
            biases[0, 3:4, :] = grad_tout[hidden_tok : hidden_tok + 1, 0:128]
            biases[0, 4:5, 0 : patches - 128] = grad_tout[hidden_tok : hidden_tok + 1, 128:patches]
            bias_reduce(0, 0).start()

    def small_second(group):
        small_reduce(0, 0, group).wait_recv()
        for far in range(4):
            small_sum[group, far] += small_core[group, far].astype(WIDE)
        for far in range(1, 4):
            small_all[group, far] = small_sum[group, far].astype(LOW)
            small_reduce(1, far, group).start()
        if group == 0:
            bias_reduce(0, 0).wait_recv()
            biases[1] = biases[0] + biases_in[0, 0]
            for far in range(1, 4):
                bias_reduce(1, far).start()

    def small_third(group):
        for far in range(1, 4):
            small_reduce(1, far, group).wait_recv()
            small_sum[group, 0] += small_plane[group, far].astype(WIDE)
        for k in range(1, planes):
            small_all[group, 0, k] = small_sum[group, 0, k].astype(LOW)
            small_reduce(2, k, group).start()
        if group == 0:
            for far in range(1, 4):
                bias_reduce(1, far).wait_recv()
            biases[2] = (biases[1] + biases_in[1, 1]) + (biases_in[1, 2] + biases_in[1, 3])
            for k in range(1, planes):
                bias_reduce(2, k).start()

    for mat in mats:
        for i in range(1, planes):
            for stage in range(1, 6):
                ag(stage, plane_at(i), mat).wait_send()
        ag(0, 1, mat).wait_send()
        rs(4, 0, mat).wait_send()

        @pl.when(inner)
        def _():
            ag(0, 3, mat).wait_send()
            for which in (0, 2):
                ag_pass(which, mat).wait_send()

    late[0] = jnp.zeros_like(late[0])
    rs_four(planes - 2)
    lax.fori_loop(0, blocks, middle_pair, 0)
    small_first(1)
    small_first(0)
    for b in range(count):
        reload_image(b).wait()
    pairs(image_norm, 0, 2)
    small_second(1)
    pairs(image_norm, 2, count)
    small_second(0)
    late_reduce(0, 0).start()
    pairs(image_backward, 0, 2)
    late_reduce(0, 0).wait_recv()
    late[1] = late[0] + late_in[0, 0]
    for far in range(1, 4):
        late_reduce(1, far).start()
    rs_three(planes - 1)
    rs_keep(planes - 1)
    small_third(1)
    pairs(image_backward, 2, count)
    small_third(0)
    late_sum = late[1]
    for far in range(1, 4):
        late_reduce(1, far).wait_recv()
        late_sum = late_sum + late_in[1, far]
    late[2] = late_sum
    for k in range(1, planes):
        late_reduce(2, k).start()
    rs_last()
    summed = [small_sum[group, 0, 0] for group in range(2)]
    tree = [biases[2]]
    for k in range(1, planes):
        for group in range(2):
            small_reduce(2, k, group).wait_recv()
        bias_reduce(2, k).wait_recv()
        summed = [summed[group] + small_z[k, group].astype(WIDE) for group in range(2)]
        tree.append(biases_in[2, k])
    for group in range(2):
        small_out[32 * group : 32 * (group + 1)] = summed[group]
    for k in range(1, planes):
        late_reduce(2, k).wait_recv()
        late_sum = late_sum + late_in[2, k]
    late_sum = pltpu.roll(padded(late_sum, 8), width - own_vec * me, 1)
    small_out[27:29, 64 : 64 + own_vec] = late_sum[0:2, 0:own_vec]
    while len(tree) > 1:
        tree = [tree[i] + tree[i + 1] for i in range(0, len(tree), 2)]
    biases_out[...] = tree[0]

    for mat in mats:
        for stage in (0, 1, 2, 5):
            rs(stage, planes - 1, mat).wait_send()
        for i in range(1, planes - 1):
            rs(3, i, mat).wait_send()
    late_reduce(0, 0).wait_send()
    for far in range(1, 4):
        late_reduce(1, far).wait_send()
    for k in range(1, planes):
        late_reduce(2, k).wait_send()
    bias_reduce(0, 0).wait_send()
    for far in range(1, 4):
        bias_reduce(1, far).wait_send()
    for k in range(1, planes):
        bias_reduce(2, k).wait_send()
    for group in range(2):
        small_reduce(0, 0, group).wait_send()
        for far in range(1, 4):
            small_reduce(1, far, group).wait_send()
        for k in range(1, planes):
            small_reduce(2, k, group).wait_send()


def finish_kernel(
    block_in,
    image_in,
    w_in,
    w_out,
    small,
    biases,
    block_out,
    image_out,
    w_in_out,
    w_out_out,
    tin,
    tout,
    gain_one,
    shift_one,
    gain_two,
    shift_two,
    c_four,
    c_in,
    c_one,
    c_two,
    sem,
):
    pieces = [(block_in.at[b], block_out.at[b]) for b in range(block_in.shape[0])]
    pieces += [(image_in.at[b], image_out.at[b]) for b in range(image_in.shape[0])]
    pieces += [(w_in, w_in_out), (w_out, w_out_out)]
    copies = [pltpu.make_async_copy(a, b, sem.at[i]) for i, (a, b) in enumerate(pieces)]
    for copy in copies:
        copy.start()
    hidden_tok, patches = c_one.shape[0], c_two.shape[0]
    unit = math.gcd(tin.shape[0], hidden_tok)
    lines_in = tin.shape[0] // unit
    first_lines = (lines_in + 1) // 2
    for i in range(lines_in):
        at, lane = (i, 0) if i < first_lines else (i - first_lines, 64)
        tin[i * unit : (i + 1) * unit] = small[at : at + 1, lane : lane + unit].reshape(unit)
    for i in range(tout.shape[0] // patches):
        tout[i * patches : i * patches + 128] = small[32 + i : 33 + i, :].reshape(128)
        tout[i * patches + 128 : (i + 1) * patches] = small[48 + i : 49 + i, 0 : patches - 128].reshape(
            patches - 128
        )
    for i, piece in enumerate((gain_two, shift_two, c_four, gain_one, shift_one)):
        own_vec = piece.shape[0]
        piece[...] = small[24 + i : 25 + i, 64 : 64 + own_vec].reshape(own_vec)
    shard = c_in.shape[0]
    c_in[...] = small[31:32, 0:shard].reshape(shard)
    for i in range(hidden_tok // 128):
        c_one[i * 128 : (i + 1) * 128] = biases[i : i + 1, :].reshape(128)
    c_two[0:128] = biases[3:4, :].reshape(128)
    c_two[128:patches] = biases[4:5, 0 : patches - 128].reshape(patches - 128)
    for copy in copies:
        copy.wait()


def fast_shards(
    images,
    mask,
    cotangent,
    w_token_in,
    w_token_out,
    bias_token_in,
    bias_token_out,
    gain_one,
    shift_one,
    gain_two,
    shift_two,
    w_expand,
    bias_expand,
    w_reduce,
    bias_reduce,
):
    devices = lax.axis_size("dp")
    planes = devices // PLANE
    count, patches, width = images.shape
    hidden_tok = bias_token_in.shape[0]
    shard = w_expand.shape[0]
    pad = -(-patches // 16) * 16
    lot = -(-patches // 8) * 8
    pair = 2 * lot
    blocks = count // 2
    chunk = 8 * shard
    half = 4 * shard

    unit = math.gcd(w_token_in.shape[0], hidden_tok)
    lines_in = w_token_in.shape[0] // unit
    hidden_pad = hidden_tok + 16

    owned = (
        w_expand,
        w_reduce,
        w_token_in,
        w_token_out,
        gain_one,
        shift_one,
        gain_two,
        shift_two,
        bias_reduce,
        bias_expand,
        bias_token_in,
        bias_token_out,
    )
    vmem = pl.BlockSpec(memory_space=pltpu.VMEM)
    hbm = pl.BlockSpec(memory_space=pl.ANY)
    shape = jax.ShapeDtypeStruct
    outs = pl.pallas_call(
        block_kernel,
        out_shape=(
            pltpu.VMEM(images.shape, WIDE),
            pltpu.VMEM(images.shape, WIDE),
            pltpu.VMEM(w_expand.shape, WIDE),
            pltpu.VMEM(w_reduce.shape, WIDE),
            pltpu.VMEM((64, 128), WIDE),
            pltpu.VMEM((8, 128), WIDE),
        ),
        in_specs=[pl.BlockSpec(memory_space=pltpu.SMEM), hbm, hbm] + [vmem] * 12,
        out_specs=[vmem] * 6,
        scratch_shapes=[
            pltpu.VMEM((count, pad, width), LOW),
            pltpu.VMEM((count, hidden_pad, width), LOW),
            pltpu.VMEM((count, hidden_tok, width), LOW),
            pltpu.VMEM(images.shape, WIDE),
            pltpu.VMEM((blocks * pair, width), LOW),
            pltpu.VMEM((blocks * pair, width), LOW),
            pltpu.VMEM((2, planes, chunk, width), LOW),
            pltpu.VMEM((blocks * pair, chunk), LOW),
            pltpu.VMEM((blocks * pair, chunk), LOW),
            pltpu.VMEM((planes, 1, chunk), WIDE),
            pltpu.VMEM((2, half, width), WIDE),
            pltpu.VMEM((2, shard, width), WIDE),
            pltpu.VMEM((2, half, width), LOW),
            pltpu.VMEM((2, 2, half, width), LOW),
            pltpu.VMEM((2, 2 * shard, width), LOW),
            pltpu.VMEM((2, 2, 2 * shard, width), LOW),
            pltpu.VMEM((2, shard, width), LOW),
            pltpu.VMEM((2, 2, shard, width), LOW),
            pltpu.VMEM((2, 2, shard, width), LOW),
            pltpu.VMEM((planes - 1, 2, shard, width), LOW),
            pltpu.VMEM((2, 2, half, width), LOW),
            pltpu.VMEM((pad, hidden_tok), WIDE),
            pltpu.VMEM((hidden_tok, pad), LOW),
            pltpu.VMEM((hidden_pad, pad), WIDE),
            pltpu.VMEM((pad, hidden_pad), LOW),
            pltpu.VMEM((8, width), WIDE),
            pltpu.VMEM((devices, 1, shard), WIDE),
            pltpu.VMEM((devices * lines_in, 128), WIDE),
            pltpu.VMEM((64, 128), WIDE),
            pltpu.VMEM((2, PLANE, planes, 32, 128), LOW),
            pltpu.VMEM((pad, hidden_tok + 128), WIDE),
            pltpu.VMEM((hidden_pad, pad), WIDE),
            pltpu.VMEM((8, width), WIDE),
            pltpu.VMEM((devices, 1, shard), WIDE),
            pltpu.VMEM((2, PLANE, planes, 32, 128), WIDE),
            pltpu.VMEM((2, 4, planes, 32, 128), LOW),
            pltpu.VMEM((2, 4, planes, 32, 128), LOW),
            pltpu.VMEM((planes, 2, 32, 128), LOW),
            pltpu.VMEM((3, 8, 128), WIDE),
            pltpu.VMEM((3, max(4, planes), 8, 128), WIDE),
            pltpu.VMEM((3, 2, width), WIDE),
            pltpu.VMEM((3, max(4, planes), 2, width), WIDE),
            pltpu.VMEM((count, patches, 4), WIDE),
            pltpu.SemaphoreType.DMA((4, count)),
            pltpu.SemaphoreType.DMA((7, planes, 2)),
            pltpu.SemaphoreType.DMA((7, planes, 2)),
            pltpu.SemaphoreType.DMA((6, planes, 2)),
            pltpu.SemaphoreType.DMA((6, planes, 2)),
        ]
        + [pltpu.SemaphoreType.DMA((3, max(4, planes), 2))] * 4
        + [pltpu.SemaphoreType.DMA((3, max(4, planes)))] * 4,
        compiler_params=pltpu.CompilerParams(
            collective_id=0, has_side_effects=True, vmem_limit_bytes=56 * 2**20
        ),
    )(
        mask,
        images,
        cotangent,
        *owned,
    )
    flat = pl.pallas_call(
        finish_kernel,
        out_shape=(
            shape(images.shape, WIDE),
            shape(images.shape, WIDE),
            shape(w_expand.shape, WIDE),
            shape(w_reduce.shape, WIDE),
            shape(w_token_in.shape, WIDE),
            shape(w_token_out.shape, WIDE),
            *[shape(gain_one.shape, WIDE)] * 5,
            shape(bias_expand.shape, WIDE),
            shape(bias_token_in.shape, WIDE),
            shape(bias_token_out.shape, WIDE),
        ),
        in_specs=[vmem] * 6,
        out_specs=[hbm] * 4 + [vmem] * 10,
        scratch_shapes=[pltpu.SemaphoreType.DMA((2 * count + 2,))],
        compiler_params=pltpu.CompilerParams(vmem_limit_bytes=16 * 2**20),
    )(*outs)
    block_output, image_grad, own_win, own_wout, *rest = flat
    g_tin, g_tout, g_one, b_one, g_two, b_two, c_four, c_in, c_one, c_two = rest
    return (
        block_output,
        image_grad,
        g_tin,
        g_tout,
        c_one,
        c_two,
        g_one,
        b_one,
        g_two,
        b_two,
        own_win,
        c_in,
        own_wout,
        c_four,
    )


def fits(devices, images, w_token_in, w_token_out, bias_token_in, gain_one, w_expand):
    planes = devices // PLANE
    patches = images.shape[1]
    hidden_tok = bias_token_in.shape[0]
    shard = w_expand.shape[0]
    unit = math.gcd(w_token_in.shape[0], hidden_tok)
    return (
        devices % PLANE == 0
        and planes == 4
        and images.shape[0] % 2 == 0
        and 6 <= images.shape[0] <= 2 * planes
        and shard % 16 == 0
        and shard <= 128
        and (4 * shard) % 128 == 0
        and 128 < patches <= 205
        and unit <= 64
        and w_token_in.shape[0] // unit <= 49
        and w_token_out.shape[0] % patches == 0
        and w_token_out.shape[0] // patches <= 16
        and gain_one.shape[0] <= 64
        and hidden_tok == 384
    )


def choose(
    images,
    mask,
    cotangent,
    w_token_in,
    w_token_out,
    bias_token_in,
    bias_token_out,
    gain_one,
    shift_one,
    gain_two,
    shift_two,
    w_expand,
    bias_expand,
    w_reduce,
    bias_reduce,
):
    args = (
        images,
        mask,
        cotangent,
        w_token_in,
        w_token_out,
        bias_token_in,
        bias_token_out,
        gain_one,
        shift_one,
        gain_two,
        shift_two,
        w_expand,
        bias_expand,
        w_reduce,
        bias_reduce,
    )
    if fits(lax.axis_size("dp"), images, w_token_in, w_token_out, bias_token_in, gain_one, w_expand):
        return fast_shards(*args)
    return shards(*args)


def shards(
    images,
    mask,
    cotangent,
    w_token_in,
    w_token_out,
    bias_token_in,
    bias_token_out,
    gain_one,
    shift_one,
    gain_two,
    shift_two,
    w_expand,
    bias_expand,
    w_reduce,
    bias_reduce,
):
    low_type = jnp.bfloat16
    wide = jnp.float32
    count, patches, width = images.shape
    hidden_tok = bias_token_in.shape[0]
    rows = count * patches
    keep = mask.astype(wide)[:, None, None]
    small_local = (
        w_token_in.astype(low_type),
        w_token_out.astype(low_type),
        gain_one.astype(low_type),
        shift_one.astype(low_type),
        gain_two.astype(low_type),
        shift_two.astype(low_type),
        bias_reduce.astype(low_type),
    )
    channel_local = (
        w_expand.astype(low_type),
        w_reduce.astype(low_type),
        bias_expand.astype(low_type),
    )
    small_all = (
        lax.all_gather(small_local[0], "dp", axis=0, tiled=True),
        lax.all_gather(small_local[1], "dp", axis=0, tiled=True),
        lax.all_gather(small_local[2], "dp", axis=0, tiled=True),
        lax.all_gather(small_local[3], "dp", axis=0, tiled=True),
        lax.all_gather(small_local[4], "dp", axis=0, tiled=True),
        lax.all_gather(small_local[5], "dp", axis=0, tiled=True),
        lax.all_gather(small_local[6], "dp", axis=0, tiled=True),
    )
    tin = small_all[0].reshape(patches, hidden_tok)
    tout = small_all[1].reshape(hidden_tok, patches)
    g_one, b_one, g_two, b_two, c_four = [piece.astype(wide) for piece in small_all[2:]]
    normed_one, scale_one = normalize(images)
    mixed_in = (normed_one * g_one + b_one).astype(low_type)
    pre_t = (
        jnp.einsum("ps,bpd->bsd", tin, mixed_in, preferred_element_type=wide)
        + bias_token_in[None, :, None]
    )
    act_t = gelu_exact(pre_t).astype(low_type)
    middle = (
        images
        + jnp.einsum("sp,bsd->bpd", tout, act_t, preferred_element_type=wide)
        + bias_token_out[None, :, None]
    )
    normed_two, scale_two = normalize(middle.reshape(rows, width))
    zed = (normed_two * g_two + b_two).astype(low_type)
    whole_channel = (
        lax.all_gather(channel_local[0], "dp", axis=0, tiled=True),
        lax.all_gather(channel_local[1], "dp", axis=0, tiled=True),
        lax.all_gather(channel_local[2], "dp", axis=0, tiled=True),
    )
    w_in, w_out, c_in = whole_channel
    pre = (
        jnp.einsum("td,fd->tf", zed, w_in, preferred_element_type=wide) + c_in.astype(wide)[None, :]
    )
    act = gelu_exact(pre).astype(low_type)
    reduced = jnp.dot(act, w_out, preferred_element_type=wide)
    block_output = (middle + (reduced + c_four).reshape(count, patches, width)) * keep
    grad_top = cotangent * keep
    grad_branch = grad_top.reshape(rows, width).astype(low_type)
    grad_c_four = jnp.sum(grad_branch.astype(wide), axis=0)
    small_all = (
        lax.all_gather(small_local[0], "dp", axis=0, tiled=True),
        lax.all_gather(small_local[1], "dp", axis=0, tiled=True),
        lax.all_gather(small_local[2], "dp", axis=0, tiled=True),
        lax.all_gather(small_local[3], "dp", axis=0, tiled=True),
        lax.all_gather(small_local[4], "dp", axis=0, tiled=True),
        lax.all_gather(small_local[5], "dp", axis=0, tiled=True),
        lax.all_gather(small_local[6], "dp", axis=0, tiled=True),
    )
    tin = small_all[0].reshape(patches, hidden_tok)
    tout = small_all[1].reshape(hidden_tok, patches)
    g_one, b_one, g_two, b_two, c_four = [piece.astype(wide) for piece in small_all[2:]]
    whole_channel = (
        lax.all_gather(channel_local[0], "dp", axis=0, tiled=True),
        lax.all_gather(channel_local[1], "dp", axis=0, tiled=True),
        lax.all_gather(channel_local[2], "dp", axis=0, tiled=True),
    )
    w_in, w_out, c_in = whole_channel
    pre = (
        jnp.einsum("td,fd->tf", zed, w_in, preferred_element_type=wide) + c_in.astype(wide)[None, :]
    )
    act = gelu_exact(pre).astype(low_type)
    grad_act = jnp.einsum("td,fd->tf", grad_branch, w_out, preferred_element_type=wide)
    grad_pre = (grad_act * gelu_slope(pre)).astype(low_type)
    grad_zed = jnp.dot(grad_pre, w_in, preferred_element_type=wide)
    grad_in = jnp.einsum("tf,td->fd", grad_pre, zed, preferred_element_type=wide)
    grad_out = jnp.einsum("tf,td->fd", act, grad_branch, preferred_element_type=wide)
    grad_cin = jnp.sum(grad_pre.astype(wide), axis=0)
    grad_zed, grad_win, grad_wout, grad_cin = (grad_zed, grad_in, grad_out, grad_cin)
    grad_g_two = jnp.sum(grad_zed * normed_two, axis=0)
    grad_b_two = jnp.sum(grad_zed, axis=0)
    grad_mid = grad_top + norm_back(grad_zed, normed_two, scale_two, g_two).reshape(
        count, patches, width
    )
    grad_back = grad_mid.astype(low_type)
    grad_c_two = jnp.sum(grad_back.astype(wide), axis=(0, 2))
    grad_tout = jnp.einsum("bsd,bpd->sp", act_t, grad_back, preferred_element_type=wide)
    grad_act_t = jnp.einsum("sp,bpd->bsd", tout, grad_back, preferred_element_type=wide)
    grad_pre_t = (grad_act_t * gelu_slope(pre_t)).astype(low_type)
    grad_c_one = jnp.sum(grad_pre_t.astype(wide), axis=(0, 2))
    grad_tin = jnp.einsum("bpd,bsd->ps", mixed_in, grad_pre_t, preferred_element_type=wide)
    grad_mixed = jnp.einsum("ps,bsd->bpd", tin, grad_pre_t, preferred_element_type=wide)
    grad_g_one = jnp.sum(grad_mixed * normed_one, axis=(0, 1))
    grad_b_one = jnp.sum(grad_mixed, axis=(0, 1))
    image_grad = grad_mid + norm_back(grad_mixed, normed_one, scale_one, g_one)
    bias_sums = lax.psum((grad_c_one, grad_c_two), "dp")
    flat_tin = grad_tin.reshape(patches * hidden_tok)
    flat_tout = grad_tout.reshape(hidden_tok * patches)
    owned = (
        lax.psum_scatter(flat_tin, "dp", scatter_dimension=0, tiled=True),
        lax.psum_scatter(flat_tout, "dp", scatter_dimension=0, tiled=True),
        lax.psum_scatter(grad_g_one, "dp", scatter_dimension=0, tiled=True),
        lax.psum_scatter(grad_b_one, "dp", scatter_dimension=0, tiled=True),
        lax.psum_scatter(grad_g_two, "dp", scatter_dimension=0, tiled=True),
        lax.psum_scatter(grad_b_two, "dp", scatter_dimension=0, tiled=True),
        lax.psum_scatter(grad_win, "dp", scatter_dimension=0, tiled=True),
        lax.psum_scatter(grad_cin, "dp", scatter_dimension=0, tiled=True),
        lax.psum_scatter(grad_wout, "dp", scatter_dimension=0, tiled=True),
        lax.psum_scatter(grad_c_four, "dp", scatter_dimension=0, tiled=True),
    )
    (
        own_tin,
        own_tout,
        own_g_one,
        own_b_one,
        own_g_two,
        own_b_two,
        own_win,
        own_cin,
        own_wout,
        own_c_four,
    ) = owned
    return (
        block_output,
        image_grad,
        own_tin,
        own_tout,
        bias_sums[0],
        bias_sums[1],
        own_g_one,
        own_b_one,
        own_g_two,
        own_b_two,
        own_win,
        own_cin,
        own_wout,
        own_c_four,
    )


def solution(mesh):
    placed = (
        P("dp", None, None),
        P("dp"),
        P("dp", None, None),
        P("dp"),
        P("dp"),
        P(),
        P(),
        P("dp"),
        P("dp"),
        P("dp"),
        P("dp"),
        P("dp", None),
        P("dp"),
        P("dp", None),
        P("dp"),
    )
    return jax.shard_map(
        choose,
        mesh=mesh,
        in_specs=placed,
        out_specs=(
            P("dp", None, None),
            P("dp", None, None),
            P("dp"),
            P("dp"),
            P(),
            P(),
            P("dp"),
            P("dp"),
            P("dp"),
            P("dp"),
            P("dp", None),
            P("dp"),
            P("dp", None),
            P("dp"),
        ),
        check_vma=False,
    )
```

```python
import math

import jax
import jax.numpy as jnp
from jax import lax
from jax.experimental import pallas as pl
from jax.experimental.pallas import tpu as pltpu
from jax.sharding import PartitionSpec as P

EPS = 1e-06


def gelu_exact(v):
    return 0.5 * v * (1.0 + lax.erf(v * 0.7071067811865476))


def gelu_slope(v):
    return 0.5 * (1.0 + lax.erf(v * 0.7071067811865476)) + v * 0.3989422804014327 * jnp.exp(
        -0.5 * v * v
    )


def norm_parts(v):
    middle = jnp.mean(v, axis=-1, keepdims=True)
    centered = v - middle
    scale = lax.rsqrt(jnp.mean(centered * centered, axis=-1, keepdims=True) + EPS)
    return (centered * scale, middle, scale)


def normalize(v):
    centered = v - jnp.mean(v, axis=-1, keepdims=True)
    scale = lax.rsqrt(jnp.mean(centered * centered, axis=-1, keepdims=True) + EPS)
    return (centered * scale, scale)


def norm_back(grad_in, normed, scale, gain):
    scaled = grad_in * gain
    return scale * (
        scaled
        - jnp.mean(scaled, axis=-1, keepdims=True)
        - normed * jnp.mean(scaled * normed, axis=-1, keepdims=True)
    )


WIDE = jnp.float32
LOW = jnp.bfloat16
MESH = pl.DeviceIdType.MESH
NT = (((1,), (1,)), ((), ()))
TN = (((0,), (0,)), ((), ()))
NN = (((1,), (0,)), ((), ()))
PLANE = 8


def dot(a, b, dims):
    return lax.dot_general(a, b, dims, preferred_element_type=WIDE)


def gelu_parts(v):
    cdf = 0.5 * (1.0 + lax.erf(v * 0.7071067811865476))
    return v * cdf, cdf + v * 0.3989422804014327 * jnp.exp(-0.5 * v * v)


def padded(v, rows):
    return jnp.concatenate([v, jnp.zeros((rows - v.shape[0], v.shape[1]), v.dtype)], axis=0)


def block_kernel(
    mask,
    images,
    cotangent,
    w_in,
    w_out,
    tin_own,
    tout_own,
    gain_one_own,
    shift_one_own,
    gain_two_own,
    shift_two_own,
    c_four_own,
    c_in_own,
    c_one,
    c_two,
    total,
    grad_zed,
    grad_in,
    grad_out,
    small_out,
    biases_out,
    mixed,
    act_t,
    slope_t,
    mid,
    zed,
    top,
    weights,
    act,
    grad_pre,
    c_in_rel,
    own_sum,
    keep_sum,
    send_one,
    recv_one,
    send_two,
    recv_two,
    send_three,
    recv_three,
    send_four,
    recv_four,
    recv_far,
    tin,
    tin_t,
    tout,
    tout_t,
    vecs,
    c_in,
    lines,
    small_own,
    small_all,
    grad_tin,
    grad_tout,
    grad_vecs,
    grad_c_in,
    small_sum,
    small_core,
    small_plane,
    small_z,
    biases,
    biases_in,
    late,
    late_in,
    figures,
    in_sem,
    ag_send,
    ag_recv,
    ah_send,
    ah_recv,
    rs_send,
    rs_recv,
    sg_send,
    sg_recv,
    ss_send,
    ss_recv,
    bs_send,
    bs_recv,
    ls_send,
    ls_recv,
):
    count, patches, width = images.shape
    planes = weights.shape[1]
    shard = w_in.shape[0]
    half = 4 * shard
    chunk = 8 * shard
    pad = mixed.shape[1]
    blocks = count // 2
    pair = zed.shape[0] // blocks
    lot = pair // 2
    me = lax.axis_index("dp")
    core = me % 2
    col = (me // 2) % 2
    row = (me // 4) % 2
    z = me // PLANE
    by_core = me + 1 - 2 * core
    by_x = me + 2 - 4 * col
    by_y = me + 4 - 8 * row
    by_both = by_x + by_y - me

    def plane_of(k):
        out, bit = z, 1
        while bit < planes:
            out = out + bit * ((k // bit) % 2) * (1 - 2 * ((z // bit) % 2))
            bit *= 2
        return out

    def by_z(k):
        return me + PLANE * (plane_of(k) - z)

    def ag(stage, k, mat):
        near, far = (by_x, by_y) if mat == 0 else (by_y, by_x)
        step = 1 if mat == 0 else 2
        if stage == 0:
            src, dst, size, to = 0, 0, shard, by_z(k)
            source = weights.at[mat, 0, pl.ds(src, size)]
        else:
            src, dst, size, to = {
                1: (0, step * shard, shard, near),
                2: (0, (3 - step) * shard, shard, far),
                3: (step * shard, 3 * shard, shard, far),
                4: (0, half, 3 * shard, by_core),
                5: (3 * shard, half + 3 * shard, shard, by_core),
            }[stage]
            source = weights.at[mat, k, pl.ds(src, size)]
        return pltpu.make_async_remote_copy(
            src_ref=source,
            dst_ref=weights.at[mat, k, pl.ds(dst, size)],
            send_sem=ag_send.at[stage, k, mat],
            recv_sem=ag_recv.at[stage, k, mat],
            device_id=(to,),
            device_id_type=MESH,
        )

    middle = ((z + 1) // 2) % 2

    def plane_at(i):
        last = planes - 1
        return (1 - middle) * ((i + 1) % planes) + middle * (i % last + last * ((last - i) // last))

    def rs(stage, i, mat):
        slot, k = i % 2, plane_at(i)
        near, far = (by_x, by_y) if mat == 0 else (by_y, by_x)
        src, dst, to = [
            lambda: (send_one.at[mat], recv_one.at[slot, mat], by_core),
            lambda: (
                send_two.at[mat, pl.ds(shard, shard)],
                recv_two.at[slot, mat, pl.ds(shard, shard)],
                near,
            ),
            lambda: (send_three.at[mat], recv_three.at[slot, mat], far),
            lambda: (send_four.at[slot, mat], recv_four.at[k - 1, mat], by_z(k)),
            lambda: (weights.at[mat, k, pl.ds(0, half)], recv_far.at[(k - 1) // 2, mat], by_z(k)),
            lambda: (send_two.at[mat, pl.ds(0, shard)], recv_two.at[slot, mat, pl.ds(0, shard)], near),
        ][stage]()
        at = k if stage in (3, 4) else i
        return pltpu.make_async_remote_copy(
            src_ref=src,
            dst_ref=dst,
            send_sem=rs_send.at[stage, at, mat],
            recv_sem=rs_recv.at[stage, at, mat],
            device_id=(to,),
            device_id_type=MESH,
        )

    def came_from(stage, k, mat):
        place = recv_four.at[k - 1, mat] if stage == 3 else recv_far.at[(k - 1) // 2, mat]
        pltpu.make_async_remote_copy(
            src_ref=place,
            dst_ref=place,
            send_sem=rs_send.at[stage, k, mat],
            recv_sem=rs_recv.at[stage, k, mat],
            device_id=(by_z(k),),
            device_id_type=MESH,
        ).wait_recv()
        return place[...].astype(WIDE)

    def small_gather(stage, k, group):
        src, dst, to = [
            lambda: (small_all.at[group, 0, 0], small_all.at[group, 0, k], by_z(k)),
            lambda: (small_all.at[group, 0], small_all.at[group, k], (me, by_x, by_y, by_both)[k]),
            lambda: (small_all.at[group, pl.ds(0, 4)], small_all.at[group, pl.ds(4, 4)], by_core),
        ][stage]()
        return pltpu.make_async_remote_copy(
            src_ref=src,
            dst_ref=dst,
            send_sem=sg_send.at[stage, k, group],
            recv_sem=sg_recv.at[stage, k, group],
            device_id=(to,),
            device_id_type=MESH,
        )

    def small_reduce(stage, k, group):
        src, dst, to = [
            lambda: (small_all.at[group, pl.ds(4, 4)], small_core.at[group], by_core),
            lambda: (small_all.at[group, k], small_plane.at[group, k], (me, by_x, by_y, by_both)[k]),
            lambda: (small_all.at[group, 0, k], small_z.at[k, group], by_z(k)),
        ][stage]()
        return pltpu.make_async_remote_copy(
            src_ref=src,
            dst_ref=dst,
            send_sem=ss_send.at[stage, k, group],
            recv_sem=ss_recv.at[stage, k, group],
            device_id=(to,),
            device_id_type=MESH,
        )

    def bias_reduce(stage, k):
        to = [lambda: by_core, lambda: (me, by_x, by_y, by_both)[k], lambda: by_z(k)][stage]()
        return pltpu.make_async_remote_copy(
            src_ref=biases.at[stage],
            dst_ref=biases_in.at[stage, k],
            send_sem=bs_send.at[stage, k],
            recv_sem=bs_recv.at[stage, k],
            device_id=(to,),
            device_id_type=MESH,
        )

    def late_reduce(stage, k):
        to = [lambda: by_core, lambda: (me, by_x, by_y, by_both)[k], lambda: by_z(k)][stage]()
        return pltpu.make_async_remote_copy(
            src_ref=late.at[stage],
            dst_ref=late_in.at[stage, k],
            send_sem=ls_send.at[stage, k],
            recv_sem=ls_recv.at[stage, k],
            device_id=(to,),
            device_id_type=MESH,
        )

    hidden_tok = c_one.shape[0]
    unit = math.gcd(tin_own.shape[0], hidden_tok)
    lines_in = tin_own.shape[0] // unit
    first_lines = (lines_in + 1) // 2
    lines_out = tout_own.shape[0] // patches
    own_vec = gain_one_own.shape[0]
    turns = hidden_tok // unit
    devices = planes * PLANE

    def place_of(d):
        dz, dy, dx, dc = d // PLANE, (d // 4) % 2, (d // 2) % 2, d % 2
        far = (dc + core) % 2 * 4 + (dy + row) % 2 * 2 + (dx + col) % 2
        k, bit = 0, 1
        while bit < planes:
            k = k + bit * ((dz // bit + z // bit) % 2)
            bit *= 2
        return far, k

    def load(b):
        return pltpu.make_async_copy(images.at[b], grad_zed.at[b], in_sem.at[0, b])

    def load_top(b):
        return pltpu.make_async_copy(cotangent.at[b], total.at[b], in_sem.at[1, b])

    def reload_image(b):
        return pltpu.make_async_copy(images.at[b], mid.at[b], in_sem.at[3, b])

    for b in range(count):
        load_top(b).start()
    for b in range(count):
        load(b).start()
    small_own[...] = jnp.zeros_like(small_own)
    for i in range(lines_in):
        at, lane = (i, 0) if i < first_lines else (i - first_lines, 64)
        small_own[at : at + 1, lane : lane + unit] = tin_own[i * unit : (i + 1) * unit].reshape(1, unit)
    for i, piece in enumerate((gain_one_own, shift_one_own, gain_two_own, shift_two_own, c_four_own)):
        small_own[24 + i : 25 + i, 64 : 64 + own_vec] = piece[...].reshape(1, own_vec)
    small_own[31:32, 0:shard] = c_in_own[...].reshape(1, shard)
    for i in range(lines_out):
        line = tout_own[i * patches : (i + 1) * patches].reshape(1, patches)
        small_own[32 + i : 33 + i, :] = line[:, 0:128]
        small_own[48 + i : 49 + i, 0 : patches - 128] = line[:, 128:patches]
    for group in range(2):
        small_all[group, 0, 0] = small_own[32 * group : 32 * (group + 1)].astype(LOW)
    weights[0, 0, 0:shard] = w_in[...].astype(LOW)
    weights[1, 0, 0:shard] = w_out[...].astype(LOW)

    barrier = pltpu.get_barrier_semaphore()
    peers = [by_core, by_x, by_y, by_both] + [by_z(k) for k in range(1, planes)]
    for peer in peers:
        pl.semaphore_signal(barrier, inc=1, device_id=(peer,), device_id_type=MESH)
    pl.semaphore_wait(barrier, len(peers))

    mats = (0, 1)
    inner = middle == 1

    def ag_half(stage, k, part, mat):
        near, far = (by_x, by_y) if mat == 0 else (by_y, by_x)
        step = 1 if mat == 0 else 2
        if stage == 0:
            src, dst, to = 0, 0, by_z(k)
        else:
            src, dst, to = ((0, step, near), (0, 3 - step, far), (step, 3, far))[stage - 1]
        rows = shard // 2
        first = part * rows
        at = (k - 1) // 2 if stage == 0 else 1 + stage
        return pltpu.make_async_remote_copy(
            src_ref=weights.at[mat, 0 if stage == 0 else k, pl.ds(src * shard + first, rows)],
            dst_ref=weights.at[mat, k, pl.ds(dst * shard + first, rows)],
            send_sem=ah_send.at[at, part, mat],
            recv_sem=ah_recv.at[at, part, mat],
            device_id=(to,),
            device_id_type=MESH,
        )

    def first_direct(part):
        k = plane_at(0)
        for mat in mats:
            ag_half(0, k, part, mat).wait_recv()
        for mat in mats:
            ag_half(1, k, part, mat).start()

    def first_far(part):
        for mat in mats:
            ag_half(2, plane_at(0), part, mat).start()

    def first_forward(part):
        for mat in mats:
            ag_half(1, plane_at(0), part, mat).wait_recv()
            ag_half(3, plane_at(0), part, mat).start()

    def first_core():
        k = plane_at(0)
        for mat in mats:
            for part in range(2):
                ag_half(2, k, part, mat).wait_recv()
            ag(4, k, mat).start()

    def first_core_last():
        k = plane_at(0)
        for mat in mats:
            for part in range(2):
                ag_half(3, k, part, mat).wait_recv()
            ag(5, k, mat).start()

    def ag_pass(which, mat):
        src, dst, to = ((1, 2, by_z(3)), (3, 2, by_z(1)), (2, 3, by_z(1)))[which]
        return pltpu.make_async_remote_copy(
            src_ref=weights.at[mat, src, pl.ds(0, shard)],
            dst_ref=weights.at[mat, dst, pl.ds(0, shard)],
            send_sem=ag_send.at[6, which, mat],
            recv_sem=ag_recv.at[0, dst, mat],
            device_id=(to,),
            device_id_type=MESH,
        )

    def ag_planes():
        for part in range(2):
            for mat in mats:
                ag_half(0, 1, part, mat).start()

            @pl.when(inner)
            def _():
                for mat in mats:
                    ag_half(0, 3, part, mat).start()

    def ag_planes_pass():
        @pl.when(inner)
        def _():
            for mat in mats:
                for part in range(2):
                    ag_half(0, 1, part, mat).wait_recv()
                ag_pass(0, mat).start()
            for mat in mats:
                ag_pass(1, mat).start()

    def ag_planes_last():
        @pl.when(inner)
        def _():
            for mat in mats:
                ag(0, 2, mat).wait_recv()
                ag_pass(2, mat).start()

    def ag_direct(k):
        @pl.when(jnp.logical_not(inner))
        def _():
            for mat in mats:
                ag(0, k, mat).wait_recv()

        for stage in (1, 2):
            for mat in mats:
                ag(stage, k, mat).start()

    def ag_forward(k):
        for mat in mats:
            ag(1, k, mat).wait_recv()
            ag(3, k, mat).start()

    def ag_core(k):
        for mat in mats:
            ag(2, k, mat).wait_recv()
            ag(4, k, mat).start()

    def ag_core_last(k):
        for mat in mats:
            ag(3, k, mat).wait_recv()
            ag(5, k, mat).start()

    def ag_ready(k):
        for mat in mats:
            ag(4, k, mat).wait_recv()
            ag(5, k, mat).wait_recv()

    for group in range(2):
        for k in range(1, planes):
            small_gather(0, k, group).start()
    for mat in mats:
        ag(1, 0, mat).start()
    ag_planes()

    grad_vecs[...] = jnp.zeros_like(grad_vecs)
    grad_tin[...] = jnp.zeros_like(grad_tin)
    grad_tout[...] = jnp.zeros_like(grad_tout)

    def channel_top(r, carry):
        tops = []
        for h in range(2):
            b = 2 * r + h
            load_top(b).wait()
            tops.append(padded(total[b] * mask[b].astype(WIDE), lot))
        rounded = jnp.concatenate(tops, axis=0).astype(LOW)
        top[pl.ds(r * pair, pair), :] = rounded
        grad_vecs[2:3, :] += jnp.sum(rounded.astype(WIDE), axis=0, keepdims=True)
        return carry

    def first_norm(b, carry):
        load(b).wait()
        mid[b], figures[b, :, 0:1], figures[b, :, 1:2] = norm_parts(grad_zed[b])
        return carry

    lax.fori_loop(0, blocks, channel_top, 0)
    for group in range(2):
        for k in range(1, planes):
            small_gather(0, k, group).wait_recv()
        for k in range(1, 4):
            small_gather(1, k, group).start()
    lax.fori_loop(0, count, first_norm, 0)
    for k in range(1, 4):
        small_gather(1, k, 0).wait_recv()
    small_gather(2, 0, 0).start()
    first_direct(0)
    first_far(0)

    tin[...] = jnp.zeros_like(tin)
    tout[...] = jnp.zeros_like(tout)

    def unpack(d, group):
        far, k = place_of(d)
        message = small_all[group, far, k].astype(WIDE)
        if group == 0:
            lines[d * lines_in : d * lines_in + first_lines, :] = message[0:first_lines, :]
            shifted = jnp.concatenate([message[0:24, 64:128], message[0:24, 0:64]], axis=1)
            lines[d * lines_in + first_lines : (d + 1) * lines_in, :] = shifted[0 : lines_in - first_lines, :]
            vecs[:, d * own_vec : (d + 1) * own_vec] = message[24:32, 64 : 64 + own_vec]
            c_in[d] = message[31:32, 0:shard]
        else:
            tout[d * lines_out : (d + 1) * lines_out, 0:128] = message[0:lines_out, :]
            tout[d * lines_out : (d + 1) * lines_out, 128:patches] = message[16 : 16 + lines_out, 0 : patches - 128]

    def unpack_half(own, group):
        for parity in range(2):

            @pl.when((core == parity) == own)
            def _():
                for d in range(parity, devices, 2):
                    unpack(d, group)

    unpack_half(True, 0)
    for k in range(1, 4):
        small_gather(1, k, 1).wait_recv()
    small_gather(2, 0, 1).start()
    unpack_half(True, 1)
    first_direct(1)
    ag_planes_pass()
    for group in range(2):
        small_gather(2, 0, group).wait_recv()
        unpack_half(False, group)
    for turn in range(turns):
        tin[0:patches, turn * unit : (turn + 1) * unit] = lines[pl.ds(turn, patches, stride=turns), :][:, 0:unit]
    for rest, into, at in ((c_one, tin, patches), (c_two, tout, hidden_tok)):
        rest = rest[...].reshape(1, rest.shape[0])
        for i in range(3):
            term = rest.astype(LOW).astype(WIDE)
            into[at + i : at + i + 1, 0 : rest.shape[1]] = term
            rest = rest - term
    tin_t[...] = tin[...].T.astype(LOW)
    tout_t[...] = tout[...].T.astype(LOW)
    ones = jnp.ones((3, width), WIDE)

    gain_one, shift_one = vecs[0:1, :], vecs[1:2, :]
    gain_two, shift_two, c_four = vecs[2:3, :], vecs[3:4, :], vecs[4:5, :]
    def singles(work, start, stop):
        def one(b, carry):
            work(b)
            return carry

        lax.fori_loop(start, stop, one, 0)

    def pairs(work, start, stop):
        def two(r, carry):
            for h in range(2):
                work(2 * r + h)
            return carry

        lax.fori_loop(start // 2, stop // 2, two, 0)

    def token_forward(b):
        fed = mid[b] * gain_one + shift_one
        mixed[b] = padded(jnp.concatenate([fed, ones], axis=0), pad).astype(LOW)
        value, slope = gelu_parts(dot(tin_t[...], mixed[b], NN))
        act_t[b] = padded(jnp.concatenate([value, ones], axis=0), act_t.shape[1]).astype(LOW)
        slope_t[b] = slope.astype(LOW)
        mid[b] = grad_zed[b] + dot(tout_t[...], act_t[b], NN)[0:patches]

    def channel_inputs(r, carry):
        parts = []
        for h in range(2):
            total[2 * r + h] = mid[2 * r + h] + c_four
            normed, _, figures[2 * r + h, :, 2:3] = norm_parts(mid[2 * r + h])
            mid[2 * r + h] = normed
            grad_zed[2 * r + h] = jnp.zeros((patches, width), WIDE)
            parts.append(padded(normed * gain_two + shift_two, lot))
        zed[pl.ds(r * pair, pair), :] = jnp.concatenate(parts, axis=0).astype(LOW)
        return carry

    first = 3
    first_forward(0)
    first_far(1)
    singles(token_forward, 0, first)
    first_forward(1)
    singles(token_forward, first, count)
    first_core()
    ag_planes_last()
    ag_direct(plane_at(1))
    lax.fori_loop(0, blocks, channel_inputs, 0)
    first_core_last()
    for k in range(planes):
        for place in range(PLANE):
            near = plane_of(k) * PLANE + (
                (row + (place // 2) % 2) % 2 * 4 + (col + place % 2) % 2 * 2 + (core + place // 4) % 2
            )
            c_in_rel[k, :, place * shard : (place + 1) * shard] = c_in[near]


    def rs_two(i, mat):
        rs(0, i, mat).wait_recv()
        slot = i % 2
        first, second = (1, 3) if mat == 0 else (2, 3)

        def part(n):
            return slice(n * shard, (n + 1) * shard)

        @pl.when(i == 0)
        def _():
            weights[mat, plane_at(i), 0:half] = (own_sum[mat] + recv_one[slot, mat].astype(WIDE)).astype(LOW)
            rs(4, 0, mat).start()

        @pl.when((i == planes - 1) & inner)
        def _():
            own_sum[mat] += came_from(4, 1, mat) + came_from(4, 3, mat)

        @pl.when(i > 1)
        def _():
            for stage in (1, 5):
                rs(stage, i - 1, mat).wait_send()

        @pl.when(i > 0)
        def _():
            for n, to, stage in ((second, part(1), 1), (first, part(0), 5)):
                send_two[mat, to] = (own_sum[mat, part(n)] + recv_one[slot, mat, part(n)].astype(WIDE)).astype(LOW)
                rs(stage, i, mat).start()
            for n in (0, 3 - first):
                own_sum[mat, part(n)] += recv_one[slot, mat, part(n)].astype(WIDE)

    def rs_three(i):
        for mat in mats:
            rs(1, i, mat).wait_recv()
            other = 2 if mat == 0 else 1

            @pl.when(i > 1)
            def _():
                rs(2, i - 1, mat).wait_send()

            send_three[mat] = (
                own_sum[mat, other * shard : (other + 1) * shard]
                + recv_two[i % 2, mat, shard : 2 * shard].astype(WIDE)
            ).astype(LOW)
            rs(2, i, mat).start()

    def rs_keep(i):
        for mat in mats:
            rs(5, i, mat).wait_recv()
            keep_sum[mat] = own_sum[mat, 0:shard] + recv_two[i % 2, mat, 0:shard].astype(WIDE)

    def rs_four(i):
        for mat in mats:
            rs(2, i, mat).wait_recv()

            send_four[i % 2, mat] = (keep_sum[mat] + recv_three[i % 2, mat].astype(WIDE)).astype(LOW)
            rs(3, i, mat).start()

    def rs_last():
        last = planes - 1
        for mat in mats:
            result = grad_in if mat == 0 else grad_out
            rs(2, last, mat).wait_recv()
            summed = keep_sum[mat] + recv_three[last % 2, mat].astype(WIDE)
            result[...] = summed + came_from(3, 2, mat)

            @pl.when(jnp.logical_not(inner))
            def _():
                result[...] += came_from(3, 1, mat) + came_from(3, 3, mat)


    tile = chunk // 3

    def channel_chunk(i, carry):
        k = plane_at(i)

        @pl.when(i == planes - 1)
        def _():
            rs_four(1)

        ag_ready(k)

        def rows(r):
            for s in range(3):
                part = slice(s * tile, (s + 1) * tile)
                pre = dot(zed[r * pair : (r + 1) * pair, :], weights[0, k, part], NT) + c_in_rel[k, :, part]
                value, slope = gelu_parts(pre)
                act[r * pair : (r + 1) * pair, part] = value.astype(LOW)
                back = (dot(top[r * pair : (r + 1) * pair, :], weights[1, k, part], NT) * slope).astype(LOW)
                grad_pre[r * pair : (r + 1) * pair, part] = back
            up = dot(act[r * pair : (r + 1) * pair, :], weights[1, k], NN)
            down = dot(grad_pre[r * pair : (r + 1) * pair, :], weights[0, k], NN)
            for h in range(2):
                total[2 * r + h] += up[h * lot : h * lot + patches]
                grad_zed[2 * r + h] += down[h * lot : h * lot + patches]

        rows(0)

        @pl.when(i == 0)
        def _():
            ag_forward(plane_at(1))

        @pl.when(i == 1)
        def _():
            ag_forward(plane_at(2))
            ag_forward(0)

        for r in range(1, blocks):
            rows(r)

        @pl.when(i == 0)
        def _():
            ag_core(plane_at(1))
            ag_direct(plane_at(2))
            for mat in mats:
                ag(2, 0, mat).start()

        @pl.when(i == 1)
        def _():
            ag_core(plane_at(2))

        @pl.when(i == 2)
        def _():
            ag_core(0)
            ag_core_last(0)

        @pl.when(i > 1)
        def _():
            rs_three(i - 1)

        @pl.when(i > 0)
        def _():
            for mat in mats:
                rs(0, i - 1, mat).wait_send()

        back_sum = jnp.sum(grad_pre[...].astype(WIDE), axis=0, keepdims=True)
        for place in range(PLANE):
            near = plane_of(k) * PLANE + (
                (row + (place // 2) % 2) % 2 * 4 + (col + place % 2) % 2 * 2 + (core + place // 4) % 2
            )
            grad_c_in[near] = back_sum[:, place * shard : (place + 1) * shard]
        send_one[1] = dot(act[:, half:chunk], top[...], TN).astype(LOW)
        send_one[0] = dot(grad_pre[:, half:chunk], zed[...], TN).astype(LOW)
        for mat in mats:
            rs(0, i, mat).start()

        @pl.when(i > 1)
        def _():
            rs_keep(i - 1)

        @pl.when(i == 0)
        def _():
            for mat in mats:
                for stage in (4, 5):
                    ag(stage, k, mat).wait_send()
                for stage in range(1, 4):
                    for part in range(2):
                        ag_half(stage, k, part, mat).wait_send()

                @pl.when(inner)
                def _():
                    ag_pass(1, mat).wait_send()

        own_sum[1] = dot(act[:, 0:half], top[...], TN)
        own_sum[0] = dot(grad_pre[:, 0:half], zed[...], TN)
        @pl.when(i < 2)
        def _():
            ag_core_last(plane_at(i + 1))

        for mat in mats:
            rs_two(i, mat)
        return carry

    lax.fori_loop(0, planes, channel_chunk, 0)

    tin_low = tin[...].astype(LOW)
    tout_low = tout[0:hidden_tok, :].astype(LOW)

    def kept(b):
        return weights.at[b // planes, b % planes, 0:pad]

    def middle_backward(b, above):
        normed = mid[b]
        down = grad_zed[b]
        grad_vecs[0:1, :] += jnp.sum(down * normed, axis=0, keepdims=True)
        grad_vecs[1:2, :] += jnp.sum(down, axis=0, keepdims=True)
        grad_mid = above + norm_back(down, normed, figures[b, :, 2:3], gain_two)
        grad_zed[b] = grad_mid
        back = padded(grad_mid, pad).astype(LOW)
        grad_tout[...] += dot(act_t[b], back, NT)
        slope_t[b] = (dot(tout_low, back, NN) * slope_t[b].astype(WIDE)).astype(LOW)
        grad_tin[:, 0:hidden_tok] += dot(mixed[b], slope_t[b], NT)

    def middle_pair(r, carry):
        above = top[pl.ds(r * pair, pair), :].astype(WIDE)
        for h in range(2):
            middle_backward(2 * r + h, above[h * lot : h * lot + patches])
        for h in range(2):
            reload_image(2 * r + h).start()
        return carry

    def image_norm(b):
        normed = (mid[b] - figures[b, :, 0:1]) * figures[b, :, 1:2]
        mid[b] = normed
        grad_mixed = dot(tin_low, slope_t[b], NN)
        kept(b)[...] = grad_mixed.astype(LOW)
        late[0, 0:1, :] += jnp.sum(grad_mixed[0:patches] * normed, axis=0, keepdims=True)
        late[0, 1:2, :] += jnp.sum(grad_mixed[0:patches], axis=0, keepdims=True)

    def image_backward(b):
        total[b] *= mask[b].astype(WIDE)
        grad_zed[b] += norm_back(kept(b)[...][0:patches].astype(WIDE), mid[b], figures[b, :, 1:2], gain_one)

    def small_first(group):
        for k in range(1, planes):
            small_gather(0, k, group).wait_send()
        for far in range(1, 4):
            small_gather(1, far, group).wait_send()
        small_gather(2, 0, group).wait_send()
        if group == 0:
            for turn in range(turns):
                lines[pl.ds(turn, patches, stride=turns), :] = grad_tin[0:patches, turn * unit : turn * unit + 128]
        for d in range(devices):
            far, k = place_of(d)
            message = small_sum.at[group, far, k]
            if group == 0:
                low = lines[d * lines_in : d * lines_in + first_lines, :]
                high = lines[d * lines_in + first_lines : (d + 1) * lines_in, :]
                message[0:first_lines, 0:64] = low[:, 0:64]
                message[0 : lines_in - first_lines, 64:128] = high[:, 0:64]
                message[24:27, 64 : 64 + own_vec] = grad_vecs[0:3, d * own_vec : (d + 1) * own_vec]
                message[31:32, 0:shard] = grad_c_in[d]
            else:
                message[0:lines_out, :] = grad_tout[d * lines_out : (d + 1) * lines_out, 0:128]
                message[16 : 16 + lines_out, 0 : patches - 128] = grad_tout[
                    d * lines_out : (d + 1) * lines_out, 128:patches
                ]
        for far in range(4, PLANE):
            small_all[group, far] = small_sum[group, far].astype(LOW)
        small_reduce(0, 0, group).start()
        if group == 0:
            biases[0] = jnp.zeros_like(biases[0])
            for i in range(hidden_tok // 128):
                biases[0, i : i + 1, :] = grad_tin[patches : patches + 1, i * 128 : (i + 1) * 128]
            biases[0, 3:4, :] = grad_tout[hidden_tok : hidden_tok + 1, 0:128]
            biases[0, 4:5, 0 : patches - 128] = grad_tout[hidden_tok : hidden_tok + 1, 128:patches]
            bias_reduce(0, 0).start()

    def small_second(group):
        small_reduce(0, 0, group).wait_recv()
        for far in range(4):
            small_sum[group, far] += small_core[group, far].astype(WIDE)
        for far in range(1, 4):
            small_all[group, far] = small_sum[group, far].astype(LOW)
            small_reduce(1, far, group).start()
        if group == 0:
            bias_reduce(0, 0).wait_recv()
            biases[1] = biases[0] + biases_in[0, 0]
            for far in range(1, 4):
                bias_reduce(1, far).start()

    def small_third(group):
        for far in range(1, 4):
            small_reduce(1, far, group).wait_recv()
            small_sum[group, 0] += small_plane[group, far].astype(WIDE)
        for k in range(1, planes):
            small_all[group, 0, k] = small_sum[group, 0, k].astype(LOW)
            small_reduce(2, k, group).start()
        if group == 0:
            for far in range(1, 4):
                bias_reduce(1, far).wait_recv()
            biases[2] = (biases[1] + biases_in[1, 1]) + (biases_in[1, 2] + biases_in[1, 3])
            for k in range(1, planes):
                bias_reduce(2, k).start()

    for mat in mats:
        for i in range(1, planes):
            for stage in range(1, 6):
                ag(stage, plane_at(i), mat).wait_send()
        for part in range(2):
            ag_half(0, 1, part, mat).wait_send()
        rs(4, 0, mat).wait_send()

        @pl.when(inner)
        def _():
            for part in range(2):
                ag_half(0, 3, part, mat).wait_send()
            for which in (0, 2):
                ag_pass(which, mat).wait_send()

    late[0] = jnp.zeros_like(late[0])
    rs_four(planes - 2)
    lax.fori_loop(0, blocks, middle_pair, 0)
    small_first(1)
    small_first(0)
    for b in range(count):
        reload_image(b).wait()
    pairs(image_norm, 0, 2)
    small_second(1)
    pairs(image_norm, 2, count)
    small_second(0)
    late_reduce(0, 0).start()
    pairs(image_backward, 0, 2)
    late_reduce(0, 0).wait_recv()
    late[1] = late[0] + late_in[0, 0]
    for far in range(1, 4):
        late_reduce(1, far).start()
    rs_three(planes - 1)
    rs_keep(planes - 1)
    small_third(1)
    pairs(image_backward, 2, count)
    small_third(0)
    late_sum = late[1]
    for far in range(1, 4):
        late_reduce(1, far).wait_recv()
        late_sum = late_sum + late_in[1, far]
    late[2] = late_sum
    for k in range(1, planes):
        late_reduce(2, k).start()
    rs_last()
    summed = [small_sum[group, 0, 0] for group in range(2)]
    tree = [biases[2]]
    for k in range(1, planes):
        for group in range(2):
            small_reduce(2, k, group).wait_recv()
        bias_reduce(2, k).wait_recv()
        summed = [summed[group] + small_z[k, group].astype(WIDE) for group in range(2)]
        tree.append(biases_in[2, k])
    for group in range(2):
        small_out[32 * group : 32 * (group + 1)] = summed[group]
    for k in range(1, planes):
        late_reduce(2, k).wait_recv()
        late_sum = late_sum + late_in[2, k]
    late_sum = pltpu.roll(padded(late_sum, 8), width - own_vec * me, 1)
    small_out[27:29, 64 : 64 + own_vec] = late_sum[0:2, 0:own_vec]
    while len(tree) > 1:
        tree = [tree[i] + tree[i + 1] for i in range(0, len(tree), 2)]
    biases_out[...] = tree[0]

    for mat in mats:
        for stage in (0, 1, 2, 5):
            rs(stage, planes - 1, mat).wait_send()
        for i in range(1, planes - 1):
            rs(3, i, mat).wait_send()
    late_reduce(0, 0).wait_send()
    for far in range(1, 4):
        late_reduce(1, far).wait_send()
    for k in range(1, planes):
        late_reduce(2, k).wait_send()
    bias_reduce(0, 0).wait_send()
    for far in range(1, 4):
        bias_reduce(1, far).wait_send()
    for k in range(1, planes):
        bias_reduce(2, k).wait_send()
    for group in range(2):
        small_reduce(0, 0, group).wait_send()
        for far in range(1, 4):
            small_reduce(1, far, group).wait_send()
        for k in range(1, planes):
            small_reduce(2, k, group).wait_send()


def finish_kernel(
    block_in,
    image_in,
    w_in,
    w_out,
    small,
    biases,
    block_out,
    image_out,
    w_in_out,
    w_out_out,
    tin,
    tout,
    gain_one,
    shift_one,
    gain_two,
    shift_two,
    c_four,
    c_in,
    c_one,
    c_two,
    sem,
):
    pieces = [(block_in.at[b], block_out.at[b]) for b in range(block_in.shape[0])]
    pieces += [(image_in.at[b], image_out.at[b]) for b in range(image_in.shape[0])]
    pieces += [(w_in, w_in_out), (w_out, w_out_out)]
    copies = [pltpu.make_async_copy(a, b, sem.at[i]) for i, (a, b) in enumerate(pieces)]
    for copy in copies:
        copy.start()
    hidden_tok, patches = c_one.shape[0], c_two.shape[0]
    unit = math.gcd(tin.shape[0], hidden_tok)
    lines_in = tin.shape[0] // unit
    first_lines = (lines_in + 1) // 2
    for i in range(lines_in):
        at, lane = (i, 0) if i < first_lines else (i - first_lines, 64)
        tin[i * unit : (i + 1) * unit] = small[at : at + 1, lane : lane + unit].reshape(unit)
    for i in range(tout.shape[0] // patches):
        tout[i * patches : i * patches + 128] = small[32 + i : 33 + i, :].reshape(128)
        tout[i * patches + 128 : (i + 1) * patches] = small[48 + i : 49 + i, 0 : patches - 128].reshape(
            patches - 128
        )
    for i, piece in enumerate((gain_two, shift_two, c_four, gain_one, shift_one)):
        own_vec = piece.shape[0]
        piece[...] = small[24 + i : 25 + i, 64 : 64 + own_vec].reshape(own_vec)
    shard = c_in.shape[0]
    c_in[...] = small[31:32, 0:shard].reshape(shard)
    for i in range(hidden_tok // 128):
        c_one[i * 128 : (i + 1) * 128] = biases[i : i + 1, :].reshape(128)
    c_two[0:128] = biases[3:4, :].reshape(128)
    c_two[128:patches] = biases[4:5, 0 : patches - 128].reshape(patches - 128)
    for copy in copies:
        copy.wait()


def fast_shards(
    images,
    mask,
    cotangent,
    w_token_in,
    w_token_out,
    bias_token_in,
    bias_token_out,
    gain_one,
    shift_one,
    gain_two,
    shift_two,
    w_expand,
    bias_expand,
    w_reduce,
    bias_reduce,
):
    devices = lax.axis_size("dp")
    planes = devices // PLANE
    count, patches, width = images.shape
    hidden_tok = bias_token_in.shape[0]
    shard = w_expand.shape[0]
    pad = -(-patches // 16) * 16
    lot = -(-patches // 8) * 8
    pair = 2 * lot
    blocks = count // 2
    chunk = 8 * shard
    half = 4 * shard

    unit = math.gcd(w_token_in.shape[0], hidden_tok)
    lines_in = w_token_in.shape[0] // unit
    hidden_pad = hidden_tok + 16

    owned = (
        w_expand,
        w_reduce,
        w_token_in,
        w_token_out,
        gain_one,
        shift_one,
        gain_two,
        shift_two,
        bias_reduce,
        bias_expand,
        bias_token_in,
        bias_token_out,
    )
    vmem = pl.BlockSpec(memory_space=pltpu.VMEM)
    hbm = pl.BlockSpec(memory_space=pl.ANY)
    shape = jax.ShapeDtypeStruct
    outs = pl.pallas_call(
        block_kernel,
        out_shape=(
            pltpu.VMEM(images.shape, WIDE),
            pltpu.VMEM(images.shape, WIDE),
            pltpu.VMEM(w_expand.shape, WIDE),
            pltpu.VMEM(w_reduce.shape, WIDE),
            pltpu.VMEM((64, 128), WIDE),
            pltpu.VMEM((8, 128), WIDE),
        ),
        in_specs=[pl.BlockSpec(memory_space=pltpu.SMEM), hbm, hbm] + [vmem] * 12,
        out_specs=[vmem] * 6,
        scratch_shapes=[
            pltpu.VMEM((count, pad, width), LOW),
            pltpu.VMEM((count, hidden_pad, width), LOW),
            pltpu.VMEM((count, hidden_tok, width), LOW),
            pltpu.VMEM(images.shape, WIDE),
            pltpu.VMEM((blocks * pair, width), LOW),
            pltpu.VMEM((blocks * pair, width), LOW),
            pltpu.VMEM((2, planes, chunk, width), LOW),
            pltpu.VMEM((blocks * pair, chunk), LOW),
            pltpu.VMEM((blocks * pair, chunk), LOW),
            pltpu.VMEM((planes, 1, chunk), WIDE),
            pltpu.VMEM((2, half, width), WIDE),
            pltpu.VMEM((2, shard, width), WIDE),
            pltpu.VMEM((2, half, width), LOW),
            pltpu.VMEM((2, 2, half, width), LOW),
            pltpu.VMEM((2, 2 * shard, width), LOW),
            pltpu.VMEM((2, 2, 2 * shard, width), LOW),
            pltpu.VMEM((2, shard, width), LOW),
            pltpu.VMEM((2, 2, shard, width), LOW),
            pltpu.VMEM((2, 2, shard, width), LOW),
            pltpu.VMEM((planes - 1, 2, shard, width), LOW),
            pltpu.VMEM((2, 2, half, width), LOW),
            pltpu.VMEM((pad, hidden_tok), WIDE),
            pltpu.VMEM((hidden_tok, pad), LOW),
            pltpu.VMEM((hidden_pad, pad), WIDE),
            pltpu.VMEM((pad, hidden_pad), LOW),
            pltpu.VMEM((8, width), WIDE),
            pltpu.VMEM((devices, 1, shard), WIDE),
            pltpu.VMEM((devices * lines_in, 128), WIDE),
            pltpu.VMEM((64, 128), WIDE),
            pltpu.VMEM((2, PLANE, planes, 32, 128), LOW),
            pltpu.VMEM((pad, hidden_tok + 128), WIDE),
            pltpu.VMEM((hidden_pad, pad), WIDE),
            pltpu.VMEM((8, width), WIDE),
            pltpu.VMEM((devices, 1, shard), WIDE),
            pltpu.VMEM((2, PLANE, planes, 32, 128), WIDE),
            pltpu.VMEM((2, 4, planes, 32, 128), LOW),
            pltpu.VMEM((2, 4, planes, 32, 128), LOW),
            pltpu.VMEM((planes, 2, 32, 128), LOW),
            pltpu.VMEM((3, 8, 128), WIDE),
            pltpu.VMEM((3, max(4, planes), 8, 128), WIDE),
            pltpu.VMEM((3, 2, width), WIDE),
            pltpu.VMEM((3, max(4, planes), 2, width), WIDE),
            pltpu.VMEM((count, patches, 4), WIDE),
            pltpu.SemaphoreType.DMA((4, count)),
            pltpu.SemaphoreType.DMA((7, planes, 2)),
            pltpu.SemaphoreType.DMA((7, planes, 2)),
            pltpu.SemaphoreType.DMA((5, 2, 2)),
            pltpu.SemaphoreType.DMA((5, 2, 2)),
            pltpu.SemaphoreType.DMA((6, planes, 2)),
            pltpu.SemaphoreType.DMA((6, planes, 2)),
        ]
        + [pltpu.SemaphoreType.DMA((3, max(4, planes), 2))] * 4
        + [pltpu.SemaphoreType.DMA((3, max(4, planes)))] * 4,
        compiler_params=pltpu.CompilerParams(
            collective_id=0, has_side_effects=True, vmem_limit_bytes=56 * 2**20
        ),
    )(
        mask,
        images,
        cotangent,
        *owned,
    )
    flat = pl.pallas_call(
        finish_kernel,
        out_shape=(
            shape(images.shape, WIDE),
            shape(images.shape, WIDE),
            shape(w_expand.shape, WIDE),
            shape(w_reduce.shape, WIDE),
            shape(w_token_in.shape, WIDE),
            shape(w_token_out.shape, WIDE),
            *[shape(gain_one.shape, WIDE)] * 5,
            shape(bias_expand.shape, WIDE),
            shape(bias_token_in.shape, WIDE),
            shape(bias_token_out.shape, WIDE),
        ),
        in_specs=[vmem] * 6,
        out_specs=[hbm] * 4 + [vmem] * 10,
        scratch_shapes=[pltpu.SemaphoreType.DMA((2 * count + 2,))],
        compiler_params=pltpu.CompilerParams(vmem_limit_bytes=16 * 2**20),
    )(*outs)
    block_output, image_grad, own_win, own_wout, *rest = flat
    g_tin, g_tout, g_one, b_one, g_two, b_two, c_four, c_in, c_one, c_two = rest
    return (
        block_output,
        image_grad,
        g_tin,
        g_tout,
        c_one,
        c_two,
        g_one,
        b_one,
        g_two,
        b_two,
        own_win,
        c_in,
        own_wout,
        c_four,
    )


def fits(devices, images, w_token_in, w_token_out, bias_token_in, gain_one, w_expand):
    planes = devices // PLANE
    patches = images.shape[1]
    hidden_tok = bias_token_in.shape[0]
    shard = w_expand.shape[0]
    unit = math.gcd(w_token_in.shape[0], hidden_tok)
    return (
        devices % PLANE == 0
        and planes == 4
        and images.shape[0] % 2 == 0
        and 6 <= images.shape[0] <= 2 * planes
        and shard % 32 == 0
        and shard <= 128
        and (4 * shard) % 128 == 0
        and 128 < patches <= 205
        and unit <= 64
        and w_token_in.shape[0] // unit <= 49
        and w_token_out.shape[0] % patches == 0
        and w_token_out.shape[0] // patches <= 16
        and gain_one.shape[0] <= 64
        and hidden_tok == 384
    )


def choose(
    images,
    mask,
    cotangent,
    w_token_in,
    w_token_out,
    bias_token_in,
    bias_token_out,
    gain_one,
    shift_one,
    gain_two,
    shift_two,
    w_expand,
    bias_expand,
    w_reduce,
    bias_reduce,
):
    args = (
        images,
        mask,
        cotangent,
        w_token_in,
        w_token_out,
        bias_token_in,
        bias_token_out,
        gain_one,
        shift_one,
        gain_two,
        shift_two,
        w_expand,
        bias_expand,
        w_reduce,
        bias_reduce,
    )
    if fits(lax.axis_size("dp"), images, w_token_in, w_token_out, bias_token_in, gain_one, w_expand):
        return fast_shards(*args)
    return shards(*args)


def shards(
    images,
    mask,
    cotangent,
    w_token_in,
    w_token_out,
    bias_token_in,
    bias_token_out,
    gain_one,
    shift_one,
    gain_two,
    shift_two,
    w_expand,
    bias_expand,
    w_reduce,
    bias_reduce,
):
    low_type = jnp.bfloat16
    wide = jnp.float32
    count, patches, width = images.shape
    hidden_tok = bias_token_in.shape[0]
    rows = count * patches
    keep = mask.astype(wide)[:, None, None]
    small_local = (
        w_token_in.astype(low_type),
        w_token_out.astype(low_type),
        gain_one.astype(low_type),
        shift_one.astype(low_type),
        gain_two.astype(low_type),
        shift_two.astype(low_type),
        bias_reduce.astype(low_type),
    )
    channel_local = (
        w_expand.astype(low_type),
        w_reduce.astype(low_type),
        bias_expand.astype(low_type),
    )
    small_all = (
        lax.all_gather(small_local[0], "dp", axis=0, tiled=True),
        lax.all_gather(small_local[1], "dp", axis=0, tiled=True),
        lax.all_gather(small_local[2], "dp", axis=0, tiled=True),
        lax.all_gather(small_local[3], "dp", axis=0, tiled=True),
        lax.all_gather(small_local[4], "dp", axis=0, tiled=True),
        lax.all_gather(small_local[5], "dp", axis=0, tiled=True),
        lax.all_gather(small_local[6], "dp", axis=0, tiled=True),
    )
    tin = small_all[0].reshape(patches, hidden_tok)
    tout = small_all[1].reshape(hidden_tok, patches)
    g_one, b_one, g_two, b_two, c_four = [piece.astype(wide) for piece in small_all[2:]]
    normed_one, scale_one = normalize(images)
    mixed_in = (normed_one * g_one + b_one).astype(low_type)
    pre_t = (
        jnp.einsum("ps,bpd->bsd", tin, mixed_in, preferred_element_type=wide)
        + bias_token_in[None, :, None]
    )
    act_t = gelu_exact(pre_t).astype(low_type)
    middle = (
        images
        + jnp.einsum("sp,bsd->bpd", tout, act_t, preferred_element_type=wide)
        + bias_token_out[None, :, None]
    )
    normed_two, scale_two = normalize(middle.reshape(rows, width))
    zed = (normed_two * g_two + b_two).astype(low_type)
    whole_channel = (
        lax.all_gather(channel_local[0], "dp", axis=0, tiled=True),
        lax.all_gather(channel_local[1], "dp", axis=0, tiled=True),
        lax.all_gather(channel_local[2], "dp", axis=0, tiled=True),
    )
    w_in, w_out, c_in = whole_channel
    pre = (
        jnp.einsum("td,fd->tf", zed, w_in, preferred_element_type=wide) + c_in.astype(wide)[None, :]
    )
    act = gelu_exact(pre).astype(low_type)
    reduced = jnp.dot(act, w_out, preferred_element_type=wide)
    block_output = (middle + (reduced + c_four).reshape(count, patches, width)) * keep
    grad_top = cotangent * keep
    grad_branch = grad_top.reshape(rows, width).astype(low_type)
    grad_c_four = jnp.sum(grad_branch.astype(wide), axis=0)
    small_all = (
        lax.all_gather(small_local[0], "dp", axis=0, tiled=True),
        lax.all_gather(small_local[1], "dp", axis=0, tiled=True),
        lax.all_gather(small_local[2], "dp", axis=0, tiled=True),
        lax.all_gather(small_local[3], "dp", axis=0, tiled=True),
        lax.all_gather(small_local[4], "dp", axis=0, tiled=True),
        lax.all_gather(small_local[5], "dp", axis=0, tiled=True),
        lax.all_gather(small_local[6], "dp", axis=0, tiled=True),
    )
    tin = small_all[0].reshape(patches, hidden_tok)
    tout = small_all[1].reshape(hidden_tok, patches)
    g_one, b_one, g_two, b_two, c_four = [piece.astype(wide) for piece in small_all[2:]]
    whole_channel = (
        lax.all_gather(channel_local[0], "dp", axis=0, tiled=True),
        lax.all_gather(channel_local[1], "dp", axis=0, tiled=True),
        lax.all_gather(channel_local[2], "dp", axis=0, tiled=True),
    )
    w_in, w_out, c_in = whole_channel
    pre = (
        jnp.einsum("td,fd->tf", zed, w_in, preferred_element_type=wide) + c_in.astype(wide)[None, :]
    )
    act = gelu_exact(pre).astype(low_type)
    grad_act = jnp.einsum("td,fd->tf", grad_branch, w_out, preferred_element_type=wide)
    grad_pre = (grad_act * gelu_slope(pre)).astype(low_type)
    grad_zed = jnp.dot(grad_pre, w_in, preferred_element_type=wide)
    grad_in = jnp.einsum("tf,td->fd", grad_pre, zed, preferred_element_type=wide)
    grad_out = jnp.einsum("tf,td->fd", act, grad_branch, preferred_element_type=wide)
    grad_cin = jnp.sum(grad_pre.astype(wide), axis=0)
    grad_zed, grad_win, grad_wout, grad_cin = (grad_zed, grad_in, grad_out, grad_cin)
    grad_g_two = jnp.sum(grad_zed * normed_two, axis=0)
    grad_b_two = jnp.sum(grad_zed, axis=0)
    grad_mid = grad_top + norm_back(grad_zed, normed_two, scale_two, g_two).reshape(
        count, patches, width
    )
    grad_back = grad_mid.astype(low_type)
    grad_c_two = jnp.sum(grad_back.astype(wide), axis=(0, 2))
    grad_tout = jnp.einsum("bsd,bpd->sp", act_t, grad_back, preferred_element_type=wide)
    grad_act_t = jnp.einsum("sp,bpd->bsd", tout, grad_back, preferred_element_type=wide)
    grad_pre_t = (grad_act_t * gelu_slope(pre_t)).astype(low_type)
    grad_c_one = jnp.sum(grad_pre_t.astype(wide), axis=(0, 2))
    grad_tin = jnp.einsum("bpd,bsd->ps", mixed_in, grad_pre_t, preferred_element_type=wide)
    grad_mixed = jnp.einsum("ps,bsd->bpd", tin, grad_pre_t, preferred_element_type=wide)
    grad_g_one = jnp.sum(grad_mixed * normed_one, axis=(0, 1))
    grad_b_one = jnp.sum(grad_mixed, axis=(0, 1))
    image_grad = grad_mid + norm_back(grad_mixed, normed_one, scale_one, g_one)
    bias_sums = lax.psum((grad_c_one, grad_c_two), "dp")
    flat_tin = grad_tin.reshape(patches * hidden_tok)
    flat_tout = grad_tout.reshape(hidden_tok * patches)
    owned = (
        lax.psum_scatter(flat_tin, "dp", scatter_dimension=0, tiled=True),
        lax.psum_scatter(flat_tout, "dp", scatter_dimension=0, tiled=True),
        lax.psum_scatter(grad_g_one, "dp", scatter_dimension=0, tiled=True),
        lax.psum_scatter(grad_b_one, "dp", scatter_dimension=0, tiled=True),
        lax.psum_scatter(grad_g_two, "dp", scatter_dimension=0, tiled=True),
        lax.psum_scatter(grad_b_two, "dp", scatter_dimension=0, tiled=True),
        lax.psum_scatter(grad_win, "dp", scatter_dimension=0, tiled=True),
        lax.psum_scatter(grad_cin, "dp", scatter_dimension=0, tiled=True),
        lax.psum_scatter(grad_wout, "dp", scatter_dimension=0, tiled=True),
        lax.psum_scatter(grad_c_four, "dp", scatter_dimension=0, tiled=True),
    )
    (
        own_tin,
        own_tout,
        own_g_one,
        own_b_one,
        own_g_two,
        own_b_two,
        own_win,
        own_cin,
        own_wout,
        own_c_four,
    ) = owned
    return (
        block_output,
        image_grad,
        own_tin,
        own_tout,
        bias_sums[0],
        bias_sums[1],
        own_g_one,
        own_b_one,
        own_g_two,
        own_b_two,
        own_win,
        own_cin,
        own_wout,
        own_c_four,
    )


def solution(mesh):
    placed = (
        P("dp", None, None),
        P("dp"),
        P("dp", None, None),
        P("dp"),
        P("dp"),
        P(),
        P(),
        P("dp"),
        P("dp"),
        P("dp"),
        P("dp"),
        P("dp", None),
        P("dp"),
        P("dp", None),
        P("dp"),
    )
    return jax.shard_map(
        choose,
        mesh=mesh,
        in_specs=placed,
        out_specs=(
            P("dp", None, None),
            P("dp", None, None),
            P("dp"),
            P("dp"),
            P(),
            P(),
            P("dp"),
            P("dp"),
            P("dp"),
            P("dp"),
            P("dp", None),
            P("dp"),
            P("dp", None),
            P("dp"),
        ),
        check_vma=False,
    )
```

```python
import math

import jax
import jax.numpy as jnp
from jax import lax
from jax.experimental import pallas as pl
from jax.experimental.pallas import tpu as pltpu
from jax.sharding import PartitionSpec as P

EPS = 1e-06


def gelu_exact(v):
    return 0.5 * v * (1.0 + lax.erf(v * 0.7071067811865476))


def gelu_slope(v):
    return 0.5 * (1.0 + lax.erf(v * 0.7071067811865476)) + v * 0.3989422804014327 * jnp.exp(
        -0.5 * v * v
    )


def norm_parts(v):
    middle = jnp.mean(v, axis=-1, keepdims=True)
    centered = v - middle
    scale = lax.rsqrt(jnp.mean(centered * centered, axis=-1, keepdims=True) + EPS)
    return (centered * scale, middle, scale)


def normalize(v):
    centered = v - jnp.mean(v, axis=-1, keepdims=True)
    scale = lax.rsqrt(jnp.mean(centered * centered, axis=-1, keepdims=True) + EPS)
    return (centered * scale, scale)


def norm_back(grad_in, normed, scale, gain):
    scaled = grad_in * gain
    return scale * (
        scaled
        - jnp.mean(scaled, axis=-1, keepdims=True)
        - normed * jnp.mean(scaled * normed, axis=-1, keepdims=True)
    )


WIDE = jnp.float32
LOW = jnp.bfloat16
MESH = pl.DeviceIdType.MESH
NT = (((1,), (1,)), ((), ()))
TN = (((0,), (0,)), ((), ()))
NN = (((1,), (0,)), ((), ()))
PLANE = 8


def dot(a, b, dims):
    return lax.dot_general(a, b, dims, preferred_element_type=WIDE)


def gelu_parts(v):
    cdf = 0.5 * (1.0 + lax.erf(v * 0.7071067811865476))
    return v * cdf, cdf + v * 0.3989422804014327 * jnp.exp2(v * v * -0.7213475204444817)


def padded(v, rows):
    return jnp.concatenate([v, jnp.zeros((rows - v.shape[0], v.shape[1]), v.dtype)], axis=0)


def block_kernel(
    mask,
    images,
    cotangent,
    w_in,
    w_out,
    tin_own,
    tout_own,
    gain_one_own,
    shift_one_own,
    gain_two_own,
    shift_two_own,
    c_four_own,
    c_in_own,
    c_one,
    c_two,
    total,
    grad_zed,
    grad_in,
    grad_out,
    small_out,
    biases_out,
    mixed,
    act_t,
    slope_t,
    mid,
    zed,
    top,
    weights,
    act,
    grad_pre,
    c_in_rel,
    own_sum,
    keep_sum,
    send_one,
    recv_one,
    send_two,
    recv_two,
    send_three,
    recv_three,
    send_four,
    recv_four,
    recv_far,
    tin,
    tin_t,
    tout,
    tout_t,
    vecs,
    c_in,
    lines,
    small_own,
    small_all,
    grad_tin,
    grad_tout,
    grad_vecs,
    grad_c_in,
    small_sum,
    small_core,
    small_plane,
    small_z,
    biases,
    biases_in,
    late,
    late_in,
    figures,
    in_sem,
    ag_send,
    ag_recv,
    ah_send,
    ah_recv,
    rs_send,
    rs_recv,
    sg_send,
    sg_recv,
    ss_send,
    ss_recv,
    bs_send,
    bs_recv,
    ls_send,
    ls_recv,
):
    count, patches, width = images.shape
    planes = weights.shape[1]
    shard = w_in.shape[0]
    half = 4 * shard
    chunk = 8 * shard
    pad = mixed.shape[1]
    blocks = count // 2
    pair = zed.shape[0] // blocks
    lot = pair // 2
    me = lax.axis_index("dp")
    core = me % 2
    col = (me // 2) % 2
    row = (me // 4) % 2
    z = me // PLANE
    by_core = me + 1 - 2 * core
    by_x = me + 2 - 4 * col
    by_y = me + 4 - 8 * row
    by_both = by_x + by_y - me

    def plane_of(k):
        out, bit = z, 1
        while bit < planes:
            out = out + bit * ((k // bit) % 2) * (1 - 2 * ((z // bit) % 2))
            bit *= 2
        return out

    def by_z(k):
        return me + PLANE * (plane_of(k) - z)

    def ag(stage, k, mat):
        near, far = (by_x, by_y) if mat == 0 else (by_y, by_x)
        step = 1 if mat == 0 else 2
        if stage == 0:
            src, dst, size, to = 0, 0, shard, by_z(k)
            source = weights.at[mat, 0, pl.ds(src, size)]
        else:
            src, dst, size, to = {
                1: (0, step * shard, shard, near),
                2: (0, (3 - step) * shard, shard, far),
                3: (step * shard, 3 * shard, shard, far),
                4: (0, half, 3 * shard, by_core),
                5: (3 * shard, half + 3 * shard, shard, by_core),
            }[stage]
            source = weights.at[mat, k, pl.ds(src, size)]
        return pltpu.make_async_remote_copy(
            src_ref=source,
            dst_ref=weights.at[mat, k, pl.ds(dst, size)],
            send_sem=ag_send.at[stage, k, mat],
            recv_sem=ag_recv.at[stage, k, mat],
            device_id=(to,),
            device_id_type=MESH,
        )

    middle = ((z + 1) // 2) % 2

    def plane_at(i):
        last = planes - 1
        return (1 - middle) * ((i + 1) % planes) + middle * (i % last + last * ((last - i) // last))

    def rs(stage, i, mat):
        slot, k = i % 2, plane_at(i)
        near, far = (by_x, by_y) if mat == 0 else (by_y, by_x)
        src, dst, to = [
            lambda: (send_one.at[mat], recv_one.at[slot, mat], by_core),
            lambda: (
                send_two.at[mat, pl.ds(shard, shard)],
                recv_two.at[slot, mat, pl.ds(shard, shard)],
                near,
            ),
            lambda: (send_three.at[mat], recv_three.at[slot, mat], far),
            lambda: (send_four.at[slot, mat], recv_four.at[k - 1, mat], by_z(k)),
            lambda: (weights.at[mat, k, pl.ds(0, half)], recv_far.at[(k - 1) // 2, mat], by_z(k)),
            lambda: (send_two.at[mat, pl.ds(0, shard)], recv_two.at[slot, mat, pl.ds(0, shard)], near),
        ][stage]()
        at = k if stage in (3, 4) else i
        return pltpu.make_async_remote_copy(
            src_ref=src,
            dst_ref=dst,
            send_sem=rs_send.at[stage, at, mat],
            recv_sem=rs_recv.at[stage, at, mat],
            device_id=(to,),
            device_id_type=MESH,
        )

    def came_from(stage, k, mat):
        place = recv_four.at[k - 1, mat] if stage == 3 else recv_far.at[(k - 1) // 2, mat]
        pltpu.make_async_remote_copy(
            src_ref=place,
            dst_ref=place,
            send_sem=rs_send.at[stage, k, mat],
            recv_sem=rs_recv.at[stage, k, mat],
            device_id=(by_z(k),),
            device_id_type=MESH,
        ).wait_recv()
        return place[...].astype(WIDE)

    def small_gather(stage, k, group):
        src, dst, to = [
            lambda: (small_all.at[group, 0, 0], small_all.at[group, 0, k], by_z(k)),
            lambda: (small_all.at[group, 0], small_all.at[group, k], (me, by_x, by_y, by_both)[k]),
            lambda: (small_all.at[group, pl.ds(0, 4)], small_all.at[group, pl.ds(4, 4)], by_core),
        ][stage]()
        return pltpu.make_async_remote_copy(
            src_ref=src,
            dst_ref=dst,
            send_sem=sg_send.at[stage, k, group],
            recv_sem=sg_recv.at[stage, k, group],
            device_id=(to,),
            device_id_type=MESH,
        )

    def small_reduce(stage, k, group):
        src, dst, to = [
            lambda: (small_all.at[group, pl.ds(4, 4)], small_core.at[group], by_core),
            lambda: (small_all.at[group, k], small_plane.at[group, k], (me, by_x, by_y, by_both)[k]),
            lambda: (small_all.at[group, 0, k], small_z.at[k, group], by_z(k)),
        ][stage]()
        return pltpu.make_async_remote_copy(
            src_ref=src,
            dst_ref=dst,
            send_sem=ss_send.at[stage, k, group],
            recv_sem=ss_recv.at[stage, k, group],
            device_id=(to,),
            device_id_type=MESH,
        )

    def bias_reduce(stage, k):
        to = [lambda: by_core, lambda: (me, by_x, by_y, by_both)[k], lambda: by_z(k)][stage]()
        return pltpu.make_async_remote_copy(
            src_ref=biases.at[stage],
            dst_ref=biases_in.at[stage, k],
            send_sem=bs_send.at[stage, k],
            recv_sem=bs_recv.at[stage, k],
            device_id=(to,),
            device_id_type=MESH,
        )

    def late_reduce(stage, k):
        to = [lambda: by_core, lambda: (me, by_x, by_y, by_both)[k], lambda: by_z(k)][stage]()
        return pltpu.make_async_remote_copy(
            src_ref=late.at[stage],
            dst_ref=late_in.at[stage, k],
            send_sem=ls_send.at[stage, k],
            recv_sem=ls_recv.at[stage, k],
            device_id=(to,),
            device_id_type=MESH,
        )

    hidden_tok = c_one.shape[0]
    unit = math.gcd(tin_own.shape[0], hidden_tok)
    lines_in = tin_own.shape[0] // unit
    first_lines = (lines_in + 1) // 2
    lines_out = tout_own.shape[0] // patches
    own_vec = gain_one_own.shape[0]
    turns = hidden_tok // unit
    devices = planes * PLANE

    def place_of(d):
        dz, dy, dx, dc = d // PLANE, (d // 4) % 2, (d // 2) % 2, d % 2
        far = (dc + core) % 2 * 4 + (dy + row) % 2 * 2 + (dx + col) % 2
        k, bit = 0, 1
        while bit < planes:
            k = k + bit * ((dz // bit + z // bit) % 2)
            bit *= 2
        return far, k

    def load(b):
        return pltpu.make_async_copy(images.at[b], grad_zed.at[b], in_sem.at[0, b])

    def load_top(b):
        return pltpu.make_async_copy(cotangent.at[b], total.at[b], in_sem.at[1, b])

    def reload_image(b):
        return pltpu.make_async_copy(images.at[b], mid.at[b], in_sem.at[3, b])

    for b in range(count):
        load_top(b).start()
    for b in range(count):
        load(b).start()
    small_own[...] = jnp.zeros_like(small_own)
    for i in range(lines_in):
        at, lane = (i, 0) if i < first_lines else (i - first_lines, 64)
        small_own[at : at + 1, lane : lane + unit] = tin_own[i * unit : (i + 1) * unit].reshape(1, unit)
    for i, piece in enumerate((gain_one_own, shift_one_own, gain_two_own, shift_two_own, c_four_own)):
        small_own[24 + i : 25 + i, 64 : 64 + own_vec] = piece[...].reshape(1, own_vec)
    small_own[31:32, 0:shard] = c_in_own[...].reshape(1, shard)
    for i in range(lines_out):
        line = tout_own[i * patches : (i + 1) * patches].reshape(1, patches)
        small_own[32 + i : 33 + i, :] = line[:, 0:128]
        small_own[48 + i : 49 + i, 0 : patches - 128] = line[:, 128:patches]
    for group in range(2):
        small_all[group, 0, 0] = small_own[32 * group : 32 * (group + 1)].astype(LOW)
    weights[0, 0, 0:shard] = w_in[...].astype(LOW)
    weights[1, 0, 0:shard] = w_out[...].astype(LOW)

    barrier = pltpu.get_barrier_semaphore()
    peers = [by_core, by_x, by_y, by_both] + [by_z(k) for k in range(1, planes)]
    for peer in peers:
        pl.semaphore_signal(barrier, inc=1, device_id=(peer,), device_id_type=MESH)
    pl.semaphore_wait(barrier, len(peers))

    mats = (0, 1)
    inner = middle == 1

    def ag_half(stage, k, part, mat):
        near, far = (by_x, by_y) if mat == 0 else (by_y, by_x)
        step = 1 if mat == 0 else 2
        if stage == 0:
            src, dst, to = 0, 0, by_z(k)
        else:
            src, dst, to = ((0, step, near), (0, 3 - step, far), (step, 3, far))[stage - 1]
        rows = shard // 2
        first = part * rows
        at = (k - 1) // 2 if stage == 0 else 1 + stage
        return pltpu.make_async_remote_copy(
            src_ref=weights.at[mat, 0 if stage == 0 else k, pl.ds(src * shard + first, rows)],
            dst_ref=weights.at[mat, k, pl.ds(dst * shard + first, rows)],
            send_sem=ah_send.at[at, part, mat],
            recv_sem=ah_recv.at[at, part, mat],
            device_id=(to,),
            device_id_type=MESH,
        )

    def first_direct(part):
        k = plane_at(0)
        for mat in mats:
            ag_half(0, k, part, mat).wait_recv()
        for mat in mats:
            ag_half(1, k, part, mat).start()

    def first_far(part):
        for mat in mats:
            ag_half(2, plane_at(0), part, mat).start()

    def first_forward(part):
        for mat in mats:
            ag_half(1, plane_at(0), part, mat).wait_recv()
            ag_half(3, plane_at(0), part, mat).start()

    def first_core():
        k = plane_at(0)
        for mat in mats:
            for part in range(2):
                ag_half(2, k, part, mat).wait_recv()
            ag(4, k, mat).start()

    def first_core_last():
        k = plane_at(0)
        for mat in mats:
            for part in range(2):
                ag_half(3, k, part, mat).wait_recv()
            ag(5, k, mat).start()

    def ag_pass(which, mat):
        src, dst, to = ((1, 2, by_z(3)), (3, 2, by_z(1)), (2, 3, by_z(1)))[which]
        return pltpu.make_async_remote_copy(
            src_ref=weights.at[mat, src, pl.ds(0, shard)],
            dst_ref=weights.at[mat, dst, pl.ds(0, shard)],
            send_sem=ag_send.at[6, which, mat],
            recv_sem=ag_recv.at[0, dst, mat],
            device_id=(to,),
            device_id_type=MESH,
        )

    def ag_planes():
        for part in range(2):
            for mat in mats:
                ag_half(0, 1, part, mat).start()

            @pl.when(inner)
            def _():
                for mat in mats:
                    ag_half(0, 3, part, mat).start()

    def ag_planes_pass():
        @pl.when(inner)
        def _():
            for mat in mats:
                for part in range(2):
                    ag_half(0, 1, part, mat).wait_recv()
                ag_pass(0, mat).start()
            for mat in mats:
                ag_pass(1, mat).start()

    def ag_planes_last():
        @pl.when(inner)
        def _():
            for mat in mats:
                ag(0, 2, mat).wait_recv()
                ag_pass(2, mat).start()

    def ag_direct(k):
        @pl.when(jnp.logical_not(inner))
        def _():
            for mat in mats:
                ag(0, k, mat).wait_recv()

        for stage in (1, 2):
            for mat in mats:
                ag(stage, k, mat).start()

    def ag_forward(k):
        for mat in mats:
            ag(1, k, mat).wait_recv()
            ag(3, k, mat).start()

    def ag_core(k):
        for mat in mats:
            ag(2, k, mat).wait_recv()
            ag(4, k, mat).start()

    def ag_core_last(k):
        for mat in mats:
            ag(3, k, mat).wait_recv()
            ag(5, k, mat).start()

    def ag_ready(k):
        for mat in mats:
            ag(4, k, mat).wait_recv()
            ag(5, k, mat).wait_recv()

    for group in range(2):
        for k in range(1, planes):
            small_gather(0, k, group).start()
    for mat in mats:
        ag(1, 0, mat).start()
    ag_planes()

    grad_vecs[...] = jnp.zeros_like(grad_vecs)
    grad_tin[...] = jnp.zeros_like(grad_tin)
    grad_tout[...] = jnp.zeros_like(grad_tout)

    def channel_top(r, carry):
        tops = []
        for h in range(2):
            b = 2 * r + h
            load_top(b).wait()
            tops.append(padded(total[b] * mask[b].astype(WIDE), lot))
        rounded = jnp.concatenate(tops, axis=0).astype(LOW)
        top[pl.ds(r * pair, pair), :] = rounded
        grad_vecs[2:3, :] += jnp.sum(rounded.astype(WIDE), axis=0, keepdims=True)
        return carry

    def first_norm(b, carry):
        load(b).wait()
        mid[b], figures[b, :, 0:1], figures[b, :, 1:2] = norm_parts(grad_zed[b])
        return carry

    lax.fori_loop(0, blocks, channel_top, 0)
    for group in range(2):
        for k in range(1, planes):
            small_gather(0, k, group).wait_recv()
        for k in range(1, 4):
            small_gather(1, k, group).start()
    lax.fori_loop(0, count, first_norm, 0)
    for k in range(1, 4):
        small_gather(1, k, 0).wait_recv()
    small_gather(2, 0, 0).start()
    first_direct(0)
    first_far(0)

    tin[...] = jnp.zeros_like(tin)
    tout[...] = jnp.zeros_like(tout)

    def unpack(d, group):
        far, k = place_of(d)
        message = small_all[group, far, k].astype(WIDE)
        if group == 0:
            lines[d * lines_in : d * lines_in + first_lines, :] = message[0:first_lines, :]
            shifted = jnp.concatenate([message[0:24, 64:128], message[0:24, 0:64]], axis=1)
            lines[d * lines_in + first_lines : (d + 1) * lines_in, :] = shifted[0 : lines_in - first_lines, :]
            vecs[:, d * own_vec : (d + 1) * own_vec] = message[24:32, 64 : 64 + own_vec]
            c_in[d] = message[31:32, 0:shard]
        else:
            tout[d * lines_out : (d + 1) * lines_out, 0:128] = message[0:lines_out, :]
            tout[d * lines_out : (d + 1) * lines_out, 128:patches] = message[16 : 16 + lines_out, 0 : patches - 128]

    def unpack_half(own, group):
        for parity in range(2):

            @pl.when((core == parity) == own)
            def _():
                for d in range(parity, devices, 2):
                    unpack(d, group)

    unpack_half(True, 0)
    for k in range(1, 4):
        small_gather(1, k, 1).wait_recv()
    small_gather(2, 0, 1).start()
    unpack_half(True, 1)
    first_direct(1)
    ag_planes_pass()
    for group in range(2):
        small_gather(2, 0, group).wait_recv()
        unpack_half(False, group)
    for turn in range(turns):
        tin[0:patches, turn * unit : (turn + 1) * unit] = lines[pl.ds(turn, patches, stride=turns), :][:, 0:unit]
    for rest, into, at in ((c_one, tin, patches), (c_two, tout, hidden_tok)):
        rest = rest[...].reshape(1, rest.shape[0])
        for i in range(3):
            term = rest.astype(LOW).astype(WIDE)
            into[at + i : at + i + 1, 0 : rest.shape[1]] = term
            rest = rest - term
    tin_t[...] = tin[...].T.astype(LOW)
    tout_t[...] = tout[...].T.astype(LOW)
    ones = jnp.ones((3, width), WIDE)

    gain_one, shift_one = vecs[0:1, :], vecs[1:2, :]
    gain_two, shift_two, c_four = vecs[2:3, :], vecs[3:4, :], vecs[4:5, :]
    def singles(work, start, stop):
        def one(b, carry):
            work(b)
            return carry

        lax.fori_loop(start, stop, one, 0)

    def pairs(work, start, stop):
        def two(r, carry):
            for h in range(2):
                work(2 * r + h)
            return carry

        lax.fori_loop(start // 2, stop // 2, two, 0)

    def token_forward(b):
        fed = mid[b] * gain_one + shift_one
        mixed[b] = padded(jnp.concatenate([fed, ones], axis=0), pad).astype(LOW)
        value, slope = gelu_parts(dot(tin_t[...], mixed[b], NN))
        act_t[b] = padded(jnp.concatenate([value, ones], axis=0), act_t.shape[1]).astype(LOW)
        slope_t[b] = slope.astype(LOW)
        mid[b] = grad_zed[b] + dot(tout_t[...], act_t[b], NN)[0:patches]

    def channel_inputs(r, carry):
        parts = []
        for h in range(2):
            total[2 * r + h] = mid[2 * r + h] + c_four
            normed, _, figures[2 * r + h, :, 2:3] = norm_parts(mid[2 * r + h])
            mid[2 * r + h] = normed
            grad_zed[2 * r + h] = jnp.zeros((patches, width), WIDE)
            parts.append(padded(normed * gain_two + shift_two, lot))
        zed[pl.ds(r * pair, pair), :] = jnp.concatenate(parts, axis=0).astype(LOW)
        return carry

    first = 3
    first_forward(0)
    first_far(1)
    singles(token_forward, 0, first)
    first_forward(1)
    singles(token_forward, first, count)
    first_core()
    ag_planes_last()
    ag_direct(plane_at(1))
    lax.fori_loop(0, blocks, channel_inputs, 0)
    first_core_last()
    for k in range(planes):
        for place in range(PLANE):
            near = plane_of(k) * PLANE + (
                (row + (place // 2) % 2) % 2 * 4 + (col + place % 2) % 2 * 2 + (core + place // 4) % 2
            )
            c_in_rel[k, :, place * shard : (place + 1) * shard] = c_in[near]


    def rs_two(i, mat):
        rs(0, i, mat).wait_recv()
        slot = i % 2
        first, second = (1, 3) if mat == 0 else (2, 3)

        def part(n):
            return slice(n * shard, (n + 1) * shard)

        @pl.when(i == 0)
        def _():
            weights[mat, plane_at(i), 0:half] = (own_sum[mat] + recv_one[slot, mat].astype(WIDE)).astype(LOW)
            rs(4, 0, mat).start()

        @pl.when((i == planes - 1) & inner)
        def _():
            own_sum[mat] += came_from(4, 1, mat) + came_from(4, 3, mat)

        @pl.when(i > 1)
        def _():
            for stage in (1, 5):
                rs(stage, i - 1, mat).wait_send()

        @pl.when(i > 0)
        def _():
            for n, to, stage in ((second, part(1), 1), (first, part(0), 5)):
                send_two[mat, to] = (own_sum[mat, part(n)] + recv_one[slot, mat, part(n)].astype(WIDE)).astype(LOW)
                rs(stage, i, mat).start()
            for n in (0, 3 - first):
                own_sum[mat, part(n)] += recv_one[slot, mat, part(n)].astype(WIDE)

    def rs_three(i):
        for mat in mats:
            rs(1, i, mat).wait_recv()
            other = 2 if mat == 0 else 1

            @pl.when(i > 1)
            def _():
                rs(2, i - 1, mat).wait_send()

            send_three[mat] = (
                own_sum[mat, other * shard : (other + 1) * shard]
                + recv_two[i % 2, mat, shard : 2 * shard].astype(WIDE)
            ).astype(LOW)
            rs(2, i, mat).start()

    def rs_keep(i):
        for mat in mats:
            rs(5, i, mat).wait_recv()
            keep_sum[mat] = own_sum[mat, 0:shard] + recv_two[i % 2, mat, 0:shard].astype(WIDE)

    def rs_four(i):
        for mat in mats:
            rs(2, i, mat).wait_recv()

            send_four[i % 2, mat] = (keep_sum[mat] + recv_three[i % 2, mat].astype(WIDE)).astype(LOW)
            rs(3, i, mat).start()

    def rs_last():
        last = planes - 1
        for mat in mats:
            result = grad_in if mat == 0 else grad_out
            rs(2, last, mat).wait_recv()
            summed = keep_sum[mat] + recv_three[last % 2, mat].astype(WIDE)
            result[...] = summed + came_from(3, 2, mat)

            @pl.when(jnp.logical_not(inner))
            def _():
                result[...] += came_from(3, 1, mat) + came_from(3, 3, mat)


    tile = chunk // 3

    def channel_chunk(i, carry):
        k = plane_at(i)

        @pl.when(i == planes - 1)
        def _():
            rs_four(1)

        ag_ready(k)

        def rows(r):
            for s in range(3):
                part = slice(s * tile, (s + 1) * tile)
                pre = dot(zed[r * pair : (r + 1) * pair, :], weights[0, k, part], NT) + c_in_rel[k, :, part]
                value, slope = gelu_parts(pre)
                act[r * pair : (r + 1) * pair, part] = value.astype(LOW)
                back = (dot(top[r * pair : (r + 1) * pair, :], weights[1, k, part], NT) * slope).astype(LOW)
                grad_pre[r * pair : (r + 1) * pair, part] = back
            up = dot(act[r * pair : (r + 1) * pair, :], weights[1, k], NN)
            down = dot(grad_pre[r * pair : (r + 1) * pair, :], weights[0, k], NN)
            for h in range(2):
                total[2 * r + h] += up[h * lot : h * lot + patches]
                grad_zed[2 * r + h] += down[h * lot : h * lot + patches]

        rows(0)

        @pl.when(i == 0)
        def _():
            ag_forward(plane_at(1))

        @pl.when(i == 1)
        def _():
            for mat in mats:
                rs_two(i - 1, mat)
            ag_forward(plane_at(2))
            ag_forward(0)

        for r in range(1, blocks):
            rows(r)

        @pl.when(i == 0)
        def _():
            ag_core(plane_at(1))
            ag_direct(plane_at(2))
            for mat in mats:
                ag(2, 0, mat).start()

        @pl.when(i == 1)
        def _():
            ag_core(plane_at(2))

        @pl.when(i == 2)
        def _():
            ag_core(0)
            ag_core_last(0)

        @pl.when(i > 1)
        def _():
            rs_three(i - 1)

        @pl.when(i > 0)
        def _():
            for mat in mats:
                rs(0, i - 1, mat).wait_send()

        back_sum = jnp.sum(grad_pre[...].astype(WIDE), axis=0, keepdims=True)
        for place in range(PLANE):
            near = plane_of(k) * PLANE + (
                (row + (place // 2) % 2) % 2 * 4 + (col + place % 2) % 2 * 2 + (core + place // 4) % 2
            )
            grad_c_in[near] = back_sum[:, place * shard : (place + 1) * shard]
        send_one[1] = dot(act[:, half:chunk], top[...], TN).astype(LOW)
        send_one[0] = dot(grad_pre[:, half:chunk], zed[...], TN).astype(LOW)
        for mat in mats:
            rs(0, i, mat).start()

        @pl.when(i > 1)
        def _():
            rs_keep(i - 1)

        @pl.when(i == 0)
        def _():
            for mat in mats:
                for stage in (4, 5):
                    ag(stage, k, mat).wait_send()
                for stage in range(1, 4):
                    for part in range(2):
                        ag_half(stage, k, part, mat).wait_send()

                @pl.when(inner)
                def _():
                    ag_pass(1, mat).wait_send()

        own_sum[1] = dot(act[:, 0:half], top[...], TN)
        own_sum[0] = dot(grad_pre[:, 0:half], zed[...], TN)
        @pl.when(i < 2)
        def _():
            ag_core_last(plane_at(i + 1))

        @pl.when(i > 0)
        def _():
            for mat in mats:
                rs_two(i, mat)

        return carry

    lax.fori_loop(0, planes, channel_chunk, 0)

    tin_low = tin[...].astype(LOW)
    tout_low = tout[0:hidden_tok, :].astype(LOW)

    def kept(b):
        return weights.at[b // planes, b % planes, 0:pad]

    def middle_backward(b, above):
        normed = mid[b]
        down = grad_zed[b]
        grad_vecs[0:1, :] += jnp.sum(down * normed, axis=0, keepdims=True)
        grad_vecs[1:2, :] += jnp.sum(down, axis=0, keepdims=True)
        grad_mid = above + norm_back(down, normed, figures[b, :, 2:3], gain_two)
        grad_zed[b] = grad_mid
        back = padded(grad_mid, pad).astype(LOW)
        grad_tout[...] += dot(act_t[b], back, NT)
        slope_t[b] = (dot(tout_low, back, NN) * slope_t[b].astype(WIDE)).astype(LOW)
        grad_tin[:, 0:hidden_tok] += dot(mixed[b], slope_t[b], NT)

    def middle_pair(r, carry):
        above = top[pl.ds(r * pair, pair), :].astype(WIDE)
        for h in range(2):
            middle_backward(2 * r + h, above[h * lot : h * lot + patches])
        for h in range(2):
            reload_image(2 * r + h).start()
        return carry

    def image_norm(b):
        normed = (mid[b] - figures[b, :, 0:1]) * figures[b, :, 1:2]
        mid[b] = normed
        grad_mixed = dot(tin_low, slope_t[b], NN)
        kept(b)[...] = grad_mixed.astype(LOW)
        late[0, 0:1, :] += jnp.sum(grad_mixed[0:patches] * normed, axis=0, keepdims=True)
        late[0, 1:2, :] += jnp.sum(grad_mixed[0:patches], axis=0, keepdims=True)

    def image_backward(b):
        total[b] *= mask[b].astype(WIDE)
        grad_zed[b] += norm_back(kept(b)[...][0:patches].astype(WIDE), mid[b], figures[b, :, 1:2], gain_one)

    def small_first(group):
        for k in range(1, planes):
            small_gather(0, k, group).wait_send()
        for far in range(1, 4):
            small_gather(1, far, group).wait_send()
        small_gather(2, 0, group).wait_send()
        if group == 0:
            for turn in range(turns):
                lines[pl.ds(turn, patches, stride=turns), :] = grad_tin[0:patches, turn * unit : turn * unit + 128]
        for d in range(devices):
            far, k = place_of(d)
            message = small_sum.at[group, far, k]
            if group == 0:
                low = lines[d * lines_in : d * lines_in + first_lines, :]
                high = lines[d * lines_in + first_lines : (d + 1) * lines_in, :]
                message[0:first_lines, 0:64] = low[:, 0:64]
                message[0 : lines_in - first_lines, 64:128] = high[:, 0:64]
                message[24:27, 64 : 64 + own_vec] = grad_vecs[0:3, d * own_vec : (d + 1) * own_vec]
                message[31:32, 0:shard] = grad_c_in[d]
            else:
                message[0:lines_out, :] = grad_tout[d * lines_out : (d + 1) * lines_out, 0:128]
                message[16 : 16 + lines_out, 0 : patches - 128] = grad_tout[
                    d * lines_out : (d + 1) * lines_out, 128:patches
                ]
        for far in range(4, PLANE):
            small_all[group, far] = small_sum[group, far].astype(LOW)
        small_reduce(0, 0, group).start()
        if group == 0:
            biases[0] = jnp.zeros_like(biases[0])
            for i in range(hidden_tok // 128):
                biases[0, i : i + 1, :] = grad_tin[patches : patches + 1, i * 128 : (i + 1) * 128]
            biases[0, 3:4, :] = grad_tout[hidden_tok : hidden_tok + 1, 0:128]
            biases[0, 4:5, 0 : patches - 128] = grad_tout[hidden_tok : hidden_tok + 1, 128:patches]
            bias_reduce(0, 0).start()

    def small_second(group):
        small_reduce(0, 0, group).wait_recv()
        for far in range(4):
            small_sum[group, far] += small_core[group, far].astype(WIDE)
        for far in range(1, 4):
            small_all[group, far] = small_sum[group, far].astype(LOW)
            small_reduce(1, far, group).start()
        if group == 0:
            bias_reduce(0, 0).wait_recv()
            biases[1] = biases[0] + biases_in[0, 0]
            for far in range(1, 4):
                bias_reduce(1, far).start()

    def small_third(group):
        for far in range(1, 4):
            small_reduce(1, far, group).wait_recv()
            small_sum[group, 0] += small_plane[group, far].astype(WIDE)
        for k in range(1, planes):
            small_all[group, 0, k] = small_sum[group, 0, k].astype(LOW)
            small_reduce(2, k, group).start()
        if group == 0:
            for far in range(1, 4):
                bias_reduce(1, far).wait_recv()
            biases[2] = (biases[1] + biases_in[1, 1]) + (biases_in[1, 2] + biases_in[1, 3])
            for k in range(1, planes):
                bias_reduce(2, k).start()

    for mat in mats:
        for i in range(1, planes):
            for stage in range(1, 6):
                ag(stage, plane_at(i), mat).wait_send()
        for part in range(2):
            ag_half(0, 1, part, mat).wait_send()
        rs(4, 0, mat).wait_send()

        @pl.when(inner)
        def _():
            for part in range(2):
                ag_half(0, 3, part, mat).wait_send()
            for which in (0, 2):
                ag_pass(which, mat).wait_send()

    late[0] = jnp.zeros_like(late[0])
    rs_four(planes - 2)
    lax.fori_loop(0, blocks, middle_pair, 0)
    small_first(1)
    small_first(0)
    for b in range(count):
        reload_image(b).wait()
    pairs(image_norm, 0, 2)
    small_second(1)
    pairs(image_norm, 2, count)
    small_second(0)
    late_reduce(0, 0).start()
    pairs(image_backward, 0, 2)
    late_reduce(0, 0).wait_recv()
    late[1] = late[0] + late_in[0, 0]
    for far in range(1, 4):
        late_reduce(1, far).start()
    rs_three(planes - 1)
    rs_keep(planes - 1)
    small_third(1)
    pairs(image_backward, 2, count)
    small_third(0)
    late_sum = late[1]
    for far in range(1, 4):
        late_reduce(1, far).wait_recv()
        late_sum = late_sum + late_in[1, far]
    late[2] = late_sum
    for k in range(1, planes):
        late_reduce(2, k).start()
    rs_last()
    summed = [small_sum[group, 0, 0] for group in range(2)]
    tree = [biases[2]]
    for k in range(1, planes):
        for group in range(2):
            small_reduce(2, k, group).wait_recv()
        bias_reduce(2, k).wait_recv()
        summed = [summed[group] + small_z[k, group].astype(WIDE) for group in range(2)]
        tree.append(biases_in[2, k])
    for group in range(2):
        small_out[32 * group : 32 * (group + 1)] = summed[group]
    for k in range(1, planes):
        late_reduce(2, k).wait_recv()
        late_sum = late_sum + late_in[2, k]
    late_sum = pltpu.roll(padded(late_sum, 8), width - own_vec * me, 1)
    small_out[27:29, 64 : 64 + own_vec] = late_sum[0:2, 0:own_vec]
    while len(tree) > 1:
        tree = [tree[i] + tree[i + 1] for i in range(0, len(tree), 2)]
    biases_out[...] = tree[0]

    for mat in mats:
        for stage in (0, 1, 2, 5):
            rs(stage, planes - 1, mat).wait_send()
        for i in range(1, planes - 1):
            rs(3, i, mat).wait_send()
    late_reduce(0, 0).wait_send()
    for far in range(1, 4):
        late_reduce(1, far).wait_send()
    for k in range(1, planes):
        late_reduce(2, k).wait_send()
    bias_reduce(0, 0).wait_send()
    for far in range(1, 4):
        bias_reduce(1, far).wait_send()
    for k in range(1, planes):
        bias_reduce(2, k).wait_send()
    for group in range(2):
        small_reduce(0, 0, group).wait_send()
        for far in range(1, 4):
            small_reduce(1, far, group).wait_send()
        for k in range(1, planes):
            small_reduce(2, k, group).wait_send()


def finish_kernel(
    block_in,
    image_in,
    w_in,
    w_out,
    small,
    biases,
    block_out,
    image_out,
    w_in_out,
    w_out_out,
    tin,
    tout,
    gain_one,
    shift_one,
    gain_two,
    shift_two,
    c_four,
    c_in,
    c_one,
    c_two,
    sem,
):
    pieces = [(block_in.at[b], block_out.at[b]) for b in range(block_in.shape[0])]
    pieces += [(image_in.at[b], image_out.at[b]) for b in range(image_in.shape[0])]
    pieces += [(w_in, w_in_out), (w_out, w_out_out)]
    copies = [pltpu.make_async_copy(a, b, sem.at[i]) for i, (a, b) in enumerate(pieces)]
    for copy in copies:
        copy.start()
    hidden_tok, patches = c_one.shape[0], c_two.shape[0]
    unit = math.gcd(tin.shape[0], hidden_tok)
    lines_in = tin.shape[0] // unit
    first_lines = (lines_in + 1) // 2
    for i in range(lines_in):
        at, lane = (i, 0) if i < first_lines else (i - first_lines, 64)
        tin[i * unit : (i + 1) * unit] = small[at : at + 1, lane : lane + unit].reshape(unit)
    for i in range(tout.shape[0] // patches):
        tout[i * patches : i * patches + 128] = small[32 + i : 33 + i, :].reshape(128)
        tout[i * patches + 128 : (i + 1) * patches] = small[48 + i : 49 + i, 0 : patches - 128].reshape(
            patches - 128
        )
    for i, piece in enumerate((gain_two, shift_two, c_four, gain_one, shift_one)):
        own_vec = piece.shape[0]
        piece[...] = small[24 + i : 25 + i, 64 : 64 + own_vec].reshape(own_vec)
    shard = c_in.shape[0]
    c_in[...] = small[31:32, 0:shard].reshape(shard)
    for i in range(hidden_tok // 128):
        c_one[i * 128 : (i + 1) * 128] = biases[i : i + 1, :].reshape(128)
    c_two[0:128] = biases[3:4, :].reshape(128)
    c_two[128:patches] = biases[4:5, 0 : patches - 128].reshape(patches - 128)
    for copy in copies:
        copy.wait()


def fast_shards(
    images,
    mask,
    cotangent,
    w_token_in,
    w_token_out,
    bias_token_in,
    bias_token_out,
    gain_one,
    shift_one,
    gain_two,
    shift_two,
    w_expand,
    bias_expand,
    w_reduce,
    bias_reduce,
):
    devices = lax.axis_size("dp")
    planes = devices // PLANE
    count, patches, width = images.shape
    hidden_tok = bias_token_in.shape[0]
    shard = w_expand.shape[0]
    pad = -(-patches // 16) * 16
    lot = -(-patches // 8) * 8
    pair = 2 * lot
    blocks = count // 2
    chunk = 8 * shard
    half = 4 * shard

    unit = math.gcd(w_token_in.shape[0], hidden_tok)
    lines_in = w_token_in.shape[0] // unit
    hidden_pad = hidden_tok + 16

    owned = (
        w_expand,
        w_reduce,
        w_token_in,
        w_token_out,
        gain_one,
        shift_one,
        gain_two,
        shift_two,
        bias_reduce,
        bias_expand,
        bias_token_in,
        bias_token_out,
    )
    vmem = pl.BlockSpec(memory_space=pltpu.VMEM)
    hbm = pl.BlockSpec(memory_space=pl.ANY)
    shape = jax.ShapeDtypeStruct
    outs = pl.pallas_call(
        block_kernel,
        out_shape=(
            pltpu.VMEM(images.shape, WIDE),
            pltpu.VMEM(images.shape, WIDE),
            pltpu.VMEM(w_expand.shape, WIDE),
            pltpu.VMEM(w_reduce.shape, WIDE),
            pltpu.VMEM((64, 128), WIDE),
            pltpu.VMEM((8, 128), WIDE),
        ),
        in_specs=[pl.BlockSpec(memory_space=pltpu.SMEM), hbm, hbm] + [vmem] * 12,
        out_specs=[vmem] * 6,
        scratch_shapes=[
            pltpu.VMEM((count, pad, width), LOW),
            pltpu.VMEM((count, hidden_pad, width), LOW),
            pltpu.VMEM((count, hidden_tok, width), LOW),
            pltpu.VMEM(images.shape, WIDE),
            pltpu.VMEM((blocks * pair, width), LOW),
            pltpu.VMEM((blocks * pair, width), LOW),
            pltpu.VMEM((2, planes, chunk, width), LOW),
            pltpu.VMEM((blocks * pair, chunk), LOW),
            pltpu.VMEM((blocks * pair, chunk), LOW),
            pltpu.VMEM((planes, 1, chunk), WIDE),
            pltpu.VMEM((2, half, width), WIDE),
            pltpu.VMEM((2, shard, width), WIDE),
            pltpu.VMEM((2, half, width), LOW),
            pltpu.VMEM((2, 2, half, width), LOW),
            pltpu.VMEM((2, 2 * shard, width), LOW),
            pltpu.VMEM((2, 2, 2 * shard, width), LOW),
            pltpu.VMEM((2, shard, width), LOW),
            pltpu.VMEM((2, 2, shard, width), LOW),
            pltpu.VMEM((2, 2, shard, width), LOW),
            pltpu.VMEM((planes - 1, 2, shard, width), LOW),
            pltpu.VMEM((2, 2, half, width), LOW),
            pltpu.VMEM((pad, hidden_tok), WIDE),
            pltpu.VMEM((hidden_tok, pad), LOW),
            pltpu.VMEM((hidden_pad, pad), WIDE),
            pltpu.VMEM((pad, hidden_pad), LOW),
            pltpu.VMEM((8, width), WIDE),
            pltpu.VMEM((devices, 1, shard), WIDE),
            pltpu.VMEM((devices * lines_in, 128), WIDE),
            pltpu.VMEM((64, 128), WIDE),
            pltpu.VMEM((2, PLANE, planes, 32, 128), LOW),
            pltpu.VMEM((pad, hidden_tok + 128), WIDE),
            pltpu.VMEM((hidden_pad, pad), WIDE),
            pltpu.VMEM((8, width), WIDE),
            pltpu.VMEM((devices, 1, shard), WIDE),
            pltpu.VMEM((2, PLANE, planes, 32, 128), WIDE),
            pltpu.VMEM((2, 4, planes, 32, 128), LOW),
            pltpu.VMEM((2, 4, planes, 32, 128), LOW),
            pltpu.VMEM((planes, 2, 32, 128), LOW),
            pltpu.VMEM((3, 8, 128), WIDE),
            pltpu.VMEM((3, max(4, planes), 8, 128), WIDE),
            pltpu.VMEM((3, 2, width), WIDE),
            pltpu.VMEM((3, max(4, planes), 2, width), WIDE),
            pltpu.VMEM((count, patches, 4), WIDE),
            pltpu.SemaphoreType.DMA((4, count)),
            pltpu.SemaphoreType.DMA((7, planes, 2)),
            pltpu.SemaphoreType.DMA((7, planes, 2)),
            pltpu.SemaphoreType.DMA((5, 2, 2)),
            pltpu.SemaphoreType.DMA((5, 2, 2)),
            pltpu.SemaphoreType.DMA((6, planes, 2)),
            pltpu.SemaphoreType.DMA((6, planes, 2)),
        ]
        + [pltpu.SemaphoreType.DMA((3, max(4, planes), 2))] * 4
        + [pltpu.SemaphoreType.DMA((3, max(4, planes)))] * 4,
        compiler_params=pltpu.CompilerParams(
            collective_id=0, has_side_effects=True, vmem_limit_bytes=56 * 2**20
        ),
    )(
        mask,
        images,
        cotangent,
        *owned,
    )
    flat = pl.pallas_call(
        finish_kernel,
        out_shape=(
            shape(images.shape, WIDE),
            shape(images.shape, WIDE),
            shape(w_expand.shape, WIDE),
            shape(w_reduce.shape, WIDE),
            shape(w_token_in.shape, WIDE),
            shape(w_token_out.shape, WIDE),
            *[shape(gain_one.shape, WIDE)] * 5,
            shape(bias_expand.shape, WIDE),
            shape(bias_token_in.shape, WIDE),
            shape(bias_token_out.shape, WIDE),
        ),
        in_specs=[vmem] * 6,
        out_specs=[hbm] * 4 + [vmem] * 10,
        scratch_shapes=[pltpu.SemaphoreType.DMA((2 * count + 2,))],
        compiler_params=pltpu.CompilerParams(vmem_limit_bytes=16 * 2**20),
    )(*outs)
    block_output, image_grad, own_win, own_wout, *rest = flat
    g_tin, g_tout, g_one, b_one, g_two, b_two, c_four, c_in, c_one, c_two = rest
    return (
        block_output,
        image_grad,
        g_tin,
        g_tout,
        c_one,
        c_two,
        g_one,
        b_one,
        g_two,
        b_two,
        own_win,
        c_in,
        own_wout,
        c_four,
    )


def fits(devices, images, w_token_in, w_token_out, bias_token_in, gain_one, w_expand):
    planes = devices // PLANE
    patches = images.shape[1]
    hidden_tok = bias_token_in.shape[0]
    shard = w_expand.shape[0]
    unit = math.gcd(w_token_in.shape[0], hidden_tok)
    return (
        devices % PLANE == 0
        and planes == 4
        and images.shape[0] % 2 == 0
        and 6 <= images.shape[0] <= 2 * planes
        and shard % 32 == 0
        and shard <= 128
        and (4 * shard) % 128 == 0
        and 128 < patches <= 205
        and unit <= 64
        and w_token_in.shape[0] // unit <= 49
        and w_token_out.shape[0] % patches == 0
        and w_token_out.shape[0] // patches <= 16
        and gain_one.shape[0] <= 64
        and hidden_tok == 384
    )


def choose(
    images,
    mask,
    cotangent,
    w_token_in,
    w_token_out,
    bias_token_in,
    bias_token_out,
    gain_one,
    shift_one,
    gain_two,
    shift_two,
    w_expand,
    bias_expand,
    w_reduce,
    bias_reduce,
):
    args = (
        images,
        mask,
        cotangent,
        w_token_in,
        w_token_out,
        bias_token_in,
        bias_token_out,
        gain_one,
        shift_one,
        gain_two,
        shift_two,
        w_expand,
        bias_expand,
        w_reduce,
        bias_reduce,
    )
    if fits(lax.axis_size("dp"), images, w_token_in, w_token_out, bias_token_in, gain_one, w_expand):
        return fast_shards(*args)
    return shards(*args)


def shards(
    images,
    mask,
    cotangent,
    w_token_in,
    w_token_out,
    bias_token_in,
    bias_token_out,
    gain_one,
    shift_one,
    gain_two,
    shift_two,
    w_expand,
    bias_expand,
    w_reduce,
    bias_reduce,
):
    low_type = jnp.bfloat16
    wide = jnp.float32
    count, patches, width = images.shape
    hidden_tok = bias_token_in.shape[0]
    rows = count * patches
    keep = mask.astype(wide)[:, None, None]
    small_local = (
        w_token_in.astype(low_type),
        w_token_out.astype(low_type),
        gain_one.astype(low_type),
        shift_one.astype(low_type),
        gain_two.astype(low_type),
        shift_two.astype(low_type),
        bias_reduce.astype(low_type),
    )
    channel_local = (
        w_expand.astype(low_type),
        w_reduce.astype(low_type),
        bias_expand.astype(low_type),
    )
    small_all = (
        lax.all_gather(small_local[0], "dp", axis=0, tiled=True),
        lax.all_gather(small_local[1], "dp", axis=0, tiled=True),
        lax.all_gather(small_local[2], "dp", axis=0, tiled=True),
        lax.all_gather(small_local[3], "dp", axis=0, tiled=True),
        lax.all_gather(small_local[4], "dp", axis=0, tiled=True),
        lax.all_gather(small_local[5], "dp", axis=0, tiled=True),
        lax.all_gather(small_local[6], "dp", axis=0, tiled=True),
    )
    tin = small_all[0].reshape(patches, hidden_tok)
    tout = small_all[1].reshape(hidden_tok, patches)
    g_one, b_one, g_two, b_two, c_four = [piece.astype(wide) for piece in small_all[2:]]
    normed_one, scale_one = normalize(images)
    mixed_in = (normed_one * g_one + b_one).astype(low_type)
    pre_t = (
        jnp.einsum("ps,bpd->bsd", tin, mixed_in, preferred_element_type=wide)
        + bias_token_in[None, :, None]
    )
    act_t = gelu_exact(pre_t).astype(low_type)
    middle = (
        images
        + jnp.einsum("sp,bsd->bpd", tout, act_t, preferred_element_type=wide)
        + bias_token_out[None, :, None]
    )
    normed_two, scale_two = normalize(middle.reshape(rows, width))
    zed = (normed_two * g_two + b_two).astype(low_type)
    whole_channel = (
        lax.all_gather(channel_local[0], "dp", axis=0, tiled=True),
        lax.all_gather(channel_local[1], "dp", axis=0, tiled=True),
        lax.all_gather(channel_local[2], "dp", axis=0, tiled=True),
    )
    w_in, w_out, c_in = whole_channel
    pre = (
        jnp.einsum("td,fd->tf", zed, w_in, preferred_element_type=wide) + c_in.astype(wide)[None, :]
    )
    act = gelu_exact(pre).astype(low_type)
    reduced = jnp.dot(act, w_out, preferred_element_type=wide)
    block_output = (middle + (reduced + c_four).reshape(count, patches, width)) * keep
    grad_top = cotangent * keep
    grad_branch = grad_top.reshape(rows, width).astype(low_type)
    grad_c_four = jnp.sum(grad_branch.astype(wide), axis=0)
    small_all = (
        lax.all_gather(small_local[0], "dp", axis=0, tiled=True),
        lax.all_gather(small_local[1], "dp", axis=0, tiled=True),
        lax.all_gather(small_local[2], "dp", axis=0, tiled=True),
        lax.all_gather(small_local[3], "dp", axis=0, tiled=True),
        lax.all_gather(small_local[4], "dp", axis=0, tiled=True),
        lax.all_gather(small_local[5], "dp", axis=0, tiled=True),
        lax.all_gather(small_local[6], "dp", axis=0, tiled=True),
    )
    tin = small_all[0].reshape(patches, hidden_tok)
    tout = small_all[1].reshape(hidden_tok, patches)
    g_one, b_one, g_two, b_two, c_four = [piece.astype(wide) for piece in small_all[2:]]
    whole_channel = (
        lax.all_gather(channel_local[0], "dp", axis=0, tiled=True),
        lax.all_gather(channel_local[1], "dp", axis=0, tiled=True),
        lax.all_gather(channel_local[2], "dp", axis=0, tiled=True),
    )
    w_in, w_out, c_in = whole_channel
    pre = (
        jnp.einsum("td,fd->tf", zed, w_in, preferred_element_type=wide) + c_in.astype(wide)[None, :]
    )
    act = gelu_exact(pre).astype(low_type)
    grad_act = jnp.einsum("td,fd->tf", grad_branch, w_out, preferred_element_type=wide)
    grad_pre = (grad_act * gelu_slope(pre)).astype(low_type)
    grad_zed = jnp.dot(grad_pre, w_in, preferred_element_type=wide)
    grad_in = jnp.einsum("tf,td->fd", grad_pre, zed, preferred_element_type=wide)
    grad_out = jnp.einsum("tf,td->fd", act, grad_branch, preferred_element_type=wide)
    grad_cin = jnp.sum(grad_pre.astype(wide), axis=0)
    grad_zed, grad_win, grad_wout, grad_cin = (grad_zed, grad_in, grad_out, grad_cin)
    grad_g_two = jnp.sum(grad_zed * normed_two, axis=0)
    grad_b_two = jnp.sum(grad_zed, axis=0)
    grad_mid = grad_top + norm_back(grad_zed, normed_two, scale_two, g_two).reshape(
        count, patches, width
    )
    grad_back = grad_mid.astype(low_type)
    grad_c_two = jnp.sum(grad_back.astype(wide), axis=(0, 2))
    grad_tout = jnp.einsum("bsd,bpd->sp", act_t, grad_back, preferred_element_type=wide)
    grad_act_t = jnp.einsum("sp,bpd->bsd", tout, grad_back, preferred_element_type=wide)
    grad_pre_t = (grad_act_t * gelu_slope(pre_t)).astype(low_type)
    grad_c_one = jnp.sum(grad_pre_t.astype(wide), axis=(0, 2))
    grad_tin = jnp.einsum("bpd,bsd->ps", mixed_in, grad_pre_t, preferred_element_type=wide)
    grad_mixed = jnp.einsum("ps,bsd->bpd", tin, grad_pre_t, preferred_element_type=wide)
    grad_g_one = jnp.sum(grad_mixed * normed_one, axis=(0, 1))
    grad_b_one = jnp.sum(grad_mixed, axis=(0, 1))
    image_grad = grad_mid + norm_back(grad_mixed, normed_one, scale_one, g_one)
    bias_sums = lax.psum((grad_c_one, grad_c_two), "dp")
    flat_tin = grad_tin.reshape(patches * hidden_tok)
    flat_tout = grad_tout.reshape(hidden_tok * patches)
    owned = (
        lax.psum_scatter(flat_tin, "dp", scatter_dimension=0, tiled=True),
        lax.psum_scatter(flat_tout, "dp", scatter_dimension=0, tiled=True),
        lax.psum_scatter(grad_g_one, "dp", scatter_dimension=0, tiled=True),
        lax.psum_scatter(grad_b_one, "dp", scatter_dimension=0, tiled=True),
        lax.psum_scatter(grad_g_two, "dp", scatter_dimension=0, tiled=True),
        lax.psum_scatter(grad_b_two, "dp", scatter_dimension=0, tiled=True),
        lax.psum_scatter(grad_win, "dp", scatter_dimension=0, tiled=True),
        lax.psum_scatter(grad_cin, "dp", scatter_dimension=0, tiled=True),
        lax.psum_scatter(grad_wout, "dp", scatter_dimension=0, tiled=True),
        lax.psum_scatter(grad_c_four, "dp", scatter_dimension=0, tiled=True),
    )
    (
        own_tin,
        own_tout,
        own_g_one,
        own_b_one,
        own_g_two,
        own_b_two,
        own_win,
        own_cin,
        own_wout,
        own_c_four,
    ) = owned
    return (
        block_output,
        image_grad,
        own_tin,
        own_tout,
        bias_sums[0],
        bias_sums[1],
        own_g_one,
        own_b_one,
        own_g_two,
        own_b_two,
        own_win,
        own_cin,
        own_wout,
        own_c_four,
    )


def solution(mesh):
    placed = (
        P("dp", None, None),
        P("dp"),
        P("dp", None, None),
        P("dp"),
        P("dp"),
        P(),
        P(),
        P("dp"),
        P("dp"),
        P("dp"),
        P("dp"),
        P("dp", None),
        P("dp"),
        P("dp", None),
        P("dp"),
    )
    return jax.shard_map(
        choose,
        mesh=mesh,
        in_specs=placed,
        out_specs=(
            P("dp", None, None),
            P("dp", None, None),
            P("dp"),
            P("dp"),
            P(),
            P(),
            P("dp"),
            P("dp"),
            P("dp"),
            P("dp"),
            P("dp", None),
            P("dp"),
            P("dp", None),
            P("dp"),
        ),
        check_vma=False,
    )
```
